32 devices in a mesh: fx: 2 (over x), fy: 4 (over z), fz: 4 (over y, core).
Axes of the slice: x: 2, y: 2, z: 4, core: 2. Of those that a mesh axis runs over, the one named last changes fastest.
Arguments:
- density: float32 [16, 32, 512], P('fx', 'fy', 'fz'), may hold values from 0.8 to 1.25
- velocity: float32 [3, 16, 32, 512], P(None, 'fx', 'fy', 'fz'), may hold values from -2 to 2
- pressure: float32 [16, 32, 512], P('fx', 'fy', 'fz'), may hold values from 0.7 to 1.4
- acoustic: float32 [512, 4, 512], P(('fx', 'fy', 'fz')), may hold values from -6 to 6
- sound_speed: float32 [512], P(('fx', 'fy', 'fz')), may hold values from 0.5 to 2
- derivative: float32 [8, 8], replicated, may hold values from -2 to 2
- mode_basis: float32 [8, 8], replicated, may hold values from -2 to 2
- neighbours: int32 [512, 6], P(('fx', 'fy', 'fz')), may hold values from 0 to 511, as said below
- block_owner: int32 [2, 4, 4, 16, 1], P('fx', 'fy', 'fz'), may hold values from 0 to 3; in each aligned block of 16 rows (0 to 15, 16 to 31, ..., all dimensions but the last counted through in order) at most 8 rows name the same one
- block_element: int32 [2, 4, 4, 16], P('fx', 'fy', 'fz'), may hold values from 0 to 15
Outputs:
- flow_state: float32 [5, 16, 32, 512], P(None, 'fx', 'fy', 'fz')
- sound_state: float32 [512, 4, 512], P(('fx', 'fy', 'fz'))
The draws below stay inside these ranges and needn't reach their ends.
Inputs may be any that keep to these rules, and one draw needn't show every extreme that they name: `neighbours`: across faces -x, -y, -z the neighbour of element e lies in e - 16 to e, across faces +x, +y, +z in e to e + 16. `block_owner`: the 16 blocks of one flow device name one fy index at most 8 times.
All inputs are finite; a program needn't handle non-finite values.
Results may differ from the reference program's by a relative error of at most 0.0001.
Values sent between devices are 32-bit elements; how exact they have to be, the bound alone decides.
No kernel may reach another device: no remote copies, remote signals or barrier semaphores. Data moves between devices by JAX's collectives and lax.ppermute only.
A program may use at most 64 MiB of HBM per device.

```python
import math
import jax
import jax.numpy as jnp
import numpy as np
from jax import lax

CX = 8
CY = 8
CZ = 128
NODES = 512
NX = 16
NY = 32
NZ = 512
BLK_DEV = 16
EL_DEV = 16
ELEMS = 512
CAP = 8
N_FX = 2
N_FY = 4
N_FZ = 4


def draw_neighbours(key, part):
    downward = jax.random.randint(jax.random.fold_in(key, 11), (ELEMS, 6), -EL_DEV, 1)
    upward = jax.random.randint(jax.random.fold_in(key, 12), (ELEMS, 6), 0, EL_DEV + 1)
    face_index = jnp.arange(6, dtype=jnp.int32)[None, :]
    is_lower = face_index % 2 == 0
    offsets = jnp.where(is_lower, downward, upward)
    element_index = jnp.arange(ELEMS, dtype=jnp.int32)[:, None]
    second = (element_index >= EL_DEV) & (element_index < 2 * EL_DEV)
    offsets = jnp.where(second, jnp.where(is_lower, -EL_DEV, EL_DEV), offsets)
    forced = (element_index % EL_DEV == 0) & (face_index == 1)
    offsets = jnp.where(forced, EL_DEV, offsets)
    return jnp.clip(element_index + offsets, 0, ELEMS - 1).astype(jnp.int32)


def plant(result, own_key, low, high):
    dims = result.shape
    spot = [jax.random.randint(jax.random.fold_in(own_key, axis), (), 0, dims[axis]) for axis in range(len(dims))]
    result = result.at[tuple(spot)].set(low)
    longest = dims.index(max(dims))
    spot[longest] = (spot[longest] + 1) % dims[longest]
    return result.at[tuple(spot)].set(high)


def block_levels(rng, extent, split, smallest, largest):
    def one(position, parts):
        heights = jax.random.uniform(jax.random.fold_in(jax.random.fold_in(rng, 6), position), (parts,), jnp.float32, smallest / len(split), largest / len(split))
        return jnp.repeat(jnp.exp(heights), extent[position] // parts).reshape((-1,) + (1,) * (len(extent) - position - 1))

    gain = one(*split[0])
    for cut in split[1:]:
        gain = gain * one(*cut)
    return gain


def deal_out(key, own, number, rows, number_of, top, most, skew):
    ranking = jax.random.permutation(key, number_of)
    packed, ordinary = portions_of(number_of, rows * top, most, skew, True), portions_of(number_of, rows * top, most, skew, False)
    places = jnp.arange(number_of)

    def named(lengths, rotation):
        used = int((lengths > 0).sum())
        fixed = max(1, used // 4)
        shifted = fixed + (places - fixed + rotation * (used - fixed)) % max(1, number_of - fixed)
        return jnp.zeros((number_of,), jnp.int32).at[ranking[jnp.where(places < fixed, places, shifted)]].set(jnp.asarray(lengths, jnp.int32))

    lengths = jnp.where(number % 4 == 0, named(packed, number // 4), named(ordinary, number - number // 4 - 1))
    mixed = jax.random.permutation(jax.random.fold_in(own, 3), number_of)
    donor, sink = mixed[0:number_of // 2 * 2:2], mixed[1:number_of // 2 * 2:2]
    margin = jnp.minimum(lengths[donor] - 1, most - lengths[sink]) // 2
    margin = jnp.where((donor == ranking[0]) | (sink == ranking[0]) | (lengths[sink] == 0), 0, jnp.maximum(margin, 0))
    shifted = jax.random.randint(jax.random.fold_in(own, 4), (number_of // 2,), 0, 1 << 20) % (margin + 1)
    lengths = lengths.at[donor].add(-shifted).at[sink].add(shifted)
    members = jnp.searchsorted(jnp.cumsum(lengths), jnp.arange(rows * top), side="right").astype(jnp.int32)
    table = members.reshape(top, rows).T
    table = table[jax.random.permutation(jax.random.fold_in(own, 1), rows)]
    rotation = jax.random.randint(jax.random.fold_in(own, 2), (rows, 1), 0, top)
    return jnp.take_along_axis(table, (jnp.arange(top)[None, :] + rotation) % top, axis=1)


def portions_of(count, total, bound, skew, full):
    portions = [(1 << 20) // math.isqrt(grade ** skew) + 1 for grade in range(1, count + 1)]
    largest = bound if full else min(bound, max(-(-total // count), total * portions[0] // sum(portions)))
    least = 1 if total - largest >= count - 1 else 0
    counts, spare = [largest] + [least] * (count - 1), total - largest - least * (count - 1)
    while spare > 0:
        free = [i for i in range(1, count) if counts[i] < largest] or [i for i in range(1, count) if counts[i] < bound]
        pool, remaining = sum([portions[i] for i in free]), spare
        for i in free:
            addition = min(bound - counts[i], max(1, remaining * portions[i] // pool), spare)
            counts[i] = counts[i] + addition
            spare = spare - addition
    return np.array(counts)


def centred(rng, extent, spread, bound, cuts=(), kind=jnp.bfloat16):
    gain = block_levels(rng, extent, cuts, -0.22, 0.18) if cuts else 1.0
    result = jax.random.normal(rng, extent, jnp.float32) * spread * gain
    return jnp.minimum(jnp.maximum(result, -bound), bound).astype(kind)


def setup_inputs(seed: int = 0) -> dict:
    arg_keys = jax.random.split(jax.random.key(seed), 11)
    density = jnp.clip(jnp.exp(math.log(1.25) - 0.4462871 * jax.random.uniform(arg_keys[0], (NX, NY, NZ), jnp.float32) ** block_levels(arg_keys[0], (NX, NY, NZ), ((0, 2), (1, 4), (2, 4)), -0.2, 0.2)), 0.8, 1.25)
    velocity = centred(arg_keys[1], (3, NX, NY, NZ), 0.5, 2.0, ((1, 2), (2, 4), (3, 4)), jnp.float32)
    pressure = jnp.clip(jnp.exp(math.log(1.4) - 0.6931472 * jax.random.uniform(arg_keys[2], (NX, NY, NZ), jnp.float32) ** block_levels(arg_keys[2], (NX, NY, NZ), ((0, 2), (1, 4), (2, 4)), -0.2, 0.2)), 0.7, 1.4)
    acoustic = centred(arg_keys[3], (ELEMS, 4, NODES), 1.0, 6.0, ((0, 32),), jnp.float32)
    sound_speed = jnp.clip(jnp.exp(math.log(2.0) - 1.3862944 * jax.random.uniform(arg_keys[4], (ELEMS,), jnp.float32) ** block_levels(arg_keys[4], (ELEMS,), ((0, 32),), -0.2, 0.2)), 0.5, 2.0)
    derivative = centred(arg_keys[5], (8, 8), 8 ** -0.5, 2.0, (), jnp.float32)
    mode_basis = centred(arg_keys[6], (8, 8), 8 ** -0.5, 2.0, (), jnp.float32)
    neighbours = draw_neighbours(jax.random.fold_in(arg_keys[10], 71), 0)
    block_owner_keys = jax.random.split(jax.random.fold_in(arg_keys[8], 1), N_FX * N_FY * N_FZ * BLK_DEV // BLK_DEV)
    block_owner_turns = jax.random.permutation(jax.random.fold_in(arg_keys[8], 3), N_FX * N_FY * N_FZ * BLK_DEV // BLK_DEV)
    block_owner = jax.vmap(lambda own, number: deal_out(jax.random.fold_in(arg_keys[8], 2), own, number, BLK_DEV, N_FY, 1, CAP, 2))(block_owner_keys, block_owner_turns).reshape((N_FX, N_FY, N_FZ, BLK_DEV, 1))
    block_element = plant(jax.random.randint(arg_keys[9], (N_FX, N_FY, N_FZ, BLK_DEV), 0, EL_DEV), jax.random.fold_in(arg_keys[9], 1), 0, EL_DEV - 1).astype(jnp.int32)
    return dict(density=density, velocity=velocity, pressure=pressure, acoustic=acoustic, sound_speed=sound_speed, derivative=derivative, mode_basis=mode_basis, neighbours=neighbours, block_owner=block_owner, block_element=block_element)


HEAT_RATIO = 1.4
TIME_STEP = 0.1
VISCOSITY = 0.05
PENALTY = 0.5
HIGHEST = lax.Precision.HIGHEST

def cut_range(values, along, start_at, stop_at):
    return lax.slice_in_dim(values, start_at, stop_at, axis=along + 1)

def interior(padded, along):
    for other in range(3):
        if other != along:
            padded = cut_range(padded, other, 1, padded.shape[other + 1] - 1)
    return padded

def flow_section(padded):
    center = padded[:, 1:-1, 1:-1, 1:-1]
    velocity_mid = center[1:4] / center[0]
    flow_rate = jnp.zeros_like(center)
    laplace = jnp.zeros_like(velocity_mid)
    slopes = []
    for along in range(3):
        stripe = interior(padded, along)
        length = stripe.shape[along + 1]
        velocity_cells = stripe[1:4] / stripe[0]
        pressure_cells = (HEAT_RATIO - 1.0) * (stripe[4] - 0.5 * lax.optimization_barrier(jnp.sum(stripe[1:4] * velocity_cells, 0)))
        signal_speed = (jnp.abs(velocity_cells[along]) + jnp.sqrt(HEAT_RATIO * jnp.abs(pressure_cells) / stripe[0]))[None]
        unit_axis = (jnp.arange(3) == along).astype(jnp.float32)
        momentum_flux = stripe[1:4] * velocity_cells[along] + unit_axis[:, None, None, None] * pressure_cells
        fluxes = jnp.concatenate([stripe[1 + along][None], momentum_flux, ((stripe[4] + pressure_cells) * velocity_cells[along])[None]], 0)
        wave_speed = jnp.maximum(cut_range(signal_speed, along, 0, length - 1), cut_range(signal_speed, along, 1, length))
        face_flux = 0.5 * (cut_range(fluxes, along, 0, length - 1) + cut_range(fluxes, along, 1, length)) - 0.5 * wave_speed * (cut_range(stripe, along, 1, length) - cut_range(stripe, along, 0, length - 1))
        flow_rate = flow_rate - (cut_range(face_flux, along, 1, length - 1) - cut_range(face_flux, along, 0, length - 2))
        laplace = laplace + cut_range(stripe[1:4], along, 2, length) + cut_range(stripe[1:4], along, 0, length - 2) - 2.0 * center[1:4]
        slopes.append(0.5 * (cut_range(velocity_cells, along, 2, length) - cut_range(velocity_cells, along, 0, length - 2)))
    empty_row = jnp.zeros_like(center[:1])
    flow_rate = flow_rate + VISCOSITY * jnp.concatenate([empty_row, laplace, empty_row], 0)
    vorticity = jnp.stack([slopes[1][2] - slopes[2][1], slopes[2][0] - slopes[0][2], slopes[0][1] - slopes[1][0]])
    lamb_vector = jnp.stack([vorticity[1] * velocity_mid[2] - vorticity[2] * velocity_mid[1], vorticity[2] * velocity_mid[0] - vorticity[0] * velocity_mid[2], vorticity[0] * velocity_mid[1] - vorticity[1] * velocity_mid[0]])
    return (flow_rate, lamb_vector)

def conserved(density, velocity, pressure):
    energy = pressure / (HEAT_RATIO - 1.0) + 0.5 * density * lax.optimization_barrier(jnp.sum(velocity * velocity, 0))
    return jnp.concatenate([density[None], density[None] * velocity, energy[None]], 0)

def face_columns():
    node_grid = np.arange(512).reshape(8, 8, 8)
    surfaces = [node_grid[0], node_grid[7], node_grid[:, 0], node_grid[:, 7], node_grid[:, :, 0], node_grid[:, :, 7]]
    columns = np.concatenate([surface.reshape(64) for surface in surfaces])
    chooser = np.zeros((512, 384))
    chooser[columns, np.arange(384)] = 1.0
    return jnp.asarray(chooser, jnp.float32)

def kron_cube(basis_one):
    return jnp.kron(basis_one, jnp.kron(basis_one, basis_one))

def derivative_tables(derivative):
    identity = jnp.eye(8, dtype=jnp.float32)
    along_x = jnp.kron(derivative.T, jnp.kron(identity, identity))
    along_y = jnp.kron(identity, jnp.kron(derivative.T, identity))
    along_z = jnp.kron(identity, jnp.kron(identity, derivative.T))
    return (jnp.concatenate([along_x, along_y, along_z], 1), jnp.concatenate([along_x, along_y, along_z], 0))

def extract(state_now, chooser):
    return jnp.dot(state_now.reshape(-1, 512), chooser, precision=HIGHEST).reshape(state_now.shape[0], 4, 384)

def face_jumps(own_faces, face_table, neighbour_rows):
    pieces = []
    for facet_index in range(6):
        opposite = facet_index ^ 1
        remote = face_table[:, :, opposite * 64:(opposite + 1) * 64][neighbour_rows[:, facet_index]]
        pieces.append(remote - own_faces[:, :, facet_index * 64:(facet_index + 1) * 64])
    return jnp.concatenate(pieces, 2)

def acoustic_rate(state_now, jumps, source, sound_speed, grad_table, div_table, chooser):
    element_count = state_now.shape[0]
    pressure_gradient = jnp.dot(state_now[:, 0], grad_table, precision=HIGHEST).reshape(element_count, 3, 512)
    divergence = jnp.dot(state_now[:, 1:4].reshape(element_count, 1536), div_table, precision=HIGHEST)
    lifted = jnp.dot(jumps.reshape(element_count * 4, 384), chooser.T, precision=HIGHEST).reshape(element_count, 4, 512)
    rate_pressure = -(sound_speed * sound_speed)[:, None] * divergence + PENALTY * lifted[:, 0]
    rate_velocity = -pressure_gradient + source + PENALTY * lifted[:, 1:4]
    return jnp.concatenate([rate_pressure[:, None], rate_velocity], 1)

def reference(density, velocity, pressure, acoustic, sound_speed, derivative, mode_basis, neighbours, block_owner, block_element):
    grad_table, div_table = derivative_tables(derivative)
    chooser = face_columns()
    basis = kron_cube(mode_basis)
    fx_index = jnp.arange(N_FX, dtype=jnp.int32)[:, None, None, None]
    fz_index = jnp.arange(N_FZ, dtype=jnp.int32)[None, None, :, None]
    element_ids = (((fx_index * N_FY + block_owner[..., 0]) * N_FZ + fz_index) * EL_DEV + block_element).reshape(-1).astype(jnp.int32)

    def section(flow_now, sound_now):
        padded = jnp.pad(flow_now, ((0, 0), (1, 1), (1, 1), (1, 1)), mode='wrap')
        flow_rate, lamb_vector = flow_section(padded)
        blocks = lamb_vector.reshape(3, N_FX, CX // 8, 8, N_FY, CY // 8, 8, N_FZ, CZ // 8, 8)
        blocks = blocks.transpose(1, 4, 7, 2, 5, 8, 0, 3, 6, 9).reshape(-1, 512)
        projected = jnp.dot(blocks, basis.T, precision=HIGHEST).reshape(-1, 1536)
        source = jax.ops.segment_sum(projected, element_ids, num_segments=ELEMS).reshape(ELEMS, 3, 512)
        own_faces = extract(sound_now, chooser)
        jumps = face_jumps(own_faces, own_faces, neighbours)
        return (flow_rate, acoustic_rate(sound_now, jumps, source, sound_speed, grad_table, div_table, chooser))
    flow_start = conserved(density, velocity, pressure)
    sound_start = acoustic
    rate_one, sound_rate = section(flow_start, sound_start)
    flow_one = flow_start + TIME_STEP * rate_one
    sound_one = sound_start + TIME_STEP * sound_rate
    rate_two, sound_rate = section(flow_one, sound_one)
    flow_two = 0.75 * flow_start + 0.25 * (flow_one + TIME_STEP * rate_two)
    sound_two = 0.75 * sound_start + 0.25 * (sound_one + TIME_STEP * sound_rate)
    rate_three, sound_rate = section(flow_two, sound_two)
    flow_state = 1.0 / 3.0 * flow_start + 2.0 / 3.0 * (flow_two + TIME_STEP * rate_three)
    sound_state = 1.0 / 3.0 * sound_start + 2.0 / 3.0 * (sound_two + TIME_STEP * sound_rate)
    return (flow_state, sound_state)
```

```python
import functools

import jax
import jax.numpy as jnp
import numpy as np
from jax import lax
from jax.experimental import pallas as pl
from jax.experimental.pallas import tpu as pltpu
from jax.sharding import PartitionSpec as P

HEAT_RATIO = 1.4
TIME_STEP = 0.1
VISCOSITY = 0.05
PENALTY = 0.5
HALO = 3
F32 = jnp.float32
BF16 = jnp.bfloat16
PARAMS = pltpu.CompilerParams(vmem_limit_bytes=24 * 1024 * 1024)
MIXES = ((0.0, 1.0), (0.75, 0.25), (1.0 / 3.0, 2.0 / 3.0))


def parts(values):
    high = values.astype(BF16)
    return high, (values - high.astype(F32)).astype(BF16)


def dot(left, right):
    return lax.dot_general(left, right, (((1,), (0,)), ((), ())), preferred_element_type=F32)


def dot_three(left, right):
    left_high, left_low = parts(left)
    right_high, right_low = parts(right)
    return dot(left_high, right_high) + dot(left_high, right_low) + dot(left_low, right_high)


def dot_exact_right(left, right):
    left_high, left_low = parts(left)
    return dot(left_high, right) + dot(left_low, right)


def call(body, outs, *operands, scratch=()):
    return pl.pallas_call(
        body,
        out_shape=[jax.ShapeDtypeStruct(shape, F32) for shape in outs],
        in_specs=[pl.BlockSpec(memory_space=pltpu.VMEM)] * len(operands),
        out_specs=[pl.BlockSpec(memory_space=pltpu.VMEM)] * len(outs),
        scratch_shapes=list(scratch),
        compiler_params=PARAMS,
    )(*operands)


def pack_start_body(density, velocity, pressure, state, low, high):
    rho = density[...]
    vel = velocity[...]
    state[0] = rho
    for k in range(3):
        state[1 + k] = rho * vel[k]
    square = vel[0] * vel[0] + vel[1] * vel[1] + vel[2] * vel[2]
    state[4] = pressure[...] / (HEAT_RATIO - 1.0) + 0.5 * rho * square
    rows = state[...].reshape(-1, 128)
    count = rows.shape[0]
    for tile in range(low.shape[0] // 8):
        piece = rows[tile * 128 : min(count, tile * 128 + 128)]
        if piece.shape[0] < 128:
            piece = jnp.concatenate([piece, jnp.zeros((128 - piece.shape[0], 128), F32)], 0)
        turned = piece.T
        low[tile * 8 : tile * 8 + 8] = turned[0:8]
        high[tile * 8 : tile * 8 + 8] = turned[120:128]


def pack_next_body(state, above, below, edge, along_x, y_low, y_high, xy_low, xy_high):
    cells_x = state.shape[1]
    row = lax.broadcasted_iota(jnp.int32, edge.shape, 0) % 8
    both = jnp.where(row < 4, above[...], below[...])
    edge[...] = both
    planes = [cells_x - HALO + i for i in range(HALO)] + list(range(HALO))
    for f in range(5):
        for s, x in enumerate(planes):
            at = (f * len(planes) + s) * 8
            along_x[at : at + 8] = state[f, x]
            at = (f * len(planes) + s) * HALO
            xy_low[at : at + HALO] = state[f, x, 0:HALO]
            xy_high[at : at + HALO] = state[f, x, 8 - HALO : 8]
        for x in range(cells_x):
            at = (f * cells_x + x) * HALO
            y_low[at : at + HALO] = state[f, x, 0:HALO]
            y_high[at : at + HALO] = state[f, x, 8 - HALO : 8]
    for message in (along_x, y_low, y_high, xy_low, xy_high):
        size = message.shape[0]
        message[size - edge.shape[0] : size] = both


def turned_edges(message):
    size = message.shape[0]
    rows = []
    for tile in range(3):
        piece = message[size - 24 + tile * 8 : size - 16 + tile * 8]
        rows.append(jnp.concatenate([piece, jnp.zeros((112, 128), F32), piece], 0).T)
    return rows


def assemble(wide, state, edge, beside, cells_x):
    six = 2 * HALO
    for dx, dy, message in [(0, 0, edge)] + beside:
        turned = turned_edges(message)
        if dx == 0:
            columns = [(HALO + x, x, x) for x in range(cells_x)]
        elif dx < 0:
            columns = [(i, cells_x - HALO + i, i) for i in range(HALO)]
        else:
            columns = [(HALO + cells_x + i, i, HALO + i) for i in range(HALO)]
        slots = cells_x if dx == 0 else six
        target = {0: (0, 8), 1: (8, 8 + HALO), -1: (16 - HALO, 16)}[dy]
        source = {0: (0, 8), 1: (0, HALO), -1: (8 - HALO, 8)}[dy]
        height = target[1] - target[0]
        for f in range(5):
            for plane, x, slot in columns:
                if dx == 0 and dy == 0:
                    wide[f, plane, 0:8, 0:128] = state[f, x]
                else:
                    at = (f * slots + slot) * height
                    wide[f, plane, target[0] : target[1], 0:128] = message[at : at + height]
                group = f * cells_x + x
                block = turned[group // 16][(group % 16) * 8 : (group % 16) * 8 + 8]
                wide[f, plane, target[0] : target[1], 128:256] = block[source[0] : source[1]]


def flow_rate_section(wide, derived, start, offset, mix, write):
    depth = wide.shape[1]

    def derive(i, _):
        rho, mx, my, mz, energy = [wide[f, i] for f in range(5)]
        inverse = 1.0 / rho
        u, v, w = mx * inverse, my * inverse, mz * inverse
        p = (HEAT_RATIO - 1.0) * (energy - 0.5 * (mx * u + my * v + mz * w))
        derived[0, i] = u
        derived[1, i] = v
        derived[2, i] = w
        derived[3, i] = p
        derived[4, i] = jnp.sqrt(HEAT_RATIO * jnp.abs(p) * inverse)
        return 0

    lax.fori_loop(0, depth, derive, 0)

    def flux(fields, other, along):
        speed, p = other[along], other[3]
        out = [fields[1 + along]]
        for k in range(3):
            value = fields[1 + k] * speed
            out.append(value + p if k == along else value)
        out.append((fields[4] + p) * speed)
        return out, jnp.abs(speed) + other[4]

    def face(left, right):
        (fields_l, flux_l, speed_l), (fields_r, flux_r, speed_r) = left, right
        speed = jnp.maximum(speed_l, speed_r)
        viscous = speed + 2.0 * VISCOSITY
        return [
            (flux_l[f] + flux_r[f])
            - (viscous if 1 <= f <= 3 else speed) * (fields_r[f] - fields_l[f])
            for f in range(5)
        ]

    def plane(i, along):
        fields = [wide[f, i] for f in range(5)]
        other = [derived[f, i] for f in range(5)]
        return (fields,) + flux(fields, other, along)

    def section(i, before):
        here = plane(i, 0)
        ahead = face(here, plane(i + 1, 0))
        total = [ahead[f] - before[f] for f in range(5)]
        for along, axis, size in ((1, 0, 16), (2, 1, 256)):
            here = plane(i, along)
            moved = (
                [pltpu.roll(a, size - 1, axis) for a in here[0]],
                [pltpu.roll(a, size - 1, axis) for a in here[1]],
                pltpu.roll(here[2], size - 1, axis),
            )
            faces = face(here, moved)
            for f in range(5):
                total[f] = total[f] + (faces[f] - pltpu.roll(faces[f], 1, axis))
        for f in range(5):
            value = wide[f, i] - (0.5 * TIME_STEP) * total[f]
            if mix[0] != 0.0:
                value = mix[0] * start[f, i + offset] + mix[1] * value
            write(i - 1, f, value)
        return tuple(ahead)

    lax.fori_loop(1, depth - 1, section, tuple(face(plane(0, 0), plane(1, 0))))


def lamb(derived, first, cells_x, lamb_rows):
    def one(x, _):
        i = first + x
        slopes = []
        slopes.append([derived[c, i + 1, 0:8, 0:128] - derived[c, i - 1, 0:8, 0:128] for c in range(3)])
        columns = [derived[c, i, :, 0:128] for c in range(3)]
        slopes.append([(pltpu.roll(a, 15, 0) - pltpu.roll(a, 1, 0))[0:8] for a in columns])
        rows = [derived[c, i, 0:8, :] for c in range(3)]
        slopes.append([(pltpu.roll(a, 255, 1) - pltpu.roll(a, 1, 1))[:, 0:128] for a in rows])
        vel = [derived[c, i, 0:8, 0:128] for c in range(3)]
        curl = [
            0.5 * (slopes[1][2] - slopes[2][1]),
            0.5 * (slopes[2][0] - slopes[0][2]),
            0.5 * (slopes[0][1] - slopes[1][0]),
        ]
        at = pl.multiple_of(x * 8, 8)
        lamb_rows[0, pl.ds(at, 8), :] = curl[1] * vel[2] - curl[2] * vel[1]
        lamb_rows[1, pl.ds(at, 8), :] = curl[2] * vel[0] - curl[0] * vel[2]
        lamb_rows[2, pl.ds(at, 8), :] = curl[0] * vel[1] - curl[1] * vel[0]
        return 0

    lax.fori_loop(0, cells_x, one, 0)


def project(lamb_rows, pair, spread, labels, send):
    peers = send.shape[0]
    fold = send.shape[1] // 24 - 0
    fold = 192 // (send.shape[1] - 8)
    group = lax.broadcasted_iota(jnp.int32, (64 // fold, 128), 1) // (128 // fold)
    height = 64 // fold
    for c in range(3):
        modes = dot_three(pair[...], lamb_rows[c])
        sent = dot_three(modes, spread[...])
        for peer in range(peers):
            mine = sent[:, peer * 128 : peer * 128 + 128]
            folded = mine[0:height]
            for g in range(1, fold):
                folded = jnp.where(group == g, mine[g * height : g * height + height], folded)
            send[peer, c * height : c * height + height] = folded
    send[:, 3 * height : 3 * height + 8] = labels[...]


def flow_first_body(places, *refs):
    state, edge = refs[0:2]
    messages = refs[2 : 2 + len(places)]
    pair, spread, labels = refs[2 + len(places) : 5 + len(places)]
    wide, out, send, derived, lamb_rows = refs[5 + len(places) :]
    cells_x = state.shape[1]
    beside = []
    for message, spots in zip(messages, places):
        beside.extend((dx, dy, message) for dx, dy in spots)
    assemble(wide, state, edge, beside, cells_x)

    def write(i, f, value):
        out[f, i] = value

    flow_rate_section(wide, derived, wide, 0, MIXES[0], write)
    lamb(derived, HALO, cells_x, lamb_rows)
    project(lamb_rows, pair, spread, labels, send)


def flow_second_body(wide, start, pair, spread, labels, out, send, derived, lamb_rows):
    def write(i, f, value):
        out[f, i] = value

    flow_rate_section(wide, derived, start, 1, MIXES[1], write)
    lamb(derived, HALO - 1, wide.shape[1] - 2 * (HALO - 1), lamb_rows)
    project(lamb_rows, pair, spread, labels, send)


def flow_third_body(wide, start, pair, spread, labels, out, send, derived, lamb_rows):
    def write(i, f, value):
        out[f, i] = value[0:8, 0:128]

    flow_rate_section(wide, derived, start, 2, MIXES[2], write)
    lamb(derived, HALO - 2, wide.shape[1] - 2 * (HALO - 2), lamb_rows)
    project(lamb_rows, pair, spread, labels, send)


def faces_out(state, rear, front):
    lane = lax.broadcasted_iota(jnp.int32, (32, 128), 1) // 16
    for c in range(4):
        front[c * 8 : c * 8 + 8] = state[c, 56:64]
        rear[c * 8 : c * 8 + 8] = state[c, 0:8]
        front[32 + c * 8 : 40 + c * 8] = state[c, pl.ds(7, 8, stride=8), :]
        rear[32 + c * 8 : 40 + c * 8] = state[c, pl.ds(0, 8, stride=8), :]
    rows = state[...].reshape(256, 128)
    last = jnp.zeros((32, 128), F32)
    first = jnp.zeros((32, 128), F32)
    for j in range(8):
        piece = rows[j * 32 : j * 32 + 32]
        last = jnp.where(lane == j, pltpu.roll(piece, (j * 16 + 16) % 128, 1), last)
        first = jnp.where(lane == j, pltpu.roll(piece, j * 16, 1) if j else piece, first)
    front[64:96] = last
    rear[64:96] = first


def lift(total, before, after, sides, factor):
    def place(face, rows, target):
        value = factor * dot_exact_right(rows, sides[face])
        for c in range(4):
            total[c, target, :] += value[c * 8 : c * 8 + 8]

    place(0, before[0:32], pl.ds(0, 8))
    place(1, after[0:32], pl.ds(56, 8))
    place(2, before[32:64], pl.ds(0, 8, stride=8))
    place(3, after[32:64], pl.ds(7, 8, stride=8))


def rate_local(state, deriv_rows, deriv_lanes, speed, sides):
    fields = [state[c] for c in range(4)]
    by_rows = dot_three(deriv_rows[...], jnp.concatenate(fields[0:3], 1))
    by_lanes = dot_three(jnp.concatenate([fields[0], fields[3]], 0), deriv_lanes[...])
    divergence = by_rows[0:64, 128:256] + by_rows[64:128, 256:384] + by_lanes[64:128]
    rates = [
        -(speed[...] * speed[...]) * divergence,
        -by_rows[0:64, 0:128],
        -by_rows[64:128, 0:128],
        -by_lanes[0:64],
    ]
    row = lax.broadcasted_iota(jnp.int32, (64, 128), 0)
    lane = lax.broadcasted_iota(jnp.int32, (64, 128), 1)
    count = jnp.zeros((64, 128), F32)
    for value in (row // 8, row % 8, lane // 16):
        count = count + jnp.where((value == 0) | (value == 7), PENALTY, 0.0)
    side = PENALTY * dot_exact_right(state[...].reshape(256, 128), sides[4])
    return [rates[c] - count * fields[c] + side[c * 64 : c * 64 + 64] for c in range(4)]


def acoustic_local_body(mix, has_source, *refs):
    if has_source:
        state, start, source, deriv_rows, deriv_lanes, speed, sides, out, front, rear = refs
    else:
        state, deriv_rows, deriv_lanes, speed, sides, out, front, rear = refs
    rates = rate_local(state, deriv_rows, deriv_lanes, speed, sides)
    for c in range(4):
        rate = rates[c]
        if has_source and c > 0:
            rate = rate + source[c - 1]
        value = state[c] + TIME_STEP * rate
        if mix[0] != 0.0:
            value = mix[0] * start[c] + mix[1] * value
        out[c] = value
    faces_out(state, rear, front)
    lift(out, front, rear, sides, TIME_STEP * mix[1] * PENALTY)


def acoustic_first_body(state, deriv_rows, deriv_lanes, speed, sides, out, front, rear):
    acoustic_local_body(MIXES[0], False, state, deriv_rows, deriv_lanes, speed, sides, out, front, rear)


def remote_part(out, before, after, sides_far, factor):
    lift(out, before, after, sides_far, factor)
    lane = lax.broadcasted_iota(jnp.int32, (32, 128), 1) // 16
    last, first = before[64:96], after[64:96]
    pieces = []
    for j in range(8):
        left = pltpu.roll(last, 128 - j * 16, 1) if j else last
        right = pltpu.roll(first, (144 - j * 16) % 128, 1) if j != 1 else first
        pieces.append(jnp.where(lane == 0, left, jnp.where(lane == 1, right, 0.0)))
    value = factor * dot_exact_right(jnp.concatenate(pieces, 0), sides_far[4])
    for c in range(4):
        out[c] += value[c * 64 : c * 64 + 64]


def acoustic_far_body(factor, has_source, last, *refs):
    refs = list(refs)
    partial, before, after, sides_far = refs[0:4]
    refs = refs[4:]
    if has_source:
        source = refs.pop(0)
    out = refs[0]
    out[...] = partial[...]
    remote_part(out, before, after, sides_far, factor)
    if has_source:
        for c in range(3):
            out[1 + c] += TIME_STEP * source[c]
    if not last:
        faces_out(out, refs[2], refs[1])


def place_body(received, out):
    peers, size = received.shape[0], received.shape[1]
    fold = 192 // (size - 8)
    height = 64 // fold
    target = lax.broadcasted_iota(jnp.int32, (128, 128), 0)
    lane = lax.broadcasted_iota(jnp.int32, (128, 128), 1)
    total = None
    for peer in range(peers):
        label = received[peer, size - 8 : size - 7, :]
        label = jnp.broadcast_to(label, (128, 128)).astype(jnp.int32)
        hit = (label == target % 16) & (lane % 8 == target // 16)
        chosen = [jnp.where(hit & (lane // (128 // fold) == g), 1.0, 0.0) for g in range(fold)]
        chosen = jnp.concatenate(chosen, 0).astype(BF16)
        high, low = parts(received[peer, 0 : size - 8])
        dims = (((1,), (1,)), ((), ()))
        value = lax.dot_general(high, chosen, dims, preferred_element_type=F32)
        value = value + lax.dot_general(low, chosen, dims, preferred_element_type=F32)
        total = value if total is None else total + value
    for c in range(3):
        for g in range(fold):
            out[c, g * height : g * height + height] = total[
                c * height : c * height + height, g * 128 : g * 128 + 128
            ]


def routing_tables(mode_basis, owners, elements, peers):
    blocks = owners.shape[0]
    capacity = max(2, 2 * blocks // peers)
    matches = (owners[:, None] == jnp.arange(peers, dtype=jnp.int32)[None, :]).astype(jnp.int32)
    order = jnp.tril(jnp.ones((blocks, blocks), jnp.int32), -1)
    before = jnp.sum(order[:, :, None] * matches[None, :, :], 1)
    position = jnp.sum(before * matches, 1)
    slot = owners * capacity + position
    chooser = jnp.arange(peers * capacity, dtype=jnp.int32)[None, :] == slot[:, None]
    labels = (jnp.sum(jnp.where(chooser, elements[:, None] + 1, 0), 0) - 1).reshape(peers, capacity)
    fold = 128 // (8 * capacity)
    spread = chooser.astype(F32)[:, None, :, None] * mode_basis.T[None, :, None, :]
    spread = spread.reshape(blocks * 8, peers, 1, capacity * 8)
    spread = jnp.broadcast_to(spread, (blocks * 8, peers, fold, capacity * 8))
    spread = spread.reshape(blocks * 8, peers * 128)
    lanes = jnp.broadcast_to(labels[:, None, :, None], (peers, fold, capacity, 8)).reshape(peers, 1, 128)
    return spread, jnp.broadcast_to(lanes, (peers, 8, 128)).astype(F32), fold


def side_tables(local):
    count = local.shape[0]
    element = jnp.arange(count, dtype=jnp.int32)
    eye = jnp.eye(8, dtype=jnp.int32)
    near, far = [], []
    for facet in range(6):
        wanted = local[:, facet][None, :]
        shift = -count if facet % 2 == 0 else count
        near.append((element[:, None] == wanted).astype(jnp.int32))
        far.append((element[:, None] + shift == wanted).astype(jnp.int32))
    first, last = np.zeros((8, 8), np.int32), np.zeros((8, 8), np.int32)
    first[7, 0] = 1
    last[0, 7] = 1

    def cross(levels, chooser):
        return (levels[:, None, :, None] * chooser[None, :, None, :]).reshape(8 * count, 8 * count)

    near_out = [cross(eye, near[f]) for f in range(4)]
    near_out.append(cross(jnp.asarray(first), near[4]) + cross(jnp.asarray(last), near[5]))
    far_out = [cross(eye, far[f]) for f in range(4)]
    put_first, put_last = np.zeros((8, 8), np.int32), np.zeros((8, 8), np.int32)
    put_first[0, 0] = 1
    put_last[1, 7] = 1
    far_out.append(cross(jnp.asarray(put_first), far[4]) + cross(jnp.asarray(put_last), far[5]))
    return jnp.stack(near_out).astype(BF16), jnp.stack(far_out).astype(BF16)


def shifted(sizes, shifts):
    pairs = []
    for index in np.ndindex(*sizes):
        source = [(i + s) % n for i, s, n in zip(index, shifts, sizes)]
        pairs.append((int(np.ravel_multi_index(source, sizes)), int(np.ravel_multi_index(index, sizes))))
    return pairs


def per_device(
    density,
    velocity,
    pressure,
    acoustic,
    sound_speed,
    derivative,
    mode_basis,
    neighbours,
    block_owner,
    block_element,
):
    size_x, size_y, size_z = lax.axis_size("fx"), lax.axis_size("fy"), lax.axis_size("fz")
    devices = size_x * size_y * size_z
    cells_x = density.shape[0]
    elements = acoustic.shape[0]
    device = lax.axis_index(("fx", "fy", "fz"))

    rows = 5 * cells_x * 8
    tiles = -(-rows // 128)
    state, low, high = call(
        pack_start_body,
        [(5, cells_x, 8, 128), (tiles * 8, 128), (tiles * 8, 128)],
        density,
        velocity,
        pressure,
    )
    above = lax.ppermute(low, "fz", shifted((size_z,), (1,)))
    below = lax.ppermute(high, "fz", shifted((size_z,), (-1,)))

    sound = acoustic.reshape(elements, 4, 64, 8).transpose(1, 2, 3, 0).reshape(4, 64, 8 * elements)
    local = neighbours - device * elements
    near, far = side_tables(local)
    eye = jnp.eye(8, dtype=F32)
    deriv_rows = jnp.concatenate([jnp.kron(derivative, eye), jnp.kron(eye, derivative)], 0)
    deriv_lanes = jnp.kron(derivative.T, jnp.eye(elements, dtype=F32))
    speed = jnp.tile(sound_speed, 8)[None, :]
    forward = [(i, i + 1) for i in range(devices - 1)]
    backward = [(i + 1, i) for i in range(devices - 1)]
    names = ("fx", "fy", "fz")

    def traces(front, rear):
        return lax.ppermute(front, names, forward), lax.ppermute(rear, names, backward)

    partial, front, rear = call(
        acoustic_first_body,
        [(4, 64, 128), (96, 128), (96, 128)],
        sound,
        deriv_rows,
        deriv_lanes,
        speed,
        near,
    )
    before, after = traces(front, rear)

    six = 2 * HALO
    tall = 5 * six * HALO
    tall = -(-tall // 8) * 8
    edge_rows = tiles * 8
    edge, along_x, y_low, y_high, xy_low, xy_high = call(
        pack_next_body,
        [
            (edge_rows, 128),
            (5 * six * 8 + edge_rows, 128),
            (5 * cells_x * HALO + edge_rows, 128),
            (5 * cells_x * HALO + edge_rows, 128),
            (tall + edge_rows, 128),
            (tall + edge_rows, 128),
        ],
        state,
        above,
        below,
    )
    flat = (size_x, size_y)
    steps = [[(1, 0), (-1, 0)]] if size_x == 2 else [[(1, 0)], [(-1, 0)]]
    places, messages = [], []
    for spots in steps:
        messages.append(lax.ppermute(along_x, ("fx", "fy"), shifted(flat, spots[0])))
        places.append(tuple(spots))
    for dy, kept in ((1, y_low), (-1, y_high)):
        messages.append(lax.ppermute(kept, ("fx", "fy"), shifted(flat, (0, dy))))
        places.append(((0, dy),))
    for dy, kept in ((1, xy_low), (-1, xy_high)):
        for spots in steps:
            messages.append(lax.ppermute(kept, ("fx", "fy"), shifted(flat, (spots[0][0], dy))))
            places.append(tuple((dx, dy) for dx, _ in spots))

    spread, labels, fold = routing_tables(
        mode_basis, block_owner.reshape(-1), block_element.reshape(-1), size_y
    )
    pair = jnp.kron(mode_basis, mode_basis)
    sent_shape = (size_y, 192 // fold + 8, 128)

    def scratch(planes):
        return [pltpu.VMEM((5, planes, 16, 256), F32), pltpu.VMEM((3, 64, 128), F32)]

    def route(send):
        got = lax.all_to_all(send, "fy", split_axis=0, concat_axis=0, tiled=True)
        return call(place_body, [(3, 64, 128)], got)[0]

    wide = cells_x + 2 * HALO
    start, flow_one, send = call(
        functools.partial(flow_first_body, tuple(places)),
        [(5, wide, 16, 256), (5, wide - 2, 16, 256), sent_shape],
        state,
        edge,
        *messages,
        pair,
        spread,
        labels,
        scratch=scratch(wide),
    )
    source = route(send)

    factors = [TIME_STEP * mix[1] * PENALTY for mix in MIXES]
    sound_one, front, rear = call(
        functools.partial(acoustic_far_body, factors[0], True, False),
        [(4, 64, 128), (96, 128), (96, 128)],
        partial,
        before,
        after,
        far,
        source,
    )
    before, after = traces(front, rear)

    flow_two, send = call(
        flow_second_body,
        [(5, wide - 4, 16, 256), sent_shape],
        flow_one,
        start,
        pair,
        spread,
        labels,
        scratch=scratch(wide - 2),
    )
    source = route(send)
    partial, _, _ = call(
        functools.partial(acoustic_local_body, MIXES[1], True),
        [(4, 64, 128), (96, 128), (96, 128)],
        sound_one,
        sound,
        source,
        deriv_rows,
        deriv_lanes,
        speed,
        near,
    )
    sound_two, front, rear = call(
        functools.partial(acoustic_far_body, factors[1], False, False),
        [(4, 64, 128), (96, 128), (96, 128)],
        partial,
        before,
        after,
        far,
    )
    before, after = traces(front, rear)

    flow_state, send = call(
        flow_third_body,
        [(5, cells_x, 8, 128), sent_shape],
        flow_two,
        start,
        pair,
        spread,
        labels,
        scratch=scratch(wide - 4),
    )
    source = route(send)
    partial, _, _ = call(
        functools.partial(acoustic_local_body, MIXES[2], True),
        [(4, 64, 128), (96, 128), (96, 128)],
        sound_two,
        sound,
        source,
        deriv_rows,
        deriv_lanes,
        speed,
        near,
    )
    sound_three = call(
        functools.partial(acoustic_far_body, factors[2], False, True),
        [(4, 64, 128)],
        partial,
        before,
        after,
        far,
    )[0]
    sound_state = sound_three.reshape(4, 64, 8, elements).transpose(3, 0, 1, 2).reshape(elements, 4, 512)
    return (flow_state, sound_state)


def solution(mesh):
    placed = (
        P("fx", "fy", "fz"),
        P(None, "fx", "fy", "fz"),
        P("fx", "fy", "fz"),
        P(("fx", "fy", "fz"), None, None),
        P(("fx", "fy", "fz")),
        P(),
        P(),
        P(("fx", "fy", "fz"), None),
        P("fx", "fy", "fz", None, None),
        P("fx", "fy", "fz", None),
    )
    return jax.shard_map(
        per_device,
        mesh=mesh,
        in_specs=placed,
        out_specs=(P(None, "fx", "fy", "fz"), P(("fx", "fy", "fz"), None, None)),
        check_vma=False,
    )
```

```python
import functools

import jax
import jax.numpy as jnp
import numpy as np
from jax import lax
from jax.experimental import pallas as pl
from jax.experimental.pallas import tpu as pltpu
from jax.sharding import PartitionSpec as P

HEAT_RATIO = 1.4
TIME_STEP = 0.1
VISCOSITY = 0.05
PENALTY = 0.5
HALO = 3
F32 = jnp.float32
BF16 = jnp.bfloat16
PARAMS = pltpu.CompilerParams(vmem_limit_bytes=24 * 1024 * 1024)
MIXES = ((0.0, 1.0), (0.75, 0.25), (1.0 / 3.0, 2.0 / 3.0))


def parts(values):
    high = values.astype(BF16)
    return high, (values - high.astype(F32)).astype(BF16)


def dot(left, right):
    return lax.dot_general(left, right, (((1,), (0,)), ((), ())), preferred_element_type=F32)


def dot_three(left, right):
    left_high, left_low = parts(left)
    right_high, right_low = parts(right)
    return dot(left_high, right_high) + dot(left_high, right_low) + dot(left_low, right_high)


def dot_full(left, right, dims=((1,), (0,))):
    return lax.dot_general(
        left, right, (dims, ((), ())), precision=lax.Precision.HIGHEST, preferred_element_type=F32
    )


def dot_exact_right(left, right):
    left_high, left_low = parts(left)
    return dot(left_high, right) + dot(left_low, right)


def call(body, outs, *operands, scratch=(), fetch=False):
    spec = pl.BlockSpec() if fetch else pl.BlockSpec(memory_space=pltpu.VMEM)
    outs = [out if isinstance(out, jax.ShapeDtypeStruct) else jax.ShapeDtypeStruct(out, F32) for out in outs]
    return pl.pallas_call(
        body,
        out_shape=outs,
        in_specs=[spec] * len(operands),
        out_specs=[pl.BlockSpec(memory_space=pltpu.VMEM)] * len(outs),
        scratch_shapes=list(scratch),
        compiler_params=PARAMS,
    )(*operands)


def pack_start_body(density, velocity, pressure, state, low, high):
    rho = density[...]
    vel = velocity[...]
    state[0] = rho
    for k in range(3):
        state[1 + k] = rho * vel[k]
    square = vel[0] * vel[0] + vel[1] * vel[1] + vel[2] * vel[2]
    state[4] = pressure[...] / (HEAT_RATIO - 1.0) + 0.5 * rho * square
    rows = state[...].reshape(-1, 128)
    count = rows.shape[0]
    for tile in range(low.shape[0] // 8):
        piece = rows[tile * 128 : min(count, tile * 128 + 128)]
        if piece.shape[0] < 128:
            piece = jnp.concatenate([piece, jnp.zeros((128 - piece.shape[0], 128), F32)], 0)
        turned = piece.T
        low[tile * 8 : tile * 8 + 8] = turned[0:8]
        high[tile * 8 : tile * 8 + 8] = turned[120:128]


def pack_next_body(state, above, below, edge, along_x, y_low, y_high, xy_low, xy_high):
    cells_x = state.shape[1]
    row = lax.broadcasted_iota(jnp.int32, edge.shape, 0) % 8
    both = jnp.where(row < 4, above[...], below[...])
    edge[...] = both
    planes = [cells_x - HALO + i for i in range(HALO)] + list(range(HALO))
    for f in range(5):
        for s, x in enumerate(planes):
            at = (f * len(planes) + s) * 8
            along_x[at : at + 8] = state[f, x]
            at = (f * len(planes) + s) * HALO
            xy_low[at : at + HALO] = state[f, x, 0:HALO]
            xy_high[at : at + HALO] = state[f, x, 8 - HALO : 8]
        for x in range(cells_x):
            at = (f * cells_x + x) * HALO
            y_low[at : at + HALO] = state[f, x, 0:HALO]
            y_high[at : at + HALO] = state[f, x, 8 - HALO : 8]
    for message in (along_x, y_low, y_high, xy_low, xy_high):
        size = message.shape[0]
        message[size - edge.shape[0] : size] = both


def turned_edges(message):
    size = message.shape[0]
    rows = []
    for tile in range(3):
        piece = message[size - 24 + tile * 8 : size - 16 + tile * 8]
        rows.append(jnp.concatenate([piece, jnp.zeros((112, 128), F32), piece], 0).T)
    return rows


def assemble(wide, state, edge, beside, cells_x):
    six = 2 * HALO
    for dx, dy, message in [(0, 0, edge)] + beside:
        turned = turned_edges(message)
        if dx == 0:
            columns = [(HALO + x, x, x) for x in range(cells_x)]
        elif dx < 0:
            columns = [(i, cells_x - HALO + i, i) for i in range(HALO)]
        else:
            columns = [(HALO + cells_x + i, i, HALO + i) for i in range(HALO)]
        slots = cells_x if dx == 0 else six
        target = {0: (0, 8), 1: (8, 8 + HALO), -1: (16 - HALO, 16)}[dy]
        source = {0: (0, 8), 1: (0, HALO), -1: (8 - HALO, 8)}[dy]
        height = target[1] - target[0]
        for f in range(5):
            for plane, x, slot in columns:
                if dx == 0 and dy == 0:
                    wide[f, plane, 0:8, 0:128] = state[f, x]
                else:
                    at = (f * slots + slot) * height
                    wide[f, plane, target[0] : target[1], 0:128] = message[at : at + height]
                group = f * cells_x + x
                block = turned[group // 16][(group % 16) * 8 : (group % 16) * 8 + 8]
                wide[f, plane, target[0] : target[1], 128:256] = block[source[0] : source[1]]


def derive_planes(wide, derived, first, last):
    def derive(i, _):
        rho, mx, my, mz, energy = [wide[f, i] for f in range(5)]
        inverse = 1.0 / rho
        u, v, w = mx * inverse, my * inverse, mz * inverse
        p = (HEAT_RATIO - 1.0) * (energy - 0.5 * (mx * u + my * v + mz * w))
        derived[0, i] = u
        derived[1, i] = v
        derived[2, i] = w
        derived[3, i] = p
        derived[4, i] = jnp.sqrt(HEAT_RATIO * jnp.abs(p) * inverse)
        return 0

    lax.fori_loop(first, last, derive, 0)


def derive_speeds(wide, derived, first, last):
    def derive(i, _):
        inverse = 1.0 / wide[0, i]
        for k in range(3):
            derived[k, i] = wide[1 + k, i] * inverse
        return 0

    lax.fori_loop(first, last, derive, 0)


def flow_rate_section(wide, derived, start, offset, mix, write, inner=False):
    depth = wide.shape[1]
    near, lanes = slice(0, 8), slice(0, 128)
    every = (slice(None), slice(None))
    windows = [(near, lanes), (slice(None), lanes), (near, slice(None))] if inner else [every] * 3
    kept = windows[0]

    def flux(fields, other, along):
        speed, p = other[along], other[3]
        out = [fields[1 + along]]
        for k in range(3):
            value = fields[1 + k] * speed
            out.append(value + p if k == along else value)
        out.append((fields[4] + p) * speed)
        return out, jnp.abs(speed) + other[4]

    def face(left, right):
        (fields_l, flux_l, speed_l), (fields_r, flux_r, speed_r) = left, right
        speed = jnp.maximum(speed_l, speed_r)
        viscous = speed + 2.0 * VISCOSITY
        return [
            (flux_l[f] + flux_r[f])
            - (viscous if 1 <= f <= 3 else speed) * (fields_r[f] - fields_l[f])
            for f in range(5)
        ]

    def plane(i, along):
        rows, columns = windows[along]
        fields = [wide[f, i, rows, columns] for f in range(5)]
        other = [derived[f, i, rows, columns] for f in range(5)]
        return (fields,) + flux(fields, other, along)

    def section(i, before):
        here = plane(i, 0)
        ahead = face(here, plane(i + 1, 0))
        total = [ahead[f] - before[f] for f in range(5)]
        for along, axis, size in ((1, 0, 16), (2, 1, 256)):
            here = plane(i, along)
            moved = (
                [pltpu.roll(a, size - 1, axis) for a in here[0]],
                [pltpu.roll(a, size - 1, axis) for a in here[1]],
                pltpu.roll(here[2], size - 1, axis),
            )
            faces = face(here, moved)
            for f in range(5):
                change = faces[f] - pltpu.roll(faces[f], 1, axis)
                total[f] = total[f] + (change[0:8, 0:128] if inner else change)
        for f in range(5):
            value = wide[f, i, kept[0], kept[1]] - (0.5 * TIME_STEP) * total[f]
            if mix[0] != 0.0:
                value = mix[0] * start[f, i + offset, kept[0], kept[1]] + mix[1] * value
            write(i - 1, f, value)
        return tuple(ahead)

    lax.fori_loop(1, depth - 1, section, tuple(face(plane(0, 0), plane(1, 0))))


def lamb(derived, first, cells_x, lamb_rows):
    def one(x, _):
        i = first + x
        slopes = []
        slopes.append([derived[c, i + 1, 0:8, 0:128] - derived[c, i - 1, 0:8, 0:128] for c in range(3)])
        columns = [derived[c, i, :, 0:128] for c in range(3)]
        slopes.append([(pltpu.roll(a, 15, 0) - pltpu.roll(a, 1, 0))[0:8] for a in columns])
        rows = [derived[c, i, 0:8, :] for c in range(3)]
        slopes.append([(pltpu.roll(a, 255, 1) - pltpu.roll(a, 1, 1))[:, 0:128] for a in rows])
        vel = [derived[c, i, 0:8, 0:128] for c in range(3)]
        curl = [
            0.5 * (slopes[1][2] - slopes[2][1]),
            0.5 * (slopes[2][0] - slopes[0][2]),
            0.5 * (slopes[0][1] - slopes[1][0]),
        ]
        at = pl.multiple_of(x * 8, 8)
        lamb_rows[0, pl.ds(at, 8), :] = curl[1] * vel[2] - curl[2] * vel[1]
        lamb_rows[1, pl.ds(at, 8), :] = curl[2] * vel[0] - curl[0] * vel[2]
        lamb_rows[2, pl.ds(at, 8), :] = curl[0] * vel[1] - curl[1] * vel[0]
        return 0

    lax.fori_loop(0, cells_x, one, 0)


def project(lamb_rows, pair, spread, labels, send):
    peers = send.shape[0]
    fold = 192 // (send.shape[1] - 8)
    group = lax.broadcasted_iota(jnp.int32, (64 // fold, 128), 1) // (128 // fold)
    height = 64 // fold
    for c in range(3):
        modes = dot_three(pair[...], lamb_rows[c])
        sent = dot_three(modes, spread[...])
        for peer in range(peers):
            mine = sent[:, peer * 128 : peer * 128 + 128]
            folded = mine[0:height]
            for g in range(1, fold):
                folded = jnp.where(group == g, mine[g * height : g * height + height], folded)
            send[peer, c * height : c * height + height] = folded
    send[:, 3 * height : 3 * height + 8] = labels[...]


def flow_sources_body(places, *refs):
    state, edge = refs[0:2]
    messages = refs[2 : 2 + len(places)]
    pair, spread, labels = refs[2 + len(places) : 5 + len(places)]
    wide, send, derived, lamb_rows = refs[5 + len(places) :]
    cells_x = state.shape[1]
    beside = []
    for message, spots in zip(messages, places):
        beside.extend((dx, dy, message) for dx, dy in spots)
    assemble(wide, state, edge, beside, cells_x)
    derive_speeds(wide, derived, HALO - 1, HALO + cells_x + 1)
    lamb(derived, HALO, cells_x, lamb_rows)
    project(lamb_rows, pair, spread, labels, send)


def flow_first_body(wide, pair, spread, labels, out, send, derived, lamb_rows):
    def write(i, f, value):
        out[f, i] = value

    planes = wide.shape[1]
    cells_x = planes - 2 * HALO
    derive_planes(wide, derived, 0, planes)
    flow_rate_section(wide, derived, wide, 0, MIXES[0], write)
    derive_speeds(out, derived, HALO - 2, HALO + cells_x)
    lamb(derived, HALO - 1, cells_x, lamb_rows)
    project(lamb_rows, pair, spread, labels, send)


def flow_last_body(wide, start, pair, spread, labels, out, send, derived, lamb_rows, second):
    def write_second(i, f, value):
        second[f, i] = value

    def write(i, f, value):
        out[f, i] = value

    planes = wide.shape[1]
    cells_x = out.shape[1]
    derive_planes(wide, derived, 0, planes)
    flow_rate_section(wide, derived, start, 1, MIXES[1], write_second)
    derive_planes(second, derived, 0, planes - 2)
    lamb(derived, 1, cells_x, lamb_rows)
    project(lamb_rows, pair, spread, labels, send)
    flow_rate_section(second, derived, start, 2, MIXES[2], write, inner=True)


def faces_out(state, rear, front):
    lane = lax.broadcasted_iota(jnp.int32, (32, 128), 1) // 16
    for c in range(4):
        front[c * 8 : c * 8 + 8] = state[c, 56:64]
        rear[c * 8 : c * 8 + 8] = state[c, 0:8]
        front[32 + c * 8 : 40 + c * 8] = state[c, pl.ds(7, 8, stride=8), :]
        rear[32 + c * 8 : 40 + c * 8] = state[c, pl.ds(0, 8, stride=8), :]
    rows = state[...].reshape(256, 128)
    last = jnp.zeros((32, 128), F32)
    first = jnp.zeros((32, 128), F32)
    for j in range(8):
        piece = rows[j * 32 : j * 32 + 32]
        last = jnp.where(lane == j, pltpu.roll(piece, (j * 16 + 16) % 128, 1), last)
        first = jnp.where(lane == j, pltpu.roll(piece, j * 16, 1) if j else piece, first)
    front[64:96] = last
    rear[64:96] = first


def lift(total, before, after, sides, factor):
    def place(face, rows, target):
        value = factor * dot_exact_right(rows, sides[face])
        for c in range(4):
            total[c, target, :] += value[c * 8 : c * 8 + 8]

    place(0, before[0:32], pl.ds(0, 8))
    place(1, after[0:32], pl.ds(56, 8))
    place(2, before[32:64], pl.ds(0, 8, stride=8))
    place(3, after[32:64], pl.ds(7, 8, stride=8))


def rate_local(state, deriv_rows, deriv_lanes, speed, sides):
    fields = [state[c] for c in range(4)]
    by_rows = dot_three(deriv_rows[...], jnp.concatenate(fields[0:3], 1))
    by_lanes = dot_three(jnp.concatenate([fields[0], fields[3]], 0), deriv_lanes[...])
    divergence = by_rows[0:64, 128:256] + by_rows[64:128, 256:384] + by_lanes[64:128]
    rates = [
        -(speed[...] * speed[...]) * divergence,
        -by_rows[0:64, 0:128],
        -by_rows[64:128, 0:128],
        -by_lanes[0:64],
    ]
    row = lax.broadcasted_iota(jnp.int32, (64, 128), 0)
    lane = lax.broadcasted_iota(jnp.int32, (64, 128), 1)
    count = jnp.zeros((64, 128), F32)
    for value in (row // 8, row % 8, lane // 16):
        count = count + jnp.where((value == 0) | (value == 7), PENALTY, 0.0)
    side = PENALTY * dot_exact_right(state[...].reshape(256, 128), sides[4])
    return [rates[c] - count * fields[c] + side[c * 64 : c * 64 + 64] for c in range(4)]


def local_update(mix, state, start, deriv_rows, deriv_lanes, speed, sides, out, front, rear):
    rates = rate_local(state, deriv_rows, deriv_lanes, speed, sides)
    for c in range(4):
        value = state[c] + TIME_STEP * rates[c]
        if mix[0] != 0.0:
            value = mix[0] * start[c] + mix[1] * value
        out[c] = value
    faces_out(state, rear, front)
    lift(out, front, rear, sides, TIME_STEP * mix[1] * PENALTY)


def acoustic_local_body(mix, state, start, deriv_rows, deriv_lanes, speed, sides, out, front, rear):
    local_update(mix, state, start, deriv_rows, deriv_lanes, speed, sides, out, front, rear)


def order_table(count, turned):
    row = lax.broadcasted_iota(jnp.int32, (4 * count, 4 * count), 0)
    column = lax.broadcasted_iota(jnp.int32, (4 * count, 4 * count), 1)
    if turned:
        row, column = column, row
    return (column == (row % count) * 4 + row // count).astype(F32)


def acoustic_first_body(given, deriv_rows, deriv_lanes, speed, sides, state, out, front, rear, turned):
    count = given.shape[0]
    rows = jnp.concatenate([given[e] for e in range(count)], 0)
    rows = dot_full(order_table(count, False), rows)
    rows = jnp.concatenate([rows, jnp.zeros((128 - 4 * count, rows.shape[1]), F32)], 0)
    turned[...] = rows.T
    lane = lax.broadcasted_iota(jnp.int32, (64, 128), 1) // count
    fields = [jnp.zeros((64, 128), F32)] * 4
    for z in range(8):
        piece = turned[pl.ds(z, 64, stride=8), :]
        for c in range(4):
            move = (z - c) * count % 128
            fields[c] = jnp.where(lane == z, pltpu.roll(piece, move, 1) if move else piece, fields[c])
    for c in range(4):
        state[c] = fields[c]
    local_update(MIXES[0], state, state, deriv_rows, deriv_lanes, speed, sides, out, front, rear)


def natural_order(state, out, turned):
    count = out.shape[0]
    lane = lax.broadcasted_iota(jnp.int32, (64, 128), 1) // count
    for z in range(8):
        value = jnp.zeros((64, 128), F32)
        for c in range(4):
            move = (c - z) * count % 128
            value = jnp.where(lane == c, pltpu.roll(state[c], move, 1) if move else state[c], value)
        turned[pl.ds(z, 64, stride=8), :] = value
    rows = dot_full(order_table(count, True), turned[...].T[0 : 4 * count])
    for e in range(count):
        out[e] = rows[4 * e : 4 * e + 4]


def remote_part(out, before, after, sides_far, factor):
    lift(out, before, after, sides_far, factor)
    lane = lax.broadcasted_iota(jnp.int32, (32, 128), 1) // 16
    last, first = before[64:96], after[64:96]
    pieces = []
    for j in range(8):
        left = pltpu.roll(last, 128 - j * 16, 1) if j else last
        right = pltpu.roll(first, (144 - j * 16) % 128, 1) if j != 1 else first
        pieces.append(jnp.where(lane == 0, left, jnp.where(lane == 1, right, 0.0)))
    value = factor * dot_exact_right(jnp.concatenate(pieces, 0), sides_far[4])
    for c in range(4):
        out[c] += value[c * 64 : c * 64 + 64]


def acoustic_far_body(mix, last, *refs):
    partial, before, after, sides_far, received = refs[0:5]
    if last:
        given_out, out, turned = refs[5:]
    else:
        out, front, rear = refs[5:]
    out[...] = partial[...]
    place(received, out, TIME_STEP * mix[1])
    remote_part(out, before, after, sides_far, TIME_STEP * mix[1] * PENALTY)
    if last:
        natural_order(out, given_out, turned)
    else:
        faces_out(out, rear, front)


def place(received, out, factor):
    peers, size = received.shape[0], received.shape[1]
    fold = 192 // (size - 8)
    height = 64 // fold
    target = lax.broadcasted_iota(jnp.int32, (128, 128), 0)
    lane = lax.broadcasted_iota(jnp.int32, (128, 128), 1)
    total = None
    for peer in range(peers):
        label = received[peer, size - 8 : size - 7, :]
        label = jnp.broadcast_to(label, (128, 128)).astype(jnp.int32)
        hit = (label == target % 16) & (lane % 8 == target // 16)
        chosen = [jnp.where(hit & (lane // (128 // fold) == g), 1.0, 0.0) for g in range(fold)]
        chosen = jnp.concatenate(chosen, 0).astype(BF16)
        high, low = parts(received[peer, 0 : size - 8])
        dims = (((1,), (1,)), ((), ()))
        value = lax.dot_general(high, chosen, dims, preferred_element_type=F32)
        value = value + lax.dot_general(low, chosen, dims, preferred_element_type=F32)
        total = value if total is None else total + value
    for c in range(3):
        for g in range(fold):
            rows = slice(g * height, g * height + height)
            out[1 + c, rows] = out[1 + c, rows] + factor * (
                total[c * height : c * height + height, g * 128 : g * 128 + 128]
            )


def kron_part(matrix, shape, rows_by, columns_by):
    row = lax.broadcasted_iota(jnp.int32, (shape[0], 8), 0)
    level = lax.broadcasted_iota(jnp.int32, (shape[0], 8), 1)
    left = (row // rows_by % 8 == level).astype(F32)
    level = lax.broadcasted_iota(jnp.int32, (8, shape[1]), 0)
    column = lax.broadcasted_iota(jnp.int32, (8, shape[1]), 1)
    right = (column // columns_by % 8 == level).astype(F32)
    return dot_full(dot_full(left, matrix), right)


def tables_body(
    derivative,
    basis,
    local,
    owner_column,
    owner_row,
    element_column,
    sound_speed,
    near,
    far,
    deriv_rows,
    deriv_lanes,
    pair,
    spread,
    labels,
    speed,
):
    count = local.shape[0]
    size = 8 * count

    def place_of(shape):
        return (lax.broadcasted_iota(jnp.int32, shape, 0), lax.broadcasted_iota(jnp.int32, shape, 1))

    row, column = place_of((count, size))
    repeat = (column % count == row).astype(F32)
    speed[...] = dot_full(sound_speed[...], repeat)
    wanted = dot_full(local[...].astype(F32), repeat, ((0,), (0,))).astype(jnp.int32)
    row, column = place_of((size, size))
    level, element = row // count, row % count
    level_out = column // count
    for facet in range(4):
        shift = -count if facet % 2 == 0 else count
        choice = jnp.broadcast_to(wanted[facet : facet + 1], (size, size))
        near[facet] = jnp.where((level == level_out) & (element == choice), 1.0, 0.0).astype(BF16)
        far[facet] = jnp.where((level == level_out) & (element + shift == choice), 1.0, 0.0).astype(BF16)
    lower = jnp.broadcast_to(wanted[4:5], (size, size))
    upper = jnp.broadcast_to(wanted[5:6], (size, size))
    hit = (level == 7) & (level_out == 0) & (element == lower)
    hit = hit | ((level == 0) & (level_out == 7) & (element == upper))
    near[4] = jnp.where(hit, 1.0, 0.0).astype(BF16)
    hit = (level == 0) & (level_out == 0) & (element - count == lower)
    hit = hit | ((level == 1) & (level_out == 7) & (element + count == upper))
    far[4] = jnp.where(hit, 1.0, 0.0).astype(BF16)

    row, column = place_of((64, 64))
    slopes, modes = derivative[...], basis[...]
    outer = kron_part(slopes, (64, 64), 8, 8)
    inner = kron_part(slopes, (64, 64), 1, 1)
    deriv_rows[0:64] = jnp.where(row % 8 == column % 8, outer, 0.0)
    deriv_rows[64:128] = jnp.where(row // 8 == column // 8, inner, 0.0)
    row, column = place_of((size, size))
    lanes = kron_part(slopes.T, (size, size), count, count)
    deriv_lanes[...] = jnp.where(row % count == column % count, lanes, 0.0)
    pair[...] = kron_part(modes, (64, 64), 8, 8) * kron_part(modes, (64, 64), 1, 1)

    blocks = owner_column.shape[0]
    peers = labels.shape[0]
    capacity = max(2, 2 * blocks // peers)
    row, column = place_of((blocks, blocks))
    earlier = (owner_column[...] == owner_row[...]) & (column < row)
    position = jnp.sum(jnp.where(earlier, 1.0, 0.0), 1, keepdims=True)
    slot = owner_column[...].astype(F32) * capacity + position
    wide = (8 * blocks, peers * 128)
    row, column = place_of((8 * blocks, blocks))
    repeat = (row // 8 == column).astype(F32)
    slot = dot_full(repeat, jnp.broadcast_to(slot, (blocks, 128)))
    element = dot_full(repeat, jnp.broadcast_to(element_column[...].astype(F32), (blocks, 128)))
    row, column = place_of((8 * blocks, 128))
    values = kron_part(modes.T, (8 * blocks, 128), 1, 1)
    inside = column % (8 * capacity) // 8
    for peer in range(peers):
        chosen = slot == (inside + peer * capacity).astype(F32)
        spread[:, peer * 128 : peer * 128 + 128] = jnp.where(chosen, values, 0.0)
        named = jnp.where(chosen & (row % 8 == 0), element + 1.0, 0.0)
        labels[peer] = jnp.broadcast_to(jnp.sum(named, 0, keepdims=True) - 1.0, (8, 128))


def shifted(sizes, shifts):
    pairs = []
    for index in np.ndindex(*sizes):
        source = [(i + s) % n for i, s, n in zip(index, shifts, sizes)]
        pairs.append((int(np.ravel_multi_index(source, sizes)), int(np.ravel_multi_index(index, sizes))))
    return pairs


def per_device(
    density,
    velocity,
    pressure,
    acoustic,
    sound_speed,
    derivative,
    mode_basis,
    neighbours,
    block_owner,
    block_element,
):
    size_x, size_y, size_z = lax.axis_size("fx"), lax.axis_size("fy"), lax.axis_size("fz")
    devices = size_x * size_y * size_z
    cells_x = density.shape[0]
    elements = acoustic.shape[0]
    device = lax.axis_index(("fx", "fy", "fz"))

    rows = 5 * cells_x * 8
    tiles = -(-rows // 128)
    state, low, high = call(
        pack_start_body,
        [(5, cells_x, 8, 128), (tiles * 8, 128), (tiles * 8, 128)],
        density,
        velocity,
        pressure,
        fetch=True,
    )
    above = lax.ppermute(low, "fz", shifted((size_z,), (1,)))
    below = lax.ppermute(high, "fz", shifted((size_z,), (-1,)))

    local = neighbours - device * elements
    size = 8 * elements
    blocks = block_owner.size
    capacity = max(2, 2 * blocks // size_y)
    fold = 128 // (8 * capacity)
    table = jax.ShapeDtypeStruct((5, size, size), BF16)
    near, far, deriv_rows, deriv_lanes, pair, spread, labels, speed = call(
        tables_body,
        [
            table,
            table,
            (128, 64),
            (size, size),
            (64, 64),
            (8 * blocks, size_y * 128),
            (size_y, 8, 128),
            (1, size),
        ],
        derivative,
        mode_basis,
        local,
        block_owner.reshape(blocks, 1),
        block_owner.reshape(1, blocks),
        block_element.reshape(blocks, 1),
        sound_speed.reshape(1, elements),
        fetch=True,
    )

    forward = [(i, i + 1) for i in range(devices - 1)]
    backward = [(i + 1, i) for i in range(devices - 1)]
    names = ("fx", "fy", "fz")

    def traces(front, rear):
        return lax.ppermute(front, names, forward), lax.ppermute(rear, names, backward)

    held = (4, 64, size)
    faces = (96, size)
    sound, partial, front, rear = call(
        acoustic_first_body,
        [held, held, faces, faces],
        acoustic,
        deriv_rows,
        deriv_lanes,
        speed,
        near,
        scratch=[pltpu.VMEM((512, 128), F32)],
    )
    before, after = traces(front, rear)

    six = 2 * HALO
    tall = 5 * six * HALO
    tall = -(-tall // 8) * 8
    edge_rows = tiles * 8
    edge, along_x, y_low, y_high, xy_low, xy_high = call(
        pack_next_body,
        [
            (edge_rows, 128),
            (5 * six * 8 + edge_rows, 128),
            (5 * cells_x * HALO + edge_rows, 128),
            (5 * cells_x * HALO + edge_rows, 128),
            (tall + edge_rows, 128),
            (tall + edge_rows, 128),
        ],
        state,
        above,
        below,
    )
    flat = (size_x, size_y)
    steps = [[(1, 0), (-1, 0)]] if size_x == 2 else [[(1, 0)], [(-1, 0)]]
    places, messages = [], []
    for spots in steps:
        messages.append(lax.ppermute(along_x, ("fx", "fy"), shifted(flat, spots[0])))
        places.append(tuple(spots))
    for dy, kept in ((1, y_low), (-1, y_high)):
        messages.append(lax.ppermute(kept, ("fx", "fy"), shifted(flat, (0, dy))))
        places.append(((0, dy),))
    for dy, kept in ((1, xy_low), (-1, xy_high)):
        for spots in steps:
            messages.append(lax.ppermute(kept, ("fx", "fy"), shifted(flat, (spots[0][0], dy))))
            places.append(tuple((dx, dy) for dx, _ in spots))

    sent = (size_y, 192 // fold + 8, 128)
    wide = cells_x + 2 * HALO
    rows_scratch = pltpu.VMEM((3, 64, 128), F32)

    def planes(count):
        return (5, count, 16, 256)

    def route(send):
        return lax.all_to_all(send, "fy", split_axis=0, concat_axis=0, tiled=True)

    start, send = call(
        functools.partial(flow_sources_body, tuple(places)),
        [planes(wide), sent],
        state,
        edge,
        *messages,
        pair,
        spread,
        labels,
        scratch=[pltpu.VMEM((3, wide, 16, 256), F32), rows_scratch],
    )
    received = route(send)
    flow_one, send_next = call(
        flow_first_body,
        [planes(wide - 2), sent],
        start,
        pair,
        spread,
        labels,
        scratch=[pltpu.VMEM(planes(wide), F32), rows_scratch],
    )
    sound_one, front, rear = call(
        functools.partial(acoustic_far_body, MIXES[0], False),
        [held, faces, faces],
        partial,
        before,
        after,
        far,
        received,
    )
    before, after = traces(front, rear)
    received = route(send_next)
    flow_state, send_next = call(
        flow_last_body,
        [(5, cells_x, 8, 128), sent],
        flow_one,
        start,
        pair,
        spread,
        labels,
        scratch=[pltpu.VMEM(planes(wide - 2), F32), rows_scratch, pltpu.VMEM(planes(wide - 4), F32)],
    )

    def local_part(mix, now):
        return call(
            functools.partial(acoustic_local_body, mix),
            [held, faces, faces],
            now,
            sound,
            deriv_rows,
            deriv_lanes,
            speed,
            near,
        )[0]

    partial = local_part(MIXES[1], sound_one)
    sound_two, front, rear = call(
        functools.partial(acoustic_far_body, MIXES[1], False),
        [held, faces, faces],
        partial,
        before,
        after,
        far,
        received,
    )
    before, after = traces(front, rear)
    received = route(send_next)
    partial = local_part(MIXES[2], sound_two)
    sound_state, _ = call(
        functools.partial(acoustic_far_body, MIXES[2], True),
        [(elements, 4, 512), held],
        partial,
        before,
        after,
        far,
        received,
        scratch=[pltpu.VMEM((512, 128), F32)],
    )
    return (flow_state, sound_state)


def solution(mesh):
    placed = (
        P("fx", "fy", "fz"),
        P(None, "fx", "fy", "fz"),
        P("fx", "fy", "fz"),
        P(("fx", "fy", "fz"), None, None),
        P(("fx", "fy", "fz")),
        P(),
        P(),
        P(("fx", "fy", "fz"), None),
        P("fx", "fy", "fz", None, None),
        P("fx", "fy", "fz", None),
    )
    return jax.shard_map(
        per_device,
        mesh=mesh,
        in_specs=placed,
        out_specs=(P(None, "fx", "fy", "fz"), P(("fx", "fy", "fz"), None, None)),
        check_vma=False,
    )
```

```python
import functools

import jax
import jax.numpy as jnp
import numpy as np
from jax import lax
from jax.experimental import pallas as pl
from jax.experimental.pallas import tpu as pltpu
from jax.sharding import PartitionSpec as P

HEAT_RATIO = 1.4
TIME_STEP = 0.1
VISCOSITY = 0.05
PENALTY = 0.5
HALO = 3
F32 = jnp.float32
BF16 = jnp.bfloat16
PARAMS = pltpu.CompilerParams(vmem_limit_bytes=24 * 1024 * 1024)
MIXES = ((0.0, 1.0), (0.75, 0.25), (1.0 / 3.0, 2.0 / 3.0))


def parts(values):
    high = values.astype(BF16)
    return high, (values - high.astype(F32)).astype(BF16)


def dot(left, right):
    return lax.dot_general(left, right, (((1,), (0,)), ((), ())), preferred_element_type=F32)


def dot_three(left, right):
    left_high, left_low = parts(left)
    right_high, right_low = parts(right)
    return dot(left_high, right_high) + dot(left_high, right_low) + dot(left_low, right_high)


def dot_full(left, right, dims=((1,), (0,))):
    return lax.dot_general(
        left, right, (dims, ((), ())), precision=lax.Precision.HIGHEST, preferred_element_type=F32
    )


def dot_exact_right(left, right):
    left_high, left_low = parts(left)
    return dot(left_high, right) + dot(left_low, right)


def call(body, outs, *operands, scratch=(), fetch=False, flags=None):
    whole = pl.BlockSpec(memory_space=pltpu.VMEM)
    outs = [out if isinstance(out, jax.ShapeDtypeStruct) else jax.ShapeDtypeStruct(out, F32) for out in outs]
    scratch = list(scratch)
    specs = [pl.BlockSpec(memory_space=pl.ANY) if fetch else whole] * len(operands)
    params = PARAMS
    kernel = body
    if fetch:
        count = len(operands)
        params = pltpu.CompilerParams(vmem_limit_bytes=60 * 1024 * 1024)
        first = 1 if flags is not None else 0
        total = first + count + len(outs)

        def kernel(*refs):
            held, sems = refs[total : total + count], refs[total + count]
            copies = [
                pltpu.make_async_copy(refs[first + i], held[i], sems.at[i]) for i in range(count)
            ]
            for copy in copies:
                copy.start()
            for copy in copies:
                copy.wait()
            body(*refs[:first], *held, *refs[first + count : total], *refs[total + count + 1 :])

        scratch = [pltpu.VMEM(o.shape, o.dtype) for o in operands] + [pltpu.SemaphoreType.DMA((count,))] + scratch
    if flags is not None:
        specs = [pl.BlockSpec(memory_space=pltpu.SMEM)] + specs
        operands = (flags,) + operands
    return pl.pallas_call(
        kernel,
        out_shape=outs,
        in_specs=specs,
        out_specs=[whole] * len(outs),
        scratch_shapes=scratch,
        compiler_params=params,
    )(*operands)


def paired(odd, to_next, to_last):
    return jnp.where(odd, to_last, to_next), jnp.where(odd, to_next, to_last)


def pack_start_body(flags, density, velocity, pressure, state, message_a, message_b):
    odd = flags[0] == 1
    rho = density[...]
    vel = velocity[...]
    state[0] = rho
    for k in range(3):
        state[1 + k] = rho * vel[k]
    square = vel[0] * vel[0] + vel[1] * vel[1] + vel[2] * vel[2]
    state[4] = pressure[...] / (HEAT_RATIO - 1.0) + 0.5 * rho * square
    rows = state[...].reshape(-1, 128)
    count = rows.shape[0]
    for tile in range(message_a.shape[0] // 8):
        piece = rows[tile * 128 : min(count, tile * 128 + 128)]
        if piece.shape[0] < 128:
            piece = jnp.concatenate([piece, jnp.zeros((128 - piece.shape[0], 128), F32)], 0)
        turned = piece.T
        first, second = paired(odd, turned[120:128], turned[0:8])
        message_a[tile * 8 : tile * 8 + 8] = first
        message_b[tile * 8 : tile * 8 + 8] = second


def pack_next_body(flags, state, got_a, got_b, edge, along_x, y_a, y_b, xy_a, xy_b):
    cells_x = state.shape[1]
    odd_z, odd = flags[0] == 1, flags[1] == 1
    row = lax.broadcasted_iota(jnp.int32, edge.shape, 0) % 8
    above, below = paired(odd_z, got_a[...], got_b[...])
    both = jnp.where(row < 4, above, below)
    edge[...] = both
    planes = [cells_x - HALO + i for i in range(HALO)] + list(range(HALO))
    for f in range(5):
        for s, x in enumerate(planes):
            at = (f * len(planes) + s) * 8
            along_x[at : at + 8] = state[f, x]
        for x in range(cells_x):
            at = (f * cells_x + x) * HALO
            first, second = paired(odd, state[f, x, 8 - HALO : 8], state[f, x, 0:HALO])
            y_a[at : at + HALO] = first
            y_b[at : at + HALO] = second
        at = f * 6
        for slot, height in ((1, 1), (2, 2), (3, 2), (4, 1)):
            x = planes[slot]
            first, second = paired(odd, state[f, x, 8 - height : 8], state[f, x, 0:height])
            xy_a[at : at + height] = first
            xy_b[at : at + height] = second
            at += height
    for message in (along_x, y_a, y_b, xy_a, xy_b):
        size = message.shape[0]
        message[size - edge.shape[0] : size] = both


def turned_edges(message):
    size = message.shape[0]
    rows = []
    for tile in range(3):
        piece = message[size - 24 + tile * 8 : size - 16 + tile * 8]
        rows.append(jnp.concatenate([piece, jnp.zeros((112, 128), F32), piece], 0).T)
    return rows


def assemble(wide, state, edge, beside, cells_x):
    for dx, dy, message in [(0, 0, edge)] + beside:
        turned = turned_edges(message)
        if dx == 0:
            columns = [(HALO + x, x, x) for x in range(cells_x)]
        elif dx < 0:
            columns = [(i, cells_x - HALO + i, i) for i in range(HALO)]
        else:
            columns = [(HALO + cells_x + i, i, HALO + i) for i in range(HALO)]
        for f in range(5):
            for plane, x, slot in columns:
                height = 8 if dy == 0 else HALO
                at = (f * (cells_x if dx == 0 else 2 * HALO) + slot) * height
                if dx != 0 and dy != 0:
                    if slot in (0, 5):
                        continue
                    height = (0, 1, 2, 2, 1)[slot]
                    at = f * 6 + (0, 0, 1, 3, 5)[slot]
                low, high = {0: (0, 8), 1: (8, 8 + height), -1: (16 - height, 16)}[dy]
                if dx == 0 and dy == 0:
                    wide[f, plane, 0:8, 0:128] = state[f, x]
                else:
                    wide[f, plane, low:high, 0:128] = message[at : at + height]
                group = f * cells_x + x
                block = turned[group // 16][(group % 16) * 8 : (group % 16) * 8 + 8]
                first = 8 - height if dy < 0 else 0
                wide[f, plane, low:high, 128:256] = block[first : first + height]


def derive_planes(wide, derived, first, last):
    def derive(i, _):
        rho, mx, my, mz, energy = [wide[f, i] for f in range(5)]
        inverse = 1.0 / rho
        u, v, w = mx * inverse, my * inverse, mz * inverse
        p = (HEAT_RATIO - 1.0) * (energy - 0.5 * (mx * u + my * v + mz * w))
        derived[0, i] = u
        derived[1, i] = v
        derived[2, i] = w
        derived[3, i] = p
        derived[4, i] = jnp.sqrt(HEAT_RATIO * jnp.abs(p) * inverse)
        return 0

    lax.fori_loop(first, last, derive, 0)


def derive_speeds(wide, derived, first, last):
    def derive(i, _):
        inverse = 1.0 / wide[0, i]
        for k in range(3):
            derived[k, i] = wide[1 + k, i] * inverse
        return 0

    lax.fori_loop(first, last, derive, 0)


def flow_rate_section(wide, derived, start, offset, mix, write, inner=False):
    depth = wide.shape[1]
    near, lanes = slice(0, 8), slice(0, 128)
    every = (slice(None), slice(None))
    windows = [(near, lanes), (slice(None), lanes), (near, slice(None))] if inner else [every] * 3
    kept = windows[0]

    def flux(fields, other, along):
        speed, p = other[along], other[3]
        out = [fields[1 + along]]
        for k in range(3):
            value = fields[1 + k] * speed
            out.append(value + p if k == along else value)
        out.append((fields[4] + p) * speed)
        return out, jnp.abs(speed) + other[4]

    def face(left, right):
        (fields_l, flux_l, speed_l), (fields_r, flux_r, speed_r) = left, right
        speed = jnp.maximum(speed_l, speed_r)
        viscous = speed + 2.0 * VISCOSITY
        return [
            (flux_l[f] + flux_r[f])
            - (viscous if 1 <= f <= 3 else speed) * (fields_r[f] - fields_l[f])
            for f in range(5)
        ]

    def plane(i, along):
        rows, columns = windows[along]
        fields = [wide[f, i, rows, columns] for f in range(5)]
        other = [derived[f, i, rows, columns] for f in range(5)]
        return (fields,) + flux(fields, other, along)

    def section(i, before):
        here = plane(i, 0)
        ahead = face(here, plane(i + 1, 0))
        total = [ahead[f] - before[f] for f in range(5)]
        for along, axis, size in ((1, 0, 16), (2, 1, 256)):
            here = plane(i, along)
            moved = (
                [pltpu.roll(a, size - 1, axis) for a in here[0]],
                [pltpu.roll(a, size - 1, axis) for a in here[1]],
                pltpu.roll(here[2], size - 1, axis),
            )
            faces = face(here, moved)
            for f in range(5):
                change = faces[f] - pltpu.roll(faces[f], 1, axis)
                total[f] = total[f] + (change[0:8, 0:128] if inner else change)
        for f in range(5):
            value = wide[f, i, kept[0], kept[1]] - (0.5 * TIME_STEP) * total[f]
            if mix[0] != 0.0:
                value = mix[0] * start[f, i + offset, kept[0], kept[1]] + mix[1] * value
            write(i - 1, f, value)
        return tuple(ahead)

    lax.fori_loop(1, depth - 1, section, tuple(face(plane(0, 0), plane(1, 0))))


def lamb(derived, first, cells_x, lamb_rows):
    def one(x, _):
        i = first + x
        slopes = []
        slopes.append([derived[c, i + 1, 0:8, 0:128] - derived[c, i - 1, 0:8, 0:128] for c in range(3)])
        columns = [derived[c, i, :, 0:128] for c in range(3)]
        slopes.append([(pltpu.roll(a, 15, 0) - pltpu.roll(a, 1, 0))[0:8] for a in columns])
        rows = [derived[c, i, 0:8, :] for c in range(3)]
        slopes.append([(pltpu.roll(a, 255, 1) - pltpu.roll(a, 1, 1))[:, 0:128] for a in rows])
        vel = [derived[c, i, 0:8, 0:128] for c in range(3)]
        curl = [
            0.5 * (slopes[1][2] - slopes[2][1]),
            0.5 * (slopes[2][0] - slopes[0][2]),
            0.5 * (slopes[0][1] - slopes[1][0]),
        ]
        at = pl.multiple_of(x * 8, 8)
        lamb_rows[0, pl.ds(at, 8), :] = curl[1] * vel[2] - curl[2] * vel[1]
        lamb_rows[1, pl.ds(at, 8), :] = curl[2] * vel[0] - curl[0] * vel[2]
        lamb_rows[2, pl.ds(at, 8), :] = curl[0] * vel[1] - curl[1] * vel[0]
        return 0

    lax.fori_loop(0, cells_x, one, 0)


def project(lamb_rows, pair, spread, labels, send):
    peers = send.shape[0]
    fold = 192 // (send.shape[1] - 8)
    group = lax.broadcasted_iota(jnp.int32, (64 // fold, 128), 1) // (128 // fold)
    height = 64 // fold
    for c in range(3):
        modes = dot_three(pair[...], lamb_rows[c])
        sent = dot_three(modes, spread[...])
        for peer in range(peers):
            mine = sent[:, peer * 128 : peer * 128 + 128]
            folded = mine[0:height]
            for g in range(1, fold):
                folded = jnp.where(group == g, mine[g * height : g * height + height], folded)
            send[peer, c * height : c * height + height] = folded
    send[:, 3 * height : 3 * height + 8] = labels[...]


def flow_sources_body(places, flags, *refs):
    state, edge = refs[0:2]
    messages = refs[2 : 2 + len(places)]
    pair, spread, labels = refs[2 + len(places) : 5 + len(places)]
    wide, send, derived, lamb_rows = refs[5 + len(places) : 9 + len(places)]
    spare = refs[9 + len(places) :]
    cells_x = state.shape[1]
    odd = flags[1] == 1
    beside, k = [], 0
    while k < len(places):
        if places[k][0][1] == 0:
            beside.extend((dx, 0, messages[k]) for dx, _ in places[k])
            k += 1
            continue
        above, below = spare[:2]
        spare = spare[2:]
        above[...], below[...] = paired(odd, messages[k][...], messages[k + 1][...])
        beside.extend((dx, 1, above) for dx, _ in places[k])
        beside.extend((dx, -1, below) for dx, _ in places[k])
        k += 2
    assemble(wide, state, edge, beside, cells_x)
    derive_speeds(wide, derived, HALO - 1, HALO + cells_x + 1)
    lamb(derived, HALO, cells_x, lamb_rows)
    project(lamb_rows, pair, spread, labels, send)


def flow_first_body(wide, out, lamb_rows, derived):
    def write(i, f, value):
        out[f, i] = value

    planes = wide.shape[1]
    cells_x = planes - 2 * HALO
    derive_planes(wide, derived, 0, planes)
    flow_rate_section(wide, derived, wide, 0, MIXES[0], write)
    derive_speeds(out, derived, HALO - 2, HALO + cells_x)
    lamb(derived, HALO - 1, cells_x, lamb_rows)


def flow_last_body(wide, start, pair, spread, labels, out, send, derived, lamb_rows, second):
    def write_second(i, f, value):
        second[f, i] = value

    def write(i, f, value):
        out[f, i] = value

    planes = wide.shape[1]
    cells_x = out.shape[1]
    derive_planes(wide, derived, 0, planes)
    flow_rate_section(wide, derived, start, 1, MIXES[1], write_second)
    derive_planes(second, derived, 0, planes - 2)
    lamb(derived, 1, cells_x, lamb_rows)
    project(lamb_rows, pair, spread, labels, send)
    flow_rate_section(second, derived, start, 2, MIXES[2], write, inner=True)


def faces_out(state, rear, front):
    lane = lax.broadcasted_iota(jnp.int32, (32, 128), 1) // 16
    for c in range(4):
        front[c * 8 : c * 8 + 8] = state[c, 56:64]
        rear[c * 8 : c * 8 + 8] = state[c, 0:8]
        front[32 + c * 8 : 40 + c * 8] = state[c, pl.ds(7, 8, stride=8), :]
        rear[32 + c * 8 : 40 + c * 8] = state[c, pl.ds(0, 8, stride=8), :]
    rows = state[...].reshape(256, 128)
    last = jnp.zeros((32, 128), F32)
    first = jnp.zeros((32, 128), F32)
    for j in range(8):
        piece = rows[j * 32 : j * 32 + 32]
        last = jnp.where(lane == j, pltpu.roll(piece, (j * 16 + 16) % 128, 1), last)
        first = jnp.where(lane == j, pltpu.roll(piece, j * 16, 1) if j else piece, first)
    front[64:96] = last
    rear[64:96] = first


def faces_sent(odd, state, message_a, message_b):
    faces_out(state, message_b, message_a)
    message_a[...], message_b[...] = paired(odd, message_a[...], message_b[...])


def lift(total, before, after, sides, factor):
    def place(face, rows, target):
        value = factor * dot_exact_right(rows, sides[face])
        for c in range(4):
            total[c, target, :] += value[c * 8 : c * 8 + 8]

    place(0, before[0:32], pl.ds(0, 8))
    place(1, after[0:32], pl.ds(56, 8))
    place(2, before[32:64], pl.ds(0, 8, stride=8))
    place(3, after[32:64], pl.ds(7, 8, stride=8))


def rate_local(state, deriv_rows, deriv_lanes, speed, sides):
    fields = [state[c] for c in range(4)]
    by_rows = dot_three(deriv_rows[...], jnp.concatenate(fields[0:3], 1))
    by_lanes = dot_three(jnp.concatenate([fields[0], fields[3]], 0), deriv_lanes[...])
    divergence = by_rows[0:64, 128:256] + by_rows[64:128, 256:384] + by_lanes[64:128]
    rates = [
        -(speed[...] * speed[...]) * divergence,
        -by_rows[0:64, 0:128],
        -by_rows[64:128, 0:128],
        -by_lanes[0:64],
    ]
    row = lax.broadcasted_iota(jnp.int32, (64, 128), 0)
    lane = lax.broadcasted_iota(jnp.int32, (64, 128), 1)
    count = jnp.zeros((64, 128), F32)
    for value in (row // 8, row % 8, lane // 16):
        count = count + jnp.where((value == 0) | (value == 7), PENALTY, 0.0)
    side = PENALTY * dot_exact_right(state[...].reshape(256, 128), sides[4])
    return [rates[c] - count * fields[c] + side[c * 64 : c * 64 + 64] for c in range(4)]


def local_update(mix, state, start, deriv_rows, deriv_lanes, speed, sides, out, front, rear):
    rates = rate_local(state, deriv_rows, deriv_lanes, speed, sides)
    for c in range(4):
        value = state[c] + TIME_STEP * rates[c]
        if mix[0] != 0.0:
            value = mix[0] * start[c] + mix[1] * value
        out[c] = value
    faces_out(state, rear, front)
    lift(out, front, rear, sides, TIME_STEP * mix[1] * PENALTY)


def acoustic_local_body(mix, state, start, deriv_rows, deriv_lanes, speed, sides, out, front, rear):
    local_update(mix, state, start, deriv_rows, deriv_lanes, speed, sides, out, front, rear)


def order_table(count, turned):
    row = lax.broadcasted_iota(jnp.int32, (4 * count, 4 * count), 0)
    column = lax.broadcasted_iota(jnp.int32, (4 * count, 4 * count), 1)
    if turned:
        row, column = column, row
    return (column == (row % count) * 4 + row // count).astype(F32)


def acoustic_first_body(
    flags, given, deriv_rows, deriv_lanes, speed, sides, state, out, message_a, message_b, turned, front, rear
):
    count = given.shape[0]
    rows = jnp.concatenate([given[e] for e in range(count)], 0)
    rows = dot_full(order_table(count, False), rows)
    rows = jnp.concatenate([rows, jnp.zeros((128 - 4 * count, rows.shape[1]), F32)], 0)
    turned[...] = rows.T
    lane = lax.broadcasted_iota(jnp.int32, (64, 128), 1) // count
    fields = [jnp.zeros((64, 128), F32)] * 4
    for z in range(8):
        piece = turned[pl.ds(z, 64, stride=8), :]
        for c in range(4):
            move = (z - c) * count % 128
            fields[c] = jnp.where(lane == z, pltpu.roll(piece, move, 1) if move else piece, fields[c])
    for c in range(4):
        state[c] = fields[c]
    local_update(MIXES[0], state, state, deriv_rows, deriv_lanes, speed, sides, out, front, rear)
    message_a[...], message_b[...] = paired(flags[0] == 1, front[...], rear[...])


def natural_order(state, out, turned):
    count = out.shape[0]
    lane = lax.broadcasted_iota(jnp.int32, (64, 128), 1) // count
    for z in range(8):
        value = jnp.zeros((64, 128), F32)
        for c in range(4):
            move = (c - z) * count % 128
            value = jnp.where(lane == c, pltpu.roll(state[c], move, 1) if move else state[c], value)
        turned[pl.ds(z, 64, stride=8), :] = value
    rows = dot_full(order_table(count, True), turned[...].T[0 : 4 * count])
    for e in range(count):
        out[e] = rows[4 * e : 4 * e + 4]


def remote_part(out, before, after, sides_far, factor):
    lift(out, before, after, sides_far, factor)
    lane = lax.broadcasted_iota(jnp.int32, (32, 128), 1) // 16
    last, first = before[64:96], after[64:96]
    pieces = []
    for j in range(8):
        left = pltpu.roll(last, 128 - j * 16, 1) if j else last
        right = pltpu.roll(first, (144 - j * 16) % 128, 1) if j != 1 else first
        pieces.append(jnp.where(lane == 0, left, jnp.where(lane == 1, right, 0.0)))
    value = factor * dot_exact_right(jnp.concatenate(pieces, 0), sides_far[4])
    for c in range(4):
        out[c] += value[c * 64 : c * 64 + 64]


def acoustic_far_body(mix, kind, flags, partial, got_a, got_b, sides_far, received, *refs):
    odd = flags[0] == 1
    if kind == "last":
        given_out, out, turned, before, after = refs
    elif kind == "first":
        lamb_rows, pair, spread, labels, out, message_a, message_b, send, before, after = refs
    else:
        out, message_a, message_b, before, after = refs
    after[...], before[...] = paired(odd, got_a[...], got_b[...])
    out[...] = partial[...]
    remote_part(out, before, after, sides_far, TIME_STEP * mix[1] * PENALTY)
    place(received, out, TIME_STEP * mix[1])
    if kind == "last":
        natural_order(out, given_out, turned)
        return
    faces_sent(odd, out, message_a, message_b)
    if kind == "first":
        project(lamb_rows, pair, spread, labels, send)


def place(received, out, factor):
    peers, size = received.shape[0], received.shape[1]
    fold = 192 // (size - 8)
    height = 64 // fold
    target = lax.broadcasted_iota(jnp.int32, (128, 128), 0)
    lane = lax.broadcasted_iota(jnp.int32, (128, 128), 1)
    total = None
    for peer in range(peers):
        label = received[peer, size - 8 : size - 7, :]
        label = jnp.broadcast_to(label, (128, 128)).astype(jnp.int32)
        hit = (label == target % 16) & (lane % 8 == target // 16)
        chosen = [jnp.where(hit & (lane // (128 // fold) == g), 1.0, 0.0) for g in range(fold)]
        chosen = jnp.concatenate(chosen, 0).astype(BF16)
        high, low = parts(received[peer, 0 : size - 8])
        dims = (((1,), (1,)), ((), ()))
        value = lax.dot_general(high, chosen, dims, preferred_element_type=F32)
        value = value + lax.dot_general(low, chosen, dims, preferred_element_type=F32)
        total = value if total is None else total + value
    for c in range(3):
        for g in range(fold):
            rows = slice(g * height, g * height + height)
            out[1 + c, rows] = out[1 + c, rows] + factor * (
                total[c * height : c * height + height, g * 128 : g * 128 + 128]
            )


def kron_part(matrix, shape, rows_by, columns_by):
    row = lax.broadcasted_iota(jnp.int32, (shape[0], 8), 0)
    level = lax.broadcasted_iota(jnp.int32, (shape[0], 8), 1)
    left = (row // rows_by % 8 == level).astype(F32)
    level = lax.broadcasted_iota(jnp.int32, (8, shape[1]), 0)
    column = lax.broadcasted_iota(jnp.int32, (8, shape[1]), 1)
    right = (column // columns_by % 8 == level).astype(F32)
    return dot_full(dot_full(left, matrix), right)


def tables_body(
    packed,
    near,
    far,
    deriv_rows,
    deriv_lanes,
    pair,
    spread,
    labels,
    speed,
):
    size = near.shape[1]
    count = size // 8
    blocks = spread.shape[0] // 8

    def place_of(shape):
        return (lax.broadcasted_iota(jnp.int32, shape, 0), lax.broadcasted_iota(jnp.int32, shape, 1))

    row, column = place_of((count, size))
    repeat = (column % count == row).astype(F32)
    speed[...] = dot_full(packed[24:25, 0:count], repeat)
    wanted = dot_full(packed[16:24, 0:count], repeat).astype(jnp.int32)
    row, column = place_of((size, size))
    level, element = row // count, row % count
    level_out = column // count
    for facet in range(4):
        shift = -count if facet % 2 == 0 else count
        choice = jnp.broadcast_to(wanted[facet : facet + 1], (size, size))
        near[facet] = jnp.where((level == level_out) & (element == choice), 1.0, 0.0).astype(BF16)
        far[facet] = jnp.where((level == level_out) & (element + shift == choice), 1.0, 0.0).astype(BF16)
    lower = jnp.broadcast_to(wanted[4:5], (size, size))
    upper = jnp.broadcast_to(wanted[5:6], (size, size))
    hit = (level == 7) & (level_out == 0) & (element == lower)
    hit = hit | ((level == 0) & (level_out == 7) & (element == upper))
    near[4] = jnp.where(hit, 1.0, 0.0).astype(BF16)
    hit = (level == 0) & (level_out == 0) & (element - count == lower)
    hit = hit | ((level == 1) & (level_out == 7) & (element + count == upper))
    far[4] = jnp.where(hit, 1.0, 0.0).astype(BF16)

    row, column = place_of((64, 64))
    slopes, modes = packed[0:8, 0:8], packed[8:16, 0:8]
    outer = kron_part(slopes, (64, 64), 8, 8)
    inner = kron_part(slopes, (64, 64), 1, 1)
    deriv_rows[0:64] = jnp.where(row % 8 == column % 8, outer, 0.0)
    deriv_rows[64:128] = jnp.where(row // 8 == column // 8, inner, 0.0)
    row, column = place_of((size, size))
    lanes = kron_part(slopes.T, (size, size), count, count)
    deriv_lanes[...] = jnp.where(row % count == column % count, lanes, 0.0)
    pair[...] = kron_part(modes, (64, 64), 8, 8) * kron_part(modes, (64, 64), 1, 1)

    peers = labels.shape[0]
    capacity = max(2, 2 * blocks // peers)
    row, column = place_of((blocks, blocks))

    def upright(values):
        return jnp.sum(jnp.where(row == column, values, 0.0), 1, keepdims=True)

    owner_row = packed[25:26, 0:blocks]
    owner_column = upright(owner_row)
    earlier = (owner_column == owner_row) & (column < row)
    position = jnp.sum(jnp.where(earlier, 1.0, 0.0), 1, keepdims=True)
    slot = owner_column * capacity + position
    element_column = upright(packed[26:27, 0:blocks])
    wide = (8 * blocks, peers * 128)
    row, column = place_of((8 * blocks, blocks))
    repeat = (row // 8 == column).astype(F32)
    slot = dot_full(repeat, jnp.broadcast_to(slot, (blocks, 128)))
    element = dot_full(repeat, jnp.broadcast_to(element_column, (blocks, 128)))
    row, column = place_of((8 * blocks, 128))
    values = kron_part(modes.T, (8 * blocks, 128), 1, 1)
    inside = column % (8 * capacity) // 8
    for peer in range(peers):
        chosen = slot == (inside + peer * capacity).astype(F32)
        spread[:, peer * 128 : peer * 128 + 128] = jnp.where(chosen, values, 0.0)
        named = jnp.where(chosen & (row % 8 == 0), element + 1.0, 0.0)
        labels[peer] = jnp.broadcast_to(jnp.sum(named, 0, keepdims=True) - 1.0, (8, 128))


def shifted(sizes, shifts):
    pairs = []
    for index in np.ndindex(*sizes):
        source = [(i + s) % n for i, s, n in zip(index, shifts, sizes)]
        pairs.append((int(np.ravel_multi_index(source, sizes)), int(np.ravel_multi_index(index, sizes))))
    return pairs


def partners(sizes, axis, second, shift_x=0):
    pairs = []
    for index in np.ndindex(*sizes):
        source = list(index)
        step = 1 if (index[axis] % 2 == 0) != second else -1
        source[axis] = (index[axis] + step) % sizes[axis]
        if shift_x:
            source[0] = (index[0] + shift_x) % sizes[0]
        pairs.append((int(np.ravel_multi_index(source, sizes)), int(np.ravel_multi_index(index, sizes))))
    return pairs


def per_device(
    density,
    velocity,
    pressure,
    acoustic,
    sound_speed,
    derivative,
    mode_basis,
    neighbours,
    block_owner,
    block_element,
):
    size_x, size_y, size_z = lax.axis_size("fx"), lax.axis_size("fy"), lax.axis_size("fz")
    devices = size_x * size_y * size_z
    cells_x = density.shape[0]
    elements = acoustic.shape[0]
    device = lax.axis_index(("fx", "fy", "fz"))

    names = ("fx", "fy", "fz")
    flags = jnp.stack([lax.axis_index("fz") % 2, lax.axis_index("fy") % 2]).astype(jnp.int32)

    rows = 5 * cells_x * 8
    tiles = -(-rows // 128)
    state, to_a, to_b = call(
        pack_start_body,
        [(5, cells_x, 8, 128), (tiles * 8, 128), (tiles * 8, 128)],
        density,
        velocity,
        pressure,
        fetch=True,
        flags=flags,
    )
    edge_a = lax.ppermute(to_a, "fz", partners((size_z,), 0, False))
    edge_b = lax.ppermute(to_b, "fz", partners((size_z,), 0, True))

    local = (neighbours - device * elements).T.astype(F32)
    size = 8 * elements
    blocks = block_owner.size
    capacity = max(2, 2 * blocks // size_y)
    fold = 128 // (8 * capacity)
    width = max(elements, blocks)
    packed = jnp.concatenate(
        [
            jnp.pad(derivative, ((0, 0), (0, width - 8))),
            jnp.pad(mode_basis, ((0, 0), (0, width - 8))),
            jnp.pad(local, ((0, 2), (0, width - elements))),
            jnp.pad(sound_speed.reshape(1, elements), ((0, 0), (0, width - elements))),
            jnp.pad(block_owner.reshape(1, blocks).astype(F32), ((0, 0), (0, width - blocks))),
            jnp.pad(block_element.reshape(1, blocks).astype(F32), ((0, 5), (0, width - blocks))),
        ],
        0,
    )
    table = jax.ShapeDtypeStruct((5, size, size), BF16)
    near, far, deriv_rows, deriv_lanes, pair, spread, labels, speed = call(
        tables_body,
        [
            table,
            table,
            (128, 64),
            (size, size),
            (64, 64),
            (8 * blocks, size_y * 128),
            (size_y, 8, 128),
            (1, size),
        ],
        packed,
    )

    near_pairs = [(i ^ 1, i) for i in range(devices)]
    far_pairs = [pair for i in range(1, devices - 1, 2) for pair in ((i, i + 1), (i + 1, i))]

    def traces(to_a, to_b):
        far_got = lax.ppermute(to_b, names, far_pairs)
        return lax.ppermute(to_a, names, near_pairs), far_got

    held = (4, 64, size)
    faces = (96, size)
    sides = [pltpu.VMEM(faces, F32)] * 2
    sound, partial, to_a, to_b = call(
        acoustic_first_body,
        [held, held, faces, faces],
        acoustic,
        deriv_rows,
        deriv_lanes,
        speed,
        near,
        scratch=[pltpu.VMEM((512, 128), F32)] + sides,
        flags=flags,
    )
    got_a, got_b = traces(to_a, to_b)

    six = 2 * HALO
    edge_rows = tiles * 8
    shapes = [
        (edge_rows, 128),
        (5 * six * 8 + edge_rows, 128),
        (5 * cells_x * HALO + edge_rows, 128),
        (5 * cells_x * HALO + edge_rows, 128),
        (32 + edge_rows, 128),
        (32 + edge_rows, 128),
    ]
    edge, along_x, y_a, y_b, xy_a, xy_b = call(pack_next_body, shapes, state, edge_a, edge_b, flags=flags)
    flat = (size_x, size_y)
    steps = [[(1, 0), (-1, 0)]] if size_x == 2 else [[(1, 0)], [(-1, 0)]]
    places, messages = [], []
    for first, second, spots in [(y_a, y_b, [(0, 0)])] + [(xy_a, xy_b, spots) for spots in steps]:
        shift = spots[0][0]
        for kept, side in ((first, False), (second, True)):
            messages.append(lax.ppermute(kept, ("fx", "fy"), partners(flat, 1, side, shift)))
            places.append(tuple((dx, 1) for dx, _ in spots))
    for spots in steps:
        messages.append(lax.ppermute(along_x, ("fx", "fy"), shifted(flat, spots[0])))
        places.append(tuple(spots))

    sent = (size_y, 192 // fold + 8, 128)
    wide = cells_x + 2 * HALO
    rows_shape = (3, 64, 128)
    rows_scratch = pltpu.VMEM(rows_shape, F32)

    def planes(count):
        return (5, count, 16, 256)

    def route(send):
        return lax.all_to_all(send, "fy", split_axis=0, concat_axis=0, tiled=True)

    spare = [pltpu.VMEM(shapes[2], F32)] * 2 + [pltpu.VMEM(shapes[4], F32)] * (2 * len(steps))
    start, send = call(
        functools.partial(flow_sources_body, tuple(places)),
        [planes(wide), sent],
        state,
        edge,
        *messages,
        pair,
        spread,
        labels,
        scratch=[pltpu.VMEM((3, wide, 16, 256), F32), rows_scratch] + spare,
        flags=flags,
    )
    received = route(send)
    flow_one, lamb_rows = call(
        flow_first_body,
        [planes(wide - 2), rows_shape],
        start,
        scratch=[pltpu.VMEM(planes(wide), F32)],
    )
    sound_one, to_a, to_b, send = call(
        functools.partial(acoustic_far_body, MIXES[0], "first"),
        [held, faces, faces, sent],
        partial,
        got_a,
        got_b,
        far,
        received,
        lamb_rows,
        pair,
        spread,
        labels,
        scratch=sides,
        flags=flags,
    )
    got_a, got_b = traces(to_a, to_b)
    received = route(send)

    def local_part(mix, now):
        return call(
            functools.partial(acoustic_local_body, mix),
            [held, faces, faces],
            now,
            sound,
            deriv_rows,
            deriv_lanes,
            speed,
            near,
        )[0]

    partial = local_part(MIXES[1], sound_one)
    flow_state, send = call(
        flow_last_body,
        [(5, cells_x, 8, 128), sent],
        flow_one,
        start,
        pair,
        spread,
        labels,
        scratch=[pltpu.VMEM(planes(wide - 2), F32), rows_scratch, pltpu.VMEM(planes(wide - 4), F32)],
    )
    sound_two, to_a, to_b = call(
        functools.partial(acoustic_far_body, MIXES[1], "second"),
        [held, faces, faces],
        partial,
        got_a,
        got_b,
        far,
        received,
        scratch=sides,
        flags=flags,
    )
    got_a, got_b = traces(to_a, to_b)
    received = route(send)
    partial = local_part(MIXES[2], sound_two)
    sound_state, _ = call(
        functools.partial(acoustic_far_body, MIXES[2], "last"),
        [(elements, 4, 512), held],
        partial,
        got_a,
        got_b,
        far,
        received,
        scratch=[pltpu.VMEM((512, 128), F32)] + sides,
        flags=flags,
    )
    return (flow_state, sound_state)


def solution(mesh):
    placed = (
        P("fx", "fy", "fz"),
        P(None, "fx", "fy", "fz"),
        P("fx", "fy", "fz"),
        P(("fx", "fy", "fz"), None, None),
        P(("fx", "fy", "fz")),
        P(),
        P(),
        P(("fx", "fy", "fz"), None),
        P("fx", "fy", "fz", None, None),
        P("fx", "fy", "fz", None),
    )
    return jax.shard_map(
        per_device,
        mesh=mesh,
        in_specs=placed,
        out_specs=(P(None, "fx", "fy", "fz"), P(("fx", "fy", "fz"), None, None)),
        check_vma=False,
    )
```

```python
import functools

import jax
import jax.numpy as jnp
import numpy as np
from jax import lax
from jax.experimental import pallas as pl
from jax.experimental.pallas import tpu as pltpu
from jax.sharding import PartitionSpec as P

HEAT_RATIO = 1.4
TIME_STEP = 0.1
VISCOSITY = 0.05
PENALTY = 0.5
HALO = 3
F32 = jnp.float32
BF16 = jnp.bfloat16
PARAMS = pltpu.CompilerParams(vmem_limit_bytes=24 * 1024 * 1024)
MIXES = ((0.0, 1.0), (0.75, 0.25), (1.0 / 3.0, 2.0 / 3.0))


def parts(values):
    high = values.astype(BF16)
    return high, (values - high.astype(F32)).astype(BF16)


def dot(left, right):
    return lax.dot_general(left, right, (((1,), (0,)), ((), ())), preferred_element_type=F32)


def dot_three(left, right):
    left_high, left_low = parts(left)
    right_high, right_low = parts(right)
    return dot(left_high, right_high) + dot(left_high, right_low) + dot(left_low, right_high)


def dot_full(left, right, dims=((1,), (0,))):
    return lax.dot_general(
        left, right, (dims, ((), ())), precision=lax.Precision.HIGHEST, preferred_element_type=F32
    )


def dot_exact_right(left, right):
    left_high, left_low = parts(left)
    return dot(left_high, right) + dot(left_low, right)


def call(body, outs, *operands, scratch=(), fetch=False, last=0):
    whole = pl.BlockSpec(memory_space=pltpu.VMEM)
    outs = [out if isinstance(out, jax.ShapeDtypeStruct) else jax.ShapeDtypeStruct(out, F32) for out in outs]
    scratch = list(scratch)
    anywhere = pl.BlockSpec(memory_space=pltpu.HBM)
    specs = [anywhere if fetch else whole] * (len(operands) - last) + [anywhere] * last
    kernel = body
    if fetch:
        count = len(operands)
        total = count + len(outs)

        def kernel(*refs):
            held, sems = refs[total : total + count], refs[total + count]
            copies = [
                pltpu.make_async_copy(refs[i], held[i], sems.at[i]) for i in range(count)
            ]
            for copy in copies:
                copy.start()
            for copy in copies:
                copy.wait()
            body(*held, *refs[count:total], *refs[total + count + 1 :])

        scratch = [pltpu.VMEM(o.shape, o.dtype) for o in operands] + [pltpu.SemaphoreType.DMA((count,))] + scratch
    return pl.pallas_call(
        kernel,
        out_shape=outs,
        in_specs=specs,
        out_specs=[whole] * len(outs),
        scratch_shapes=scratch,
        compiler_params=PARAMS,
    )(*operands)


def is_odd(axis):
    return lax.axis_index(axis) % 2 == 1


def paired(odd, to_next, to_last):
    return jnp.where(odd, to_last, to_next), jnp.where(odd, to_next, to_last)


def pack_start_body(density, velocity, pressure, state, message_a, message_b):
    odd = is_odd("fz")
    rho = density[...]
    vel = velocity[...]
    state[0] = rho
    for k in range(3):
        state[1 + k] = rho * vel[k]
    square = vel[0] * vel[0] + vel[1] * vel[1] + vel[2] * vel[2]
    state[4] = pressure[...] / (HEAT_RATIO - 1.0) + 0.5 * rho * square
    rows = state[...].reshape(-1, 128)
    count = rows.shape[0]
    for tile in range(message_a.shape[0] // 8):
        piece = rows[tile * 128 : min(count, tile * 128 + 128)]
        if piece.shape[0] < 128:
            piece = jnp.concatenate([piece, jnp.zeros((128 - piece.shape[0], 128), F32)], 0)
        turned = piece.T
        first, second = paired(odd, turned[120:128], turned[0:8])
        message_a[tile * 8 : tile * 8 + 8] = first
        message_b[tile * 8 : tile * 8 + 8] = second


def pack_next_body(state, got_a, got_b, _, edge, along_x, y_a, y_b, xy_a, xy_b):
    cells_x = state.shape[1]
    odd_z, odd = is_odd("fz"), is_odd("fy")
    row = lax.broadcasted_iota(jnp.int32, edge.shape, 0) % 8
    above, below = paired(odd_z, got_a[...], got_b[...])
    both = jnp.where(row < 4, above, below)
    edge[...] = both
    planes = [cells_x - HALO + i for i in range(HALO)] + list(range(HALO))
    for f in range(5):
        for s, x in enumerate(planes):
            at = (f * len(planes) + s) * 8
            along_x[at : at + 8] = state[f, x]
        for x in range(cells_x):
            at = (f * cells_x + x) * HALO
            first, second = paired(odd, state[f, x, 8 - HALO : 8], state[f, x, 0:HALO])
            y_a[at : at + HALO] = first
            y_b[at : at + HALO] = second
        at = f * 6
        for slot, height in ((1, 1), (2, 2), (3, 2), (4, 1)):
            x = planes[slot]
            first, second = paired(odd, state[f, x, 8 - height : 8], state[f, x, 0:height])
            xy_a[at : at + height] = first
            xy_b[at : at + height] = second
            at += height
    for message in (along_x, y_a, y_b, xy_a, xy_b):
        size = message.shape[0]
        message[size - edge.shape[0] : size] = both


def turned_edges(message):
    size = message.shape[0]
    rows = []
    for tile in range(3):
        piece = message[size - 24 + tile * 8 : size - 16 + tile * 8]
        rows.append(jnp.concatenate([piece, jnp.zeros((112, 128), F32), piece], 0).T)
    return rows


def assemble(wide, state, edge, beside, cells_x):
    for dx, dy, message in [(0, 0, edge)] + beside:
        turned = turned_edges(message)
        if dx == 0:
            columns = [(HALO + x, x, x) for x in range(cells_x)]
        elif dx < 0:
            columns = [(i, cells_x - HALO + i, i) for i in range(HALO)]
        else:
            columns = [(HALO + cells_x + i, i, HALO + i) for i in range(HALO)]
        for f in range(5):
            for plane, x, slot in columns:
                height = 8 if dy == 0 else HALO
                at = (f * (cells_x if dx == 0 else 2 * HALO) + slot) * height
                if dx != 0 and dy != 0:
                    if slot in (0, 5):
                        continue
                    height = (0, 1, 2, 2, 1)[slot]
                    at = f * 6 + (0, 0, 1, 3, 5)[slot]
                low, high = {0: (0, 8), 1: (8, 8 + height), -1: (16 - height, 16)}[dy]
                if dx == 0 and dy == 0:
                    wide[f, plane, 0:8, 0:128] = state[f, x]
                else:
                    wide[f, plane, low:high, 0:128] = message[at : at + height]
                group = f * cells_x + x
                block = turned[group // 16][(group % 16) * 8 : (group % 16) * 8 + 8]
                first = 8 - height if dy < 0 else 0
                wide[f, plane, low:high, 128:256] = block[first : first + height]


def derive_planes(wide, derived, first, last):
    def derive(i, _):
        rho, mx, my, mz, energy = [wide[f, i] for f in range(5)]
        inverse = 1.0 / rho
        u, v, w = mx * inverse, my * inverse, mz * inverse
        p = (HEAT_RATIO - 1.0) * (energy - 0.5 * (mx * u + my * v + mz * w))
        derived[0, i] = u
        derived[1, i] = v
        derived[2, i] = w
        derived[3, i] = p
        derived[4, i] = jnp.sqrt(HEAT_RATIO * jnp.abs(p) * inverse)
        return 0

    lax.fori_loop(first, last, derive, 0)


def derive_speeds(wide, derived, first, last):
    def derive(i, _):
        inverse = 1.0 / wide[0, i]
        for k in range(3):
            derived[k, i] = wide[1 + k, i] * inverse
        return 0

    lax.fori_loop(first, last, derive, 0)


def flow_rate_section(wide, derived, start, offset, mix, write, inner=False):
    depth = wide.shape[1]
    near, lanes = slice(0, 8), slice(0, 128)
    every = (slice(None), slice(None))
    windows = [(near, lanes), (slice(None), lanes), (near, slice(None))] if inner else [every] * 3
    kept = windows[0]

    def flux(fields, other, along):
        speed, p = other[along], other[3]
        out = [fields[1 + along]]
        for k in range(3):
            value = fields[1 + k] * speed
            out.append(value + p if k == along else value)
        out.append((fields[4] + p) * speed)
        return out, jnp.abs(speed) + other[4]

    def face(left, right):
        (fields_l, flux_l, speed_l), (fields_r, flux_r, speed_r) = left, right
        speed = jnp.maximum(speed_l, speed_r)
        viscous = speed + 2.0 * VISCOSITY
        return [
            (flux_l[f] + flux_r[f])
            - (viscous if 1 <= f <= 3 else speed) * (fields_r[f] - fields_l[f])
            for f in range(5)
        ]

    def plane(i, along):
        rows, columns = windows[along]
        fields = [wide[f, i, rows, columns] for f in range(5)]
        other = [derived[f, i, rows, columns] for f in range(5)]
        return (fields,) + flux(fields, other, along)

    def section(i, before):
        here = plane(i, 0)
        ahead = face(here, plane(i + 1, 0))
        total = [ahead[f] - before[f] for f in range(5)]
        for along, axis, size in ((1, 0, 16), (2, 1, 256)):
            here = plane(i, along)
            moved = (
                [pltpu.roll(a, size - 1, axis) for a in here[0]],
                [pltpu.roll(a, size - 1, axis) for a in here[1]],
                pltpu.roll(here[2], size - 1, axis),
            )
            faces = face(here, moved)
            for f in range(5):
                change = faces[f] - pltpu.roll(faces[f], 1, axis)
                total[f] = total[f] + (change[0:8, 0:128] if inner else change)
        for f in range(5):
            value = wide[f, i, kept[0], kept[1]] - (0.5 * TIME_STEP) * total[f]
            if mix[0] != 0.0:
                value = mix[0] * start[f, i + offset, kept[0], kept[1]] + mix[1] * value
            write(i - 1, f, value)
        return tuple(ahead)

    lax.fori_loop(1, depth - 1, section, tuple(face(plane(0, 0), plane(1, 0))))


def lamb(derived, first, cells_x, lamb_rows):
    def one(x, _):
        i = first + x
        slopes = []
        slopes.append([derived[c, i + 1, 0:8, 0:128] - derived[c, i - 1, 0:8, 0:128] for c in range(3)])
        columns = [derived[c, i, :, 0:128] for c in range(3)]
        slopes.append([(pltpu.roll(a, 15, 0) - pltpu.roll(a, 1, 0))[0:8] for a in columns])
        rows = [derived[c, i, 0:8, :] for c in range(3)]
        slopes.append([(pltpu.roll(a, 255, 1) - pltpu.roll(a, 1, 1))[:, 0:128] for a in rows])
        vel = [derived[c, i, 0:8, 0:128] for c in range(3)]
        curl = [
            0.5 * (slopes[1][2] - slopes[2][1]),
            0.5 * (slopes[2][0] - slopes[0][2]),
            0.5 * (slopes[0][1] - slopes[1][0]),
        ]
        at = pl.multiple_of(x * 8, 8)
        lamb_rows[0, pl.ds(at, 8), :] = curl[1] * vel[2] - curl[2] * vel[1]
        lamb_rows[1, pl.ds(at, 8), :] = curl[2] * vel[0] - curl[0] * vel[2]
        lamb_rows[2, pl.ds(at, 8), :] = curl[0] * vel[1] - curl[1] * vel[0]
        return 0

    lax.fori_loop(0, cells_x, one, 0)


def project(lamb_rows, pair, spread, send):
    peers = send.shape[0]
    for c in range(3):
        sent = dot_three(dot_three(pair[...], lamb_rows[c]), spread[...])
        for peer in range(peers):
            send[peer, c] = sent[:, peer * 128 : peer * 128 + 128]


def flow_sources_body(places, *refs):
    state, edge = refs[0:2]
    messages = refs[2 : 2 + len(places)]
    pair, spread, _ = refs[2 + len(places) : 5 + len(places)]
    wide, send, derived, lamb_rows = refs[5 + len(places) : 9 + len(places)]
    spare = refs[9 + len(places) :]
    cells_x = state.shape[1]
    odd = is_odd("fy")
    beside, k = [], 0
    while k < len(places):
        if places[k][0][1] == 0:
            beside.extend((dx, 0, messages[k]) for dx, _ in places[k])
            k += 1
            continue
        above, below = spare[:2]
        spare = spare[2:]
        above[...], below[...] = paired(odd, messages[k][...], messages[k + 1][...])
        beside.extend((dx, 1, above) for dx, _ in places[k])
        beside.extend((dx, -1, below) for dx, _ in places[k])
        k += 2
    assemble(wide, state, edge, beside, cells_x)
    derive_speeds(wide, derived, HALO - 1, HALO + cells_x + 1)
    lamb(derived, HALO, cells_x, lamb_rows)
    project(lamb_rows, pair, spread, send)


def flow_first_body(wide, pair, spread, out, send, derived, lamb_rows):
    def write(i, f, value):
        out[f, i] = value

    planes = wide.shape[1]
    cells_x = planes - 2 * HALO
    derive_planes(wide, derived, 0, planes)
    flow_rate_section(wide, derived, wide, 0, MIXES[0], write)
    derive_speeds(out, derived, HALO - 2, HALO + cells_x)
    lamb(derived, HALO - 1, cells_x, lamb_rows)
    project(lamb_rows, pair, spread, send)


def flow_last_body(wide, start, pair, spread, out, send, derived, lamb_rows, second):
    def write_second(i, f, value):
        second[f, i] = value

    def write(i, f, value):
        out[f, i] = value

    planes = wide.shape[1]
    cells_x = out.shape[1]
    derive_planes(wide, derived, 0, planes)
    flow_rate_section(wide, derived, start, 1, MIXES[1], write_second)
    derive_planes(second, derived, 0, planes - 2)
    lamb(derived, 1, cells_x, lamb_rows)
    project(lamb_rows, pair, spread, send)
    flow_rate_section(second, derived, start, 2, MIXES[2], write, inner=True)


def faces_out(state, rear, front):
    lane = lax.broadcasted_iota(jnp.int32, (32, 128), 1) // 16
    for c in range(4):
        front[c * 8 : c * 8 + 8] = state[c, 56:64]
        rear[c * 8 : c * 8 + 8] = state[c, 0:8]
        front[32 + c * 8 : 40 + c * 8] = state[c, pl.ds(7, 8, stride=8), :]
        rear[32 + c * 8 : 40 + c * 8] = state[c, pl.ds(0, 8, stride=8), :]
    rows = state[...].reshape(256, 128)
    last = jnp.zeros((32, 128), F32)
    first = jnp.zeros((32, 128), F32)
    for j in range(8):
        piece = rows[j * 32 : j * 32 + 32]
        last = jnp.where(lane == j, pltpu.roll(piece, (j * 16 + 16) % 128, 1), last)
        first = jnp.where(lane == j, pltpu.roll(piece, j * 16, 1) if j else piece, first)
    front[64:96] = last
    rear[64:96] = first


def faces_sent(odd, state, message_a, message_b):
    faces_out(state, message_b, message_a)
    message_a[...], message_b[...] = paired(odd, message_a[...], message_b[...])


def lift(total, before, after, sides, factor):
    def place(face, rows, target):
        value = factor * dot_exact_right(rows, sides[face])
        for c in range(4):
            total[c, target, :] += value[c * 8 : c * 8 + 8]

    place(0, before[0:32], pl.ds(0, 8))
    place(1, after[0:32], pl.ds(56, 8))
    place(2, before[32:64], pl.ds(0, 8, stride=8))
    place(3, after[32:64], pl.ds(7, 8, stride=8))


def rate_local(state, deriv_rows, deriv_lanes, speed, sides):
    fields = [state[c] for c in range(4)]
    by_rows = dot_three(deriv_rows[...], jnp.concatenate(fields[0:3], 1))
    by_lanes = dot_three(jnp.concatenate([fields[0], fields[3]], 0), deriv_lanes[...])
    divergence = by_rows[0:64, 128:256] + by_rows[64:128, 256:384] + by_lanes[64:128]
    rates = [
        -(speed[...] * speed[...]) * divergence,
        -by_rows[0:64, 0:128],
        -by_rows[64:128, 0:128],
        -by_lanes[0:64],
    ]
    row = lax.broadcasted_iota(jnp.int32, (64, 128), 0)
    lane = lax.broadcasted_iota(jnp.int32, (64, 128), 1)
    count = jnp.zeros((64, 128), F32)
    for value in (row // 8, row % 8, lane // 16):
        count = count + jnp.where((value == 0) | (value == 7), PENALTY, 0.0)
    side = PENALTY * dot_exact_right(state[...].reshape(256, 128), sides[4])
    return [rates[c] - count * fields[c] + side[c * 64 : c * 64 + 64] for c in range(4)]


def acoustic_local_body(mix, state, start, deriv_rows, deriv_lanes, speed, sides, out, front, rear):
    rates = rate_local(state, deriv_rows, deriv_lanes, speed, sides)
    for c in range(4):
        value = state[c] + TIME_STEP * rates[c]
        if mix[0] != 0.0:
            value = mix[0] * start[c] + mix[1] * value
        out[c] = value
    faces_out(state, rear, front)
    lift(out, front, rear, sides, TIME_STEP * mix[1] * PENALTY)


def order_table(count, turned):
    row = lax.broadcasted_iota(jnp.int32, (4 * count, 4 * count), 0)
    column = lax.broadcasted_iota(jnp.int32, (4 * count, 4 * count), 1)
    if turned:
        row, column = column, row
    return (column == (row % count) * 4 + row // count).astype(F32)


def acoustic_start_body(given, _, state, message_a, message_b, turned):
    count = given.shape[0]
    rows = jnp.concatenate([given[e] for e in range(count)], 0)
    rows = dot_full(order_table(count, False), rows)
    rows = jnp.concatenate([rows, jnp.zeros((128 - 4 * count, rows.shape[1]), F32)], 0)
    turned[...] = rows.T
    lane = lax.broadcasted_iota(jnp.int32, (64, 128), 1) // count
    fields = [jnp.zeros((64, 128), F32)] * 4
    for z in range(8):
        piece = turned[pl.ds(z, 64, stride=8), :]
        for c in range(4):
            move = (z - c) * count % 128
            fields[c] = jnp.where(lane == z, pltpu.roll(piece, move, 1) if move else piece, fields[c])
    for c in range(4):
        state[c] = fields[c]
    faces_sent(is_odd("fz"), state, message_a, message_b)


def natural_order(state, out, turned):
    count = out.shape[0]
    lane = lax.broadcasted_iota(jnp.int32, (64, 128), 1) // count
    for z in range(8):
        value = jnp.zeros((64, 128), F32)
        for c in range(4):
            move = (c - z) * count % 128
            value = jnp.where(lane == c, pltpu.roll(state[c], move, 1) if move else state[c], value)
        turned[pl.ds(z, 64, stride=8), :] = value
    rows = dot_full(order_table(count, True), turned[...].T[0 : 4 * count])
    for e in range(count):
        out[e] = rows[4 * e : 4 * e + 4]


def remote_part(out, before, after, sides_far, factor):
    lift(out, before, after, sides_far, factor)
    lane = lax.broadcasted_iota(jnp.int32, (32, 128), 1) // 16
    last, first = before[64:96], after[64:96]
    pieces = []
    for j in range(8):
        left = pltpu.roll(last, 128 - j * 16, 1) if j else last
        right = pltpu.roll(first, (144 - j * 16) % 128, 1) if j != 1 else first
        pieces.append(jnp.where(lane == 0, left, jnp.where(lane == 1, right, 0.0)))
    value = factor * dot_exact_right(jnp.concatenate(pieces, 0), sides_far[4])
    for c in range(4):
        out[c] += value[c * 64 : c * 64 + 64]


def acoustic_far_body(mix, last, partial, got_a, got_b, sides_far, received, *refs):
    if last:
        given_out, before, after, source, sem, out, turned = refs
    else:
        out, message_a, message_b, before, after, source, sem = refs
    copy = pltpu.make_async_copy(received, source, sem)
    copy.start()
    odd = is_odd("fz")
    after[...], before[...] = paired(odd, got_a[...], got_b[...])
    out[...] = partial[...]
    remote_part(out, before, after, sides_far, TIME_STEP * mix[1] * PENALTY)
    copy.wait()
    for c in range(3):
        out[1 + c] += (TIME_STEP * mix[1]) * source[0, c]
    if last:
        natural_order(out, given_out, turned)
    else:
        faces_sent(odd, out, message_a, message_b)


def kron_part(matrix, shape, rows_by, columns_by):
    row = lax.broadcasted_iota(jnp.int32, (shape[0], 8), 0)
    level = lax.broadcasted_iota(jnp.int32, (shape[0], 8), 1)
    left = (row // rows_by % 8 == level).astype(F32)
    level = lax.broadcasted_iota(jnp.int32, (8, shape[1]), 0)
    column = lax.broadcasted_iota(jnp.int32, (8, shape[1]), 1)
    right = (column // columns_by % 8 == level).astype(F32)
    return dot_full(dot_full(left, matrix), right)


def tables_body(
    packed,
    near,
    far,
    deriv_rows,
    deriv_lanes,
    pair,
    spread,
    speed,
):
    size = near.shape[1]
    count = size // 8
    blocks = spread.shape[0] // 8

    def place_of(shape):
        return (lax.broadcasted_iota(jnp.int32, shape, 0), lax.broadcasted_iota(jnp.int32, shape, 1))

    row, column = place_of((count, size))
    repeat = (column % count == row).astype(F32)
    speed[...] = dot_full(packed[24:25, 0:count], repeat)
    wanted = dot_full(packed[16:24, 0:count], repeat).astype(jnp.int32)
    row, column = place_of((size, size))
    level, element = row // count, row % count
    level_out = column // count
    for facet in range(4):
        shift = -count if facet % 2 == 0 else count
        choice = jnp.broadcast_to(wanted[facet : facet + 1], (size, size))
        near[facet] = jnp.where((level == level_out) & (element == choice), 1.0, 0.0).astype(BF16)
        far[facet] = jnp.where((level == level_out) & (element + shift == choice), 1.0, 0.0).astype(BF16)
    lower = jnp.broadcast_to(wanted[4:5], (size, size))
    upper = jnp.broadcast_to(wanted[5:6], (size, size))
    hit = (level == 7) & (level_out == 0) & (element == lower)
    hit = hit | ((level == 0) & (level_out == 7) & (element == upper))
    near[4] = jnp.where(hit, 1.0, 0.0).astype(BF16)
    hit = (level == 0) & (level_out == 0) & (element - count == lower)
    hit = hit | ((level == 1) & (level_out == 7) & (element + count == upper))
    far[4] = jnp.where(hit, 1.0, 0.0).astype(BF16)

    row, column = place_of((64, 64))
    slopes, modes = packed[0:8, 0:8], packed[8:16, 0:8]
    outer = kron_part(slopes, (64, 64), 8, 8)
    inner = kron_part(slopes, (64, 64), 1, 1)
    deriv_rows[0:64] = jnp.where(row % 8 == column % 8, outer, 0.0)
    deriv_rows[64:128] = jnp.where(row // 8 == column // 8, inner, 0.0)
    row, column = place_of((size, size))
    lanes = kron_part(slopes.T, (size, size), count, count)
    deriv_lanes[...] = jnp.where(row % count == column % count, lanes, 0.0)
    pair[...] = kron_part(modes, (64, 64), 8, 8) * kron_part(modes, (64, 64), 1, 1)

    row, column = place_of((blocks, blocks))

    def upright(values):
        values = jnp.sum(jnp.where(row == column, values, 0.0), 1, keepdims=True)
        return dot_full(repeat, jnp.broadcast_to(values, (blocks, size)))

    row_wide, column_wide = place_of((8 * blocks, blocks))
    repeat = (row_wide // 8 == column_wide).astype(F32)
    owner = upright(packed[25:26, 0:blocks])
    element = upright(packed[26:27, 0:blocks])
    _, column_wide = place_of((8 * blocks, size))
    values = kron_part(modes.T, (8 * blocks, size), 1, count)
    values = jnp.where(element == (column_wide % count).astype(F32), values, 0.0)
    for peer in range(spread.shape[1] // size):
        spread[:, peer * size : peer * size + size] = jnp.where(owner == float(peer), values, 0.0)


def shifted(sizes, shifts):
    pairs = []
    for index in np.ndindex(*sizes):
        source = [(i + s) % n for i, s, n in zip(index, shifts, sizes)]
        pairs.append((int(np.ravel_multi_index(source, sizes)), int(np.ravel_multi_index(index, sizes))))
    return pairs


def partners(sizes, axis, second, shift_x=0):
    pairs = []
    for index in np.ndindex(*sizes):
        source = list(index)
        step = 1 if (index[axis] % 2 == 0) != second else -1
        source[axis] = (index[axis] + step) % sizes[axis]
        if shift_x:
            source[0] = (index[0] + shift_x) % sizes[0]
        pairs.append((int(np.ravel_multi_index(source, sizes)), int(np.ravel_multi_index(index, sizes))))
    return pairs


def per_device(
    density,
    velocity,
    pressure,
    acoustic,
    sound_speed,
    derivative,
    mode_basis,
    neighbours,
    block_owner,
    block_element,
):
    size_x, size_y, size_z = lax.axis_size("fx"), lax.axis_size("fy"), lax.axis_size("fz")
    devices = size_x * size_y * size_z
    cells_x = density.shape[0]
    elements = acoustic.shape[0]
    device = lax.axis_index(("fx", "fy", "fz"))

    names = ("fx", "fy", "fz")

    rows = 5 * cells_x * 8
    tiles = -(-rows // 128)
    state, to_a, to_b = call(
        pack_start_body,
        [(5, cells_x, 8, 128), (tiles * 8, 128), (tiles * 8, 128)],
        density,
        velocity,
        pressure,
        fetch=True,
    )
    edge_a = lax.ppermute(to_a, "fz", partners((size_z,), 0, False))
    edge_b = lax.ppermute(to_b, "fz", partners((size_z,), 0, True))

    near_pairs = [(i ^ 1, i) for i in range(devices)]
    far_pairs = [pair for i in range(1, devices - 1, 2) for pair in ((i, i + 1), (i + 1, i))]

    def traces(to_a, to_b):
        far_got = lax.ppermute(to_b, names, far_pairs)
        return lax.ppermute(to_a, names, near_pairs), far_got

    size = 8 * elements
    held = (4, 64, size)
    faces = (96, size)
    sides = [pltpu.VMEM(faces, F32)] * 2
    far_scratch = sides + [pltpu.VMEM((1, 3, 64, size), F32), pltpu.SemaphoreType.DMA]
    sound, to_a, to_b = call(
        acoustic_start_body,
        [held, faces, faces],
        acoustic,
        to_a,
        scratch=[pltpu.VMEM((512, 128), F32)],
        last=1,
    )
    got_a, got_b = traces(to_a, to_b)

    six = 2 * HALO
    edge_rows = tiles * 8
    shapes = [
        (edge_rows, 128),
        (5 * six * 8 + edge_rows, 128),
        (5 * cells_x * HALO + edge_rows, 128),
        (5 * cells_x * HALO + edge_rows, 128),
        (32 + edge_rows, 128),
        (32 + edge_rows, 128),
    ]
    edge, along_x, y_a, y_b, xy_a, xy_b = call(pack_next_body, shapes, state, edge_a, edge_b, got_a, last=1)
    flat = (size_x, size_y)
    steps = [[(1, 0), (-1, 0)]] if size_x == 2 else [[(1, 0)], [(-1, 0)]]
    places, messages = [], []
    for first, second, spots in [(y_a, y_b, [(0, 0)])] + [(xy_a, xy_b, spots) for spots in steps]:
        shift = spots[0][0]
        for kept, side in ((first, False), (second, True)):
            messages.append(lax.ppermute(kept, ("fx", "fy"), partners(flat, 1, side, shift)))
            places.append(tuple((dx, 1) for dx, _ in spots))
    for spots in steps:
        messages.append(lax.ppermute(along_x, ("fx", "fy"), shifted(flat, spots[0])))
        places.append(tuple(spots))

    local = (neighbours - device * elements).T.astype(F32)
    blocks = block_owner.size
    width = max(elements, blocks)
    packed = jnp.concatenate(
        [
            jnp.pad(derivative, ((0, 0), (0, width - 8))),
            jnp.pad(mode_basis, ((0, 0), (0, width - 8))),
            jnp.pad(local, ((0, 2), (0, width - elements))),
            jnp.pad(sound_speed.reshape(1, elements), ((0, 0), (0, width - elements))),
            jnp.pad(block_owner.reshape(1, blocks).astype(F32), ((0, 0), (0, width - blocks))),
            jnp.pad(block_element.reshape(1, blocks).astype(F32), ((0, 5), (0, width - blocks))),
        ],
        0,
    )
    table = jax.ShapeDtypeStruct((5, size, size), BF16)
    near, far, deriv_rows, deriv_lanes, pair, spread, speed = call(
        tables_body,
        [
            table,
            table,
            (128, 64),
            (size, size),
            (64, 64),
            (8 * blocks, size_y * size),
            (1, size),
        ],
        packed,
    )

    sent = (size_y, 3, 64, size)
    wide = cells_x + 2 * HALO
    rows_scratch = pltpu.VMEM((3, 64, 128), F32)

    def planes(count):
        return (5, count, 16, 256)

    def route(send):
        return lax.psum_scatter(send, "fy", scatter_dimension=0, tiled=True)

    spare = [pltpu.VMEM(shapes[2], F32)] * 2 + [pltpu.VMEM(shapes[4], F32)] * (2 * len(steps))
    start, send = call(
        functools.partial(flow_sources_body, tuple(places)),
        [planes(wide), sent],
        state,
        edge,
        *messages,
        pair,
        spread,
        got_b,
        scratch=[pltpu.VMEM((3, wide, 16, 256), F32), rows_scratch] + spare,
        last=1,
    )
    received = route(send)
    flow_one, send = call(
        flow_first_body,
        [planes(wide - 2), sent],
        start,
        pair,
        spread,
        scratch=[pltpu.VMEM(planes(wide), F32), rows_scratch],
    )
    received_next = route(send)
    def local_part(mix, now):
        return call(
            functools.partial(acoustic_local_body, mix),
            [held],
            now,
            sound,
            deriv_rows,
            deriv_lanes,
            speed,
            near,
            scratch=sides,
        )[0]

    partial = local_part(MIXES[0], sound)
    sound_one, to_a, to_b = call(
        functools.partial(acoustic_far_body, MIXES[0], False),
        [held, faces, faces],
        partial,
        got_a,
        got_b,
        far,
        received,
        scratch=far_scratch,
        last=1,
    )
    got_a, got_b = traces(to_a, to_b)
    received = received_next

    partial = local_part(MIXES[1], sound_one)
    flow_state, send = call(
        flow_last_body,
        [(5, cells_x, 8, 128), sent],
        flow_one,
        start,
        pair,
        spread,
        scratch=[pltpu.VMEM(planes(wide - 2), F32), rows_scratch, pltpu.VMEM(planes(wide - 4), F32)],
    )
    sound_two, to_a, to_b = call(
        functools.partial(acoustic_far_body, MIXES[1], False),
        [held, faces, faces],
        partial,
        got_a,
        got_b,
        far,
        received,
        scratch=far_scratch,
        last=1,
    )
    got_a, got_b = traces(to_a, to_b)
    received = route(send)
    partial = local_part(MIXES[2], sound_two)
    sound_state = call(
        functools.partial(acoustic_far_body, MIXES[2], True),
        [(elements, 4, 512)],
        partial,
        got_a,
        got_b,
        far,
        received,
        scratch=far_scratch + [pltpu.VMEM(held, F32), pltpu.VMEM((512, 128), F32)],
        last=1,
    )[0]
    return (flow_state, sound_state)


def solution(mesh):
    placed = (
        P("fx", "fy", "fz"),
        P(None, "fx", "fy", "fz"),
        P("fx", "fy", "fz"),
        P(("fx", "fy", "fz"), None, None),
        P(("fx", "fy", "fz")),
        P(),
        P(),
        P(("fx", "fy", "fz"), None),
        P("fx", "fy", "fz", None, None),
        P("fx", "fy", "fz", None),
    )
    return jax.shard_map(
        per_device,
        mesh=mesh,
        in_specs=placed,
        out_specs=(P(None, "fx", "fy", "fz"), P(("fx", "fy", "fz"), None, None)),
        check_vma=False,
    )
```

```python
import functools

import jax
import jax.numpy as jnp
import numpy as np
from jax import lax
from jax.experimental import pallas as pl
from jax.experimental.pallas import tpu as pltpu
from jax.sharding import PartitionSpec as P

HEAT_RATIO = 1.4
TIME_STEP = 0.1
VISCOSITY = 0.05
PENALTY = 0.5
HALO = 3
F32 = jnp.float32
BF16 = jnp.bfloat16
PARAMS = pltpu.CompilerParams(vmem_limit_bytes=24 * 1024 * 1024)
MIXES = ((0.0, 1.0), (0.75, 0.25), (1.0 / 3.0, 2.0 / 3.0))


def parts(values):
    high = values.astype(BF16)
    return high, (values - high.astype(F32)).astype(BF16)


def dot(left, right):
    return lax.dot_general(left, right, (((1,), (0,)), ((), ())), preferred_element_type=F32)


def dot_three(left, right):
    left_high, left_low = parts(left)
    right_high, right_low = parts(right)
    return dot(left_high, right_high) + dot(left_high, right_low) + dot(left_low, right_high)


def dot_full(left, right, dims=((1,), (0,))):
    return lax.dot_general(
        left, right, (dims, ((), ())), precision=lax.Precision.HIGHEST, preferred_element_type=F32
    )


def dot_exact_right(left, right):
    left_high, left_low = parts(left)
    return dot(left_high, right) + dot(left_low, right)


def call(body, outs, *operands, scratch=(), fetch=False, last=0):
    whole = pl.BlockSpec(memory_space=pltpu.VMEM)
    outs = [out if isinstance(out, jax.ShapeDtypeStruct) else jax.ShapeDtypeStruct(out, F32) for out in outs]
    scratch = list(scratch)
    anywhere = pl.BlockSpec(memory_space=pltpu.HBM)
    specs = [anywhere if fetch else whole] * (len(operands) - last) + [anywhere] * last
    kernel = body
    if fetch:
        count = len(operands)
        total = count + len(outs)

        def kernel(*refs):
            held, sems = refs[total : total + count], refs[total + count]
            copies = [
                pltpu.make_async_copy(refs[i], held[i], sems.at[i]) for i in range(count)
            ]
            for copy in copies:
                copy.start()
            for copy in copies:
                copy.wait()
            body(*held, *refs[count:total], *refs[total + count + 1 :])

        scratch = [pltpu.VMEM(o.shape, o.dtype) for o in operands] + [pltpu.SemaphoreType.DMA((count,))] + scratch
    return pl.pallas_call(
        kernel,
        out_shape=outs,
        in_specs=specs,
        out_specs=[whole] * len(outs),
        scratch_shapes=scratch,
        compiler_params=PARAMS,
    )(*operands)


def capacity_of(peers, blocks):
    return max(2, 2 * blocks // peers)


def fold_of(peers, blocks):
    return 128 // (8 * capacity_of(peers, blocks))


def is_odd(axis):
    return lax.axis_index(axis) % 2 == 1


def paired(odd, to_next, to_last):
    return jnp.where(odd, to_last, to_next), jnp.where(odd, to_next, to_last)


def pack_start_body(state, message_a, message_b):
    odd = is_odd("fz")
    rows = state[...].reshape(-1, 128)
    count = rows.shape[0]
    for tile in range(message_a.shape[0] // 8):
        piece = rows[tile * 128 : min(count, tile * 128 + 128)]
        if piece.shape[0] < 128:
            piece = jnp.concatenate([piece, jnp.zeros((128 - piece.shape[0], 128), F32)], 0)
        turned = piece.T
        first, second = paired(odd, turned[120:128], turned[0:8])
        message_a[tile * 8 : tile * 8 + 8] = first
        message_b[tile * 8 : tile * 8 + 8] = second


def pack_next_body(state, got_a, got_b, _, edge, along_x, y_a, y_b, xy_a, xy_b):
    cells_x = state.shape[1]
    odd_z, odd = is_odd("fz"), is_odd("fy")
    row = lax.broadcasted_iota(jnp.int32, edge.shape, 0) % 8
    above, below = paired(odd_z, got_a[...], got_b[...])
    both = jnp.where(row < 4, above, below)
    edge[...] = both
    planes = [cells_x - HALO + i for i in range(HALO)] + list(range(HALO))
    for f in range(5):
        for s, x in enumerate(planes):
            at = (f * len(planes) + s) * 8
            along_x[at : at + 8] = state[f, x]
        for x in range(cells_x):
            at = (f * cells_x + x) * HALO
            first, second = paired(odd, state[f, x, 8 - HALO : 8], state[f, x, 0:HALO])
            y_a[at : at + HALO] = first
            y_b[at : at + HALO] = second
        at = f * 6
        for slot, height in ((1, 1), (2, 2), (3, 2), (4, 1)):
            x = planes[slot]
            first, second = paired(odd, state[f, x, 8 - height : 8], state[f, x, 0:height])
            xy_a[at : at + height] = first
            xy_b[at : at + height] = second
            at += height
    for message in (along_x, y_a, y_b, xy_a, xy_b):
        size = message.shape[0]
        message[size - edge.shape[0] : size] = both


def turned_edges(message):
    size = message.shape[0]
    rows = []
    for tile in range(3):
        piece = message[size - 24 + tile * 8 : size - 16 + tile * 8]
        rows.append(jnp.concatenate([piece, jnp.zeros((112, 128), F32), piece], 0).T)
    return rows


def assemble(wide, state, edge, beside, cells_x):
    for dx, dy, message in [(0, 0, edge)] + beside:
        turned = turned_edges(message)
        if dx == 0:
            columns = [(HALO + x, x, x) for x in range(cells_x)]
        elif dx < 0:
            columns = [(i, cells_x - HALO + i, i) for i in range(HALO)]
        else:
            columns = [(HALO + cells_x + i, i, HALO + i) for i in range(HALO)]
        for f in range(5):
            for plane, x, slot in columns:
                height = 8 if dy == 0 else HALO
                at = (f * (cells_x if dx == 0 else 2 * HALO) + slot) * height
                if dx != 0 and dy != 0:
                    if slot in (0, 5):
                        continue
                    height = (0, 1, 2, 2, 1)[slot]
                    at = f * 6 + (0, 0, 1, 3, 5)[slot]
                low, high = {0: (0, 8), 1: (8, 8 + height), -1: (16 - height, 16)}[dy]
                if dx == 0 and dy == 0:
                    wide[f, plane, 0:8, 0:128] = state[f, x]
                else:
                    wide[f, plane, low:high, 0:128] = message[at : at + height]
                group = f * cells_x + x
                block = turned[group // 16][(group % 16) * 8 : (group % 16) * 8 + 8]
                first = 8 - height if dy < 0 else 0
                wide[f, plane, low:high, 128:256] = block[first : first + height]


def derive_planes(wide, derived, first, last):
    def derive(i, _):
        rho, mx, my, mz, energy = [wide[f, i] for f in range(5)]
        inverse = 1.0 / rho
        u, v, w = mx * inverse, my * inverse, mz * inverse
        p = (HEAT_RATIO - 1.0) * (energy - 0.5 * (mx * u + my * v + mz * w))
        derived[0, i] = u
        derived[1, i] = v
        derived[2, i] = w
        derived[3, i] = p
        derived[4, i] = jnp.sqrt(HEAT_RATIO * jnp.abs(p) * inverse)
        return 0

    lax.fori_loop(first, last, derive, 0)


def derive_speeds(wide, derived, first, last):
    def derive(i, _):
        inverse = 1.0 / wide[0, i]
        for k in range(3):
            derived[k, i] = wide[1 + k, i] * inverse
        return 0

    lax.fori_loop(first, last, derive, 0)


def flow_rate_section(wide, derived, start, offset, mix, write, inner=False):
    depth = wide.shape[1]
    near, lanes = slice(0, 8), slice(0, 128)
    every = (slice(None), slice(None))
    windows = [(near, lanes), (slice(None), lanes), (near, slice(None))] if inner else [every] * 3
    kept = windows[0]

    def flux(fields, other, along):
        speed, p = other[along], other[3]
        out = [fields[1 + along]]
        for k in range(3):
            value = fields[1 + k] * speed
            out.append(value + p if k == along else value)
        out.append((fields[4] + p) * speed)
        return out, jnp.abs(speed) + other[4]

    def face(left, right):
        (fields_l, flux_l, speed_l), (fields_r, flux_r, speed_r) = left, right
        speed = jnp.maximum(speed_l, speed_r)
        viscous = speed + 2.0 * VISCOSITY
        return [
            (flux_l[f] + flux_r[f])
            - (viscous if 1 <= f <= 3 else speed) * (fields_r[f] - fields_l[f])
            for f in range(5)
        ]

    def plane(i, along):
        rows, columns = windows[along]
        fields = [wide[f, i, rows, columns] for f in range(5)]
        other = [derived[f, i, rows, columns] for f in range(5)]
        return (fields,) + flux(fields, other, along)

    def section(i, before):
        here = plane(i, 0)
        ahead = face(here, plane(i + 1, 0))
        total = [ahead[f] - before[f] for f in range(5)]
        for along, axis, size in ((1, 0, 16), (2, 1, 256)):
            here = plane(i, along)
            moved = (
                [pltpu.roll(a, size - 1, axis) for a in here[0]],
                [pltpu.roll(a, size - 1, axis) for a in here[1]],
                pltpu.roll(here[2], size - 1, axis),
            )
            faces = face(here, moved)
            for f in range(5):
                change = faces[f] - pltpu.roll(faces[f], 1, axis)
                total[f] = total[f] + (change[0:8, 0:128] if inner else change)
        for f in range(5):
            value = wide[f, i, kept[0], kept[1]] - (0.5 * TIME_STEP) * total[f]
            if mix[0] != 0.0:
                value = mix[0] * start[f, i + offset, kept[0], kept[1]] + mix[1] * value
            write(i - 1, f, value)
        return tuple(ahead)

    lax.fori_loop(1, depth - 1, section, tuple(face(plane(0, 0), plane(1, 0))))


def lamb(derived, first, cells_x, lamb_rows):
    def one(x, _):
        i = first + x
        slopes = []
        slopes.append([derived[c, i + 1, 0:8, 0:128] - derived[c, i - 1, 0:8, 0:128] for c in range(3)])
        columns = [derived[c, i, :, 0:128] for c in range(3)]
        slopes.append([(pltpu.roll(a, 15, 0) - pltpu.roll(a, 1, 0))[0:8] for a in columns])
        rows = [derived[c, i, 0:8, :] for c in range(3)]
        slopes.append([(pltpu.roll(a, 255, 1) - pltpu.roll(a, 1, 1))[:, 0:128] for a in rows])
        vel = [derived[c, i, 0:8, 0:128] for c in range(3)]
        curl = [
            0.5 * (slopes[1][2] - slopes[2][1]),
            0.5 * (slopes[2][0] - slopes[0][2]),
            0.5 * (slopes[0][1] - slopes[1][0]),
        ]
        at = pl.multiple_of(x * 8, 8)
        lamb_rows[0, pl.ds(at, 8), :] = curl[1] * vel[2] - curl[2] * vel[1]
        lamb_rows[1, pl.ds(at, 8), :] = curl[2] * vel[0] - curl[0] * vel[2]
        lamb_rows[2, pl.ds(at, 8), :] = curl[0] * vel[1] - curl[1] * vel[0]
        return 0

    lax.fori_loop(0, cells_x, one, 0)


def project(lamb_rows, pair, spread, send, base):
    peers = send.shape[0]
    fold = fold_of(peers, spread.shape[0] // 8)
    height = 64 // fold
    group = lax.broadcasted_iota(jnp.int32, (height, 128), 1) // (128 // fold)
    for c in range(3):
        sent = dot_three(dot_three(pair[...], lamb_rows[c]), spread[...])
        for peer in range(peers):
            mine = sent[:, peer * 128 : peer * 128 + 128]
            folded = mine[0:height]
            for g in range(1, fold):
                folded = jnp.where(group == g, mine[g * height : g * height + height], folded)
            send[peer, base + c * height : base + c * height + height] = folded


def flow_sources_body(places, *refs):
    state, edge = refs[0:2]
    messages = refs[2 : 2 + len(places)]
    pair, spread, labels, _ = refs[2 + len(places) : 6 + len(places)]
    wide, send, derived, lamb_rows = refs[6 + len(places) : 10 + len(places)]
    spare = refs[10 + len(places) :]
    cells_x = state.shape[1]
    odd = is_odd("fy")
    beside, k = [], 0
    while k < len(places):
        if places[k][0][1] == 0:
            beside.extend((dx, 0, messages[k]) for dx, _ in places[k])
            k += 1
            continue
        above, below = spare[:2]
        spare = spare[2:]
        above[...], below[...] = paired(odd, messages[k][...], messages[k + 1][...])
        beside.extend((dx, 1, above) for dx, _ in places[k])
        beside.extend((dx, -1, below) for dx, _ in places[k])
        k += 2
    assemble(wide, state, edge, beside, cells_x)
    derive_speeds(wide, derived, HALO - 1, HALO + cells_x + 1)
    lamb(derived, HALO, cells_x, lamb_rows)
    project(lamb_rows, pair, spread, send, 0)
    send[:, send.shape[1] - 8 :] = labels[...]


def flow_stages_body(wide, pair, spread, labels, out, send, derived, lamb_rows, first, second):
    def writer(target):
        def write(i, f, value):
            target[f, i] = value

        return write

    planes = wide.shape[1]
    cells_x = out.shape[1]
    size = (send.shape[1] - 8) // 2
    derive_planes(wide, derived, 0, planes)
    flow_rate_section(wide, derived, wide, 0, MIXES[0], writer(first))
    derive_planes(first, derived, 0, planes - 2)
    lamb(derived, 2, cells_x, lamb_rows)
    project(lamb_rows, pair, spread, send, 0)
    flow_rate_section(first, derived, wide, 1, MIXES[1], writer(second))
    derive_planes(second, derived, 0, planes - 4)
    lamb(derived, 1, cells_x, lamb_rows)
    project(lamb_rows, pair, spread, send, size)
    send[:, 2 * size :] = labels[...]
    flow_rate_section(second, derived, wide, 2, MIXES[2], writer(out), inner=True)


def faces_out(state, rear, front):
    lane = lax.broadcasted_iota(jnp.int32, (32, 128), 1) // 16
    for c in range(4):
        front[c * 8 : c * 8 + 8] = state[c, 56:64]
        rear[c * 8 : c * 8 + 8] = state[c, 0:8]
        front[32 + c * 8 : 40 + c * 8] = state[c, pl.ds(7, 8, stride=8), :]
        rear[32 + c * 8 : 40 + c * 8] = state[c, pl.ds(0, 8, stride=8), :]
    rows = state[...].reshape(256, 128)
    last = jnp.zeros((32, 128), F32)
    first = jnp.zeros((32, 128), F32)
    for j in range(8):
        piece = rows[j * 32 : j * 32 + 32]
        last = jnp.where(lane == j, pltpu.roll(piece, (j * 16 + 16) % 128, 1), last)
        first = jnp.where(lane == j, pltpu.roll(piece, j * 16, 1) if j else piece, first)
    front[64:96] = last
    rear[64:96] = first


def faces_sent(odd, state, message_a, message_b):
    faces_out(state, message_b, message_a)
    message_a[...], message_b[...] = paired(odd, message_a[...], message_b[...])


def lift(total, before, after, sides, factor):
    def place(face, rows, target):
        value = factor * dot_exact_right(rows, sides[face])
        for c in range(4):
            total[c, target, :] += value[c * 8 : c * 8 + 8]

    place(0, before[0:32], pl.ds(0, 8))
    place(1, after[0:32], pl.ds(56, 8))
    place(2, before[32:64], pl.ds(0, 8, stride=8))
    place(3, after[32:64], pl.ds(7, 8, stride=8))


def rate_local(state, deriv_rows, deriv_lanes, speed, sides):
    fields = [state[c] for c in range(4)]
    by_rows = dot_three(deriv_rows[...], jnp.concatenate(fields[0:3], 1))
    by_lanes = dot_three(jnp.concatenate([fields[0], fields[3]], 0), deriv_lanes[...])
    divergence = by_rows[0:64, 128:256] + by_rows[64:128, 256:384] + by_lanes[64:128]
    rates = [
        -(speed[...] * speed[...]) * divergence,
        -by_rows[0:64, 0:128],
        -by_rows[64:128, 0:128],
        -by_lanes[0:64],
    ]
    row = lax.broadcasted_iota(jnp.int32, (64, 128), 0)
    lane = lax.broadcasted_iota(jnp.int32, (64, 128), 1)
    count = jnp.zeros((64, 128), F32)
    for value in (row // 8, row % 8, lane // 16):
        count = count + jnp.where((value == 0) | (value == 7), PENALTY, 0.0)
    side = PENALTY * dot_exact_right(state[...].reshape(256, 128), sides[4])
    return [rates[c] - count * fields[c] + side[c * 64 : c * 64 + 64] for c in range(4)]


def acoustic_local_body(mix, state, start, deriv_rows, deriv_lanes, speed, sides, out, front, rear):
    rates = rate_local(state, deriv_rows, deriv_lanes, speed, sides)
    for c in range(4):
        value = state[c] + TIME_STEP * rates[c]
        if mix[0] != 0.0:
            value = mix[0] * start[c] + mix[1] * value
        out[c] = value
    faces_out(state, rear, front)
    lift(out, front, rear, sides, TIME_STEP * mix[1] * PENALTY)


def order_table(count, turned):
    row = lax.broadcasted_iota(jnp.int32, (4 * count, 4 * count), 0)
    column = lax.broadcasted_iota(jnp.int32, (4 * count, 4 * count), 1)
    if turned:
        row, column = column, row
    return (column == (row % count) * 4 + row // count).astype(F32)


def acoustic_start_body(given, _, state, message_a, message_b, turned):
    count = given.shape[0]
    rows = jnp.concatenate([given[e] for e in range(count)], 0)
    rows = dot_full(order_table(count, False), rows)
    rows = jnp.concatenate([rows, jnp.zeros((128 - 4 * count, rows.shape[1]), F32)], 0)
    turned[...] = rows.T
    lane = lax.broadcasted_iota(jnp.int32, (64, 128), 1) // count
    fields = [jnp.zeros((64, 128), F32)] * 4
    for z in range(8):
        piece = turned[pl.ds(z, 64, stride=8), :]
        for c in range(4):
            move = (z - c) * count % 128
            fields[c] = jnp.where(lane == z, pltpu.roll(piece, move, 1) if move else piece, fields[c])
    for c in range(4):
        state[c] = fields[c]
    faces_sent(is_odd("fz"), state, message_a, message_b)


def natural_order(state, out, turned):
    count = out.shape[0]
    lane = lax.broadcasted_iota(jnp.int32, (64, 128), 1) // count
    for z in range(8):
        value = jnp.zeros((64, 128), F32)
        for c in range(4):
            move = (c - z) * count % 128
            value = jnp.where(lane == c, pltpu.roll(state[c], move, 1) if move else state[c], value)
        turned[pl.ds(z, 64, stride=8), :] = value
    rows = dot_full(order_table(count, True), turned[...].T[0 : 4 * count])
    for e in range(count):
        out[e] = rows[4 * e : 4 * e + 4]


def remote_part(out, before, after, sides_far, factor):
    lift(out, before, after, sides_far, factor)
    lane = lax.broadcasted_iota(jnp.int32, (32, 128), 1) // 16
    last, first = before[64:96], after[64:96]
    pieces = []
    for j in range(8):
        left = pltpu.roll(last, 128 - j * 16, 1) if j else last
        right = pltpu.roll(first, (144 - j * 16) % 128, 1) if j != 1 else first
        pieces.append(jnp.where(lane == 0, left, jnp.where(lane == 1, right, 0.0)))
    value = factor * dot_exact_right(jnp.concatenate(pieces, 0), sides_far[4])
    for c in range(4):
        out[c] += value[c * 64 : c * 64 + 64]


def acoustic_far_body(mix, kind, partial, got_a, got_b, sides_far, received, *refs):
    if kind == "last":
        given_out, before, after, out, turned = refs
    elif kind == "first":
        _, out, message_a, message_b, before, after, source = refs
        place_body(received, source)
        received = source
    else:
        out, message_a, message_b, before, after = refs
    odd = is_odd("fz")
    after[...], before[...] = paired(odd, got_a[...], got_b[...])
    out[0] = partial[0]
    for c in range(3):
        out[1 + c] = partial[1 + c] + (TIME_STEP * mix[1]) * received[c]
    remote_part(out, before, after, sides_far, TIME_STEP * mix[1] * PENALTY)
    if kind == "last":
        natural_order(out, given_out, turned)
    else:
        faces_sent(odd, out, message_a, message_b)


def place_body(received, *outs):
    peers, size = received.shape[0], received.shape[1]
    fold = 192 * len(outs) // (size - 8)
    height = 64 // fold
    target = lax.broadcasted_iota(jnp.int32, (128, 128), 0)
    lane = lax.broadcasted_iota(jnp.int32, (128, 128), 1)
    total = None
    for peer in range(peers):
        label = received[peer, size - 8 : size - 7, :]
        label = jnp.broadcast_to(label, (128, 128)).astype(jnp.int32)
        hit = (label == target % 16) & (lane % 8 == target // 16)
        chosen = [jnp.where(hit & (lane // (128 // fold) == g), 1.0, 0.0) for g in range(fold)]
        chosen = jnp.concatenate(chosen, 0).astype(BF16)
        high, low = parts(received[peer, 0 : size - 8])
        dims = (((1,), (1,)), ((), ()))
        value = lax.dot_general(high, chosen, dims, preferred_element_type=F32)
        value = value + lax.dot_general(low, chosen, dims, preferred_element_type=F32)
        total = value if total is None else total + value
    for k, out in enumerate(outs):
        for c in range(3):
            for g in range(fold):
                at = (k * 3 + c) * height
                out[c, g * height : g * height + height] = total[at : at + height, g * 128 : g * 128 + 128]


def kron_part(matrix, shape, rows_by, columns_by):
    row = lax.broadcasted_iota(jnp.int32, (shape[0], 8), 0)
    level = lax.broadcasted_iota(jnp.int32, (shape[0], 8), 1)
    left = (row // rows_by % 8 == level).astype(F32)
    level = lax.broadcasted_iota(jnp.int32, (8, shape[1]), 0)
    column = lax.broadcasted_iota(jnp.int32, (8, shape[1]), 1)
    right = (column // columns_by % 8 == level).astype(F32)
    return dot_full(dot_full(left, matrix), right)


def tables_body(
    packed,
    near,
    far,
    deriv_rows,
    deriv_lanes,
    pair,
    spread,
    labels,
    speed,
):
    size = near.shape[1]
    count = size // 8
    blocks = spread.shape[0] // 8

    def place_of(shape):
        return (lax.broadcasted_iota(jnp.int32, shape, 0), lax.broadcasted_iota(jnp.int32, shape, 1))

    row, column = place_of((count, size))
    repeat = (column % count == row).astype(F32)
    speed[...] = dot_full(packed[24:25, 0:count], repeat)
    wanted = dot_full(packed[16:24, 0:count], repeat).astype(jnp.int32)
    row, column = place_of((size, size))
    level, element = row // count, row % count
    level_out = column // count
    for facet in range(4):
        shift = -count if facet % 2 == 0 else count
        choice = jnp.broadcast_to(wanted[facet : facet + 1], (size, size))
        near[facet] = jnp.where((level == level_out) & (element == choice), 1.0, 0.0).astype(BF16)
        far[facet] = jnp.where((level == level_out) & (element + shift == choice), 1.0, 0.0).astype(BF16)
    lower = jnp.broadcast_to(wanted[4:5], (size, size))
    upper = jnp.broadcast_to(wanted[5:6], (size, size))
    hit = (level == 7) & (level_out == 0) & (element == lower)
    hit = hit | ((level == 0) & (level_out == 7) & (element == upper))
    near[4] = jnp.where(hit, 1.0, 0.0).astype(BF16)
    hit = (level == 0) & (level_out == 0) & (element - count == lower)
    hit = hit | ((level == 1) & (level_out == 7) & (element + count == upper))
    far[4] = jnp.where(hit, 1.0, 0.0).astype(BF16)

    row, column = place_of((64, 64))
    slopes, modes = packed[0:8, 0:8], packed[8:16, 0:8]
    outer = kron_part(slopes, (64, 64), 8, 8)
    inner = kron_part(slopes, (64, 64), 1, 1)
    deriv_rows[0:64] = jnp.where(row % 8 == column % 8, outer, 0.0)
    deriv_rows[64:128] = jnp.where(row // 8 == column // 8, inner, 0.0)
    row, column = place_of((size, size))
    lanes = kron_part(slopes.T, (size, size), count, count)
    deriv_lanes[...] = jnp.where(row % count == column % count, lanes, 0.0)
    pair[...] = kron_part(modes, (64, 64), 8, 8) * kron_part(modes, (64, 64), 1, 1)

    peers = labels.shape[0]
    capacity = capacity_of(peers, blocks)
    row, column = place_of((blocks, blocks))

    def upright(values):
        return jnp.sum(jnp.where(row == column, values, 0.0), 1, keepdims=True)

    owner_row = packed[25:26, 0:blocks]
    owner_column = upright(owner_row)
    earlier = (owner_column == owner_row) & (column < row)
    position = jnp.sum(jnp.where(earlier, 1.0, 0.0), 1, keepdims=True)
    slot = owner_column * capacity + position
    element_column = upright(packed[26:27, 0:blocks])
    row, column = place_of((8 * blocks, blocks))
    repeat = (row // 8 == column).astype(F32)
    slot = dot_full(repeat, jnp.broadcast_to(slot, (blocks, 128)))
    element = dot_full(repeat, jnp.broadcast_to(element_column, (blocks, 128)))
    row, column = place_of((8 * blocks, 128))
    values = kron_part(modes.T, (8 * blocks, 128), 1, 1)
    inside = column % (8 * capacity) // 8
    for peer in range(peers):
        chosen = slot == (inside + peer * capacity).astype(F32)
        spread[:, peer * 128 : peer * 128 + 128] = jnp.where(chosen, values, 0.0)
        named = jnp.where(chosen & (row % 8 == 0), element + 1.0, 0.0)
        labels[peer] = jnp.broadcast_to(jnp.sum(named, 0, keepdims=True) - 1.0, (8, 128))


def shifted(sizes, shifts):
    pairs = []
    for index in np.ndindex(*sizes):
        source = [(i + s) % n for i, s, n in zip(index, shifts, sizes)]
        pairs.append((int(np.ravel_multi_index(source, sizes)), int(np.ravel_multi_index(index, sizes))))
    return pairs


def partners(sizes, axis, second, shift_x=0):
    pairs = []
    for index in np.ndindex(*sizes):
        source = list(index)
        step = 1 if (index[axis] % 2 == 0) != second else -1
        source[axis] = (index[axis] + step) % sizes[axis]
        if shift_x:
            source[0] = (index[0] + shift_x) % sizes[0]
        pairs.append((int(np.ravel_multi_index(source, sizes)), int(np.ravel_multi_index(index, sizes))))
    return pairs


def per_device(
    density,
    velocity,
    pressure,
    acoustic,
    sound_speed,
    derivative,
    mode_basis,
    neighbours,
    block_owner,
    block_element,
):
    size_x, size_y, size_z = lax.axis_size("fx"), lax.axis_size("fy"), lax.axis_size("fz")
    devices = size_x * size_y * size_z
    cells_x = density.shape[0]
    elements = acoustic.shape[0]
    device = lax.axis_index(("fx", "fy", "fz"))

    names = ("fx", "fy", "fz")

    rows = 5 * cells_x * 8
    tiles = -(-rows // 128)
    square = velocity[0] * velocity[0] + velocity[1] * velocity[1] + velocity[2] * velocity[2]
    energy = pressure / (HEAT_RATIO - 1.0) + 0.5 * density * square
    rest = ((0, 0), (0, 0), (0, 0))
    state = jnp.pad(density[None], ((0, 4),) + rest) + jnp.pad(density * velocity, ((1, 1),) + rest)
    state = state + jnp.pad(energy[None], ((4, 0),) + rest)
    to_a, to_b = call(pack_start_body, [(tiles * 8, 128), (tiles * 8, 128)], state)
    edge_a = lax.ppermute(to_a, "fz", partners((size_z,), 0, False))
    edge_b = lax.ppermute(to_b, "fz", partners((size_z,), 0, True))

    near_pairs = [(i ^ 1, i) for i in range(devices)]
    far_pairs = [pair for i in range(1, devices - 1, 2) for pair in ((i, i + 1), (i + 1, i))]

    def traces(to_a, to_b):
        far_got = lax.ppermute(to_b, names, far_pairs)
        return lax.ppermute(to_a, names, near_pairs), far_got

    size = 8 * elements
    held = (4, 64, size)
    faces = (96, size)
    sides = [pltpu.VMEM(faces, F32)] * 2
    sound, to_a, to_b = call(
        acoustic_start_body,
        [held, faces, faces],
        acoustic,
        to_a,
        scratch=[pltpu.VMEM((512, 128), F32)],
        last=1,
    )
    got_a, got_b = traces(to_a, to_b)

    six = 2 * HALO
    edge_rows = tiles * 8
    shapes = [
        (edge_rows, 128),
        (5 * six * 8 + edge_rows, 128),
        (5 * cells_x * HALO + edge_rows, 128),
        (5 * cells_x * HALO + edge_rows, 128),
        (32 + edge_rows, 128),
        (32 + edge_rows, 128),
    ]
    edge, along_x, y_a, y_b, xy_a, xy_b = call(pack_next_body, shapes, state, edge_a, edge_b, got_a, last=1)
    flat = (size_x, size_y)
    steps = [[(1, 0), (-1, 0)]] if size_x == 2 else [[(1, 0)], [(-1, 0)]]
    places, messages = [], []
    for first, second, spots in [(y_a, y_b, [(0, 0)])] + [(xy_a, xy_b, spots) for spots in steps]:
        shift = spots[0][0]
        for kept, side in ((first, False), (second, True)):
            messages.append(lax.ppermute(kept, ("fx", "fy"), partners(flat, 1, side, shift)))
            places.append(tuple((dx, 1) for dx, _ in spots))
    for spots in steps:
        messages.append(lax.ppermute(along_x, ("fx", "fy"), shifted(flat, spots[0])))
        places.append(tuple(spots))

    local = (neighbours - device * elements).T
    blocks = block_owner.size
    width = max(elements, blocks)

    def piece(values, first):
        values = values.astype(F32)
        return jnp.pad(values, ((first, 32 - first - values.shape[0]), (0, width - values.shape[1])))

    packed = (
        piece(derivative, 0)
        + piece(mode_basis, 8)
        + piece(local, 16)
        + piece(sound_speed.reshape(1, elements), 24)
        + piece(block_owner.reshape(1, blocks), 25)
        + piece(block_element.reshape(1, blocks), 26)
    )
    table = jax.ShapeDtypeStruct((5, size, size), BF16)
    near, far, deriv_rows, deriv_lanes, pair, spread, labels, speed = call(
        tables_body,
        [
            table,
            table,
            (128, 64),
            (size, size),
            (64, 64),
            (8 * blocks, size_y * 128),
            (size_y, 8, 128),
            (1, size),
        ],
        packed,
    )

    fold = fold_of(size_y, blocks)
    wide = cells_x + 2 * HALO
    rows_scratch = pltpu.VMEM((3, 64, 128), F32)

    def planes(count):
        return (5, count, 16, 256)

    def route(send):
        return lax.all_to_all(send, "fy", split_axis=0, concat_axis=0, tiled=True)

    spare = [pltpu.VMEM(shapes[2], F32)] * 2 + [pltpu.VMEM(shapes[4], F32)] * (2 * len(steps))
    start, send = call(
        functools.partial(flow_sources_body, tuple(places)),
        [planes(wide), (size_y, 192 // fold + 8, 128)],
        state,
        edge,
        *messages,
        pair,
        spread,
        labels,
        got_b,
        scratch=[pltpu.VMEM((3, wide, 16, 256), F32), rows_scratch] + spare,
        last=1,
    )
    received = route(send)
    flow_state, send = call(
        flow_stages_body,
        [(5, cells_x, 8, 128), (size_y, 2 * 192 // fold + 8, 128)],
        start,
        pair,
        spread,
        labels,
        scratch=[
            pltpu.VMEM(planes(wide), F32),
            rows_scratch,
            pltpu.VMEM(planes(wide - 2), F32),
            pltpu.VMEM(planes(wide - 4), F32),
        ],
    )

    def local_part(mix, now):
        return call(
            functools.partial(acoustic_local_body, mix),
            [held],
            now,
            sound,
            deriv_rows,
            deriv_lanes,
            speed,
            near,
            scratch=sides,
        )[0]

    partial = local_part(MIXES[0], sound)
    sound_one, to_a, to_b = call(
        functools.partial(acoustic_far_body, MIXES[0], "first"),
        [held, faces, faces],
        partial,
        got_a,
        got_b,
        far,
        received,
        send,
        scratch=sides + [rows_scratch],
        last=1,
    )
    source_two, source_three = call(place_body, [(3, 64, 128)] * 2, route(send))
    got_a, got_b = traces(to_a, to_b)
    partial = local_part(MIXES[1], sound_one)
    sound_two, to_a, to_b = call(
        functools.partial(acoustic_far_body, MIXES[1], "second"),
        [held, faces, faces],
        partial,
        got_a,
        got_b,
        far,
        source_two,
        scratch=sides,
    )
    got_a, got_b = traces(to_a, to_b)
    partial = local_part(MIXES[2], sound_two)
    sound_state = call(
        functools.partial(acoustic_far_body, MIXES[2], "last"),
        [(elements, 4, 512)],
        partial,
        got_a,
        got_b,
        far,
        source_three,
        scratch=sides + [pltpu.VMEM(held, F32), pltpu.VMEM((512, 128), F32)],
    )[0]
    return (flow_state, sound_state)


def solution(mesh):
    placed = (
        P("fx", "fy", "fz"),
        P(None, "fx", "fy", "fz"),
        P("fx", "fy", "fz"),
        P(("fx", "fy", "fz"), None, None),
        P(("fx", "fy", "fz")),
        P(),
        P(),
        P(("fx", "fy", "fz"), None),
        P("fx", "fy", "fz", None, None),
        P("fx", "fy", "fz", None),
    )
    return jax.shard_map(
        per_device,
        mesh=mesh,
        in_specs=placed,
        out_specs=(P(None, "fx", "fy", "fz"), P(("fx", "fy", "fz"), None, None)),
        check_vma=False,
    )
```

```python
import functools

import jax
import jax.numpy as jnp
import numpy as np
from jax import lax
from jax.experimental import pallas as pl
from jax.experimental.pallas import tpu as pltpu
from jax.sharding import PartitionSpec as P

HEAT_RATIO = 1.4
TIME_STEP = 0.1
VISCOSITY = 0.05
PENALTY = 0.5
HALO = 3
F32 = jnp.float32
BF16 = jnp.bfloat16
PARAMS = pltpu.CompilerParams(vmem_limit_bytes=24 * 1024 * 1024)
MIXES = ((0.0, 1.0), (0.75, 0.25), (1.0 / 3.0, 2.0 / 3.0))


def parts(values):
    high = values.astype(BF16)
    return high, (values - high.astype(F32)).astype(BF16)


def dot(left, right):
    return lax.dot_general(left, right, (((1,), (0,)), ((), ())), preferred_element_type=F32)


def dot_three(left, right):
    left_high, left_low = parts(left)
    right_high, right_low = parts(right)
    return dot(left_high, right_high) + dot(left_high, right_low) + dot(left_low, right_high)


def dot_full(left, right, dims=((1,), (0,))):
    return lax.dot_general(
        left, right, (dims, ((), ())), precision=lax.Precision.HIGHEST, preferred_element_type=F32
    )


def dot_exact_right(left, right):
    left_high, left_low = parts(left)
    return dot(left_high, right) + dot(left_low, right)


def call(body, outs, *operands, scratch=(), fetch=False, last=0):
    whole = pl.BlockSpec(memory_space=pltpu.VMEM)
    outs = [out if isinstance(out, jax.ShapeDtypeStruct) else jax.ShapeDtypeStruct(out, F32) for out in outs]
    scratch = list(scratch)
    anywhere = pl.BlockSpec(memory_space=pltpu.HBM)
    specs = [anywhere if fetch else whole] * (len(operands) - last) + [anywhere] * last
    kernel = body
    if fetch:
        count = len(operands)
        total = count + len(outs)

        def kernel(*refs):
            held, sems = refs[total : total + count], refs[total + count]
            copies = [
                pltpu.make_async_copy(refs[i], held[i], sems.at[i]) for i in range(count)
            ]
            for copy in copies:
                copy.start()
            for copy in copies:
                copy.wait()
            body(*held, *refs[count:total], *refs[total + count + 1 :])

        scratch = [pltpu.VMEM(o.shape, o.dtype) for o in operands] + [pltpu.SemaphoreType.DMA((count,))] + scratch
    return pl.pallas_call(
        kernel,
        out_shape=outs,
        in_specs=specs,
        out_specs=[whole] * len(outs),
        scratch_shapes=scratch,
        compiler_params=PARAMS,
    )(*operands)


def capacity_of(peers, blocks):
    return max(2, 2 * blocks // peers)


def fold_of(peers, blocks):
    return 128 // (8 * capacity_of(peers, blocks))


def is_odd(axis):
    return lax.axis_index(axis) % 2 == 1


def paired(odd, to_next, to_last):
    return jnp.where(odd, to_last, to_next), jnp.where(odd, to_next, to_last)


def pack_start_body(state, message_a, message_b):
    odd = is_odd("fz")
    rows = state[...].reshape(-1, 128)
    count = rows.shape[0]
    for tile in range(message_a.shape[0] // 8):
        piece = rows[tile * 128 : min(count, tile * 128 + 128)]
        if piece.shape[0] < 128:
            piece = jnp.concatenate([piece, jnp.zeros((128 - piece.shape[0], 128), F32)], 0)
        turned = piece.T
        first, second = paired(odd, turned[120:128], turned[0:8])
        message_a[tile * 8 : tile * 8 + 8] = first
        message_b[tile * 8 : tile * 8 + 8] = second


def pack_next_body(state, sent_a, sent_b, got_a, got_b, _, edge, along_x, y_a, y_b, xy_a, xy_b):
    cells_x = state.shape[1]
    odd_z, odd = is_odd("fz"), is_odd("fy")
    high, low = paired(odd_z, sent_a[...], sent_b[...])
    above, below = paired(odd_z, got_a[...], got_b[...])
    row = lax.broadcasted_iota(jnp.int32, (8, 128), 0)
    x_of_lane = lax.broadcasted_iota(jnp.int32, (16, 128), 1) // 8 % cells_x
    for tile in range(high.shape[0] // 8):
        rows = slice(tile * 8, tile * 8 + 8)
        upper = jnp.where(row < 3, pltpu.roll(high[rows], 3, 0), pltpu.roll(above[rows], 3, 0))
        lower = jnp.where(row < 3, pltpu.roll(below[rows], 3, 0), pltpu.roll(low[rows], 3, 0))
        slots = jnp.concatenate([upper, lower], 0)
        spread = jnp.concatenate([jnp.where(x_of_lane == x, slots, 0.0) for x in range(8)], 0).T
        for half in range(16 // cells_x):
            f = tile * (16 // cells_x) + half
            if f < 5:
                at = half * cells_x * 8
                total = spread[at : at + 8]
                for x in range(1, cells_x):
                    total = total + spread[at + x * 8 : at + x * 8 + 8]
                edge[f * 8 : f * 8 + 8] = total
    planes = [cells_x - HALO + i for i in range(HALO)] + list(range(HALO))
    for f in range(5):
        for s, x in enumerate(planes):
            at = (f * len(planes) + s) * 8
            along_x[at : at + 8] = state[f, x]
        for x in range(cells_x):
            at = (f * cells_x + x) * HALO
            first, second = paired(odd, state[f, x, 8 - HALO : 8], state[f, x, 0:HALO])
            y_a[at : at + HALO] = first
            y_b[at : at + HALO] = second
        at = f * 6
        for slot, height in ((1, 1), (2, 2), (3, 2), (4, 1)):
            x = planes[slot]
            first, second = paired(odd, state[f, x, 8 - height : 8], state[f, x, 0:height])
            xy_a[at : at + height] = first
            xy_b[at : at + height] = second
            at += height
    for message in (along_x, y_a, y_b, xy_a, xy_b):
        size = message.shape[0]
        message[size - 40 : size] = edge[...]


def assemble(wide, rim, state, edge, beside, cells_x):
    for dx, dy, message in beside:
        if dx == 0:
            columns = [(HALO + x, x) for x in range(cells_x)]
        elif dx < 0:
            columns = [(i, i) for i in range(HALO)]
        else:
            columns = [(HALO + cells_x + i, HALO + i) for i in range(HALO)]
        for f in range(5):
            for plane, slot in columns:
                height = 8 if dy == 0 else HALO
                at = (f * (cells_x if dx == 0 else 2 * HALO) + slot) * height
                if dx != 0 and dy != 0:
                    if slot in (0, 5):
                        continue
                    height = (0, 1, 2, 2, 1)[slot]
                    at = f * 6 + (0, 0, 1, 3, 5)[slot]
                low, high = {0: (0, 8), 1: (8, 8 + height), -1: (16 - height, 16)}[dy]
                wide[f, plane, low:high] = message[at : at + height]
    edges = {(dx, dy): message for dx, dy, message in beside}
    edges[0, 0] = edge
    row = lax.broadcasted_iota(jnp.int32, (8, 128), 0)
    lane = lax.broadcasted_iota(jnp.int32, (8, 128), 1)

    def part(f, dx, dy):
        message = edges[dx, dy]
        at = message.shape[0] - 40 + f * 8
        return message[at : at + 8]

    def beyond(f, dy):
        if edges[1, dy] is edges[-1, dy]:
            return part(f, 1, dy)
        return jnp.where(lane < 64, part(f, 1, dy), part(f, -1, dy))

    for f in range(5):
        for x in range(cells_x):
            wide[f, HALO + x, 0:8] = state[f, x]
        rim[f, 0:8, 0:128] = part(f, 0, 0)
        rim[f, 0:8, 128:256] = beyond(f, 0)
        rim[f, 8:16, 0:128] = jnp.where(row < 4, part(f, 0, 1), part(f, 0, -1))
        rim[f, 8:16, 128:256] = jnp.where(row < 4, beyond(f, 1), beyond(f, -1))


def primitive(rho, mx, my, mz, energy):
    inverse = 1.0 / rho
    u, v, w = mx * inverse, my * inverse, mz * inverse
    p = (HEAT_RATIO - 1.0) * (energy - 0.5 * (mx * u + my * v + mz * w))
    return u, v, w, p, jnp.sqrt(HEAT_RATIO * jnp.abs(p) * inverse)


def derive_planes(wide, derived, first, last):
    def derive(i, _):
        for k, value in enumerate(primitive(*[wide[f, i] for f in range(5)])):
            derived[k, i] = value
        return 0

    lax.fori_loop(first, last, derive, 0)


def derive_speeds(wide, derived, first, last):
    def derive(i, _):
        inverse = 1.0 / wide[0, i]
        for k in range(3):
            derived[k, i] = wide[1 + k, i] * inverse
        return 0

    lax.fori_loop(first, last, derive, 0)


def with_flux(fields, other, along):
    speed, p = other[along], other[3]
    out = [fields[1 + along]]
    for k in range(3):
        value = fields[1 + k] * speed
        out.append(value + p if k == along else value)
    out.append((fields[4] + p) * speed)
    return fields, out, jnp.abs(speed) + other[4]


def face(left, right):
    (fields_l, flux_l, speed_l), (fields_r, flux_r, speed_r) = left, right
    speed = jnp.maximum(speed_l, speed_r)
    viscous = speed + 2.0 * VISCOSITY
    return [
        (flux_l[f] + flux_r[f]) - (viscous if 1 <= f <= 3 else speed) * (fields_r[f] - fields_l[f])
        for f in range(5)
    ]


def rolled(here, shift, axis):
    fields, flux, speed = here
    return (
        [pltpu.roll(a, shift, axis) for a in fields],
        [pltpu.roll(a, shift, axis) for a in flux],
        pltpu.roll(speed, shift, axis),
    )


def rim_section(fields, start, mix):
    other = primitive(*fields)
    here = with_flux(fields, other, 2)
    along_z = face(here, rolled(here, 255, 1))
    if mix is None:
        return other, along_z, None
    total = [g - pltpu.roll(g, 1, 1) for g in along_z]
    for along, step, axis, size in ((0, 16, 1, 256), (1, 1, 0, 16)):
        here = with_flux(fields, other, along)
        faces = face(here, rolled(here, size - step, axis))
        total = [total[f] + (faces[f] - pltpu.roll(faces[f], step, axis)) for f in range(5)]
    out = []
    for f in range(5):
        value = fields[f] - (0.5 * TIME_STEP) * total[f]
        out.append(mix[0] * start[f] + mix[1] * value if mix[0] != 0.0 else value)
    return other, along_z, out


def to_ends(values, after, rows, first, last, ends):
    slot = lax.broadcasted_iota(jnp.int32, (rows, 256), 1) % 16
    for f, value in enumerate(values):
        value = value[0:rows]
        value = jnp.where(slot == 9, pltpu.roll(value, 9 - after, 1), value)
        for x in range(first, last):
            at = x % 16 // 8 * 128
            move = (118 - x % 8 * 16) % 128
            tile = value[:, at : at + 128]
            ends[f, x - first, 0:rows] = pltpu.roll(tile, move, 1) if move else tile


def flow_rate_section(wide, derived, ends, start, offset, mix, write, inner=False):
    depth = wide.shape[1]
    rows = slice(0, 8) if inner else slice(None)
    windows = [rows, slice(None), rows]
    lane = lax.broadcasted_iota(jnp.int32, (8 if inner else 16, 128), 1)

    def plane(i, along):
        kept = windows[along]
        fields = [wide[f, i, kept] for f in range(5)]
        return with_flux(fields, [derived[f, i, kept] for f in range(5)], along)

    def section(i, before):
        ahead = face(plane(i, 0), plane(i + 1, 0))
        total = [ahead[f] - before[f] for f in range(5)]
        here = plane(i, 1)
        faces = face(here, rolled(here, 15, 0))
        for f in range(5):
            change = faces[f] - pltpu.roll(faces[f], 1, 0)
            total[f] = total[f] + (change[0:8] if inner else change)
        here = plane(i, 2)
        faces = face(here, rolled(here, 127, 1))
        for f in range(5):
            end = ends[f, i - 1, rows]
            value = jnp.where(lane == 127, end, faces[f])
            total[f] = total[f] + (value - jnp.where(lane == 0, end, pltpu.roll(value, 1, 1)))
        for f in range(5):
            value = wide[f, i, rows] - (0.5 * TIME_STEP) * total[f]
            if mix[0] != 0.0:
                value = mix[0] * start[f, i + offset, rows] + mix[1] * value
            write(i - 1, f, value)
        return tuple(ahead)

    lax.fori_loop(1, depth - 1, section, tuple(face(plane(0, 0), plane(1, 0))))


def lamb(derived, ends, first, cells_x, lamb_rows):
    lane = lax.broadcasted_iota(jnp.int32, (8, 128), 1)

    def one(x, _):
        i = first + x
        vel = [derived[c, i, 0:8] for c in range(3)]
        along_x = [derived[c, i + 1, 0:8] - derived[c, i - 1, 0:8] for c in range(3)]
        columns = [derived[c, i] for c in range(3)]
        along_y = [(pltpu.roll(a, 15, 0) - pltpu.roll(a, 1, 0))[0:8] for a in columns]
        along_z = []
        for c in range(2):
            end = ends[c, x, 0:8]
            after = jnp.where(lane == 127, end, pltpu.roll(vel[c], 127, 1))
            along_z.append(after - jnp.where(lane == 0, end, pltpu.roll(vel[c], 1, 1)))
        curl = [
            0.5 * (along_y[2] - along_z[1]),
            0.5 * (along_z[0] - along_x[2]),
            0.5 * (along_x[1] - along_y[0]),
        ]
        at = pl.multiple_of(x * 8, 8)
        lamb_rows[0, pl.ds(at, 8), :] = curl[1] * vel[2] - curl[2] * vel[1]
        lamb_rows[1, pl.ds(at, 8), :] = curl[2] * vel[0] - curl[0] * vel[2]
        lamb_rows[2, pl.ds(at, 8), :] = curl[0] * vel[1] - curl[1] * vel[0]
        return 0

    lax.fori_loop(0, cells_x, one, 0)


def project(lamb_rows, pair, spread, send, base):
    peers = send.shape[0]
    fold = fold_of(peers, spread.shape[0] // 8)
    height = 64 // fold
    group = lax.broadcasted_iota(jnp.int32, (height, 128), 1) // (128 // fold)
    for c in range(3):
        sent = dot_three(dot_three(pair[...], lamb_rows[c]), spread[...])
        for peer in range(peers):
            mine = sent[:, peer * 128 : peer * 128 + 128]
            folded = mine[0:height]
            for g in range(1, fold):
                folded = jnp.where(group == g, mine[g * height : g * height + height], folded)
            send[peer, base + c * height : base + c * height + height] = folded


def flow_sources_body(places, *refs):
    state, edge = refs[0:2]
    messages = refs[2 : 2 + len(places)]
    pair, spread, labels, _ = refs[2 + len(places) : 6 + len(places)]
    wide, rim, send, derived, lamb_rows, ends = refs[6 + len(places) : 12 + len(places)]
    spare = refs[12 + len(places) :]
    cells_x = state.shape[1]
    odd = is_odd("fy")
    beside, k = [], 0
    while k < len(places):
        if places[k][0][1] == 0:
            beside.extend((dx, 0, messages[k]) for dx, _ in places[k])
            k += 1
            continue
        above, below = spare[:2]
        spare = spare[2:]
        above[...], below[...] = paired(odd, messages[k][...], messages[k + 1][...])
        beside.extend((dx, 1, above) for dx, _ in places[k])
        beside.extend((dx, -1, below) for dx, _ in places[k])
        k += 2
    assemble(wide, rim, state, edge, beside, cells_x)
    derive_speeds(wide, derived, HALO - 1, HALO + cells_x + 1)
    inverse = 1.0 / rim[0, 0:8]
    to_ends([rim[1, 0:8] * inverse, rim[2, 0:8] * inverse], 3, 8, 0, cells_x, ends)
    lamb(derived, ends, HALO, cells_x, lamb_rows)
    project(lamb_rows, pair, spread, send, 0)
    send[:, send.shape[1] - 8 :] = labels[...]


def flow_stages_body(wide, rim, pair, spread, labels, out, send, derived, lamb_rows, ends, first, second):
    def writer(target):
        def write(i, f, value):
            target[f, i] = value

        return write

    planes = wide.shape[1]
    cells_x = out.shape[1]
    size = (send.shape[1] - 8) // 2
    rim_start = [rim[f] for f in range(5)]
    derive_planes(wide, derived, 0, planes)
    _, along_z, rim_first = rim_section(rim_start, None, MIXES[0])
    to_ends(along_z, 2, 16, -2, cells_x + 2, ends)
    flow_rate_section(wide, derived, ends, wide, 0, MIXES[0], writer(first))
    derive_planes(first, derived, 0, planes - 2)
    other, along_z, rim_second = rim_section(rim_first, [rim[f] for f in range(5)], MIXES[1])
    to_ends(other[0:2], 3, 8, 0, cells_x, ends)
    lamb(derived, ends, 2, cells_x, lamb_rows)
    project(lamb_rows, pair, spread, send, 0)
    to_ends(along_z, 2, 16, -1, cells_x + 1, ends)
    flow_rate_section(first, derived, ends, wide, 1, MIXES[1], writer(second))
    derive_planes(second, derived, 0, planes - 4)
    other, along_z, _ = rim_section(rim_second, None, None)
    to_ends(other[0:2], 3, 8, 0, cells_x, ends)
    lamb(derived, ends, 1, cells_x, lamb_rows)
    project(lamb_rows, pair, spread, send, size)
    send[:, 2 * size :] = labels[...]
    to_ends(along_z, 2, 8, 0, cells_x, ends)
    flow_rate_section(second, derived, ends, wide, 2, MIXES[2], writer(out), inner=True)


def faces_out(state, rear, front):
    lane = lax.broadcasted_iota(jnp.int32, (32, 128), 1) // 16
    for c in range(4):
        front[c * 8 : c * 8 + 8] = state[c, 56:64]
        rear[c * 8 : c * 8 + 8] = state[c, 0:8]
        front[32 + c * 8 : 40 + c * 8] = state[c, pl.ds(7, 8, stride=8), :]
        rear[32 + c * 8 : 40 + c * 8] = state[c, pl.ds(0, 8, stride=8), :]
    rows = state[...].reshape(256, 128)
    last = jnp.zeros((32, 128), F32)
    first = jnp.zeros((32, 128), F32)
    for j in range(8):
        piece = rows[j * 32 : j * 32 + 32]
        last = jnp.where(lane == j, pltpu.roll(piece, (j * 16 + 16) % 128, 1), last)
        first = jnp.where(lane == j, pltpu.roll(piece, j * 16, 1) if j else piece, first)
    front[64:96] = last
    rear[64:96] = first


def faces_sent(odd, state, message_a, message_b):
    faces_out(state, message_b, message_a)
    message_a[...], message_b[...] = paired(odd, message_a[...], message_b[...])


def lift(total, before, after, sides, factor):
    def place(face, rows, target):
        value = factor * dot_exact_right(rows, sides[face])
        for c in range(4):
            total[c, target, :] += value[c * 8 : c * 8 + 8]

    place(0, before[0:32], pl.ds(0, 8))
    place(1, after[0:32], pl.ds(56, 8))
    place(2, before[32:64], pl.ds(0, 8, stride=8))
    place(3, after[32:64], pl.ds(7, 8, stride=8))


def rate_local(state, deriv_rows, deriv_lanes, speed, sides):
    fields = [state[c] for c in range(4)]
    by_rows = dot_three(deriv_rows[...], jnp.concatenate(fields[0:3], 1))
    by_lanes = dot_three(jnp.concatenate([fields[0], fields[3]], 0), deriv_lanes[...])
    divergence = by_rows[0:64, 128:256] + by_rows[64:128, 256:384] + by_lanes[64:128]
    rates = [
        -(speed[...] * speed[...]) * divergence,
        -by_rows[0:64, 0:128],
        -by_rows[64:128, 0:128],
        -by_lanes[0:64],
    ]
    row = lax.broadcasted_iota(jnp.int32, (64, 128), 0)
    lane = lax.broadcasted_iota(jnp.int32, (64, 128), 1)
    count = jnp.zeros((64, 128), F32)
    for value in (row // 8, row % 8, lane // 16):
        count = count + jnp.where((value == 0) | (value == 7), PENALTY, 0.0)
    side = PENALTY * dot_exact_right(state[...].reshape(256, 128), sides[4])
    return [rates[c] - count * fields[c] + side[c * 64 : c * 64 + 64] for c in range(4)]


def acoustic_local_body(mix, state, start, deriv_rows, deriv_lanes, speed, sides, out, front, rear):
    rates = rate_local(state, deriv_rows, deriv_lanes, speed, sides)
    for c in range(4):
        value = state[c] + TIME_STEP * rates[c]
        if mix[0] != 0.0:
            value = mix[0] * start[c] + mix[1] * value
        out[c] = value
    faces_out(state, rear, front)
    lift(out, front, rear, sides, TIME_STEP * mix[1] * PENALTY)


def order_table(count, turned):
    row = lax.broadcasted_iota(jnp.int32, (4 * count, 4 * count), 0)
    column = lax.broadcasted_iota(jnp.int32, (4 * count, 4 * count), 1)
    if turned:
        row, column = column, row
    return (column == (row % count) * 4 + row // count).astype(F32)


def acoustic_start_body(given, _, state, message_a, message_b, turned):
    count = given.shape[0]
    rows = jnp.concatenate([given[e] for e in range(count)], 0)
    rows = dot_full(order_table(count, False), rows)
    rows = jnp.concatenate([rows, jnp.zeros((128 - 4 * count, rows.shape[1]), F32)], 0)
    turned[...] = rows.T
    lane = lax.broadcasted_iota(jnp.int32, (64, 128), 1) // count
    fields = [jnp.zeros((64, 128), F32)] * 4
    for z in range(8):
        piece = turned[pl.ds(z, 64, stride=8), :]
        for c in range(4):
            move = (z - c) * count % 128
            fields[c] = jnp.where(lane == z, pltpu.roll(piece, move, 1) if move else piece, fields[c])
    for c in range(4):
        state[c] = fields[c]
    faces_sent(is_odd("fz"), state, message_a, message_b)


def natural_order(state, out, turned):
    count = out.shape[0]
    lane = lax.broadcasted_iota(jnp.int32, (64, 128), 1) // count
    for z in range(8):
        value = jnp.zeros((64, 128), F32)
        for c in range(4):
            move = (c - z) * count % 128
            value = jnp.where(lane == c, pltpu.roll(state[c], move, 1) if move else state[c], value)
        turned[pl.ds(z, 64, stride=8), :] = value
    rows = dot_full(order_table(count, True), turned[...].T[0 : 4 * count])
    for e in range(count):
        out[e] = rows[4 * e : 4 * e + 4]


def remote_part(out, before, after, sides_far, factor):
    lift(out, before, after, sides_far, factor)
    lane = lax.broadcasted_iota(jnp.int32, (32, 128), 1) // 16
    last, first = before[64:96], after[64:96]
    pieces = []
    for j in range(8):
        left = pltpu.roll(last, 128 - j * 16, 1) if j else last
        right = pltpu.roll(first, (144 - j * 16) % 128, 1) if j != 1 else first
        pieces.append(jnp.where(lane == 0, left, jnp.where(lane == 1, right, 0.0)))
    value = factor * dot_exact_right(jnp.concatenate(pieces, 0), sides_far[4])
    for c in range(4):
        out[c] += value[c * 64 : c * 64 + 64]


def acoustic_far_body(mix, kind, partial, got_a, got_b, sides_far, received, *refs):
    if kind == "last":
        given_out, before, after, out, turned = refs
    elif kind == "first":
        _, out, message_a, message_b, before, after, source = refs
        place_body(received, source)
        received = source
    else:
        out, message_a, message_b, before, after = refs
    odd = is_odd("fz")
    after[...], before[...] = paired(odd, got_a[...], got_b[...])
    out[0] = partial[0]
    for c in range(3):
        out[1 + c] = partial[1 + c] + (TIME_STEP * mix[1]) * received[c]
    remote_part(out, before, after, sides_far, TIME_STEP * mix[1] * PENALTY)
    if kind == "last":
        natural_order(out, given_out, turned)
    else:
        faces_sent(odd, out, message_a, message_b)


def place_body(received, *outs):
    peers, size = received.shape[0], received.shape[1]
    fold = 192 * len(outs) // (size - 8)
    height = 64 // fold
    target = lax.broadcasted_iota(jnp.int32, (128, 128), 0)
    lane = lax.broadcasted_iota(jnp.int32, (128, 128), 1)
    total = None
    for peer in range(peers):
        label = received[peer, size - 8 : size - 7, :]
        label = jnp.broadcast_to(label, (128, 128)).astype(jnp.int32)
        hit = (label == target % 16) & (lane % 8 == target // 16)
        chosen = [jnp.where(hit & (lane // (128 // fold) == g), 1.0, 0.0) for g in range(fold)]
        chosen = jnp.concatenate(chosen, 0).astype(BF16)
        high, low = parts(received[peer, 0 : size - 8])
        dims = (((1,), (1,)), ((), ()))
        value = lax.dot_general(high, chosen, dims, preferred_element_type=F32)
        value = value + lax.dot_general(low, chosen, dims, preferred_element_type=F32)
        total = value if total is None else total + value
    for k, out in enumerate(outs):
        for c in range(3):
            for g in range(fold):
                at = (k * 3 + c) * height
                out[c, g * height : g * height + height] = total[at : at + height, g * 128 : g * 128 + 128]


def kron_part(matrix, shape, rows_by, columns_by):
    row = lax.broadcasted_iota(jnp.int32, (shape[0], 8), 0)
    level = lax.broadcasted_iota(jnp.int32, (shape[0], 8), 1)
    left = (row // rows_by % 8 == level).astype(F32)
    level = lax.broadcasted_iota(jnp.int32, (8, shape[1]), 0)
    column = lax.broadcasted_iota(jnp.int32, (8, shape[1]), 1)
    right = (column // columns_by % 8 == level).astype(F32)
    return dot_full(dot_full(left, matrix), right)


def tables_body(
    packed,
    near,
    far,
    deriv_rows,
    deriv_lanes,
    pair,
    spread,
    labels,
    speed,
):
    size = near.shape[1]
    count = size // 8
    blocks = spread.shape[0] // 8

    def place_of(shape):
        return (lax.broadcasted_iota(jnp.int32, shape, 0), lax.broadcasted_iota(jnp.int32, shape, 1))

    row, column = place_of((count, size))
    repeat = (column % count == row).astype(F32)
    speed[...] = dot_full(packed[24:25, 0:count], repeat)
    wanted = dot_full(packed[16:24, 0:count], repeat).astype(jnp.int32)
    row, column = place_of((size, size))
    level, element = row // count, row % count
    level_out = column // count
    for facet in range(4):
        shift = -count if facet % 2 == 0 else count
        choice = jnp.broadcast_to(wanted[facet : facet + 1], (size, size))
        near[facet] = jnp.where((level == level_out) & (element == choice), 1.0, 0.0).astype(BF16)
        far[facet] = jnp.where((level == level_out) & (element + shift == choice), 1.0, 0.0).astype(BF16)
    lower = jnp.broadcast_to(wanted[4:5], (size, size))
    upper = jnp.broadcast_to(wanted[5:6], (size, size))
    hit = (level == 7) & (level_out == 0) & (element == lower)
    hit = hit | ((level == 0) & (level_out == 7) & (element == upper))
    near[4] = jnp.where(hit, 1.0, 0.0).astype(BF16)
    hit = (level == 0) & (level_out == 0) & (element - count == lower)
    hit = hit | ((level == 1) & (level_out == 7) & (element + count == upper))
    far[4] = jnp.where(hit, 1.0, 0.0).astype(BF16)

    row, column = place_of((64, 64))
    slopes, modes = packed[0:8, 0:8], packed[8:16, 0:8]
    outer = kron_part(slopes, (64, 64), 8, 8)
    inner = kron_part(slopes, (64, 64), 1, 1)
    deriv_rows[0:64] = jnp.where(row % 8 == column % 8, outer, 0.0)
    deriv_rows[64:128] = jnp.where(row // 8 == column // 8, inner, 0.0)
    row, column = place_of((size, size))
    lanes = kron_part(slopes.T, (size, size), count, count)
    deriv_lanes[...] = jnp.where(row % count == column % count, lanes, 0.0)
    pair[...] = kron_part(modes, (64, 64), 8, 8) * kron_part(modes, (64, 64), 1, 1)

    peers = labels.shape[0]
    capacity = capacity_of(peers, blocks)
    row, column = place_of((blocks, blocks))

    def upright(values):
        return jnp.sum(jnp.where(row == column, values, 0.0), 1, keepdims=True)

    owner_row = packed[25:26, 0:blocks]
    owner_column = upright(owner_row)
    earlier = (owner_column == owner_row) & (column < row)
    position = jnp.sum(jnp.where(earlier, 1.0, 0.0), 1, keepdims=True)
    slot = owner_column * capacity + position
    element_column = upright(packed[26:27, 0:blocks])
    row, column = place_of((8 * blocks, blocks))
    repeat = (row // 8 == column).astype(F32)
    slot = dot_full(repeat, jnp.broadcast_to(slot, (blocks, 128)))
    element = dot_full(repeat, jnp.broadcast_to(element_column, (blocks, 128)))
    row, column = place_of((8 * blocks, 128))
    values = kron_part(modes.T, (8 * blocks, 128), 1, 1)
    inside = column % (8 * capacity) // 8
    for peer in range(peers):
        chosen = slot == (inside + peer * capacity).astype(F32)
        spread[:, peer * 128 : peer * 128 + 128] = jnp.where(chosen, values, 0.0)
        named = jnp.where(chosen & (row % 8 == 0), element + 1.0, 0.0)
        labels[peer] = jnp.broadcast_to(jnp.sum(named, 0, keepdims=True) - 1.0, (8, 128))


def shifted(sizes, shifts):
    pairs = []
    for index in np.ndindex(*sizes):
        source = [(i + s) % n for i, s, n in zip(index, shifts, sizes)]
        pairs.append((int(np.ravel_multi_index(source, sizes)), int(np.ravel_multi_index(index, sizes))))
    return pairs


def partners(sizes, axis, second, shift_x=0):
    pairs = []
    for index in np.ndindex(*sizes):
        source = list(index)
        step = 1 if (index[axis] % 2 == 0) != second else -1
        source[axis] = (index[axis] + step) % sizes[axis]
        if shift_x:
            source[0] = (index[0] + shift_x) % sizes[0]
        pairs.append((int(np.ravel_multi_index(source, sizes)), int(np.ravel_multi_index(index, sizes))))
    return pairs


def per_device(
    density,
    velocity,
    pressure,
    acoustic,
    sound_speed,
    derivative,
    mode_basis,
    neighbours,
    block_owner,
    block_element,
):
    size_x, size_y, size_z = lax.axis_size("fx"), lax.axis_size("fy"), lax.axis_size("fz")
    devices = size_x * size_y * size_z
    cells_x = density.shape[0]
    elements = acoustic.shape[0]
    device = lax.axis_index(("fx", "fy", "fz"))

    names = ("fx", "fy", "fz")

    rows = 5 * cells_x * 8
    tiles = -(-rows // 128)
    square = velocity[0] * velocity[0] + velocity[1] * velocity[1] + velocity[2] * velocity[2]
    energy = pressure / (HEAT_RATIO - 1.0) + 0.5 * density * square
    rest = ((0, 0), (0, 0), (0, 0))
    state = jnp.pad(density[None], ((0, 4),) + rest) + jnp.pad(density * velocity, ((1, 1),) + rest)
    state = state + jnp.pad(energy[None], ((4, 0),) + rest)
    flow_a, flow_b = call(pack_start_body, [(tiles * 8, 128), (tiles * 8, 128)], state)
    edge_a = lax.ppermute(flow_a, "fz", partners((size_z,), 0, False))
    edge_b = lax.ppermute(flow_b, "fz", partners((size_z,), 0, True))

    near_pairs = [(i ^ 1, i) for i in range(devices)]
    far_pairs = [pair for i in range(1, devices - 1, 2) for pair in ((i, i + 1), (i + 1, i))]

    def traces(to_a, to_b):
        far_got = lax.ppermute(to_b, names, far_pairs)
        return lax.ppermute(to_a, names, near_pairs), far_got

    size = 8 * elements
    held = (4, 64, size)
    faces = (96, size)
    sides = [pltpu.VMEM(faces, F32)] * 2
    sound, to_a, to_b = call(
        acoustic_start_body,
        [held, faces, faces],
        acoustic,
        flow_a,
        scratch=[pltpu.VMEM((512, 128), F32)],
        last=1,
    )
    got_a, got_b = traces(to_a, to_b)

    six = 2 * HALO
    edge_rows = 5 * 8
    shapes = [
        (edge_rows, 128),
        (5 * six * 8 + edge_rows, 128),
        (5 * cells_x * HALO + edge_rows, 128),
        (5 * cells_x * HALO + edge_rows, 128),
        (32 + edge_rows, 128),
        (32 + edge_rows, 128),
    ]
    edge, along_x, y_a, y_b, xy_a, xy_b = call(
        pack_next_body, shapes, state, flow_a, flow_b, edge_a, edge_b, got_a, last=1
    )
    flat = (size_x, size_y)
    steps = [[(1, 0), (-1, 0)]] if size_x == 2 else [[(1, 0)], [(-1, 0)]]
    places, messages = [], []
    for first, second, spots in [(y_a, y_b, [(0, 0)])] + [(xy_a, xy_b, spots) for spots in steps]:
        shift = spots[0][0]
        for kept, side in ((first, False), (second, True)):
            messages.append(lax.ppermute(kept, ("fx", "fy"), partners(flat, 1, side, shift)))
            places.append(tuple((dx, 1) for dx, _ in spots))
    for spots in steps:
        messages.append(lax.ppermute(along_x, ("fx", "fy"), shifted(flat, spots[0])))
        places.append(tuple(spots))

    local = (neighbours - device * elements).T
    blocks = block_owner.size
    width = max(elements, blocks)

    def piece(values, first):
        values = values.astype(F32)
        return jnp.pad(values, ((first, 32 - first - values.shape[0]), (0, width - values.shape[1])))

    packed = (
        piece(derivative, 0)
        + piece(mode_basis, 8)
        + piece(local, 16)
        + piece(sound_speed.reshape(1, elements), 24)
        + piece(block_owner.reshape(1, blocks), 25)
        + piece(block_element.reshape(1, blocks), 26)
    )
    table = jax.ShapeDtypeStruct((5, size, size), BF16)
    near, far, deriv_rows, deriv_lanes, pair, spread, labels, speed = call(
        tables_body,
        [
            table,
            table,
            (128, 64),
            (size, size),
            (64, 64),
            (8 * blocks, size_y * 128),
            (size_y, 8, 128),
            (1, size),
        ],
        packed,
    )

    fold = fold_of(size_y, blocks)
    wide = cells_x + 2 * HALO
    rows_scratch = pltpu.VMEM((3, 64, 128), F32)

    def planes(count):
        return (5, count, 16, 128)

    def route(send):
        return lax.all_to_all(send, "fy", split_axis=0, concat_axis=0, tiled=True)

    spare = [pltpu.VMEM(shapes[2], F32)] * 2 + [pltpu.VMEM(shapes[4], F32)] * (2 * len(steps))
    start, rim, send = call(
        functools.partial(flow_sources_body, tuple(places)),
        [planes(wide), (5, 16, 256), (size_y, 192 // fold + 8, 128)],
        state,
        edge,
        *messages,
        pair,
        spread,
        labels,
        got_b,
        scratch=[
            pltpu.VMEM((3, wide, 16, 128), F32),
            rows_scratch,
            pltpu.VMEM((2, cells_x, 8, 128), F32),
        ]
        + spare,
        last=1,
    )
    received = route(send)
    flow_state, send = call(
        flow_stages_body,
        [(5, cells_x, 8, 128), (size_y, 2 * 192 // fold + 8, 128)],
        start,
        rim,
        pair,
        spread,
        labels,
        scratch=[
            pltpu.VMEM(planes(wide), F32),
            rows_scratch,
            pltpu.VMEM(planes(wide - 2), F32),
            pltpu.VMEM(planes(wide - 2), F32),
            pltpu.VMEM(planes(wide - 4), F32),
        ],
    )

    def local_part(mix, now):
        return call(
            functools.partial(acoustic_local_body, mix),
            [held],
            now,
            sound,
            deriv_rows,
            deriv_lanes,
            speed,
            near,
            scratch=sides,
        )[0]

    partial = local_part(MIXES[0], sound)
    sound_one, to_a, to_b = call(
        functools.partial(acoustic_far_body, MIXES[0], "first"),
        [held, faces, faces],
        partial,
        got_a,
        got_b,
        far,
        received,
        send,
        scratch=sides + [rows_scratch],
        last=1,
    )
    source_two, source_three = call(place_body, [(3, 64, 128)] * 2, route(send))
    got_a, got_b = traces(to_a, to_b)
    partial = local_part(MIXES[1], sound_one)
    sound_two, to_a, to_b = call(
        functools.partial(acoustic_far_body, MIXES[1], "second"),
        [held, faces, faces],
        partial,
        got_a,
        got_b,
        far,
        source_two,
        scratch=sides,
    )
    got_a, got_b = traces(to_a, to_b)
    partial = local_part(MIXES[2], sound_two)
    sound_state = call(
        functools.partial(acoustic_far_body, MIXES[2], "last"),
        [(elements, 4, 512)],
        partial,
        got_a,
        got_b,
        far,
        source_three,
        scratch=sides + [pltpu.VMEM(held, F32), pltpu.VMEM((512, 128), F32)],
    )[0]
    return (flow_state, sound_state)


def solution(mesh):
    placed = (
        P("fx", "fy", "fz"),
        P(None, "fx", "fy", "fz"),
        P("fx", "fy", "fz"),
        P(("fx", "fy", "fz"), None, None),
        P(("fx", "fy", "fz")),
        P(),
        P(),
        P(("fx", "fy", "fz"), None),
        P("fx", "fy", "fz", None, None),
        P("fx", "fy", "fz", None),
    )
    return jax.shard_map(
        per_device,
        mesh=mesh,
        in_specs=placed,
        out_specs=(P(None, "fx", "fy", "fz"), P(("fx", "fy", "fz"), None, None)),
        check_vma=False,
    )
```

```python
import functools

import jax
import jax.numpy as jnp
import numpy as np
from jax import lax
from jax.experimental import pallas as pl
from jax.experimental.pallas import tpu as pltpu
from jax.sharding import PartitionSpec as P

HEAT_RATIO = 1.4
TIME_STEP = 0.1
VISCOSITY = 0.05
PENALTY = 0.5
HALO = 3
F32 = jnp.float32
BF16 = jnp.bfloat16
PARAMS = pltpu.CompilerParams(vmem_limit_bytes=24 * 1024 * 1024)
MIXES = ((0.0, 1.0), (0.75, 0.25), (1.0 / 3.0, 2.0 / 3.0))


def parts(values):
    high = values.astype(BF16)
    return high, (values - high.astype(F32)).astype(BF16)


def dot(left, right):
    return lax.dot_general(left, right, (((1,), (0,)), ((), ())), preferred_element_type=F32)


def dot_three(left, right):
    left_high, left_low = parts(left)
    right_high, right_low = parts(right)
    return dot(left_high, right_high) + dot(left_high, right_low) + dot(left_low, right_high)


def dot_full(left, right, dims=((1,), (0,))):
    return lax.dot_general(
        left, right, (dims, ((), ())), precision=lax.Precision.HIGHEST, preferred_element_type=F32
    )


def dot_exact_right(left, right):
    left_high, left_low = parts(left)
    return dot(left_high, right) + dot(left_low, right)


def call(body, outs, *operands, scratch=(), fetch=False, last=0):
    whole = pl.BlockSpec(memory_space=pltpu.VMEM)
    outs = [out if isinstance(out, jax.ShapeDtypeStruct) else jax.ShapeDtypeStruct(out, F32) for out in outs]
    scratch = list(scratch)
    anywhere = pl.BlockSpec(memory_space=pltpu.HBM)
    specs = [anywhere if fetch else whole] * (len(operands) - last) + [anywhere] * last
    kernel = body
    if fetch:
        count = len(operands)
        total = count + len(outs)

        def kernel(*refs):
            held, sems = refs[total : total + count], refs[total + count]
            copies = [
                pltpu.make_async_copy(refs[i], held[i], sems.at[i]) for i in range(count)
            ]
            for copy in copies:
                copy.start()
            for copy in copies:
                copy.wait()
            body(*held, *refs[count:total], *refs[total + count + 1 :])

        scratch = [pltpu.VMEM(o.shape, o.dtype) for o in operands] + [pltpu.SemaphoreType.DMA((count,))] + scratch
    return pl.pallas_call(
        kernel,
        out_shape=outs,
        in_specs=specs,
        out_specs=[whole] * len(outs),
        scratch_shapes=scratch,
        compiler_params=PARAMS,
    )(*operands)


def capacity_of(peers, blocks):
    return max(2, 2 * blocks // peers)


def fold_of(peers, blocks):
    return 128 // (8 * capacity_of(peers, blocks))


def is_odd(axis):
    return lax.axis_index(axis) % 2 == 1


def paired(odd, to_next, to_last):
    return jnp.where(odd, to_last, to_next), jnp.where(odd, to_next, to_last)


def pack_start_body(state, message_a, message_b):
    odd = is_odd("fz")
    rows = state[...].reshape(-1, 128)
    count = rows.shape[0]
    for tile in range(message_a.shape[0] // 8):
        piece = rows[tile * 128 : min(count, tile * 128 + 128)]
        if piece.shape[0] < 128:
            piece = jnp.concatenate([piece, jnp.zeros((128 - piece.shape[0], 128), F32)], 0)
        turned = piece.T
        first, second = paired(odd, turned[120:128], turned[0:8])
        message_a[tile * 8 : tile * 8 + 8] = first
        message_b[tile * 8 : tile * 8 + 8] = second


def pack_next_body(
    state, sent_a, sent_b, got_a, got_b, _, edge, along_x, y_a, y_b, xy_a, xy_b
):
    cells_x = state.shape[1]
    odd_z, odd = is_odd("fz"), is_odd("fy")
    high, low = paired(odd_z, sent_a[...], sent_b[...])
    above, below = paired(odd_z, got_a[...], got_b[...])
    row = lax.broadcasted_iota(jnp.int32, (8, 128), 0)
    x_of_lane = lax.broadcasted_iota(jnp.int32, (16, 128), 1) // 8 % cells_x
    for tile in range(high.shape[0] // 8):
        rows = slice(tile * 8, tile * 8 + 8)
        upper = jnp.where(row < 3, pltpu.roll(high[rows], 3, 0), pltpu.roll(above[rows], 3, 0))
        lower = jnp.where(row < 3, pltpu.roll(below[rows], 3, 0), pltpu.roll(low[rows], 3, 0))
        slots = jnp.concatenate([upper, lower], 0)
        spread = jnp.concatenate([jnp.where(x_of_lane == x, slots, 0.0) for x in range(8)], 0).T
        for half in range(16 // cells_x):
            f = tile * (16 // cells_x) + half
            if f < 5:
                at = half * cells_x * 8
                total = spread[at : at + 8]
                for x in range(1, cells_x):
                    total = total + spread[at + x * 8 : at + x * 8 + 8]
                edge[f * 8 : f * 8 + 8] = total
    planes = [cells_x - HALO + i for i in range(HALO)] + list(range(HALO))
    for f in range(5):
        for s, x in enumerate(planes):
            at = (f * len(planes) + s) * 8
            along_x[at : at + 8] = state[f, x]
        for x in range(cells_x):
            at = (f * cells_x + x) * HALO
            first, second = paired(odd, state[f, x, 8 - HALO : 8], state[f, x, 0:HALO])
            y_a[at : at + HALO] = first
            y_b[at : at + HALO] = second
        at = f * 6
        for slot, height in ((1, 1), (2, 2), (3, 2), (4, 1)):
            x = planes[slot]
            first, second = paired(odd, state[f, x, 8 - height : 8], state[f, x, 0:height])
            xy_a[at : at + height] = first
            xy_b[at : at + height] = second
            at += height
    for message in (along_x, y_a, y_b, xy_a, xy_b):
        size = message.shape[0]
        message[size - 40 : size] = edge[...]


def assemble(wide, rim, state, edge, beside, cells_x):
    for dx, dy, message in beside:
        if dx == 0:
            columns = [(HALO + x, x) for x in range(cells_x)]
        elif dx < 0:
            columns = [(i, i) for i in range(HALO)]
        else:
            columns = [(HALO + cells_x + i, HALO + i) for i in range(HALO)]
        for f in range(5):
            for plane, slot in columns:
                height = 8 if dy == 0 else HALO
                at = (f * (cells_x if dx == 0 else 2 * HALO) + slot) * height
                if dx != 0 and dy != 0:
                    if slot in (0, 5):
                        continue
                    height = (0, 1, 2, 2, 1)[slot]
                    at = f * 6 + (0, 0, 1, 3, 5)[slot]
                low, high = {0: (0, 8), 1: (8, 8 + height), -1: (16 - height, 16)}[dy]
                wide[f, plane, low:high] = message[at : at + height]
    edges = {(dx, dy): message for dx, dy, message in beside}
    edges[0, 0] = edge
    row = lax.broadcasted_iota(jnp.int32, (8, 128), 0)
    lane = lax.broadcasted_iota(jnp.int32, (8, 128), 1)

    def part(f, dx, dy):
        message = edges[dx, dy]
        at = message.shape[0] - 40 + f * 8
        return message[at : at + 8]

    def beyond(f, dy):
        if edges[1, dy] is edges[-1, dy]:
            return part(f, 1, dy)
        return jnp.where(lane < 64, part(f, 1, dy), part(f, -1, dy))

    for f in range(5):
        for x in range(cells_x):
            wide[f, HALO + x, 0:8] = state[f, x]
        rim[f, 0:8, 0:128] = part(f, 0, 0)
        rim[f, 0:8, 128:256] = beyond(f, 0)
        rim[f, 8:16, 0:128] = jnp.where(row < 4, part(f, 0, 1), part(f, 0, -1))
        rim[f, 8:16, 128:256] = jnp.where(row < 4, beyond(f, 1), beyond(f, -1))


def primitive(rho, mx, my, mz, energy):
    inverse = 1.0 / rho
    u, v, w = mx * inverse, my * inverse, mz * inverse
    p = (HEAT_RATIO - 1.0) * (energy - 0.5 * (mx * u + my * v + mz * w))
    return u, v, w, p, jnp.sqrt(HEAT_RATIO * jnp.abs(p) * inverse)


def chunks(first, last, size):
    return [(i, min(i + size, last)) for i in range(first, last, size)]


def derive_planes(wide, derived, first, last):
    for i, j in chunks(first, last, 4):
        for k, value in enumerate(primitive(*[wide[f, i:j] for f in range(5)])):
            derived[k, i:j] = value


def derive_speeds(wide, derived, first, last):
    for i, j in chunks(first, last, 5):
        inverse = 1.0 / wide[0, i:j]
        for k in range(3):
            derived[k, i:j] = wide[1 + k, i:j] * inverse


def with_flux(fields, other, along):
    speed, p = other[along], other[3]
    out = [fields[1 + along]]
    for k in range(3):
        value = fields[1 + k] * speed
        out.append(value + p if k == along else value)
    out.append((fields[4] + p) * speed)
    return fields, out, jnp.abs(speed) + other[4]


def face(left, right):
    (fields_l, flux_l, speed_l), (fields_r, flux_r, speed_r) = left, right
    speed = jnp.maximum(speed_l, speed_r)
    viscous = speed + 2.0 * VISCOSITY
    return [
        (flux_l[f] + flux_r[f]) - (viscous if 1 <= f <= 3 else speed) * (fields_r[f] - fields_l[f])
        for f in range(5)
    ]


def rolled(here, shift, axis):
    fields, flux, speed = here
    return (
        [pltpu.roll(a, shift, axis) for a in fields],
        [pltpu.roll(a, shift, axis) for a in flux],
        pltpu.roll(speed, shift, axis),
    )


def rim_section(fields, start, mix):
    other = primitive(*fields)
    here = with_flux(fields, other, 2)
    along_z = face(here, rolled(here, 255, 1))
    if mix is None:
        return other, along_z, None
    total = [g - pltpu.roll(g, 1, 1) for g in along_z]
    for along, step, axis, size in ((0, 16, 1, 256), (1, 1, 0, 16)):
        here = with_flux(fields, other, along)
        faces = face(here, rolled(here, size - step, axis))
        total = [total[f] + (faces[f] - pltpu.roll(faces[f], step, axis)) for f in range(5)]
    out = []
    for f in range(5):
        value = fields[f] - (0.5 * TIME_STEP) * total[f]
        out.append(mix[0] * start[f] + mix[1] * value if mix[0] != 0.0 else value)
    return other, along_z, out


def to_ends(values, after, rows, first, last, ends):
    slot = lax.broadcasted_iota(jnp.int32, (rows, 256), 1) % 16
    for f, value in enumerate(values):
        value = value[0:rows]
        value = jnp.where(slot == 9, pltpu.roll(value, 9 - after, 1), value)
        for x in range(first, last):
            at = x % 16 // 8 * 128
            move = (118 - x % 8 * 16) % 128
            tile = value[:, at : at + 128]
            ends[f, x - first, 0:rows] = pltpu.roll(tile, move, 1) if move else tile


def flow_rate_section(wide, derived, ends, start, offset, mix, write, inner=False):
    depth = wide.shape[1]
    rows = slice(0, 8) if inner else slice(None)
    size = 4 if inner else 2

    def planes(i, j, kept, along):
        fields = [wide[f, i:j, kept] for f in range(5)]
        return with_flux(fields, [derived[f, i:j, kept] for f in range(5)], along)

    def cut(here, i, j):
        return [a[i:j] for a in here[0]], [a[i:j] for a in here[1]], here[2][i:j]

    for i, j in chunks(1, depth - 1, size):
        count = j - i
        lane = lax.broadcasted_iota(jnp.int32, (count, 8 if inner else 16, 128), 2)
        here = planes(i - 1, j + 1, rows, 0)
        faces = face(cut(here, 0, count + 1), cut(here, 1, count + 2))
        total = [g[1:] - g[:-1] for g in faces]
        here = planes(i, j, slice(None), 1)
        faces = face(here, rolled(here, 15, 1))
        for f in range(5):
            change = faces[f] - pltpu.roll(faces[f], 1, 1)
            total[f] = total[f] + (change[:, 0:8] if inner else change)
        here = planes(i, j, rows, 2)
        faces = face(here, rolled(here, 127, 2))
        for f in range(5):
            end = ends[f, i - 1 : j - 1, rows]
            value = jnp.where(lane == 127, end, faces[f])
            total[f] = total[f] + (value - jnp.where(lane == 0, end, pltpu.roll(value, 1, 2)))
        for f in range(5):
            value = wide[f, i:j, rows] - (0.5 * TIME_STEP) * total[f]
            if mix[0] != 0.0:
                value = mix[0] * start[f, i + offset : j + offset, rows] + mix[1] * value
            write(slice(i - 1, j - 1), f, value)


def lamb(derived, ends, first, cells_x, lamb_rows):
    for i, j in chunks(first, first + cells_x, 4):
        count = j - i
        lane = lax.broadcasted_iota(jnp.int32, (count, 8, 128), 2)
        vel = [derived[c, i:j, 0:8] for c in range(3)]
        along_x = [derived[c, i + 1 : j + 1, 0:8] - derived[c, i - 1 : j - 1, 0:8] for c in range(3)]
        along_y = []
        for c in range(3):
            column = derived[c, i:j]
            along_y.append((pltpu.roll(column, 15, 1) - pltpu.roll(column, 1, 1))[:, 0:8])
        along_z = []
        for c in range(2):
            end = ends[c, i - first : j - first, 0:8]
            after = jnp.where(lane == 127, end, pltpu.roll(vel[c], 127, 2))
            along_z.append(after - jnp.where(lane == 0, end, pltpu.roll(vel[c], 1, 2)))
        curl = [
            0.5 * (along_y[2] - along_z[1]),
            0.5 * (along_z[0] - along_x[2]),
            0.5 * (along_x[1] - along_y[0]),
        ]
        at = slice((i - first) * 8, (j - first) * 8)
        lamb_rows[0, at] = (curl[1] * vel[2] - curl[2] * vel[1]).reshape(count * 8, 128)
        lamb_rows[1, at] = (curl[2] * vel[0] - curl[0] * vel[2]).reshape(count * 8, 128)
        lamb_rows[2, at] = (curl[0] * vel[1] - curl[1] * vel[0]).reshape(count * 8, 128)


def project(lamb_rows, pair, spread, send, base):
    peers = send.shape[0]
    fold = fold_of(peers, spread.shape[0] // 8)
    height = 64 // fold
    group = lax.broadcasted_iota(jnp.int32, (height, 128), 1) // (128 // fold)
    modes = dot_three(pair[...], jnp.concatenate([lamb_rows[c] for c in range(3)], 1))
    modes = jnp.concatenate([modes[:, c * 128 : c * 128 + 128] for c in range(3)], 0)
    sent = dot_three(modes, spread[...])
    for c in range(3):
        for peer in range(peers):
            mine = sent[c * 64 : c * 64 + 64, peer * 128 : peer * 128 + 128]
            folded = mine[0:height]
            for g in range(1, fold):
                folded = jnp.where(group == g, mine[g * height : g * height + height], folded)
            send[peer, base + c * height : base + c * height + height] = folded


def flow_sources_body(places, *refs):
    state, edge = refs[0:2]
    messages = refs[2 : 2 + len(places)]
    pair, spread, labels = refs[2 + len(places) : 5 + len(places)]
    wide, rim, send, derived, lamb_rows, ends = refs[5 + len(places) : 11 + len(places)]
    spare = refs[11 + len(places) :]
    cells_x = state.shape[1]
    odd = is_odd("fy")
    beside, k = [], 0
    while k < len(places):
        if places[k][0][1] == 0:
            beside.extend((dx, 0, messages[k]) for dx, _ in places[k])
            k += 1
            continue
        above, below = spare[:2]
        spare = spare[2:]
        above[...], below[...] = paired(odd, messages[k][...], messages[k + 1][...])
        beside.extend((dx, 1, above) for dx, _ in places[k])
        beside.extend((dx, -1, below) for dx, _ in places[k])
        k += 2
    assemble(wide, rim, state, edge, beside, cells_x)
    derive_speeds(wide, derived, HALO - 1, HALO + cells_x + 1)
    inverse = 1.0 / rim[0, 0:8]
    to_ends([rim[1, 0:8] * inverse, rim[2, 0:8] * inverse], 3, 8, 0, cells_x, ends)
    lamb(derived, ends, HALO, cells_x, lamb_rows)
    project(lamb_rows, pair, spread, send, 0)
    send[:, send.shape[1] - 8 :] = labels[...]


def flow_stages_body(wide, rim, pair, spread, labels, _, out, send, derived, lamb_rows, ends, first, second):
    def writer(target):
        def write(i, f, value):
            target[f, i] = value

        return write

    planes = wide.shape[1]
    cells_x = out.shape[1]
    size = (send.shape[1] - 8) // 2
    rim_start = [rim[f] for f in range(5)]
    derive_planes(wide, derived, 0, planes)
    _, along_z, rim_first = rim_section(rim_start, None, MIXES[0])
    to_ends(along_z, 2, 16, -2, cells_x + 2, ends)
    flow_rate_section(wide, derived, ends, wide, 0, MIXES[0], writer(first))
    derive_planes(first, derived, 0, planes - 2)
    other, along_z, rim_second = rim_section(rim_first, [rim[f] for f in range(5)], MIXES[1])
    to_ends(other[0:2], 3, 8, 0, cells_x, ends)
    lamb(derived, ends, 2, cells_x, lamb_rows)
    project(lamb_rows, pair, spread, send, 0)
    to_ends(along_z, 2, 16, -1, cells_x + 1, ends)
    flow_rate_section(first, derived, ends, wide, 1, MIXES[1], writer(second))
    derive_planes(second, derived, 0, planes - 4)
    other, along_z, _ = rim_section(rim_second, None, None)
    to_ends(other[0:2], 3, 8, 0, cells_x, ends)
    lamb(derived, ends, 1, cells_x, lamb_rows)
    project(lamb_rows, pair, spread, send, size)
    send[:, 2 * size :] = labels[...]
    to_ends(along_z, 2, 8, 0, cells_x, ends)
    flow_rate_section(second, derived, ends, wide, 2, MIXES[2], writer(out), inner=True)


def faces_out(state, rear, front):
    lane = lax.broadcasted_iota(jnp.int32, (32, 128), 1) // 16
    for c in range(4):
        front[c * 8 : c * 8 + 8] = state[c, 56:64]
        rear[c * 8 : c * 8 + 8] = state[c, 0:8]
        front[32 + c * 8 : 40 + c * 8] = state[c, pl.ds(7, 8, stride=8), :]
        rear[32 + c * 8 : 40 + c * 8] = state[c, pl.ds(0, 8, stride=8), :]
    rows = state[...].reshape(256, 128)
    last = jnp.zeros((32, 128), F32)
    first = jnp.zeros((32, 128), F32)
    for j in range(8):
        piece = rows[j * 32 : j * 32 + 32]
        last = jnp.where(lane == j, pltpu.roll(piece, (j * 16 + 16) % 128, 1), last)
        first = jnp.where(lane == j, pltpu.roll(piece, j * 16, 1) if j else piece, first)
    front[64:96] = last
    rear[64:96] = first


def faces_sent(odd, state, message_a, message_b):
    faces_out(state, message_b, message_a)
    message_a[...], message_b[...] = paired(odd, message_a[...], message_b[...])


def lift(total, before, after, sides, factor):
    def place(face, rows, target):
        value = factor * dot_exact_right(rows, sides[face])
        for c in range(4):
            total[c, target, :] += value[c * 8 : c * 8 + 8]

    place(0, before[0:32], pl.ds(0, 8))
    place(1, after[0:32], pl.ds(56, 8))
    place(2, before[32:64], pl.ds(0, 8, stride=8))
    place(3, after[32:64], pl.ds(7, 8, stride=8))


def rate_local(state, deriv_rows, deriv_lanes, speed, sides):
    fields = [state[c] for c in range(4)]
    by_rows = dot_three(deriv_rows[...], jnp.concatenate(fields[0:3], 1))
    by_lanes = dot_three(jnp.concatenate([fields[0], fields[3]], 0), deriv_lanes[...])
    divergence = by_rows[0:64, 128:256] + by_rows[64:128, 256:384] + by_lanes[64:128]
    rates = [
        -(speed[...] * speed[...]) * divergence,
        -by_rows[0:64, 0:128],
        -by_rows[64:128, 0:128],
        -by_lanes[0:64],
    ]
    row = lax.broadcasted_iota(jnp.int32, (64, 128), 0)
    lane = lax.broadcasted_iota(jnp.int32, (64, 128), 1)
    count = jnp.zeros((64, 128), F32)
    for value in (row // 8, row % 8, lane // 16):
        count = count + jnp.where((value == 0) | (value == 7), PENALTY, 0.0)
    side = PENALTY * dot_exact_right(state[...].reshape(256, 128), sides[4])
    return [rates[c] - count * fields[c] + side[c * 64 : c * 64 + 64] for c in range(4)]


def acoustic_local_body(mix, state, start, deriv_rows, deriv_lanes, speed, sides, out, front, rear):
    rates = rate_local(state, deriv_rows, deriv_lanes, speed, sides)
    for c in range(4):
        value = state[c] + TIME_STEP * rates[c]
        if mix[0] != 0.0:
            value = mix[0] * start[c] + mix[1] * value
        out[c] = value
    faces_out(state, rear, front)
    lift(out, front, rear, sides, TIME_STEP * mix[1] * PENALTY)


def acoustic_start_body(given, _, state, message_a, message_b, turned, stored):
    count = given.shape[0]
    for e in range(count):
        for t in range(4):
            stored[t, 4 * e : 4 * e + 4] = given[e, :, t * 128 : t * 128 + 128]
    for t in range(4):
        rows = [stored[t, pl.ds(c, count, stride=4), :] for c in range(4)]
        rows = jnp.concatenate(rows + [jnp.zeros((128 - 4 * count, 128), F32)], 0)
        turned[t * 128 : t * 128 + 128] = rows.T
    lane = lax.broadcasted_iota(jnp.int32, (64, 128), 1) // count
    fields = [jnp.zeros((64, 128), F32)] * 4
    for z in range(8):
        piece = turned[pl.ds(z, 64, stride=8), :]
        for c in range(4):
            move = (z - c) * count % 128
            fields[c] = jnp.where(lane == z, pltpu.roll(piece, move, 1) if move else piece, fields[c])
    for c in range(4):
        state[c] = fields[c]
    faces_sent(is_odd("fz"), state, message_a, message_b)


def natural_order(state, out, turned, stored):
    count = out.shape[0]
    lane = lax.broadcasted_iota(jnp.int32, (64, 128), 1) // count
    for z in range(8):
        value = jnp.zeros((64, 128), F32)
        for c in range(4):
            move = (c - z) * count % 128
            value = jnp.where(lane == c, pltpu.roll(state[c], move, 1) if move else state[c], value)
        turned[pl.ds(z, 64, stride=8), :] = value
    for t in range(4):
        rows = turned[t * 128 : t * 128 + 128].T
        for c in range(4):
            stored[t, pl.ds(c, count, stride=4), :] = rows[c * count : c * count + count]
    for e in range(count):
        for t in range(4):
            out[e, :, t * 128 : t * 128 + 128] = stored[t, 4 * e : 4 * e + 4]


def remote_part(out, before, after, sides_far, factor):
    lift(out, before, after, sides_far, factor)
    lane = lax.broadcasted_iota(jnp.int32, (32, 128), 1) // 16
    last, first = before[64:96], after[64:96]
    pieces = []
    for j in range(8):
        left = pltpu.roll(last, 128 - j * 16, 1) if j else last
        right = pltpu.roll(first, (144 - j * 16) % 128, 1) if j != 1 else first
        pieces.append(jnp.where(lane == 0, left, jnp.where(lane == 1, right, 0.0)))
    value = factor * dot_exact_right(jnp.concatenate(pieces, 0), sides_far[4])
    for c in range(4):
        out[c] += value[c * 64 : c * 64 + 64]


def acoustic_far_body(mix, kind, partial, got_a, got_b, sides_far, received, *refs):
    if kind == "last":
        given_out, before, after, out, turned, stored = refs
    elif kind == "first":
        _, out, message_a, message_b, before, after, source = refs
        place_body(received, source)
        received = source
    else:
        out, message_a, message_b, before, after = refs
    odd = is_odd("fz")
    after[...], before[...] = paired(odd, got_a[...], got_b[...])
    out[0] = partial[0]
    for c in range(3):
        out[1 + c] = partial[1 + c] + (TIME_STEP * mix[1]) * received[c]
    remote_part(out, before, after, sides_far, TIME_STEP * mix[1] * PENALTY)
    if kind == "last":
        natural_order(out, given_out, turned, stored)
    else:
        faces_sent(odd, out, message_a, message_b)


def place_body(received, *outs):
    peers, size = received.shape[0], received.shape[1]
    fold = 192 * len(outs) // (size - 8)
    height = 64 // fold
    target = lax.broadcasted_iota(jnp.int32, (128, 128), 0)
    lane = lax.broadcasted_iota(jnp.int32, (128, 128), 1)
    total = None
    for peer in range(peers):
        label = received[peer, size - 8 : size - 7, :]
        label = jnp.broadcast_to(label, (128, 128)).astype(jnp.int32)
        hit = (label == target % 16) & (lane % 8 == target // 16)
        chosen = [jnp.where(hit & (lane // (128 // fold) == g), 1.0, 0.0) for g in range(fold)]
        chosen = jnp.concatenate(chosen, 0).astype(BF16)
        high, low = parts(received[peer, 0 : size - 8])
        dims = (((1,), (1,)), ((), ()))
        value = lax.dot_general(high, chosen, dims, preferred_element_type=F32)
        value = value + lax.dot_general(low, chosen, dims, preferred_element_type=F32)
        total = value if total is None else total + value
    for k, out in enumerate(outs):
        for c in range(3):
            for g in range(fold):
                at = (k * 3 + c) * height
                out[c, g * height : g * height + height] = total[at : at + height, g * 128 : g * 128 + 128]


def kron_part(matrix, shape, rows_by, columns_by):
    row = lax.broadcasted_iota(jnp.int32, (shape[0], 8), 0)
    level = lax.broadcasted_iota(jnp.int32, (shape[0], 8), 1)
    left = (row // rows_by % 8 == level).astype(F32)
    level = lax.broadcasted_iota(jnp.int32, (8, shape[1]), 0)
    column = lax.broadcasted_iota(jnp.int32, (8, shape[1]), 1)
    right = (column // columns_by % 8 == level).astype(F32)
    return dot_full(dot_full(left, matrix), right)


def tables_body(
    packed,
    faces,
    faces_out,
    near,
    far,
    deriv_rows,
    deriv_lanes,
    pair,
    spread,
    labels,
    speed,
):
    faces_out[...] = faces[...]
    size = near.shape[1]
    count = size // 8
    blocks = spread.shape[0] // 8

    def place_of(shape):
        return (lax.broadcasted_iota(jnp.int32, shape, 0), lax.broadcasted_iota(jnp.int32, shape, 1))

    row, column = place_of((count, size))
    repeat = (column % count == row).astype(F32)
    speed[...] = dot_full(packed[24:25, 0:count], repeat)
    wanted = dot_full(packed[16:24, 0:count], repeat).astype(jnp.int32)
    row, column = place_of((size, size))
    level, element = row // count, row % count
    level_out = column // count
    for facet in range(4):
        shift = -count if facet % 2 == 0 else count
        choice = jnp.broadcast_to(wanted[facet : facet + 1], (size, size))
        near[facet] = jnp.where((level == level_out) & (element == choice), 1.0, 0.0).astype(BF16)
        far[facet] = jnp.where((level == level_out) & (element + shift == choice), 1.0, 0.0).astype(BF16)
    lower = jnp.broadcast_to(wanted[4:5], (size, size))
    upper = jnp.broadcast_to(wanted[5:6], (size, size))
    hit = (level == 7) & (level_out == 0) & (element == lower)
    hit = hit | ((level == 0) & (level_out == 7) & (element == upper))
    near[4] = jnp.where(hit, 1.0, 0.0).astype(BF16)
    hit = (level == 0) & (level_out == 0) & (element - count == lower)
    hit = hit | ((level == 1) & (level_out == 7) & (element + count == upper))
    far[4] = jnp.where(hit, 1.0, 0.0).astype(BF16)

    row, column = place_of((64, 64))
    slopes, modes = packed[0:8, 0:8], packed[8:16, 0:8]
    outer = kron_part(slopes, (64, 64), 8, 8)
    inner = kron_part(slopes, (64, 64), 1, 1)
    deriv_rows[0:64] = jnp.where(row % 8 == column % 8, outer, 0.0)
    deriv_rows[64:128] = jnp.where(row // 8 == column // 8, inner, 0.0)
    row, column = place_of((size, size))
    lanes = kron_part(slopes.T, (size, size), count, count)
    deriv_lanes[...] = jnp.where(row % count == column % count, lanes, 0.0)
    pair[...] = kron_part(modes, (64, 64), 8, 8) * kron_part(modes, (64, 64), 1, 1)

    peers = labels.shape[0]
    capacity = capacity_of(peers, blocks)
    row, column = place_of((blocks, blocks))

    def upright(values):
        return jnp.sum(jnp.where(row == column, values, 0.0), 1, keepdims=True)

    owner_row = packed[25:26, 0:blocks]
    owner_column = upright(owner_row)
    earlier = (owner_column == owner_row) & (column < row)
    position = jnp.sum(jnp.where(earlier, 1.0, 0.0), 1, keepdims=True)
    slot = owner_column * capacity + position
    element_column = upright(packed[26:27, 0:blocks])
    row, column = place_of((8 * blocks, blocks))
    repeat = (row // 8 == column).astype(F32)
    slot = dot_full(repeat, jnp.broadcast_to(slot, (blocks, 128)))
    element = dot_full(repeat, jnp.broadcast_to(element_column, (blocks, 128)))
    row, column = place_of((8 * blocks, 128))
    values = kron_part(modes.T, (8 * blocks, 128), 1, 1)
    inside = column % (8 * capacity) // 8
    for peer in range(peers):
        chosen = slot == (inside + peer * capacity).astype(F32)
        spread[:, peer * 128 : peer * 128 + 128] = jnp.where(chosen, values, 0.0)
        named = jnp.where(chosen & (row % 8 == 0), element + 1.0, 0.0)
        labels[peer] = jnp.broadcast_to(jnp.sum(named, 0, keepdims=True) - 1.0, (8, 128))


def shifted(sizes, shifts):
    pairs = []
    for index in np.ndindex(*sizes):
        source = [(i + s) % n for i, s, n in zip(index, shifts, sizes)]
        pairs.append((int(np.ravel_multi_index(source, sizes)), int(np.ravel_multi_index(index, sizes))))
    return pairs


def partners(sizes, axis, second, shift_x=0):
    pairs = []
    for index in np.ndindex(*sizes):
        source = list(index)
        step = 1 if (index[axis] % 2 == 0) != second else -1
        source[axis] = (index[axis] + step) % sizes[axis]
        if shift_x:
            source[0] = (index[0] + shift_x) % sizes[0]
        pairs.append((int(np.ravel_multi_index(source, sizes)), int(np.ravel_multi_index(index, sizes))))
    return pairs


def per_device(
    density,
    velocity,
    pressure,
    acoustic,
    sound_speed,
    derivative,
    mode_basis,
    neighbours,
    block_owner,
    block_element,
):
    size_x, size_y, size_z = lax.axis_size("fx"), lax.axis_size("fy"), lax.axis_size("fz")
    devices = size_x * size_y * size_z
    cells_x = density.shape[0]
    elements = acoustic.shape[0]
    device = lax.axis_index(("fx", "fy", "fz"))

    names = ("fx", "fy", "fz")

    rows = 5 * cells_x * 8
    tiles = -(-rows // 128)
    square = velocity[0] * velocity[0] + velocity[1] * velocity[1] + velocity[2] * velocity[2]
    energy = pressure / (HEAT_RATIO - 1.0) + 0.5 * density * square
    rest = ((0, 0), (0, 0), (0, 0))
    state = jnp.pad(density[None], ((0, 4),) + rest) + jnp.pad(density * velocity, ((1, 1),) + rest)
    state = state + jnp.pad(energy[None], ((4, 0),) + rest)
    flow_a, flow_b = call(pack_start_body, [(tiles * 8, 128), (tiles * 8, 128)], state)
    edge_a = lax.ppermute(flow_a, "fz", partners((size_z,), 0, False))
    edge_b = lax.ppermute(flow_b, "fz", partners((size_z,), 0, True))

    near_pairs = [(i ^ 1, i) for i in range(devices)]
    far_pairs = [pair for i in range(1, devices - 1, 2) for pair in ((i, i + 1), (i + 1, i))]

    def traces(to_a, to_b):
        far_got = lax.ppermute(to_b, names, far_pairs)
        return lax.ppermute(to_a, names, near_pairs), far_got

    size = 8 * elements
    held = (4, 64, size)
    faces = (96, size)
    sides = [pltpu.VMEM(faces, F32)] * 2
    turning = [pltpu.VMEM((512, 128), F32), pltpu.VMEM((4, 4 * elements, 128), F32)]
    sound, to_a, to_b = call(
        acoustic_start_body,
        [held, faces, faces],
        acoustic,
        edge_a,
        scratch=turning,
        last=1,
    )
    got_a = lax.ppermute(to_a, names, near_pairs)

    six = 2 * HALO
    edge_rows = 5 * 8
    shapes = [
        (edge_rows, 128),
        (5 * six * 8 + edge_rows, 128),
        (5 * cells_x * HALO + edge_rows, 128),
        (5 * cells_x * HALO + edge_rows, 128),
        (32 + edge_rows, 128),
        (32 + edge_rows, 128),
    ]
    edge, along_x, y_a, y_b, xy_a, xy_b = call(
        pack_next_body, shapes, state, flow_a, flow_b, edge_a, edge_b, got_a, last=1
    )
    flat = (size_x, size_y)
    steps = [[(1, 0), (-1, 0)]] if size_x == 2 else [[(1, 0)], [(-1, 0)]]
    places, messages = [], []
    for first, second, spots in [(y_a, y_b, [(0, 0)])] + [(xy_a, xy_b, spots) for spots in steps]:
        shift = spots[0][0]
        for kept, side in ((first, False), (second, True)):
            messages.append(lax.ppermute(kept, ("fx", "fy"), partners(flat, 1, side, shift)))
            places.append(tuple((dx, 1) for dx, _ in spots))
    for spots in steps:
        messages.append(lax.ppermute(along_x, ("fx", "fy"), shifted(flat, spots[0])))
        places.append(tuple(spots))

    local = (neighbours - device * elements).T
    blocks = block_owner.size
    width = max(elements, blocks)

    def piece(values, first):
        values = values.astype(F32)
        return jnp.pad(values, ((first, 32 - first - values.shape[0]), (0, width - values.shape[1])))

    packed = (
        piece(derivative, 0)
        + piece(mode_basis, 8)
        + piece(local, 16)
        + piece(sound_speed.reshape(1, elements), 24)
        + piece(block_owner.reshape(1, blocks), 25)
        + piece(block_element.reshape(1, blocks), 26)
    )
    table = jax.ShapeDtypeStruct((5, size, size), BF16)
    to_b, near, far, deriv_rows, deriv_lanes, pair, spread, labels, speed = call(
        tables_body,
        [
            faces,
            table,
            table,
            (128, 64),
            (size, size),
            (64, 64),
            (8 * blocks, size_y * 128),
            (size_y, 8, 128),
            (1, size),
        ],
        packed,
        to_b,
    )
    got_b = lax.ppermute(to_b, names, far_pairs)

    fold = fold_of(size_y, blocks)
    wide = cells_x + 2 * HALO
    rows_scratch = pltpu.VMEM((3, 64, 128), F32)

    def planes(count):
        return (5, count, 16, 128)

    def route(send):
        return lax.all_to_all(send, "fy", split_axis=0, concat_axis=0, tiled=True)

    spare = [pltpu.VMEM(shapes[2], F32)] * 2 + [pltpu.VMEM(shapes[4], F32)] * (2 * len(steps))
    start, rim, send = call(
        functools.partial(flow_sources_body, tuple(places)),
        [planes(wide), (5, 16, 256), (size_y, 192 // fold + 8, 128)],
        state,
        edge,
        *messages,
        pair,
        spread,
        labels,
        scratch=[
            pltpu.VMEM((3, wide, 16, 128), F32),
            rows_scratch,
            pltpu.VMEM((2, cells_x, 8, 128), F32),
        ]
        + spare,
    )
    received = route(send)
    flow_state, send = call(
        flow_stages_body,
        [(5, cells_x, 8, 128), (size_y, 2 * 192 // fold + 8, 128)],
        start,
        rim,
        pair,
        spread,
        labels,
        got_b,
        last=1,
        scratch=[
            pltpu.VMEM(planes(wide), F32),
            rows_scratch,
            pltpu.VMEM(planes(wide - 2), F32),
            pltpu.VMEM(planes(wide - 2), F32),
            pltpu.VMEM(planes(wide - 4), F32),
        ],
    )

    def local_part(mix, now):
        return call(
            functools.partial(acoustic_local_body, mix),
            [held],
            now,
            sound,
            deriv_rows,
            deriv_lanes,
            speed,
            near,
            scratch=sides,
        )[0]

    partial = local_part(MIXES[0], sound)
    sound_one, to_a, to_b = call(
        functools.partial(acoustic_far_body, MIXES[0], "first"),
        [held, faces, faces],
        partial,
        got_a,
        got_b,
        far,
        received,
        send,
        scratch=sides + [rows_scratch],
        last=1,
    )
    source_two, source_three = call(place_body, [(3, 64, 128)] * 2, route(send))
    got_a, got_b = traces(to_a, to_b)
    partial = local_part(MIXES[1], sound_one)
    sound_two, to_a, to_b = call(
        functools.partial(acoustic_far_body, MIXES[1], "second"),
        [held, faces, faces],
        partial,
        got_a,
        got_b,
        far,
        source_two,
        scratch=sides,
    )
    got_a, got_b = traces(to_a, to_b)
    partial = local_part(MIXES[2], sound_two)
    sound_state = call(
        functools.partial(acoustic_far_body, MIXES[2], "last"),
        [(elements, 4, 512)],
        partial,
        got_a,
        got_b,
        far,
        source_three,
        scratch=sides + [pltpu.VMEM(held, F32)] + turning,
    )[0]
    return (flow_state, sound_state)


def solution(mesh):
    placed = (
        P("fx", "fy", "fz"),
        P(None, "fx", "fy", "fz"),
        P("fx", "fy", "fz"),
        P(("fx", "fy", "fz"), None, None),
        P(("fx", "fy", "fz")),
        P(),
        P(),
        P(("fx", "fy", "fz"), None),
        P("fx", "fy", "fz", None, None),
        P("fx", "fy", "fz", None),
    )
    return jax.shard_map(
        per_device,
        mesh=mesh,
        in_specs=placed,
        out_specs=(P(None, "fx", "fy", "fz"), P(("fx", "fy", "fz"), None, None)),
        check_vma=False,
    )
```

```python
import functools

import jax
import jax.numpy as jnp
import numpy as np
from jax import lax
from jax.experimental import pallas as pl
from jax.experimental.pallas import tpu as pltpu
from jax.sharding import PartitionSpec as P

HEAT_RATIO = 1.4
TIME_STEP = 0.1
VISCOSITY = 0.05
PENALTY = 0.5
HALO = 3
F32 = jnp.float32
BF16 = jnp.bfloat16
PARAMS = pltpu.CompilerParams(vmem_limit_bytes=24 * 1024 * 1024)
MIXES = ((0.0, 1.0), (0.75, 0.25), (1.0 / 3.0, 2.0 / 3.0))


def parts(values):
    high = values.astype(BF16)
    return high, (values - high.astype(F32)).astype(BF16)


def dot(left, right):
    return lax.dot_general(left, right, (((1,), (0,)), ((), ())), preferred_element_type=F32)


def dot_three(left, right):
    left_high, left_low = parts(left)
    right_high, right_low = parts(right)
    return dot(left_high, right_high) + dot(left_high, right_low) + dot(left_low, right_high)


def dot_full(left, right, dims=((1,), (0,))):
    return lax.dot_general(
        left, right, (dims, ((), ())), precision=lax.Precision.HIGHEST, preferred_element_type=F32
    )


def dot_exact_right(left, right):
    left_high, left_low = parts(left)
    return dot(left_high, right) + dot(left_low, right)


def call(body, outs, *operands, scratch=(), fetch=False, last=0):
    whole = pl.BlockSpec(memory_space=pltpu.VMEM)
    outs = [out if isinstance(out, jax.ShapeDtypeStruct) else jax.ShapeDtypeStruct(out, F32) for out in outs]
    scratch = list(scratch)
    anywhere = pl.BlockSpec(memory_space=pltpu.HBM)
    specs = [anywhere if fetch else whole] * (len(operands) - last) + [anywhere] * last
    kernel = body
    if fetch:
        count = len(operands)
        total = count + len(outs)

        def kernel(*refs):
            held, sems = refs[total : total + count], refs[total + count]
            copies = [
                pltpu.make_async_copy(refs[i], held[i], sems.at[i]) for i in range(count)
            ]
            for copy in copies:
                copy.start()
            for copy in copies:
                copy.wait()
            body(*held, *refs[count:total], *refs[total + count + 1 :])

        scratch = [pltpu.VMEM(o.shape, o.dtype) for o in operands] + [pltpu.SemaphoreType.DMA((count,))] + scratch
    return pl.pallas_call(
        kernel,
        out_shape=outs,
        in_specs=specs,
        out_specs=[whole] * len(outs),
        scratch_shapes=scratch,
        compiler_params=PARAMS,
    )(*operands)


def capacity_of(peers, blocks):
    return max(2, 2 * blocks // peers)


def fold_of(peers, blocks):
    return 128 // (8 * capacity_of(peers, blocks))


def is_odd(axis):
    return lax.axis_index(axis) % 2 == 1


def paired(odd, to_next, to_last):
    return jnp.where(odd, to_last, to_next), jnp.where(odd, to_next, to_last)


def pack_start_body(state, message_a, message_b):
    odd = is_odd("fz")
    rows = state[...].reshape(-1, 128)
    count = rows.shape[0]
    for tile in range(message_a.shape[0] // 8):
        piece = rows[tile * 128 : min(count, tile * 128 + 128)]
        if piece.shape[0] < 128:
            piece = jnp.concatenate([piece, jnp.zeros((128 - piece.shape[0], 128), F32)], 0)
        turned = piece.T
        first, second = paired(odd, turned[120:128], turned[0:8])
        message_a[tile * 8 : tile * 8 + 8] = first
        message_b[tile * 8 : tile * 8 + 8] = second


def pack_next_body(
    state, sent_a, sent_b, got_a, got_b, _, edge, along_x, y_a, y_b, xy_a, xy_b
):
    cells_x = state.shape[1]
    odd_z, odd = is_odd("fz"), is_odd("fy")
    high, low = paired(odd_z, sent_a[...], sent_b[...])
    above, below = paired(odd_z, got_a[...], got_b[...])
    row = lax.broadcasted_iota(jnp.int32, (8, 128), 0)
    x_of_lane = lax.broadcasted_iota(jnp.int32, (16, 128), 1) // 8 % cells_x
    for tile in range(high.shape[0] // 8):
        rows = slice(tile * 8, tile * 8 + 8)
        upper = jnp.where(row < 3, pltpu.roll(high[rows], 3, 0), pltpu.roll(above[rows], 3, 0))
        lower = jnp.where(row < 3, pltpu.roll(below[rows], 3, 0), pltpu.roll(low[rows], 3, 0))
        slots = jnp.concatenate([upper, lower], 0)
        spread = jnp.concatenate([jnp.where(x_of_lane == x, slots, 0.0) for x in range(8)], 0).T
        for half in range(16 // cells_x):
            f = tile * (16 // cells_x) + half
            if f < 5:
                at = half * cells_x * 8
                total = spread[at : at + 8]
                for x in range(1, cells_x):
                    total = total + spread[at + x * 8 : at + x * 8 + 8]
                edge[f * 8 : f * 8 + 8] = total
    planes = [cells_x - HALO + i for i in range(HALO)] + list(range(HALO))
    for f in range(5):
        for s, x in enumerate(planes):
            at = (f * len(planes) + s) * 8
            along_x[at : at + 8] = state[f, x]
        for x in range(cells_x):
            at = (f * cells_x + x) * HALO
            first, second = paired(odd, state[f, x, 8 - HALO : 8], state[f, x, 0:HALO])
            y_a[at : at + HALO] = first
            y_b[at : at + HALO] = second
        at = f * 6
        for slot, height in ((1, 1), (2, 2), (3, 2), (4, 1)):
            x = planes[slot]
            first, second = paired(odd, state[f, x, 8 - height : 8], state[f, x, 0:height])
            xy_a[at : at + height] = first
            xy_b[at : at + height] = second
            at += height
    for message in (along_x, y_a, y_b, xy_a, xy_b):
        size = message.shape[0]
        message[size - 40 : size] = edge[...]


def assemble(wide, rim, state, edge, beside, cells_x):
    for dx, dy, message in beside:
        if dx == 0:
            columns = [(HALO + x, x) for x in range(cells_x)]
        elif dx < 0:
            columns = [(i, i) for i in range(HALO)]
        else:
            columns = [(HALO + cells_x + i, HALO + i) for i in range(HALO)]
        for f in range(5):
            for plane, slot in columns:
                height = 8 if dy == 0 else HALO
                at = (f * (cells_x if dx == 0 else 2 * HALO) + slot) * height
                if dx != 0 and dy != 0:
                    if slot in (0, 5):
                        continue
                    height = (0, 1, 2, 2, 1)[slot]
                    at = f * 6 + (0, 0, 1, 3, 5)[slot]
                low, high = {0: (0, 8), 1: (8, 8 + height), -1: (16 - height, 16)}[dy]
                wide[f, plane, low:high] = message[at : at + height]
    edges = {(dx, dy): message for dx, dy, message in beside}
    edges[0, 0] = edge
    row = lax.broadcasted_iota(jnp.int32, (8, 128), 0)
    lane = lax.broadcasted_iota(jnp.int32, (8, 128), 1)

    def part(f, dx, dy):
        message = edges[dx, dy]
        at = message.shape[0] - 40 + f * 8
        return message[at : at + 8]

    def beyond(f, dy):
        if edges[1, dy] is edges[-1, dy]:
            return part(f, 1, dy)
        return jnp.where(lane < 64, part(f, 1, dy), part(f, -1, dy))

    for f in range(5):
        for x in range(cells_x):
            wide[f, HALO + x, 0:8] = state[f, x]
        rim[f, 0:8, 0:128] = part(f, 0, 0)
        rim[f, 0:8, 128:256] = beyond(f, 0)
        rim[f, 8:16, 0:128] = jnp.where(row < 4, part(f, 0, 1), part(f, 0, -1))
        rim[f, 8:16, 128:256] = jnp.where(row < 4, beyond(f, 1), beyond(f, -1))


def primitive(rho, mx, my, mz, energy):
    inverse = 1.0 / rho
    u, v, w = mx * inverse, my * inverse, mz * inverse
    p = (HEAT_RATIO - 1.0) * (energy - 0.5 * (mx * u + my * v + mz * w))
    return u, v, w, p, jnp.sqrt(HEAT_RATIO * jnp.abs(p) * inverse)


def chunks(first, last, size):
    return [(i, min(i + size, last)) for i in range(first, last, size)]


def derive_planes(wide, derived, first, last):
    for i, j in chunks(first, last, 4):
        for k, value in enumerate(primitive(*[wide[f, i:j] for f in range(5)])):
            derived[k, i:j] = value


def derive_speeds(wide, derived, first, last):
    for i, j in chunks(first, last, 5):
        inverse = 1.0 / wide[0, i:j]
        for k in range(3):
            derived[k, i:j] = wide[1 + k, i:j] * inverse


def with_flux(fields, other, along):
    speed, p = other[along], other[3]
    out = [fields[1 + along]]
    for k in range(3):
        value = fields[1 + k] * speed
        out.append(value + p if k == along else value)
    out.append((fields[4] + p) * speed)
    return fields, out, jnp.abs(speed) + other[4]


def face(left, right):
    (fields_l, flux_l, speed_l), (fields_r, flux_r, speed_r) = left, right
    speed = jnp.maximum(speed_l, speed_r)
    viscous = speed + 2.0 * VISCOSITY
    return [
        (flux_l[f] + flux_r[f]) - (viscous if 1 <= f <= 3 else speed) * (fields_r[f] - fields_l[f])
        for f in range(5)
    ]


def rolled(here, shift, axis):
    fields, flux, speed = here
    return (
        [pltpu.roll(a, shift, axis) for a in fields],
        [pltpu.roll(a, shift, axis) for a in flux],
        pltpu.roll(speed, shift, axis),
    )


def rim_section(fields, start, mix):
    other = primitive(*fields)
    here = with_flux(fields, other, 2)
    along_z = face(here, rolled(here, 255, 1))
    if mix is None:
        return other, along_z, None
    total = [g - pltpu.roll(g, 1, 1) for g in along_z]
    for along, step, axis, size in ((0, 16, 1, 256), (1, 1, 0, 16)):
        here = with_flux(fields, other, along)
        faces = face(here, rolled(here, size - step, axis))
        total = [total[f] + (faces[f] - pltpu.roll(faces[f], step, axis)) for f in range(5)]
    out = []
    for f in range(5):
        value = fields[f] - (0.5 * TIME_STEP) * total[f]
        out.append(mix[0] * start[f] + mix[1] * value if mix[0] != 0.0 else value)
    return other, along_z, out


def to_ends(values, after, rows, first, last, ends):
    slot = lax.broadcasted_iota(jnp.int32, (rows, 256), 1) % 16
    for f, value in enumerate(values):
        value = value[0:rows]
        value = jnp.where(slot == 9, pltpu.roll(value, 9 - after, 1), value)
        for x in range(first, last):
            at = x % 16 // 8 * 128
            move = (118 - x % 8 * 16) % 128
            tile = value[:, at : at + 128]
            ends[f, x - first, 0:rows] = pltpu.roll(tile, move, 1) if move else tile


def flow_rate_section(wide, derived, ends, start, offset, mix, write, inner=False):
    depth = wide.shape[1]
    rows = slice(0, 8) if inner else slice(None)
    size = 4 if inner else 2

    def planes(i, j, kept, along):
        fields = [wide[f, i:j, kept] for f in range(5)]
        return with_flux(fields, [derived[f, i:j, kept] for f in range(5)], along)

    def cut(here, i, j):
        return [a[i:j] for a in here[0]], [a[i:j] for a in here[1]], here[2][i:j]

    for i, j in chunks(1, depth - 1, size):
        count = j - i
        lane = lax.broadcasted_iota(jnp.int32, (count, 8 if inner else 16, 128), 2)
        here = planes(i - 1, j + 1, rows, 0)
        faces = face(cut(here, 0, count + 1), cut(here, 1, count + 2))
        total = [g[1:] - g[:-1] for g in faces]
        here = planes(i, j, slice(None), 1)
        faces = face(here, rolled(here, 15, 1))
        for f in range(5):
            change = faces[f] - pltpu.roll(faces[f], 1, 1)
            total[f] = total[f] + (change[:, 0:8] if inner else change)
        here = planes(i, j, rows, 2)
        faces = face(here, rolled(here, 127, 2))
        for f in range(5):
            end = ends[f, i - 1 : j - 1, rows]
            value = jnp.where(lane == 127, end, faces[f])
            total[f] = total[f] + (value - jnp.where(lane == 0, end, pltpu.roll(value, 1, 2)))
        for f in range(5):
            value = wide[f, i:j, rows] - (0.5 * TIME_STEP) * total[f]
            if mix[0] != 0.0:
                value = mix[0] * start[f, i + offset : j + offset, rows] + mix[1] * value
            write(slice(i - 1, j - 1), f, value)


def lamb(derived, ends, first, cells_x, lamb_rows):
    for i, j in chunks(first, first + cells_x, 4):
        count = j - i
        lane = lax.broadcasted_iota(jnp.int32, (count, 8, 128), 2)
        vel = [derived[c, i:j, 0:8] for c in range(3)]
        along_x = [derived[c, i + 1 : j + 1, 0:8] - derived[c, i - 1 : j - 1, 0:8] for c in range(3)]
        along_y = []
        for c in range(3):
            column = derived[c, i:j]
            along_y.append((pltpu.roll(column, 15, 1) - pltpu.roll(column, 1, 1))[:, 0:8])
        along_z = []
        for c in range(2):
            end = ends[c, i - first : j - first, 0:8]
            after = jnp.where(lane == 127, end, pltpu.roll(vel[c], 127, 2))
            along_z.append(after - jnp.where(lane == 0, end, pltpu.roll(vel[c], 1, 2)))
        curl = [
            0.5 * (along_y[2] - along_z[1]),
            0.5 * (along_z[0] - along_x[2]),
            0.5 * (along_x[1] - along_y[0]),
        ]
        at = slice((i - first) * 8, (j - first) * 8)
        lamb_rows[0, at] = (curl[1] * vel[2] - curl[2] * vel[1]).reshape(count * 8, 128)
        lamb_rows[1, at] = (curl[2] * vel[0] - curl[0] * vel[2]).reshape(count * 8, 128)
        lamb_rows[2, at] = (curl[0] * vel[1] - curl[1] * vel[0]).reshape(count * 8, 128)


def project(lamb_rows, pair, spread, send, base):
    peers = send.shape[0]
    fold = fold_of(peers, spread.shape[0] // 8)
    height = 64 // fold
    group = lax.broadcasted_iota(jnp.int32, (height, 128), 1) // (128 // fold)
    modes = dot_three(pair[...], jnp.concatenate([lamb_rows[c] for c in range(3)], 1))
    modes = jnp.concatenate([modes[:, c * 128 : c * 128 + 128] for c in range(3)], 0)
    sent = dot_three(modes, spread[...])
    for c in range(3):
        for peer in range(peers):
            mine = sent[c * 64 : c * 64 + 64, peer * 128 : peer * 128 + 128]
            folded = mine[0:height]
            for g in range(1, fold):
                folded = jnp.where(group == g, mine[g * height : g * height + height], folded)
            send[peer, base + c * height : base + c * height + height] = folded


def flow_sources_body(places, *refs):
    state, edge = refs[0:2]
    messages = refs[2 : 2 + len(places)]
    pair, spread, labels, _ = refs[2 + len(places) : 6 + len(places)]
    wide, rim, send, derived, lamb_rows, ends = refs[6 + len(places) : 12 + len(places)]
    spare = refs[12 + len(places) :]
    cells_x = state.shape[1]
    odd = is_odd("fy")
    beside, k = [], 0
    while k < len(places):
        if places[k][0][1] == 0:
            beside.extend((dx, 0, messages[k]) for dx, _ in places[k])
            k += 1
            continue
        above, below = spare[:2]
        spare = spare[2:]
        above[...], below[...] = paired(odd, messages[k][...], messages[k + 1][...])
        beside.extend((dx, 1, above) for dx, _ in places[k])
        beside.extend((dx, -1, below) for dx, _ in places[k])
        k += 2
    assemble(wide, rim, state, edge, beside, cells_x)
    derive_speeds(wide, derived, HALO - 1, HALO + cells_x + 1)
    inverse = 1.0 / rim[0, 0:8]
    to_ends([rim[1, 0:8] * inverse, rim[2, 0:8] * inverse], 3, 8, 0, cells_x, ends)
    lamb(derived, ends, HALO, cells_x, lamb_rows)
    project(lamb_rows, pair, spread, send, 0)
    send[:, send.shape[1] - 8 :] = labels[...]


def writer(target):
    def write(i, f, value):
        target[f, i] = value

    return write


def flow_stages_body(wide, rim, pair, spread, labels, second, derived, ends_out, send, lamb_rows, ends, first):
    planes = wide.shape[1]
    cells_x = planes - 2 * HALO
    size = (send.shape[1] - 8) // 2
    rim_start = [rim[f] for f in range(5)]
    derive_planes(wide, derived, 0, planes)
    _, along_z, rim_first = rim_section(rim_start, None, MIXES[0])
    to_ends(along_z, 2, 16, -2, cells_x + 2, ends)
    flow_rate_section(wide, derived, ends, wide, 0, MIXES[0], writer(first))
    derive_planes(first, derived, 0, planes - 2)
    other, along_z, rim_second = rim_section(rim_first, [rim[f] for f in range(5)], MIXES[1])
    to_ends(other[0:2], 3, 8, 0, cells_x, ends)
    lamb(derived, ends, 2, cells_x, lamb_rows)
    project(lamb_rows, pair, spread, send, 0)
    to_ends(along_z, 2, 16, -1, cells_x + 1, ends)
    flow_rate_section(first, derived, ends, wide, 1, MIXES[1], writer(second))
    derive_planes(second, derived, 0, planes - 4)
    other, along_z, _ = rim_section(rim_second, None, None)
    to_ends(other[0:2], 3, 8, 0, cells_x, ends)
    lamb(derived, ends, 1, cells_x, lamb_rows)
    project(lamb_rows, pair, spread, send, size)
    send[:, 2 * size :] = labels[...]
    to_ends(along_z, 2, 8, 0, cells_x, ends_out)


def flow_last_body(second, derived, ends, wide, out):
    flow_rate_section(second, derived, ends, wide, 2, MIXES[2], writer(out), inner=True)


def faces_out(state, rear, front):
    lane = lax.broadcasted_iota(jnp.int32, (32, 128), 1) // 16
    for c in range(4):
        front[c * 8 : c * 8 + 8] = state[c, 56:64]
        rear[c * 8 : c * 8 + 8] = state[c, 0:8]
        front[32 + c * 8 : 40 + c * 8] = state[c, pl.ds(7, 8, stride=8), :]
        rear[32 + c * 8 : 40 + c * 8] = state[c, pl.ds(0, 8, stride=8), :]
    rows = state[...].reshape(256, 128)
    last = jnp.zeros((32, 128), F32)
    first = jnp.zeros((32, 128), F32)
    for j in range(8):
        piece = rows[j * 32 : j * 32 + 32]
        last = jnp.where(lane == j, pltpu.roll(piece, (j * 16 + 16) % 128, 1), last)
        first = jnp.where(lane == j, pltpu.roll(piece, j * 16, 1) if j else piece, first)
    front[64:96] = last
    rear[64:96] = first


def faces_sent(odd, state, message_a, message_b):
    faces_out(state, message_b, message_a)
    message_a[...], message_b[...] = paired(odd, message_a[...], message_b[...])


def lift(total, before, after, sides, factor):
    def place(face, rows, target):
        value = factor * dot_exact_right(rows, sides[face])
        for c in range(4):
            total[c, target, :] += value[c * 8 : c * 8 + 8]

    place(0, before[0:32], pl.ds(0, 8))
    place(1, after[0:32], pl.ds(56, 8))
    place(2, before[32:64], pl.ds(0, 8, stride=8))
    place(3, after[32:64], pl.ds(7, 8, stride=8))


def rate_local(state, deriv_rows, deriv_lanes, speed, sides):
    fields = [state[c] for c in range(4)]
    by_rows = dot_three(deriv_rows[...], jnp.concatenate(fields[0:3], 1))
    by_lanes = dot_three(jnp.concatenate([fields[0], fields[3]], 0), deriv_lanes[...])
    divergence = by_rows[0:64, 128:256] + by_rows[64:128, 256:384] + by_lanes[64:128]
    rates = [
        -(speed[...] * speed[...]) * divergence,
        -by_rows[0:64, 0:128],
        -by_rows[64:128, 0:128],
        -by_lanes[0:64],
    ]
    row = lax.broadcasted_iota(jnp.int32, (64, 128), 0)
    lane = lax.broadcasted_iota(jnp.int32, (64, 128), 1)
    count = jnp.zeros((64, 128), F32)
    for value in (row // 8, row % 8, lane // 16):
        count = count + jnp.where((value == 0) | (value == 7), PENALTY, 0.0)
    side = PENALTY * dot_exact_right(state[...].reshape(256, 128), sides[4])
    return [rates[c] - count * fields[c] + side[c * 64 : c * 64 + 64] for c in range(4)]


def acoustic_local_body(mix, state, start, deriv_rows, deriv_lanes, speed, sides, out, front, rear):
    rates = rate_local(state, deriv_rows, deriv_lanes, speed, sides)
    for c in range(4):
        value = state[c] + TIME_STEP * rates[c]
        if mix[0] != 0.0:
            value = mix[0] * start[c] + mix[1] * value
        out[c] = value
    faces_out(state, rear, front)
    lift(out, front, rear, sides, TIME_STEP * mix[1] * PENALTY)


def acoustic_start_body(given, _, state, message_a, message_b, turned, stored):
    count = given.shape[0]
    for e in range(count):
        for t in range(4):
            stored[t, 4 * e : 4 * e + 4] = given[e, :, t * 128 : t * 128 + 128]
    for t in range(4):
        rows = [stored[t, pl.ds(c, count, stride=4), :] for c in range(4)]
        rows = jnp.concatenate(rows + [jnp.zeros((128 - 4 * count, 128), F32)], 0)
        turned[t * 128 : t * 128 + 128] = rows.T
    lane = lax.broadcasted_iota(jnp.int32, (64, 128), 1) // count
    fields = [jnp.zeros((64, 128), F32)] * 4
    for z in range(8):
        piece = turned[pl.ds(z, 64, stride=8), :]
        for c in range(4):
            move = (z - c) * count % 128
            fields[c] = jnp.where(lane == z, pltpu.roll(piece, move, 1) if move else piece, fields[c])
    for c in range(4):
        state[c] = fields[c]
    faces_sent(is_odd("fz"), state, message_a, message_b)


def natural_order(state, out, turned, stored):
    count = out.shape[0]
    lane = lax.broadcasted_iota(jnp.int32, (64, 128), 1) // count
    for z in range(8):
        value = jnp.zeros((64, 128), F32)
        for c in range(4):
            move = (c - z) * count % 128
            value = jnp.where(lane == c, pltpu.roll(state[c], move, 1) if move else state[c], value)
        turned[pl.ds(z, 64, stride=8), :] = value
    for t in range(4):
        rows = turned[t * 128 : t * 128 + 128].T
        for c in range(4):
            stored[t, pl.ds(c, count, stride=4), :] = rows[c * count : c * count + count]
    for e in range(count):
        for t in range(4):
            out[e, :, t * 128 : t * 128 + 128] = stored[t, 4 * e : 4 * e + 4]


def remote_part(out, before, after, sides_far, factor):
    lift(out, before, after, sides_far, factor)
    lane = lax.broadcasted_iota(jnp.int32, (32, 128), 1) // 16
    last, first = before[64:96], after[64:96]
    pieces = []
    for j in range(8):
        left = pltpu.roll(last, 128 - j * 16, 1) if j else last
        right = pltpu.roll(first, (144 - j * 16) % 128, 1) if j != 1 else first
        pieces.append(jnp.where(lane == 0, left, jnp.where(lane == 1, right, 0.0)))
    value = factor * dot_exact_right(jnp.concatenate(pieces, 0), sides_far[4])
    for c in range(4):
        out[c] += value[c * 64 : c * 64 + 64]


def acoustic_far_body(mix, kind, partial, got_a, got_b, sides_far, received, *refs):
    if kind == "last":
        given_out, before, after, out, turned, stored = refs
    elif kind == "first":
        _, out, message_a, message_b, before, after, source = refs
        place_body(received, source)
        received = source
    else:
        out, message_a, message_b, before, after = refs
    odd = is_odd("fz")
    after[...], before[...] = paired(odd, got_a[...], got_b[...])
    out[0] = partial[0]
    for c in range(3):
        out[1 + c] = partial[1 + c] + (TIME_STEP * mix[1]) * received[c]
    remote_part(out, before, after, sides_far, TIME_STEP * mix[1] * PENALTY)
    if kind == "last":
        natural_order(out, given_out, turned, stored)
    else:
        faces_sent(odd, out, message_a, message_b)


def place_body(received, *outs):
    peers, size = received.shape[0], received.shape[1]
    fold = 192 * len(outs) // (size - 8)
    height = 64 // fold
    target = lax.broadcasted_iota(jnp.int32, (128, 128), 0)
    lane = lax.broadcasted_iota(jnp.int32, (128, 128), 1)
    total = None
    for peer in range(peers):
        label = received[peer, size - 8 : size - 7, :]
        label = jnp.broadcast_to(label, (128, 128)).astype(jnp.int32)
        hit = (label == target % 16) & (lane % 8 == target // 16)
        chosen = [jnp.where(hit & (lane // (128 // fold) == g), 1.0, 0.0) for g in range(fold)]
        chosen = jnp.concatenate(chosen, 0).astype(BF16)
        high, low = parts(received[peer, 0 : size - 8])
        dims = (((1,), (1,)), ((), ()))
        value = lax.dot_general(high, chosen, dims, preferred_element_type=F32)
        value = value + lax.dot_general(low, chosen, dims, preferred_element_type=F32)
        total = value if total is None else total + value
    for k, out in enumerate(outs):
        for c in range(3):
            for g in range(fold):
                at = (k * 3 + c) * height
                out[c, g * height : g * height + height] = total[at : at + height, g * 128 : g * 128 + 128]


def kron_part(matrix, shape, rows_by, columns_by):
    row = lax.broadcasted_iota(jnp.int32, (shape[0], 8), 0)
    level = lax.broadcasted_iota(jnp.int32, (shape[0], 8), 1)
    left = (row // rows_by % 8 == level).astype(F32)
    level = lax.broadcasted_iota(jnp.int32, (8, shape[1]), 0)
    column = lax.broadcasted_iota(jnp.int32, (8, shape[1]), 1)
    right = (column // columns_by % 8 == level).astype(F32)
    return dot_full(dot_full(left, matrix), right)


def tables_body(
    packed,
    near,
    far,
    deriv_rows,
    deriv_lanes,
    pair,
    spread,
    labels,
    speed,
):
    size = near.shape[1]
    count = size // 8
    blocks = spread.shape[0] // 8

    def place_of(shape):
        return (lax.broadcasted_iota(jnp.int32, shape, 0), lax.broadcasted_iota(jnp.int32, shape, 1))

    row, column = place_of((count, size))
    repeat = (column % count == row).astype(F32)
    speed[...] = dot_full(packed[24:25, 0:count], repeat)
    wanted = dot_full(packed[16:24, 0:count], repeat).astype(jnp.int32)
    row, column = place_of((size, size))
    level, element = row // count, row % count
    level_out = column // count
    for facet in range(4):
        shift = -count if facet % 2 == 0 else count
        choice = jnp.broadcast_to(wanted[facet : facet + 1], (size, size))
        near[facet] = jnp.where((level == level_out) & (element == choice), 1.0, 0.0).astype(BF16)
        far[facet] = jnp.where((level == level_out) & (element + shift == choice), 1.0, 0.0).astype(BF16)
    lower = jnp.broadcast_to(wanted[4:5], (size, size))
    upper = jnp.broadcast_to(wanted[5:6], (size, size))
    hit = (level == 7) & (level_out == 0) & (element == lower)
    hit = hit | ((level == 0) & (level_out == 7) & (element == upper))
    near[4] = jnp.where(hit, 1.0, 0.0).astype(BF16)
    hit = (level == 0) & (level_out == 0) & (element - count == lower)
    hit = hit | ((level == 1) & (level_out == 7) & (element + count == upper))
    far[4] = jnp.where(hit, 1.0, 0.0).astype(BF16)

    row, column = place_of((64, 64))
    slopes, modes = packed[0:8, 0:8], packed[8:16, 0:8]
    outer = kron_part(slopes, (64, 64), 8, 8)
    inner = kron_part(slopes, (64, 64), 1, 1)
    deriv_rows[0:64] = jnp.where(row % 8 == column % 8, outer, 0.0)
    deriv_rows[64:128] = jnp.where(row // 8 == column // 8, inner, 0.0)
    row, column = place_of((size, size))
    lanes = kron_part(slopes.T, (size, size), count, count)
    deriv_lanes[...] = jnp.where(row % count == column % count, lanes, 0.0)
    pair[...] = kron_part(modes, (64, 64), 8, 8) * kron_part(modes, (64, 64), 1, 1)

    peers = labels.shape[0]
    capacity = capacity_of(peers, blocks)
    row, column = place_of((blocks, blocks))

    def upright(values):
        return jnp.sum(jnp.where(row == column, values, 0.0), 1, keepdims=True)

    owner_row = packed[25:26, 0:blocks]
    owner_column = upright(owner_row)
    earlier = (owner_column == owner_row) & (column < row)
    position = jnp.sum(jnp.where(earlier, 1.0, 0.0), 1, keepdims=True)
    slot = owner_column * capacity + position
    element_column = upright(packed[26:27, 0:blocks])
    row, column = place_of((8 * blocks, blocks))
    repeat = (row // 8 == column).astype(F32)
    slot = dot_full(repeat, jnp.broadcast_to(slot, (blocks, 128)))
    element = dot_full(repeat, jnp.broadcast_to(element_column, (blocks, 128)))
    row, column = place_of((8 * blocks, 128))
    values = kron_part(modes.T, (8 * blocks, 128), 1, 1)
    inside = column % (8 * capacity) // 8
    for peer in range(peers):
        chosen = slot == (inside + peer * capacity).astype(F32)
        spread[:, peer * 128 : peer * 128 + 128] = jnp.where(chosen, values, 0.0)
        named = jnp.where(chosen & (row % 8 == 0), element + 1.0, 0.0)
        labels[peer] = jnp.broadcast_to(jnp.sum(named, 0, keepdims=True) - 1.0, (8, 128))


def shifted(sizes, shifts):
    pairs = []
    for index in np.ndindex(*sizes):
        source = [(i + s) % n for i, s, n in zip(index, shifts, sizes)]
        pairs.append((int(np.ravel_multi_index(source, sizes)), int(np.ravel_multi_index(index, sizes))))
    return pairs


def partners(sizes, axis, second, shift_x=0):
    pairs = []
    for index in np.ndindex(*sizes):
        source = list(index)
        step = 1 if (index[axis] % 2 == 0) != second else -1
        source[axis] = (index[axis] + step) % sizes[axis]
        if shift_x:
            source[0] = (index[0] + shift_x) % sizes[0]
        pairs.append((int(np.ravel_multi_index(source, sizes)), int(np.ravel_multi_index(index, sizes))))
    return pairs


def per_device(
    density,
    velocity,
    pressure,
    acoustic,
    sound_speed,
    derivative,
    mode_basis,
    neighbours,
    block_owner,
    block_element,
):
    size_x, size_y, size_z = lax.axis_size("fx"), lax.axis_size("fy"), lax.axis_size("fz")
    devices = size_x * size_y * size_z
    cells_x = density.shape[0]
    elements = acoustic.shape[0]
    device = lax.axis_index(("fx", "fy", "fz"))

    names = ("fx", "fy", "fz")

    rows = 5 * cells_x * 8
    tiles = -(-rows // 128)
    square = velocity[0] * velocity[0] + velocity[1] * velocity[1] + velocity[2] * velocity[2]
    energy = pressure / (HEAT_RATIO - 1.0) + 0.5 * density * square
    rest = ((0, 0), (0, 0), (0, 0))
    state = jnp.pad(density[None], ((0, 4),) + rest) + jnp.pad(density * velocity, ((1, 1),) + rest)
    state = state + jnp.pad(energy[None], ((4, 0),) + rest)
    flow_a, flow_b = call(pack_start_body, [(tiles * 8, 128), (tiles * 8, 128)], state)
    edge_a = lax.ppermute(flow_a, "fz", partners((size_z,), 0, False))
    edge_b = lax.ppermute(flow_b, "fz", partners((size_z,), 0, True))

    near_pairs = [(i ^ 1, i) for i in range(devices)]
    far_pairs = [pair for i in range(1, devices - 1, 2) for pair in ((i, i + 1), (i + 1, i))]

    def traces(to_a, to_b):
        far_got = lax.ppermute(to_b, names, far_pairs)
        return lax.ppermute(to_a, names, near_pairs), far_got

    size = 8 * elements
    held = (4, 64, size)
    faces = (96, size)
    sides = [pltpu.VMEM(faces, F32)] * 2
    turning = [pltpu.VMEM((512, 128), F32), pltpu.VMEM((4, 4 * elements, 128), F32)]
    sound, to_a, to_b = call(
        acoustic_start_body,
        [held, faces, faces],
        acoustic,
        edge_a,
        scratch=turning,
        last=1,
    )
    got_a, got_b = traces(to_a, to_b)

    six = 2 * HALO
    edge_rows = 5 * 8
    shapes = [
        (edge_rows, 128),
        (5 * six * 8 + edge_rows, 128),
        (5 * cells_x * HALO + edge_rows, 128),
        (5 * cells_x * HALO + edge_rows, 128),
        (32 + edge_rows, 128),
        (32 + edge_rows, 128),
    ]
    edge, along_x, y_a, y_b, xy_a, xy_b = call(
        pack_next_body, shapes, state, flow_a, flow_b, edge_a, edge_b, got_a, last=1
    )
    flat = (size_x, size_y)
    steps = [[(1, 0), (-1, 0)]] if size_x == 2 else [[(1, 0)], [(-1, 0)]]
    pairs = [(y_a, y_b, [(0, 0)])] + [(xy_a, xy_b, spots) for spots in steps]
    moved = {}
    for second in (True, False):
        for k in reversed(range(len(pairs))):
            kept, shift = pairs[k][1 if second else 0], pairs[k][2][0][0]
            moved[k, second] = lax.ppermute(kept, ("fx", "fy"), partners(flat, 1, second, shift))
    places, messages = [], []
    for k, (_, _, spots) in enumerate(pairs):
        for second in (False, True):
            messages.append(moved[k, second])
            places.append(tuple((dx, 1) for dx, _ in spots))
    for spots in steps:
        messages.append(lax.ppermute(along_x, ("fx", "fy"), shifted(flat, spots[0])))
        places.append(tuple(spots))

    local = (neighbours - device * elements).T
    blocks = block_owner.size
    width = max(elements, blocks)

    def piece(values, first):
        values = values.astype(F32)
        return jnp.pad(values, ((first, 32 - first - values.shape[0]), (0, width - values.shape[1])))

    packed = (
        piece(derivative, 0)
        + piece(mode_basis, 8)
        + piece(local, 16)
        + piece(sound_speed.reshape(1, elements), 24)
        + piece(block_owner.reshape(1, blocks), 25)
        + piece(block_element.reshape(1, blocks), 26)
    )
    table = jax.ShapeDtypeStruct((5, size, size), BF16)
    near, far, deriv_rows, deriv_lanes, pair, spread, labels, speed = call(
        tables_body,
        [
            table,
            table,
            (128, 64),
            (size, size),
            (64, 64),
            (8 * blocks, size_y * 128),
            (size_y, 8, 128),
            (1, size),
        ],
        packed,
    )

    fold = fold_of(size_y, blocks)
    wide = cells_x + 2 * HALO
    rows_scratch = pltpu.VMEM((3, 64, 128), F32)

    def planes(count):
        return (5, count, 16, 128)

    def route(send):
        return lax.all_to_all(send, "fy", split_axis=0, concat_axis=0, tiled=True)

    spare = [pltpu.VMEM(shapes[2], F32)] * 2 + [pltpu.VMEM(shapes[4], F32)] * (2 * len(steps))
    start, rim, send = call(
        functools.partial(flow_sources_body, tuple(places)),
        [planes(wide), (5, 16, 256), (size_y, 192 // fold + 8, 128)],
        state,
        edge,
        *messages,
        pair,
        spread,
        labels,
        got_b,
        last=1,
        scratch=[
            pltpu.VMEM((3, wide, 16, 128), F32),
            rows_scratch,
            pltpu.VMEM((2, cells_x, 8, 128), F32),
        ]
        + spare,
    )
    received = route(send)
    second, derived, ends, send = call(
        flow_stages_body,
        [
            planes(wide - 4),
            planes(wide),
            (5, cells_x, 8, 128),
            (size_y, 2 * 192 // fold + 8, 128),
        ],
        start,
        rim,
        pair,
        spread,
        labels,
        scratch=[rows_scratch, pltpu.VMEM(planes(wide - 2), F32), pltpu.VMEM(planes(wide - 2), F32)],
    )

    def local_part(mix, now):
        return call(
            functools.partial(acoustic_local_body, mix),
            [held],
            now,
            sound,
            deriv_rows,
            deriv_lanes,
            speed,
            near,
            scratch=sides,
        )[0]

    partial = local_part(MIXES[0], sound)
    sound_one, to_a, to_b = call(
        functools.partial(acoustic_far_body, MIXES[0], "first"),
        [held, faces, faces],
        partial,
        got_a,
        got_b,
        far,
        received,
        send,
        scratch=sides + [rows_scratch],
        last=1,
    )
    source_two, source_three = call(place_body, [(3, 64, 128)] * 2, route(send))
    got_a, got_b = traces(to_a, to_b)
    flow_state = call(flow_last_body, [(5, cells_x, 8, 128)], second, derived, ends, start)[0]
    partial = local_part(MIXES[1], sound_one)
    sound_two, to_a, to_b = call(
        functools.partial(acoustic_far_body, MIXES[1], "second"),
        [held, faces, faces],
        partial,
        got_a,
        got_b,
        far,
        source_two,
        scratch=sides,
    )
    got_a, got_b = traces(to_a, to_b)
    partial = local_part(MIXES[2], sound_two)
    sound_state = call(
        functools.partial(acoustic_far_body, MIXES[2], "last"),
        [(elements, 4, 512)],
        partial,
        got_a,
        got_b,
        far,
        source_three,
        scratch=sides + [pltpu.VMEM(held, F32)] + turning,
    )[0]
    return (flow_state, sound_state)


def solution(mesh):
    placed = (
        P("fx", "fy", "fz"),
        P(None, "fx", "fy", "fz"),
        P("fx", "fy", "fz"),
        P(("fx", "fy", "fz"), None, None),
        P(("fx", "fy", "fz")),
        P(),
        P(),
        P(("fx", "fy", "fz"), None),
        P("fx", "fy", "fz", None, None),
        P("fx", "fy", "fz", None),
    )
    return jax.shard_map(
        per_device,
        mesh=mesh,
        in_specs=placed,
        out_specs=(P(None, "fx", "fy", "fz"), P(("fx", "fy", "fz"), None, None)),
        check_vma=False,
    )
```

```python
import functools

import jax
import jax.numpy as jnp
import numpy as np
from jax import lax
from jax.experimental import pallas as pl
from jax.experimental.pallas import tpu as pltpu
from jax.sharding import PartitionSpec as P

HEAT_RATIO = 1.4
TIME_STEP = 0.1
VISCOSITY = 0.05
PENALTY = 0.5
HALO = 3
F32 = jnp.float32
BF16 = jnp.bfloat16
PARAMS = pltpu.CompilerParams(vmem_limit_bytes=24 * 1024 * 1024)
MIXES = ((0.0, 1.0), (0.75, 0.25), (1.0 / 3.0, 2.0 / 3.0))


def parts(values):
    high = values.astype(BF16)
    return high, (values - high.astype(F32)).astype(BF16)


def dot(left, right):
    return lax.dot_general(left, right, (((1,), (0,)), ((), ())), preferred_element_type=F32)


def dot_three(left, right):
    left_high, left_low = parts(left)
    right_high, right_low = parts(right)
    return dot(left_high, right_high) + dot(left_high, right_low) + dot(left_low, right_high)


def dot_full(left, right, dims=((1,), (0,))):
    return lax.dot_general(
        left, right, (dims, ((), ())), precision=lax.Precision.HIGHEST, preferred_element_type=F32
    )


def dot_exact_right(left, right):
    left_high, left_low = parts(left)
    return dot(left_high, right) + dot(left_low, right)


def call(body, outs, *operands, scratch=(), last=0, cost=None):
    whole = pl.BlockSpec(memory_space=pltpu.VMEM)
    outs = [out if isinstance(out, jax.ShapeDtypeStruct) else jax.ShapeDtypeStruct(out, F32) for out in outs]
    anywhere = pl.BlockSpec(memory_space=pl.ANY)
    return pl.pallas_call(
        body,
        out_shape=outs,
        in_specs=[whole] * (len(operands) - last) + [anywhere] * last,
        out_specs=[whole] * len(outs),
        scratch_shapes=list(scratch),
        compiler_params=PARAMS,
        cost_estimate=None if cost is None else pl.CostEstimate(flops=cost, bytes_accessed=cost, transcendentals=0),
    )(*operands)


def capacity_of(peers, blocks):
    return max(2, 2 * blocks // peers)


def fold_of(peers, blocks):
    return 128 // (8 * capacity_of(peers, blocks))


def is_odd(axis):
    return lax.axis_index(axis) % 2 == 1


def paired(odd, to_next, to_last):
    return jnp.where(odd, to_last, to_next), jnp.where(odd, to_next, to_last)


def pack_start_body(state, message_a, message_b):
    odd = is_odd("fz")
    rows = state[...].reshape(-1, 128)
    count = rows.shape[0]
    for tile in range(message_a.shape[0] // 8):
        piece = rows[tile * 128 : min(count, tile * 128 + 128)]
        if piece.shape[0] < 128:
            piece = jnp.concatenate([piece, jnp.zeros((128 - piece.shape[0], 128), F32)], 0)
        turned = piece.T
        first, second = paired(odd, turned[120:128], turned[0:8])
        message_a[tile * 8 : tile * 8 + 8] = first
        message_b[tile * 8 : tile * 8 + 8] = second


def pack_next_body(state, sent_a, sent_b, got_a, got_b, _, edge, along_x):
    cells_x = state.shape[1]
    odd_z = is_odd("fz")
    high, low = paired(odd_z, sent_a[...], sent_b[...])
    above, below = paired(odd_z, got_a[...], got_b[...])
    row = lax.broadcasted_iota(jnp.int32, (8, 128), 0)
    x_of_lane = lax.broadcasted_iota(jnp.int32, (16, 128), 1) // 8 % cells_x
    for tile in range(high.shape[0] // 8):
        rows = slice(tile * 8, tile * 8 + 8)
        upper = jnp.where(row < 3, pltpu.roll(high[rows], 3, 0), pltpu.roll(above[rows], 3, 0))
        lower = jnp.where(row < 3, pltpu.roll(below[rows], 3, 0), pltpu.roll(low[rows], 3, 0))
        slots = jnp.concatenate([upper, lower], 0)
        spread = jnp.concatenate([jnp.where(x_of_lane == x, slots, 0.0) for x in range(8)], 0).T
        for half in range(16 // cells_x):
            f = tile * (16 // cells_x) + half
            if f < 5:
                at = half * cells_x * 8
                total = spread[at : at + 8]
                for x in range(1, cells_x):
                    total = total + spread[at + x * 8 : at + x * 8 + 8]
                edge[f * 8 : f * 8 + 8] = total
    for f in range(5):
        for s, x in enumerate(x_planes(cells_x)):
            at = (f * 2 * HALO + s) * 8
            along_x[at : at + 8] = state[f, x]
    size = along_x.shape[0]
    along_x[size - 40 : size] = edge[...]


def x_planes(cells_x):
    return [cells_x - HALO + i for i in range(HALO)] + list(range(HALO))


def sides_of(beside_x):
    return beside_x[0], beside_x[-1]


def beyond(beside_x, f):
    after, before = sides_of(beside_x)
    at = after.shape[0] - 40 + f * 8
    if after is before:
        return after[at : at + 8]
    lane = lax.broadcasted_iota(jnp.int32, (8, 128), 1)
    return jnp.where(lane < 64, after[at : at + 8], before[at : at + 8])


def pack_last_body(state, edge, *refs):
    beside_x, (y_a, y_b) = refs[:-2], refs[-2:]
    cells_x = state.shape[1]
    odd = is_odd("fy")
    after, before = sides_of(beside_x)

    def put(at, values, height):
        first, second = paired(odd, values[8 - height : 8], values[0:height])
        y_a[at : at + height] = first
        y_b[at : at + height] = second

    lines = 5 * cells_x * HALO
    for f in range(5):
        for x in range(cells_x):
            put((f * cells_x + x) * HALO, state[f, x], HALO)
        at = lines + f * 6
        for slot, height in ((1, 1), (2, 2), (3, 2), (4, 1)):
            source = (f * 2 * HALO + slot) * 8
            put(at, (before if slot < HALO else after)[source : source + 8], height)
            at += height
        for message in (y_a, y_b):
            at = message.shape[0] - 80 + f * 8
            message[at : at + 8] = edge[f * 8 : f * 8 + 8]
            message[at + 40 : at + 48] = beyond(beside_x, f)


def assemble(wide, rim, state, edge, beside_x, above, below):
    cells_x = state.shape[1]
    after, before = sides_of(beside_x)
    lines = 5 * cells_x * HALO
    row = lax.broadcasted_iota(jnp.int32, (8, 128), 0)
    for f in range(5):
        for x in range(cells_x):
            wide[f, HALO + x, 0:8] = state[f, x]
            at = (f * cells_x + x) * HALO
            wide[f, HALO + x, 8 : 8 + HALO] = above[at : at + HALO]
            wide[f, HALO + x, 16 - HALO : 16] = below[at : at + HALO]
        for slot in range(2 * HALO):
            plane = slot if slot < HALO else cells_x + slot
            at = (f * 2 * HALO + slot) * 8
            wide[f, plane, 0:8] = (before if slot < HALO else after)[at : at + 8]
        at = lines + f * 6
        for slot, height in ((1, 1), (2, 2), (3, 2), (4, 1)):
            plane = slot if slot < HALO else cells_x + slot
            wide[f, plane, 8 : 8 + height] = above[at : at + height]
            wide[f, plane, 16 - height : 16] = below[at : at + height]
            at += height
        rim[f, 0:8, 0:128] = edge[f * 8 : f * 8 + 8]
        rim[f, 0:8, 128:256] = beyond(beside_x, f)
        at = above.shape[0] - 80 + f * 8
        rim[f, 8:16, 0:128] = jnp.where(row < 4, above[at : at + 8], below[at : at + 8])
        at += 40
        rim[f, 8:16, 128:256] = jnp.where(row < 4, above[at : at + 8], below[at : at + 8])


def primitive(rho, mx, my, mz, energy):
    inverse = 1.0 / rho
    u, v, w = mx * inverse, my * inverse, mz * inverse
    p = (HEAT_RATIO - 1.0) * (energy - 0.5 * (mx * u + my * v + mz * w))
    return u, v, w, p, jnp.sqrt(HEAT_RATIO * jnp.abs(p) * inverse)


def chunks(first, last, size):
    return [(i, min(i + size, last)) for i in range(first, last, size)]


def derive_planes(wide, derived, first, last):
    for i, j in chunks(first, last, 4):
        for k, value in enumerate(primitive(*[wide[f, i:j] for f in range(5)])):
            derived[k, i:j] = value


def derive_speeds(wide, derived, first, last):
    for i, j in chunks(first, last, 5):
        inverse = 1.0 / wide[0, i:j]
        for k in range(3):
            derived[k, i:j] = wide[1 + k, i:j] * inverse


def with_flux(fields, other, along):
    speed, p = other[along], other[3]
    out = [fields[1 + along]]
    for k in range(3):
        value = fields[1 + k] * speed
        out.append(value + p if k == along else value)
    out.append((fields[4] + p) * speed)
    return fields, out, jnp.abs(speed) + other[4]


def face(left, right):
    (fields_l, flux_l, speed_l), (fields_r, flux_r, speed_r) = left, right
    speed = jnp.maximum(speed_l, speed_r)
    viscous = speed + 2.0 * VISCOSITY
    return [
        (flux_l[f] + flux_r[f]) - (viscous if 1 <= f <= 3 else speed) * (fields_r[f] - fields_l[f])
        for f in range(5)
    ]


def rolled(here, shift, axis):
    fields, flux, speed = here
    return (
        [pltpu.roll(a, shift, axis) for a in fields],
        [pltpu.roll(a, shift, axis) for a in flux],
        pltpu.roll(speed, shift, axis),
    )


def rim_section(fields, start, mix):
    other = primitive(*fields)
    here = with_flux(fields, other, 2)
    along_z = face(here, rolled(here, 255, 1))
    if mix is None:
        return other, along_z, None
    total = [g - pltpu.roll(g, 1, 1) for g in along_z]
    for along, step, axis, size in ((0, 16, 1, 256), (1, 1, 0, 16)):
        here = with_flux(fields, other, along)
        faces = face(here, rolled(here, size - step, axis))
        total = [total[f] + (faces[f] - pltpu.roll(faces[f], step, axis)) for f in range(5)]
    out = []
    for f in range(5):
        value = fields[f] - (0.5 * TIME_STEP) * total[f]
        out.append(mix[0] * start[f] + mix[1] * value if mix[0] != 0.0 else value)
    return other, along_z, out


def to_ends(values, after, rows, first, last, ends):
    slot = lax.broadcasted_iota(jnp.int32, (rows, 256), 1) % 16
    for f, value in enumerate(values):
        value = value[0:rows]
        value = jnp.where(slot == 9, pltpu.roll(value, 9 - after, 1), value)
        for x in range(first, last):
            at = x % 16 // 8 * 128
            move = (118 - x % 8 * 16) % 128
            tile = value[:, at : at + 128]
            ends[f, x - first, 0:rows] = pltpu.roll(tile, move, 1) if move else tile


def flow_rate_section(wide, derived, ends, start, offset, mix, write, inner=False):
    depth = wide.shape[1]
    rows = slice(0, 8) if inner else slice(None)
    size = 4 if inner else 2

    def planes(i, j, kept, along):
        fields = [wide[f, i:j, kept] for f in range(5)]
        return with_flux(fields, [derived[f, i:j, kept] for f in range(5)], along)

    def cut(here, i, j):
        return [a[i:j] for a in here[0]], [a[i:j] for a in here[1]], here[2][i:j]

    for i, j in chunks(1, depth - 1, size):
        count = j - i
        lane = lax.broadcasted_iota(jnp.int32, (count, 8 if inner else 16, 128), 2)
        here = planes(i - 1, j + 1, rows, 0)
        faces = face(cut(here, 0, count + 1), cut(here, 1, count + 2))
        total = [g[1:] - g[:-1] for g in faces]
        here = planes(i, j, slice(None), 1)
        faces = face(here, rolled(here, 15, 1))
        for f in range(5):
            change = faces[f] - pltpu.roll(faces[f], 1, 1)
            total[f] = total[f] + (change[:, 0:8] if inner else change)
        here = planes(i, j, rows, 2)
        faces = face(here, rolled(here, 127, 2))
        for f in range(5):
            end = ends[f, i - 1 : j - 1, rows]
            value = jnp.where(lane == 127, end, faces[f])
            total[f] = total[f] + (value - jnp.where(lane == 0, end, pltpu.roll(value, 1, 2)))
        for f in range(5):
            value = wide[f, i:j, rows] - (0.5 * TIME_STEP) * total[f]
            if mix[0] != 0.0:
                value = mix[0] * start[f, i + offset : j + offset, rows] + mix[1] * value
            write(slice(i - 1, j - 1), f, value)


def lamb(derived, ends, first, cells_x, lamb_rows):
    for i, j in chunks(first, first + cells_x, 4):
        count = j - i
        lane = lax.broadcasted_iota(jnp.int32, (count, 8, 128), 2)
        vel = [derived[c, i:j, 0:8] for c in range(3)]
        along_x = [derived[c, i + 1 : j + 1, 0:8] - derived[c, i - 1 : j - 1, 0:8] for c in range(3)]
        along_y = []
        for c in range(3):
            column = derived[c, i:j]
            along_y.append((pltpu.roll(column, 15, 1) - pltpu.roll(column, 1, 1))[:, 0:8])
        along_z = []
        for c in range(2):
            end = ends[c, i - first : j - first, 0:8]
            after = jnp.where(lane == 127, end, pltpu.roll(vel[c], 127, 2))
            along_z.append(after - jnp.where(lane == 0, end, pltpu.roll(vel[c], 1, 2)))
        curl = [
            0.5 * (along_y[2] - along_z[1]),
            0.5 * (along_z[0] - along_x[2]),
            0.5 * (along_x[1] - along_y[0]),
        ]
        at = slice((i - first) * 8, (j - first) * 8)
        lamb_rows[0, at] = (curl[1] * vel[2] - curl[2] * vel[1]).reshape(count * 8, 128)
        lamb_rows[1, at] = (curl[2] * vel[0] - curl[0] * vel[2]).reshape(count * 8, 128)
        lamb_rows[2, at] = (curl[0] * vel[1] - curl[1] * vel[0]).reshape(count * 8, 128)


def project(lamb_rows, pair, spread, send, base):
    peers = send.shape[0]
    fold = fold_of(peers, spread.shape[0] // 8)
    height = 64 // fold
    group = lax.broadcasted_iota(jnp.int32, (height, 128), 1) // (128 // fold)
    modes = dot_three(pair[...], jnp.concatenate([lamb_rows[c] for c in range(3)], 1))
    modes = jnp.concatenate([modes[:, c * 128 : c * 128 + 128] for c in range(3)], 0)
    sent = dot_three(modes, spread[...])
    for c in range(3):
        for peer in range(peers):
            mine = sent[c * 64 : c * 64 + 64, peer * 128 : peer * 128 + 128]
            folded = mine[0:height]
            for g in range(1, fold):
                folded = jnp.where(group == g, mine[g * height : g * height + height], folded)
            send[peer, base + c * height : base + c * height + height] = folded


def flow_sources_body(count, state, edge, *refs):
    beside_x = refs[:count]
    got_a, got_b, pair, spread, labels, _ = refs[count : count + 6]
    wide, rim, send, derived, lamb_rows, ends, above, below = refs[count + 6 :]
    cells_x = state.shape[1]
    above[...], below[...] = paired(is_odd("fy"), got_a[...], got_b[...])
    assemble(wide, rim, state, edge, beside_x, above, below)
    derive_speeds(wide, derived, HALO - 1, HALO + cells_x + 1)
    inverse = 1.0 / rim[0, 0:8]
    to_ends([rim[1, 0:8] * inverse, rim[2, 0:8] * inverse], 3, 8, 0, cells_x, ends)
    lamb(derived, ends, HALO, cells_x, lamb_rows)
    project(lamb_rows, pair, spread, send, 0)
    send[:, send.shape[1] - 8 :] = labels[...]


def writer(target):
    def write(i, f, value):
        target[f, i] = value

    return write


def flow_stages_body(wide, rim, pair, spread, labels, second, derived, ends_out, send, lamb_rows, ends, first):
    planes = wide.shape[1]
    cells_x = planes - 2 * HALO
    size = (send.shape[1] - 8) // 2
    rim_start = [rim[f] for f in range(5)]
    derive_planes(wide, derived, 0, planes)
    _, along_z, rim_first = rim_section(rim_start, None, MIXES[0])
    to_ends(along_z, 2, 16, -2, cells_x + 2, ends)
    flow_rate_section(wide, derived, ends, wide, 0, MIXES[0], writer(first))
    derive_planes(first, derived, 0, planes - 2)
    other, along_z, rim_second = rim_section(rim_first, [rim[f] for f in range(5)], MIXES[1])
    to_ends(other[0:2], 3, 8, 0, cells_x, ends)
    lamb(derived, ends, 2, cells_x, lamb_rows)
    project(lamb_rows, pair, spread, send, 0)
    to_ends(along_z, 2, 16, -1, cells_x + 1, ends)
    flow_rate_section(first, derived, ends, wide, 1, MIXES[1], writer(second))
    derive_planes(second, derived, 0, planes - 4)
    other, along_z, _ = rim_section(rim_second, None, None)
    to_ends(other[0:2], 3, 8, 0, cells_x, ends)
    lamb(derived, ends, 1, cells_x, lamb_rows)
    project(lamb_rows, pair, spread, send, size)
    send[:, 2 * size :] = labels[...]
    to_ends(along_z, 2, 8, 0, cells_x, ends_out)


def flow_last_body(second, derived, ends, wide, out):
    flow_rate_section(second, derived, ends, wide, 2, MIXES[2], writer(out), inner=True)


def faces_out(state, rear, front):
    lane = lax.broadcasted_iota(jnp.int32, (32, 128), 1) // 16
    for c in range(4):
        front[c * 8 : c * 8 + 8] = state[c, 56:64]
        rear[c * 8 : c * 8 + 8] = state[c, 0:8]
        front[32 + c * 8 : 40 + c * 8] = state[c, pl.ds(7, 8, stride=8), :]
        rear[32 + c * 8 : 40 + c * 8] = state[c, pl.ds(0, 8, stride=8), :]
    rows = state[...].reshape(256, 128)
    last = jnp.zeros((32, 128), F32)
    first = jnp.zeros((32, 128), F32)
    for j in range(8):
        piece = rows[j * 32 : j * 32 + 32]
        last = jnp.where(lane == j, pltpu.roll(piece, (j * 16 + 16) % 128, 1), last)
        first = jnp.where(lane == j, pltpu.roll(piece, j * 16, 1) if j else piece, first)
    front[64:96] = last
    rear[64:96] = first


def faces_sent(odd, state, message_a, message_b):
    faces_out(state, message_b, message_a)
    message_a[...], message_b[...] = paired(odd, message_a[...], message_b[...])


def lift(total, before, after, sides, factor):
    def place(face, rows, target):
        value = factor * dot_exact_right(rows, sides[face])
        for c in range(4):
            total[c, target, :] += value[c * 8 : c * 8 + 8]

    place(0, before[0:32], pl.ds(0, 8))
    place(1, after[0:32], pl.ds(56, 8))
    place(2, before[32:64], pl.ds(0, 8, stride=8))
    place(3, after[32:64], pl.ds(7, 8, stride=8))


def rate_local(state, deriv_rows, deriv_lanes, speed, sides):
    fields = [state[c] for c in range(4)]
    by_rows = dot_three(deriv_rows[...], jnp.concatenate(fields[0:3], 1))
    by_lanes = dot_three(jnp.concatenate([fields[0], fields[3]], 0), deriv_lanes[...])
    divergence = by_rows[0:64, 128:256] + by_rows[64:128, 256:384] + by_lanes[64:128]
    rates = [
        -(speed[...] * speed[...]) * divergence,
        -by_rows[0:64, 0:128],
        -by_rows[64:128, 0:128],
        -by_lanes[0:64],
    ]
    row = lax.broadcasted_iota(jnp.int32, (64, 128), 0)
    lane = lax.broadcasted_iota(jnp.int32, (64, 128), 1)
    count = jnp.zeros((64, 128), F32)
    for value in (row // 8, row % 8, lane // 16):
        count = count + jnp.where((value == 0) | (value == 7), PENALTY, 0.0)
    side = PENALTY * dot_exact_right(state[...].reshape(256, 128), sides[4])
    return [rates[c] - count * fields[c] + side[c * 64 : c * 64 + 64] for c in range(4)]


def acoustic_local_body(mix, state, start, deriv_rows, deriv_lanes, speed, sides, out, front, rear):
    rates = rate_local(state, deriv_rows, deriv_lanes, speed, sides)
    for c in range(4):
        value = state[c] + TIME_STEP * rates[c]
        if mix[0] != 0.0:
            value = mix[0] * start[c] + mix[1] * value
        out[c] = value
    faces_out(state, rear, front)
    lift(out, front, rear, sides, TIME_STEP * mix[1] * PENALTY)


def acoustic_start_body(given, _, state, message_a, message_b, turned, stored):
    count = given.shape[0]
    for e in range(count):
        for t in range(4):
            stored[t, 4 * e : 4 * e + 4] = given[e, :, t * 128 : t * 128 + 128]
    for t in range(4):
        rows = [stored[t, pl.ds(c, count, stride=4), :] for c in range(4)]
        rows = jnp.concatenate(rows + [jnp.zeros((128 - 4 * count, 128), F32)], 0)
        turned[t * 128 : t * 128 + 128] = rows.T
    lane = lax.broadcasted_iota(jnp.int32, (64, 128), 1) // count
    fields = [jnp.zeros((64, 128), F32)] * 4
    for z in range(8):
        piece = turned[pl.ds(z, 64, stride=8), :]
        for c in range(4):
            move = (z - c) * count % 128
            fields[c] = jnp.where(lane == z, pltpu.roll(piece, move, 1) if move else piece, fields[c])
    for c in range(4):
        state[c] = fields[c]
    size = message_a.shape[0]
    faces_sent(is_odd("fz"), state, message_a, message_b.at[0:size])
    message_b[size:] = jnp.zeros((message_b.shape[0] - size, 128), F32)


def natural_order(state, out, turned, stored):
    count = out.shape[0]
    lane = lax.broadcasted_iota(jnp.int32, (64, 128), 1) // count
    for z in range(8):
        value = jnp.zeros((64, 128), F32)
        for c in range(4):
            move = (c - z) * count % 128
            value = jnp.where(lane == c, pltpu.roll(state[c], move, 1) if move else state[c], value)
        turned[pl.ds(z, 64, stride=8), :] = value
    for t in range(4):
        rows = turned[t * 128 : t * 128 + 128].T
        for c in range(4):
            stored[t, pl.ds(c, count, stride=4), :] = rows[c * count : c * count + count]
    for e in range(count):
        for t in range(4):
            out[e, :, t * 128 : t * 128 + 128] = stored[t, 4 * e : 4 * e + 4]


def remote_part(out, before, after, sides_far, factor):
    lift(out, before, after, sides_far, factor)
    lane = lax.broadcasted_iota(jnp.int32, (32, 128), 1) // 16
    last, first = before[64:96], after[64:96]
    pieces = []
    for j in range(8):
        left = pltpu.roll(last, 128 - j * 16, 1) if j else last
        right = pltpu.roll(first, (144 - j * 16) % 128, 1) if j != 1 else first
        pieces.append(jnp.where(lane == 0, left, jnp.where(lane == 1, right, 0.0)))
    value = factor * dot_exact_right(jnp.concatenate(pieces, 0), sides_far[4])
    for c in range(4):
        out[c] += value[c * 64 : c * 64 + 64]


def acoustic_far_body(mix, kind, partial, got_a, got_b, sides_far, received, *refs):
    if kind == "last":
        given_out, before, after, out, turned, stored = refs
    elif kind == "first":
        _, out, message_a, message_b, before, after, source = refs
        place_body(received, source)
        received = source
    else:
        out, message_a, message_b, before, after = refs
    odd = is_odd("fz")
    after[...], before[...] = paired(odd, got_a[0:96], got_b[0:96])
    out[0] = partial[0]
    for c in range(3):
        out[1 + c] = partial[1 + c] + (TIME_STEP * mix[1]) * received[c]
    remote_part(out, before, after, sides_far, TIME_STEP * mix[1] * PENALTY)
    if kind == "last":
        natural_order(out, given_out, turned, stored)
    else:
        faces_sent(odd, out, message_a, message_b)


def place_body(received, *outs):
    peers, size = received.shape[0], received.shape[1]
    fold = 192 * len(outs) // (size - 8)
    height = 64 // fold
    target = lax.broadcasted_iota(jnp.int32, (128, 128), 0)
    lane = lax.broadcasted_iota(jnp.int32, (128, 128), 1)
    total = None
    for peer in range(peers):
        label = received[peer, size - 8 : size - 7, :]
        label = jnp.broadcast_to(label, (128, 128)).astype(jnp.int32)
        hit = (label == target % 16) & (lane % 8 == target // 16)
        chosen = [jnp.where(hit & (lane // (128 // fold) == g), 1.0, 0.0) for g in range(fold)]
        chosen = jnp.concatenate(chosen, 0).astype(BF16)
        high, low = parts(received[peer, 0 : size - 8])
        dims = (((1,), (1,)), ((), ()))
        value = lax.dot_general(high, chosen, dims, preferred_element_type=F32)
        value = value + lax.dot_general(low, chosen, dims, preferred_element_type=F32)
        total = value if total is None else total + value
    for k, out in enumerate(outs):
        for c in range(3):
            for g in range(fold):
                at = (k * 3 + c) * height
                out[c, g * height : g * height + height] = total[at : at + height, g * 128 : g * 128 + 128]


def kron_part(matrix, shape, rows_by, columns_by):
    row = lax.broadcasted_iota(jnp.int32, (shape[0], 8), 0)
    level = lax.broadcasted_iota(jnp.int32, (shape[0], 8), 1)
    left = (row // rows_by % 8 == level).astype(F32)
    level = lax.broadcasted_iota(jnp.int32, (8, shape[1]), 0)
    column = lax.broadcasted_iota(jnp.int32, (8, shape[1]), 1)
    right = (column // columns_by % 8 == level).astype(F32)
    return dot_full(dot_full(left, matrix), right)


def tables_body(
    packed,
    near,
    far,
    deriv_rows,
    deriv_lanes,
    pair,
    spread,
    labels,
    speed,
):
    size = near.shape[1]
    count = size // 8
    blocks = spread.shape[0] // 8

    def place_of(shape):
        return (lax.broadcasted_iota(jnp.int32, shape, 0), lax.broadcasted_iota(jnp.int32, shape, 1))

    row, column = place_of((count, size))
    repeat = (column % count == row).astype(F32)
    speed[...] = dot_full(packed[24:25, 0:count], repeat)
    wanted = dot_full(packed[16:24, 0:count], repeat).astype(jnp.int32)
    row, column = place_of((size, size))
    level, element = row // count, row % count
    level_out = column // count
    for facet in range(4):
        shift = -count if facet % 2 == 0 else count
        choice = jnp.broadcast_to(wanted[facet : facet + 1], (size, size))
        near[facet] = jnp.where((level == level_out) & (element == choice), 1.0, 0.0).astype(BF16)
        far[facet] = jnp.where((level == level_out) & (element + shift == choice), 1.0, 0.0).astype(BF16)
    lower = jnp.broadcast_to(wanted[4:5], (size, size))
    upper = jnp.broadcast_to(wanted[5:6], (size, size))
    hit = (level == 7) & (level_out == 0) & (element == lower)
    hit = hit | ((level == 0) & (level_out == 7) & (element == upper))
    near[4] = jnp.where(hit, 1.0, 0.0).astype(BF16)
    hit = (level == 0) & (level_out == 0) & (element - count == lower)
    hit = hit | ((level == 1) & (level_out == 7) & (element + count == upper))
    far[4] = jnp.where(hit, 1.0, 0.0).astype(BF16)

    row, column = place_of((64, 64))
    slopes, modes = packed[0:8, 0:8], packed[8:16, 0:8]
    outer = kron_part(slopes, (64, 64), 8, 8)
    inner = kron_part(slopes, (64, 64), 1, 1)
    deriv_rows[0:64] = jnp.where(row % 8 == column % 8, outer, 0.0)
    deriv_rows[64:128] = jnp.where(row // 8 == column // 8, inner, 0.0)
    row, column = place_of((size, size))
    lanes = kron_part(slopes.T, (size, size), count, count)
    deriv_lanes[...] = jnp.where(row % count == column % count, lanes, 0.0)
    pair[...] = kron_part(modes, (64, 64), 8, 8) * kron_part(modes, (64, 64), 1, 1)

    peers = labels.shape[0]
    capacity = capacity_of(peers, blocks)
    row, column = place_of((blocks, blocks))

    def upright(values):
        return jnp.sum(jnp.where(row == column, values, 0.0), 1, keepdims=True)

    owner_row = packed[25:26, 0:blocks]
    owner_column = upright(owner_row)
    earlier = (owner_column == owner_row) & (column < row)
    position = jnp.sum(jnp.where(earlier, 1.0, 0.0), 1, keepdims=True)
    slot = owner_column * capacity + position
    element_column = upright(packed[26:27, 0:blocks])
    row, column = place_of((8 * blocks, blocks))
    repeat = (row // 8 == column).astype(F32)
    slot = dot_full(repeat, jnp.broadcast_to(slot, (blocks, 128)))
    element = dot_full(repeat, jnp.broadcast_to(element_column, (blocks, 128)))
    row, column = place_of((8 * blocks, 128))
    values = kron_part(modes.T, (8 * blocks, 128), 1, 1)
    inside = column % (8 * capacity) // 8
    for peer in range(peers):
        chosen = slot == (inside + peer * capacity).astype(F32)
        spread[:, peer * 128 : peer * 128 + 128] = jnp.where(chosen, values, 0.0)
        named = jnp.where(chosen & (row % 8 == 0), element + 1.0, 0.0)
        labels[peer] = jnp.broadcast_to(jnp.sum(named, 0, keepdims=True) - 1.0, (8, 128))


def shifted(sizes, shifts):
    pairs = []
    for index in np.ndindex(*sizes):
        source = [(i + s) % n for i, s, n in zip(index, shifts, sizes)]
        pairs.append((int(np.ravel_multi_index(source, sizes)), int(np.ravel_multi_index(index, sizes))))
    return pairs


def partners(sizes, axis, second):
    pairs = []
    for index in np.ndindex(*sizes):
        source = list(index)
        step = 1 if (index[axis] % 2 == 0) != second else -1
        source[axis] = (index[axis] + step) % sizes[axis]
        pairs.append((int(np.ravel_multi_index(source, sizes)), int(np.ravel_multi_index(index, sizes))))
    return pairs


def per_device(
    density,
    velocity,
    pressure,
    acoustic,
    sound_speed,
    derivative,
    mode_basis,
    neighbours,
    block_owner,
    block_element,
):
    size_x, size_y, size_z = lax.axis_size("fx"), lax.axis_size("fy"), lax.axis_size("fz")
    devices = size_x * size_y * size_z
    cells_x = density.shape[0]
    elements = acoustic.shape[0]
    device = lax.axis_index(("fx", "fy", "fz"))

    names = ("fx", "fy", "fz")

    rows = 5 * cells_x * 8
    tiles = -(-rows // 128)
    square = velocity[0] * velocity[0] + velocity[1] * velocity[1] + velocity[2] * velocity[2]
    energy = pressure / (HEAT_RATIO - 1.0) + 0.5 * density * square
    rest = ((0, 0), (0, 0), (0, 0))
    state = jnp.pad(density[None], ((0, 4),) + rest) + jnp.pad(density * velocity, ((1, 1),) + rest)
    state = state + jnp.pad(energy[None], ((4, 0),) + rest)
    flow_a, flow_b = call(pack_start_body, [(tiles * 8, 128), (tiles * 8, 128)], state)
    edge_a = lax.ppermute(flow_a, "fz", partners((size_z,), 0, False))
    edge_b = lax.ppermute(flow_b, "fz", partners((size_z,), 0, True))

    near_pairs = [(i ^ 1, i) for i in range(devices)]
    far_pairs = [pair for i in range(1, devices - 1, 2) for pair in ((i, i + 1), (i + 1, i))]

    def traces(to_a, to_b):
        far_got = lax.ppermute(to_b, names, far_pairs)
        return lax.ppermute(to_a, names, near_pairs), far_got

    size = 8 * elements
    held = (4, 64, size)
    faces = (96, size)
    sides = [pltpu.VMEM(faces, F32)] * 2
    turning = [pltpu.VMEM((512, 128), F32), pltpu.VMEM((4, 4 * elements, 128), F32)]
    sound, to_a, to_b = call(
        acoustic_start_body,
        [held, faces, (3 * faces[0], size)],
        acoustic,
        edge_a,
        scratch=turning,
        last=1,
    )
    got_a, got_b = traces(to_a, to_b)

    edge, along_x = call(
        pack_next_body,
        [(40, 128), (5 * 2 * HALO * 8 + 40, 128)],
        state,
        flow_a,
        flow_b,
        edge_a,
        edge_b,
        got_a,
        last=1,
    )
    beside_x = [
        lax.ppermute(along_x, "fx", shifted((size_x,), (step,))) for step in ((1,) if size_x == 2 else (1, -1))
    ]
    y_shape = (5 * cells_x * HALO + 32 + 80, 128)
    y_a, y_b = call(pack_last_body, [y_shape, y_shape], state, edge, *beside_x, cost=1)
    y_second = lax.ppermute(y_b, "fy", partners((size_y,), 0, True))
    y_first = lax.ppermute(y_a, "fy", partners((size_y,), 0, False))

    local = (neighbours - device * elements).T
    blocks = block_owner.size
    width = max(elements, blocks)

    def piece(values, first):
        values = values.astype(F32)
        return jnp.pad(values, ((first, 32 - first - values.shape[0]), (0, width - values.shape[1])))

    packed = (
        piece(derivative, 0)
        + piece(mode_basis, 8)
        + piece(local, 16)
        + piece(sound_speed.reshape(1, elements), 24)
        + piece(block_owner.reshape(1, blocks), 25)
        + piece(block_element.reshape(1, blocks), 26)
    )
    table = jax.ShapeDtypeStruct((5, size, size), BF16)
    near, far, deriv_rows, deriv_lanes, pair, spread, labels, speed = call(
        tables_body,
        [
            table,
            table,
            (128, 64),
            (size, size),
            (64, 64),
            (8 * blocks, size_y * 128),
            (size_y, 8, 128),
            (1, size),
        ],
        packed,
        cost=1,
    )

    fold = fold_of(size_y, blocks)
    wide = cells_x + 2 * HALO
    rows_scratch = pltpu.VMEM((3, 64, 128), F32)

    def planes(count):
        return (5, count, 16, 128)

    def route(send):
        return lax.all_to_all(send, "fy", split_axis=0, concat_axis=0, tiled=True)

    start, rim, send = call(
        functools.partial(flow_sources_body, len(beside_x)),
        [planes(wide), (5, 16, 256), (size_y, 192 // fold + 8, 128)],
        state,
        edge,
        *beside_x,
        y_first,
        y_second,
        pair,
        spread,
        labels,
        got_b,
        last=1,
        scratch=[
            pltpu.VMEM((3, wide, 16, 128), F32),
            rows_scratch,
            pltpu.VMEM((2, cells_x, 8, 128), F32),
            pltpu.VMEM(y_shape, F32),
            pltpu.VMEM(y_shape, F32),
        ],
    )
    received = route(send)
    second, derived, ends, send = call(
        flow_stages_body,
        [
            planes(wide - 4),
            planes(wide),
            (5, cells_x, 8, 128),
            (size_y, 2 * 192 // fold + 8, 128),
        ],
        start,
        rim,
        pair,
        spread,
        labels,
        scratch=[rows_scratch, pltpu.VMEM(planes(wide - 2), F32), pltpu.VMEM(planes(wide - 2), F32)],
    )

    def local_part(mix, now):
        return call(
            functools.partial(acoustic_local_body, mix),
            [held],
            now,
            sound,
            deriv_rows,
            deriv_lanes,
            speed,
            near,
            scratch=sides,
            cost=1,
        )[0]

    partial = local_part(MIXES[0], sound)
    sound_one, to_a, to_b = call(
        functools.partial(acoustic_far_body, MIXES[0], "first"),
        [held, faces, faces],
        partial,
        got_a,
        got_b,
        far,
        received,
        send,
        scratch=sides + [rows_scratch],
        last=1,
    )
    source_two, source_three = call(place_body, [(3, 64, 128)] * 2, route(send))
    got_a, got_b = traces(to_a, to_b)
    flow_state = call(flow_last_body, [(5, cells_x, 8, 128)], second, derived, ends, start)[0]
    partial = local_part(MIXES[1], sound_one)
    sound_two, to_a, to_b = call(
        functools.partial(acoustic_far_body, MIXES[1], "second"),
        [held, faces, faces],
        partial,
        got_a,
        got_b,
        far,
        source_two,
        scratch=sides,
    )
    got_a, got_b = traces(to_a, to_b)
    partial = local_part(MIXES[2], sound_two)
    sound_state = call(
        functools.partial(acoustic_far_body, MIXES[2], "last"),
        [(elements, 4, 512)],
        partial,
        got_a,
        got_b,
        far,
        source_three,
        scratch=sides + [pltpu.VMEM(held, F32)] + turning,
    )[0]
    return (flow_state, sound_state)


def solution(mesh):
    placed = (
        P("fx", "fy", "fz"),
        P(None, "fx", "fy", "fz"),
        P("fx", "fy", "fz"),
        P(("fx", "fy", "fz"), None, None),
        P(("fx", "fy", "fz")),
        P(),
        P(),
        P(("fx", "fy", "fz"), None),
        P("fx", "fy", "fz", None, None),
        P("fx", "fy", "fz", None),
    )
    return jax.shard_map(
        per_device,
        mesh=mesh,
        in_specs=placed,
        out_specs=(P(None, "fx", "fy", "fz"), P(("fx", "fy", "fz"), None, None)),
        check_vma=False,
    )
```

```python
import functools

import jax
import jax.numpy as jnp
import numpy as np
from jax import lax
from jax.experimental import pallas as pl
from jax.experimental.pallas import tpu as pltpu
from jax.sharding import PartitionSpec as P

HEAT_RATIO = 1.4
TIME_STEP = 0.1
VISCOSITY = 0.05
PENALTY = 0.5
HALO = 3
F32 = jnp.float32
BF16 = jnp.bfloat16
PARAMS = pltpu.CompilerParams(vmem_limit_bytes=24 * 1024 * 1024)
MIXES = ((0.0, 1.0), (0.75, 0.25), (1.0 / 3.0, 2.0 / 3.0))


def parts(values):
    high = values.astype(BF16)
    return high, (values - high.astype(F32)).astype(BF16)


def dot(left, right):
    return lax.dot_general(left, right, (((1,), (0,)), ((), ())), preferred_element_type=F32)


def dot_three(left, right):
    left_high, left_low = parts(left)
    right_high, right_low = parts(right)
    return dot(left_high, right_high) + dot(left_high, right_low) + dot(left_low, right_high)


def dot_full(left, right, dims=((1,), (0,))):
    return lax.dot_general(
        left, right, (dims, ((), ())), precision=lax.Precision.HIGHEST, preferred_element_type=F32
    )


def dot_exact_right(left, right):
    left_high, left_low = parts(left)
    return dot(left_high, right) + dot(left_low, right)


def call(body, outs, *operands, scratch=(), last=0, cost=None):
    whole = pl.BlockSpec(memory_space=pltpu.VMEM)
    outs = [out if isinstance(out, jax.ShapeDtypeStruct) else jax.ShapeDtypeStruct(out, F32) for out in outs]
    anywhere = pl.BlockSpec(memory_space=pl.ANY)
    return pl.pallas_call(
        body,
        out_shape=outs,
        in_specs=[whole] * (len(operands) - last) + [anywhere] * last,
        out_specs=[whole] * len(outs),
        scratch_shapes=list(scratch),
        compiler_params=PARAMS,
        cost_estimate=None if cost is None else pl.CostEstimate(flops=cost, bytes_accessed=cost, transcendentals=0),
    )(*operands)


def capacity_of(peers, blocks):
    return max(2, 2 * blocks // peers)


def fold_of(peers, blocks):
    return 128 // (8 * capacity_of(peers, blocks))


def is_odd(axis):
    return lax.axis_index(axis) % 2 == 1


def paired(odd, to_next, to_last):
    return jnp.where(odd, to_last, to_next), jnp.where(odd, to_next, to_last)


def pack_start_body(state, message_a, message_b):
    odd = is_odd("fz")
    rows = state[...].reshape(-1, 128)
    count = rows.shape[0]
    for tile in range(message_a.shape[0] // 8):
        piece = rows[tile * 128 : min(count, tile * 128 + 128)]
        if piece.shape[0] < 128:
            piece = jnp.concatenate([piece, jnp.zeros((128 - piece.shape[0], 128), F32)], 0)
        turned = piece.T
        first, second = paired(odd, turned[120:128], turned[0:8])
        message_a[tile * 8 : tile * 8 + 8] = first
        message_b[tile * 8 : tile * 8 + 8] = second


def pack_next_body(state, sent_a, sent_b, got_a, got_b, _, edge, along_x):
    cells_x = state.shape[1]
    odd_z = is_odd("fz")
    high, low = paired(odd_z, sent_a[...], sent_b[...])
    above, below = paired(odd_z, got_a[...], got_b[...])
    row = lax.broadcasted_iota(jnp.int32, (8, 128), 0)
    x_of_lane = lax.broadcasted_iota(jnp.int32, (16, 128), 1) // 8 % cells_x
    for tile in range(high.shape[0] // 8):
        rows = slice(tile * 8, tile * 8 + 8)
        upper = jnp.where(row < 3, pltpu.roll(high[rows], 3, 0), pltpu.roll(above[rows], 3, 0))
        lower = jnp.where(row < 3, pltpu.roll(below[rows], 3, 0), pltpu.roll(low[rows], 3, 0))
        slots = jnp.concatenate([upper, lower], 0)
        spread = jnp.concatenate([jnp.where(x_of_lane == x, slots, 0.0) for x in range(8)], 0).T
        for half in range(16 // cells_x):
            f = tile * (16 // cells_x) + half
            if f < 5:
                at = half * cells_x * 8
                total = spread[at : at + 8]
                for x in range(1, cells_x):
                    total = total + spread[at + x * 8 : at + x * 8 + 8]
                edge[f * 8 : f * 8 + 8] = total
    for f in range(5):
        for s, x in enumerate(x_planes(cells_x)):
            at = (f * 2 * HALO + s) * 8
            along_x[at : at + 8] = state[f, x]
    size = along_x.shape[0]
    along_x[size - 40 : size] = edge[...]


def x_planes(cells_x):
    return [cells_x - HALO + i for i in range(HALO)] + list(range(HALO))


def sides_of(beside_x):
    return beside_x[0], beside_x[-1]


def beyond(beside_x, f):
    after, before = sides_of(beside_x)
    at = after.shape[0] - 40 + f * 8
    if after is before:
        return after[at : at + 8]
    lane = lax.broadcasted_iota(jnp.int32, (8, 128), 1)
    return jnp.where(lane < 64, after[at : at + 8], before[at : at + 8])


def pack_last_body(state, edge, *refs):
    beside_x, (y_a, y_b) = refs[:-2], refs[-2:]
    cells_x = state.shape[1]
    odd = is_odd("fy")
    after, before = sides_of(beside_x)

    def put(at, values, height):
        first, second = paired(odd, values[8 - height : 8], values[0:height])
        y_a[at : at + height] = first
        y_b[at : at + height] = second

    lines = 5 * cells_x * HALO
    for f in range(5):
        for x in range(cells_x):
            put((f * cells_x + x) * HALO, state[f, x], HALO)
        at = lines + f * 6
        for slot, height in ((1, 1), (2, 2), (3, 2), (4, 1)):
            source = (f * 2 * HALO + slot) * 8
            put(at, (before if slot < HALO else after)[source : source + 8], height)
            at += height
        put(lines + 30 + f * 2, edge[f * 8 : f * 8 + 8], 2)
        put(lines + 40 + f, beyond(beside_x, f), 1)


def assemble(wide, rim, state, edge, beside_x, above, below):
    cells_x = state.shape[1]
    after, before = sides_of(beside_x)
    lines = 5 * cells_x * HALO
    for f in range(5):
        for x in range(cells_x):
            wide[f, HALO + x, 0:8] = state[f, x]
            at = (f * cells_x + x) * HALO
            wide[f, HALO + x, 8 : 8 + HALO] = above[at : at + HALO]
            wide[f, HALO + x, 16 - HALO : 16] = below[at : at + HALO]
        for slot in range(2 * HALO):
            plane = slot if slot < HALO else cells_x + slot
            at = (f * 2 * HALO + slot) * 8
            wide[f, plane, 0:8] = (before if slot < HALO else after)[at : at + 8]
        at = lines + f * 6
        for slot, height in ((1, 1), (2, 2), (3, 2), (4, 1)):
            plane = slot if slot < HALO else cells_x + slot
            wide[f, plane, 8 : 8 + height] = above[at : at + height]
            wide[f, plane, 16 - height : 16] = below[at : at + height]
            at += height
        rim[f, 0:8, 0:128] = edge[f * 8 : f * 8 + 8]
        rim[f, 0:8, 128:256] = beyond(beside_x, f)
        at = lines + 30 + f * 2
        rim[f, 8:10, 0:128] = above[at : at + 2]
        rim[f, 14:16, 0:128] = below[at : at + 2]
        at = lines + 40 + f
        rim[f, 8:9, 128:256] = above[at : at + 1]
        rim[f, 15:16, 128:256] = below[at : at + 1]


def primitive(rho, mx, my, mz, energy):
    inverse = 1.0 / rho
    u, v, w = mx * inverse, my * inverse, mz * inverse
    p = (HEAT_RATIO - 1.0) * (energy - 0.5 * (mx * u + my * v + mz * w))
    return u, v, w, p, jnp.sqrt(HEAT_RATIO * jnp.abs(p) * inverse)


def chunks(first, last, size):
    return [(i, min(i + size, last)) for i in range(first, last, size)]


def derive_planes(wide, derived, first, last):
    for i, j in chunks(first, last, 4):
        for k, value in enumerate(primitive(*[wide[f, i:j] for f in range(5)])):
            derived[k, i:j] = value


def derive_speeds(wide, derived, first, last):
    for i, j in chunks(first, last, 5):
        inverse = 1.0 / wide[0, i:j]
        for k in range(3):
            derived[k, i:j] = wide[1 + k, i:j] * inverse


def with_flux(fields, other, along):
    speed, p = other[along], other[3]
    out = [fields[1 + along]]
    for k in range(3):
        value = fields[1 + k] * speed
        out.append(value + p if k == along else value)
    out.append((fields[4] + p) * speed)
    return fields, out, jnp.abs(speed) + other[4]


def face(left, right):
    (fields_l, flux_l, speed_l), (fields_r, flux_r, speed_r) = left, right
    speed = jnp.maximum(speed_l, speed_r)
    viscous = speed + 2.0 * VISCOSITY
    return [
        (flux_l[f] + flux_r[f]) - (viscous if 1 <= f <= 3 else speed) * (fields_r[f] - fields_l[f])
        for f in range(5)
    ]


def rolled(here, shift, axis):
    fields, flux, speed = here
    return (
        [pltpu.roll(a, shift, axis) for a in fields],
        [pltpu.roll(a, shift, axis) for a in flux],
        pltpu.roll(speed, shift, axis),
    )


def rim_section(fields, start, mix):
    other = primitive(*fields)
    here = with_flux(fields, other, 2)
    along_z = face(here, rolled(here, 255, 1))
    if mix is None:
        return other, along_z, None
    total = [g - pltpu.roll(g, 1, 1) for g in along_z]
    for along, step, axis, size in ((0, 16, 1, 256), (1, 1, 0, 16)):
        here = with_flux(fields, other, along)
        faces = face(here, rolled(here, size - step, axis))
        total = [total[f] + (faces[f] - pltpu.roll(faces[f], step, axis)) for f in range(5)]
    out = []
    for f in range(5):
        value = fields[f] - (0.5 * TIME_STEP) * total[f]
        out.append(mix[0] * start[f] + mix[1] * value if mix[0] != 0.0 else value)
    return other, along_z, out


def to_ends(values, after, rows, first, last, ends):
    slot = lax.broadcasted_iota(jnp.int32, (rows, 256), 1) % 16
    for f, value in enumerate(values):
        value = value[0:rows]
        value = jnp.where(slot == 9, pltpu.roll(value, 9 - after, 1), value)
        for x in range(first, last):
            at = x % 16 // 8 * 128
            move = (118 - x % 8 * 16) % 128
            tile = value[:, at : at + 128]
            ends[f, x - first, 0:rows] = pltpu.roll(tile, move, 1) if move else tile


def flow_rate_section(wide, derived, ends, start, offset, mix, write, inner=False):
    depth = wide.shape[1]
    rows = slice(0, 8) if inner else slice(None)
    size = 4 if inner else 2

    def planes(i, j, kept, along):
        fields = [wide[f, i:j, kept] for f in range(5)]
        return with_flux(fields, [derived[f, i:j, kept] for f in range(5)], along)

    def cut(here, i, j):
        return [a[i:j] for a in here[0]], [a[i:j] for a in here[1]], here[2][i:j]

    for i, j in chunks(1, depth - 1, size):
        count = j - i
        lane = lax.broadcasted_iota(jnp.int32, (count, 8 if inner else 16, 128), 2)
        here = planes(i - 1, j + 1, rows, 0)
        faces = face(cut(here, 0, count + 1), cut(here, 1, count + 2))
        total = [g[1:] - g[:-1] for g in faces]
        here = planes(i, j, slice(None), 1)
        faces = face(here, rolled(here, 15, 1))
        for f in range(5):
            change = faces[f] - pltpu.roll(faces[f], 1, 1)
            total[f] = total[f] + (change[:, 0:8] if inner else change)
        here = planes(i, j, rows, 2)
        faces = face(here, rolled(here, 127, 2))
        for f in range(5):
            end = ends[f, i - 1 : j - 1, rows]
            value = jnp.where(lane == 127, end, faces[f])
            total[f] = total[f] + (value - jnp.where(lane == 0, end, pltpu.roll(value, 1, 2)))
        for f in range(5):
            value = wide[f, i:j, rows] - (0.5 * TIME_STEP) * total[f]
            if mix[0] != 0.0:
                value = mix[0] * start[f, i + offset : j + offset, rows] + mix[1] * value
            write(slice(i - 1, j - 1), f, value)


def lamb(derived, ends, first, cells_x, lamb_rows):
    for i, j in chunks(first, first + cells_x, 4):
        count = j - i
        lane = lax.broadcasted_iota(jnp.int32, (count, 8, 128), 2)
        vel = [derived[c, i:j, 0:8] for c in range(3)]
        along_x = [derived[c, i + 1 : j + 1, 0:8] - derived[c, i - 1 : j - 1, 0:8] for c in range(3)]
        along_y = []
        for c in range(3):
            column = derived[c, i:j]
            along_y.append((pltpu.roll(column, 15, 1) - pltpu.roll(column, 1, 1))[:, 0:8])
        along_z = []
        for c in range(2):
            end = ends[c, i - first : j - first, 0:8]
            after = jnp.where(lane == 127, end, pltpu.roll(vel[c], 127, 2))
            along_z.append(after - jnp.where(lane == 0, end, pltpu.roll(vel[c], 1, 2)))
        curl = [
            0.5 * (along_y[2] - along_z[1]),
            0.5 * (along_z[0] - along_x[2]),
            0.5 * (along_x[1] - along_y[0]),
        ]
        at = slice((i - first) * 8, (j - first) * 8)
        lamb_rows[0, at] = (curl[1] * vel[2] - curl[2] * vel[1]).reshape(count * 8, 128)
        lamb_rows[1, at] = (curl[2] * vel[0] - curl[0] * vel[2]).reshape(count * 8, 128)
        lamb_rows[2, at] = (curl[0] * vel[1] - curl[1] * vel[0]).reshape(count * 8, 128)


def project(lamb_rows, pair, spread, send, base):
    peers = send.shape[0]
    fold = fold_of(peers, spread.shape[0] // 8)
    height = 64 // fold
    group = lax.broadcasted_iota(jnp.int32, (height, 128), 1) // (128 // fold)
    modes = dot_three(pair[...], jnp.concatenate([lamb_rows[c] for c in range(3)], 1))
    modes = jnp.concatenate([modes[:, c * 128 : c * 128 + 128] for c in range(3)], 0)
    sent = dot_three(modes, spread[...])
    for c in range(3):
        for peer in range(peers):
            mine = sent[c * 64 : c * 64 + 64, peer * 128 : peer * 128 + 128]
            folded = mine[0:height]
            for g in range(1, fold):
                folded = jnp.where(group == g, mine[g * height : g * height + height], folded)
            send[peer, base + c * height : base + c * height + height] = folded


def flow_sources_body(count, state, edge, *refs):
    beside_x = refs[:count]
    got_a, got_b, pair, spread, labels, _ = refs[count : count + 6]
    wide, rim, send, derived, lamb_rows, ends, above, below = refs[count + 6 :]
    cells_x = state.shape[1]
    above[...], below[...] = paired(is_odd("fy"), got_a[...], got_b[...])
    assemble(wide, rim, state, edge, beside_x, above, below)
    derive_speeds(wide, derived, HALO - 1, HALO + cells_x + 1)
    inverse = 1.0 / rim[0, 0:8]
    to_ends([rim[1, 0:8] * inverse, rim[2, 0:8] * inverse], 3, 8, 0, cells_x, ends)
    lamb(derived, ends, HALO, cells_x, lamb_rows)
    project(lamb_rows, pair, spread, send, 0)
    send[:, send.shape[1] - 8 :] = labels[...]


def writer(target):
    def write(i, f, value):
        target[f, i] = value

    return write


def flow_stages_body(wide, rim, pair, spread, labels, second, derived, ends_out, send, lamb_rows, ends, first):
    planes = wide.shape[1]
    cells_x = planes - 2 * HALO
    size = (send.shape[1] - 8) // 2
    rim_start = [rim[f] for f in range(5)]
    derive_planes(wide, derived, 0, planes)
    _, along_z, rim_first = rim_section(rim_start, None, MIXES[0])
    to_ends(along_z, 2, 16, -2, cells_x + 2, ends)
    flow_rate_section(wide, derived, ends, wide, 0, MIXES[0], writer(first))
    derive_planes(first, derived, 0, planes - 2)
    other, along_z, rim_second = rim_section(rim_first, [rim[f] for f in range(5)], MIXES[1])
    to_ends(other[0:2], 3, 8, 0, cells_x, ends)
    lamb(derived, ends, 2, cells_x, lamb_rows)
    project(lamb_rows, pair, spread, send, 0)
    to_ends(along_z, 2, 16, -1, cells_x + 1, ends)
    flow_rate_section(first, derived, ends, wide, 1, MIXES[1], writer(second))
    derive_planes(second, derived, 0, planes - 4)
    other, along_z, _ = rim_section(rim_second, None, None)
    to_ends(other[0:2], 3, 8, 0, cells_x, ends)
    lamb(derived, ends, 1, cells_x, lamb_rows)
    project(lamb_rows, pair, spread, send, size)
    send[:, 2 * size :] = labels[...]
    to_ends(along_z, 2, 8, 0, cells_x, ends_out)


def flow_last_body(second, derived, ends, wide, out):
    flow_rate_section(second, derived, ends, wide, 2, MIXES[2], writer(out), inner=True)


def faces_out(state, rear, front):
    lane = lax.broadcasted_iota(jnp.int32, (32, 128), 1) // 16
    for c in range(4):
        front[c * 8 : c * 8 + 8] = state[c, 56:64]
        rear[c * 8 : c * 8 + 8] = state[c, 0:8]
        front[32 + c * 8 : 40 + c * 8] = state[c, pl.ds(7, 8, stride=8), :]
        rear[32 + c * 8 : 40 + c * 8] = state[c, pl.ds(0, 8, stride=8), :]
    rows = state[...].reshape(256, 128)
    last = jnp.zeros((32, 128), F32)
    first = jnp.zeros((32, 128), F32)
    for j in range(8):
        piece = rows[j * 32 : j * 32 + 32]
        last = jnp.where(lane == j, pltpu.roll(piece, (j * 16 + 16) % 128, 1), last)
        first = jnp.where(lane == j, pltpu.roll(piece, j * 16, 1) if j else piece, first)
    front[64:96] = last
    rear[64:96] = first


def faces_sent(odd, state, message_a, message_b):
    size = message_a.shape[0]
    faces_out(state, message_b, message_a)
    message_a[...], message_b[0:size] = paired(odd, message_a[...], message_b[0:size])
    message_b[size:] = jnp.zeros((message_b.shape[0] - size, 128), F32)


def lift(total, before, after, sides, factor):
    def place(face, rows, target):
        value = factor * dot_exact_right(rows, sides[face])
        for c in range(4):
            total[c, target, :] += value[c * 8 : c * 8 + 8]

    place(0, before[0:32], pl.ds(0, 8))
    place(1, after[0:32], pl.ds(56, 8))
    place(2, before[32:64], pl.ds(0, 8, stride=8))
    place(3, after[32:64], pl.ds(7, 8, stride=8))


def rate_local(state, deriv_rows, deriv_lanes, speed, sides):
    fields = [state[c] for c in range(4)]
    by_rows = dot_three(deriv_rows[...], jnp.concatenate(fields[0:3], 1))
    by_lanes = dot_three(jnp.concatenate([fields[0], fields[3]], 0), deriv_lanes[...])
    divergence = by_rows[0:64, 128:256] + by_rows[64:128, 256:384] + by_lanes[64:128]
    rates = [
        -(speed[...] * speed[...]) * divergence,
        -by_rows[0:64, 0:128],
        -by_rows[64:128, 0:128],
        -by_lanes[0:64],
    ]
    row = lax.broadcasted_iota(jnp.int32, (64, 128), 0)
    lane = lax.broadcasted_iota(jnp.int32, (64, 128), 1)
    count = jnp.zeros((64, 128), F32)
    for value in (row // 8, row % 8, lane // 16):
        count = count + jnp.where((value == 0) | (value == 7), PENALTY, 0.0)
    side = PENALTY * dot_exact_right(state[...].reshape(256, 128), sides[4])
    return [rates[c] - count * fields[c] + side[c * 64 : c * 64 + 64] for c in range(4)]


def acoustic_local_body(mix, state, start, deriv_rows, deriv_lanes, speed, sides, out, front, rear):
    rates = rate_local(state, deriv_rows, deriv_lanes, speed, sides)
    for c in range(4):
        value = state[c] + TIME_STEP * rates[c]
        if mix[0] != 0.0:
            value = mix[0] * start[c] + mix[1] * value
        out[c] = value
    faces_out(state, rear, front)
    lift(out, front, rear, sides, TIME_STEP * mix[1] * PENALTY)


def acoustic_start_body(given, _, state, message_a, message_b, turned, stored):
    count = given.shape[0]
    for e in range(count):
        for t in range(4):
            stored[t, 4 * e : 4 * e + 4] = given[e, :, t * 128 : t * 128 + 128]
    for t in range(4):
        rows = [stored[t, pl.ds(c, count, stride=4), :] for c in range(4)]
        rows = jnp.concatenate(rows + [jnp.zeros((128 - 4 * count, 128), F32)], 0)
        turned[t * 128 : t * 128 + 128] = rows.T
    lane = lax.broadcasted_iota(jnp.int32, (64, 128), 1) // count
    fields = [jnp.zeros((64, 128), F32)] * 4
    for z in range(8):
        piece = turned[pl.ds(z, 64, stride=8), :]
        for c in range(4):
            move = (z - c) * count % 128
            fields[c] = jnp.where(lane == z, pltpu.roll(piece, move, 1) if move else piece, fields[c])
    for c in range(4):
        state[c] = fields[c]
    faces_sent(is_odd("fz"), state, message_a, message_b)


def natural_order(state, out, turned, stored):
    count = out.shape[0]
    lane = lax.broadcasted_iota(jnp.int32, (64, 128), 1) // count
    for z in range(8):
        value = jnp.zeros((64, 128), F32)
        for c in range(4):
            move = (c - z) * count % 128
            value = jnp.where(lane == c, pltpu.roll(state[c], move, 1) if move else state[c], value)
        turned[pl.ds(z, 64, stride=8), :] = value
    for t in range(4):
        rows = turned[t * 128 : t * 128 + 128].T
        for c in range(4):
            stored[t, pl.ds(c, count, stride=4), :] = rows[c * count : c * count + count]
    for e in range(count):
        for t in range(4):
            out[e, :, t * 128 : t * 128 + 128] = stored[t, 4 * e : 4 * e + 4]


def remote_part(out, before, after, sides_far, factor):
    lift(out, before, after, sides_far, factor)
    lane = lax.broadcasted_iota(jnp.int32, (32, 128), 1) // 16
    last, first = before[64:96], after[64:96]
    pieces = []
    for j in range(8):
        left = pltpu.roll(last, 128 - j * 16, 1) if j else last
        right = pltpu.roll(first, (144 - j * 16) % 128, 1) if j != 1 else first
        pieces.append(jnp.where(lane == 0, left, jnp.where(lane == 1, right, 0.0)))
    value = factor * dot_exact_right(jnp.concatenate(pieces, 0), sides_far[4])
    for c in range(4):
        out[c] += value[c * 64 : c * 64 + 64]


def acoustic_far_body(mix, kind, partial, got_a, got_b, sides_far, received, *refs):
    if kind == "last":
        given_out, before, after, out, turned, stored = refs
    elif kind == "first":
        _, out, message_a, message_b, before, after, source = refs
        place_body(received, source)
        received = source
    else:
        out, message_a, message_b, before, after = refs
    odd = is_odd("fz")
    after[...], before[...] = paired(odd, got_a[0:96], got_b[0:96])
    out[0] = partial[0]
    for c in range(3):
        out[1 + c] = partial[1 + c] + (TIME_STEP * mix[1]) * received[c]
    remote_part(out, before, after, sides_far, TIME_STEP * mix[1] * PENALTY)
    if kind == "last":
        natural_order(out, given_out, turned, stored)
    else:
        faces_sent(odd, out, message_a, message_b)


def place_body(received, *outs):
    peers, size = received.shape[0], received.shape[1]
    fold = 192 * len(outs) // (size - 8)
    height = 64 // fold
    target = lax.broadcasted_iota(jnp.int32, (128, 128), 0)
    lane = lax.broadcasted_iota(jnp.int32, (128, 128), 1)
    total = None
    for peer in range(peers):
        label = received[peer, size - 8 : size - 7, :]
        label = jnp.broadcast_to(label, (128, 128)).astype(jnp.int32)
        hit = (label == target % 16) & (lane % 8 == target // 16)
        chosen = [jnp.where(hit & (lane // (128 // fold) == g), 1.0, 0.0) for g in range(fold)]
        chosen = jnp.concatenate(chosen, 0).astype(BF16)
        high, low = parts(received[peer, 0 : size - 8])
        dims = (((1,), (1,)), ((), ()))
        value = lax.dot_general(high, chosen, dims, preferred_element_type=F32)
        value = value + lax.dot_general(low, chosen, dims, preferred_element_type=F32)
        total = value if total is None else total + value
    for k, out in enumerate(outs):
        for c in range(3):
            for g in range(fold):
                at = (k * 3 + c) * height
                out[c, g * height : g * height + height] = total[at : at + height, g * 128 : g * 128 + 128]


def kron_part(matrix, shape, rows_by, columns_by):
    row = lax.broadcasted_iota(jnp.int32, (shape[0], 8), 0)
    level = lax.broadcasted_iota(jnp.int32, (shape[0], 8), 1)
    left = (row // rows_by % 8 == level).astype(F32)
    level = lax.broadcasted_iota(jnp.int32, (8, shape[1]), 0)
    column = lax.broadcasted_iota(jnp.int32, (8, shape[1]), 1)
    right = (column // columns_by % 8 == level).astype(F32)
    return dot_full(dot_full(left, matrix), right)


def tables_body(
    packed,
    near,
    far,
    deriv_rows,
    deriv_lanes,
    pair,
    spread,
    labels,
    speed,
):
    size = near.shape[1]
    count = size // 8
    blocks = spread.shape[0] // 8

    def place_of(shape):
        return (lax.broadcasted_iota(jnp.int32, shape, 0), lax.broadcasted_iota(jnp.int32, shape, 1))

    row, column = place_of((count, size))
    repeat = (column % count == row).astype(F32)
    speed[...] = dot_full(packed[24:25, 0:count], repeat)
    wanted = dot_full(packed[16:24, 0:count], repeat).astype(jnp.int32)
    row, column = place_of((size, size))
    level, element = row // count, row % count
    level_out = column // count
    for facet in range(4):
        shift = -count if facet % 2 == 0 else count
        choice = jnp.broadcast_to(wanted[facet : facet + 1], (size, size))
        near[facet] = jnp.where((level == level_out) & (element == choice), 1.0, 0.0).astype(BF16)
        far[facet] = jnp.where((level == level_out) & (element + shift == choice), 1.0, 0.0).astype(BF16)
    lower = jnp.broadcast_to(wanted[4:5], (size, size))
    upper = jnp.broadcast_to(wanted[5:6], (size, size))
    hit = (level == 7) & (level_out == 0) & (element == lower)
    hit = hit | ((level == 0) & (level_out == 7) & (element == upper))
    near[4] = jnp.where(hit, 1.0, 0.0).astype(BF16)
    hit = (level == 0) & (level_out == 0) & (element - count == lower)
    hit = hit | ((level == 1) & (level_out == 7) & (element + count == upper))
    far[4] = jnp.where(hit, 1.0, 0.0).astype(BF16)

    row, column = place_of((64, 64))
    slopes, modes = packed[0:8, 0:8], packed[8:16, 0:8]
    outer = kron_part(slopes, (64, 64), 8, 8)
    inner = kron_part(slopes, (64, 64), 1, 1)
    deriv_rows[0:64] = jnp.where(row % 8 == column % 8, outer, 0.0)
    deriv_rows[64:128] = jnp.where(row // 8 == column // 8, inner, 0.0)
    row, column = place_of((size, size))
    lanes = kron_part(slopes.T, (size, size), count, count)
    deriv_lanes[...] = jnp.where(row % count == column % count, lanes, 0.0)
    pair[...] = kron_part(modes, (64, 64), 8, 8) * kron_part(modes, (64, 64), 1, 1)

    peers = labels.shape[0]
    capacity = capacity_of(peers, blocks)
    row, column = place_of((blocks, blocks))

    def upright(values):
        return jnp.sum(jnp.where(row == column, values, 0.0), 1, keepdims=True)

    owner_row = packed[25:26, 0:blocks]
    owner_column = upright(owner_row)
    earlier = (owner_column == owner_row) & (column < row)
    position = jnp.sum(jnp.where(earlier, 1.0, 0.0), 1, keepdims=True)
    slot = owner_column * capacity + position
    element_column = upright(packed[26:27, 0:blocks])
    row, column = place_of((8 * blocks, blocks))
    repeat = (row // 8 == column).astype(F32)
    slot = dot_full(repeat, jnp.broadcast_to(slot, (blocks, 128)))
    element = dot_full(repeat, jnp.broadcast_to(element_column, (blocks, 128)))
    row, column = place_of((8 * blocks, 128))
    values = kron_part(modes.T, (8 * blocks, 128), 1, 1)
    inside = column % (8 * capacity) // 8
    for peer in range(peers):
        chosen = slot == (inside + peer * capacity).astype(F32)
        spread[:, peer * 128 : peer * 128 + 128] = jnp.where(chosen, values, 0.0)
        named = jnp.where(chosen & (row % 8 == 0), element + 1.0, 0.0)
        labels[peer] = jnp.broadcast_to(jnp.sum(named, 0, keepdims=True) - 1.0, (8, 128))


def shifted(sizes, shifts):
    pairs = []
    for index in np.ndindex(*sizes):
        source = [(i + s) % n for i, s, n in zip(index, shifts, sizes)]
        pairs.append((int(np.ravel_multi_index(source, sizes)), int(np.ravel_multi_index(index, sizes))))
    return pairs


def partners(sizes, axis, second):
    pairs = []
    for index in np.ndindex(*sizes):
        source = list(index)
        step = 1 if (index[axis] % 2 == 0) != second else -1
        source[axis] = (index[axis] + step) % sizes[axis]
        pairs.append((int(np.ravel_multi_index(source, sizes)), int(np.ravel_multi_index(index, sizes))))
    return pairs


def per_device(
    density,
    velocity,
    pressure,
    acoustic,
    sound_speed,
    derivative,
    mode_basis,
    neighbours,
    block_owner,
    block_element,
):
    size_x, size_y, size_z = lax.axis_size("fx"), lax.axis_size("fy"), lax.axis_size("fz")
    devices = size_x * size_y * size_z
    cells_x = density.shape[0]
    elements = acoustic.shape[0]
    device = lax.axis_index(("fx", "fy", "fz"))

    names = ("fx", "fy", "fz")

    rows = 5 * cells_x * 8
    tiles = -(-rows // 128)
    square = velocity[0] * velocity[0] + velocity[1] * velocity[1] + velocity[2] * velocity[2]
    energy = pressure / (HEAT_RATIO - 1.0) + 0.5 * density * square
    rest = ((0, 0), (0, 0), (0, 0))
    state = jnp.pad(density[None], ((0, 4),) + rest) + jnp.pad(density * velocity, ((1, 1),) + rest)
    state = state + jnp.pad(energy[None], ((4, 0),) + rest)
    flow_a, flow_b = call(pack_start_body, [(tiles * 8, 128), (tiles * 8, 128)], state)
    edge_a = lax.ppermute(flow_a, "fz", partners((size_z,), 0, False))
    edge_b = lax.ppermute(flow_b, "fz", partners((size_z,), 0, True))

    near_pairs = [(i ^ 1, i) for i in range(devices)]
    far_pairs = [pair for i in range(1, devices - 1, 2) for pair in ((i, i + 1), (i + 1, i))]

    def traces(to_a, to_b):
        far_got = lax.ppermute(to_b, names, far_pairs)
        return lax.ppermute(to_a, names, near_pairs), far_got

    size = 8 * elements
    held = (4, 64, size)
    faces = (96, size)
    sides = [pltpu.VMEM(faces, F32)] * 2
    turning = [pltpu.VMEM((512, 128), F32), pltpu.VMEM((4, 4 * elements, 128), F32)]
    sound, to_a, to_b = call(
        acoustic_start_body,
        [held, faces, (3 * faces[0], size)],
        acoustic,
        edge_a,
        scratch=turning,
        last=1,
    )
    got_a, got_b = traces(to_a, to_b)

    edge, along_x = call(
        pack_next_body,
        [(40, 128), (5 * 2 * HALO * 8 + 40, 128)],
        state,
        flow_a,
        flow_b,
        edge_a,
        edge_b,
        got_a,
        last=1,
    )
    beside_x = [
        lax.ppermute(along_x, "fx", shifted((size_x,), (step,))) for step in ((1,) if size_x == 2 else (1, -1))
    ]
    y_shape = (5 * cells_x * HALO + 48, 128)
    y_a, y_b = call(pack_last_body, [y_shape, y_shape], state, edge, *beside_x, cost=1)
    y_second = lax.ppermute(y_b, "fy", partners((size_y,), 0, True))
    y_first = lax.ppermute(y_a, "fy", partners((size_y,), 0, False))

    local = (neighbours - device * elements).T
    blocks = block_owner.size
    width = max(elements, blocks)

    def piece(values, first):
        values = values.astype(F32)
        return jnp.pad(values, ((first, 32 - first - values.shape[0]), (0, width - values.shape[1])))

    packed = (
        piece(derivative, 0)
        + piece(mode_basis, 8)
        + piece(local, 16)
        + piece(sound_speed.reshape(1, elements), 24)
        + piece(block_owner.reshape(1, blocks), 25)
        + piece(block_element.reshape(1, blocks), 26)
    )
    table = jax.ShapeDtypeStruct((5, size, size), BF16)
    near, far, deriv_rows, deriv_lanes, pair, spread, labels, speed = call(
        tables_body,
        [
            table,
            table,
            (128, 64),
            (size, size),
            (64, 64),
            (8 * blocks, size_y * 128),
            (size_y, 8, 128),
            (1, size),
        ],
        packed,
        cost=1,
    )

    fold = fold_of(size_y, blocks)
    wide = cells_x + 2 * HALO
    rows_scratch = pltpu.VMEM((3, 64, 128), F32)

    def planes(count):
        return (5, count, 16, 128)

    def route(send):
        return lax.all_to_all(send, "fy", split_axis=0, concat_axis=0, tiled=True)

    start, rim, send = call(
        functools.partial(flow_sources_body, len(beside_x)),
        [planes(wide), (5, 16, 256), (size_y, 192 // fold + 8, 128)],
        state,
        edge,
        *beside_x,
        y_first,
        y_second,
        pair,
        spread,
        labels,
        got_b,
        last=1,
        scratch=[
            pltpu.VMEM((3, wide, 16, 128), F32),
            rows_scratch,
            pltpu.VMEM((2, cells_x, 8, 128), F32),
            pltpu.VMEM(y_shape, F32),
            pltpu.VMEM(y_shape, F32),
        ],
    )
    received = route(send)
    second, derived, ends, send = call(
        flow_stages_body,
        [
            planes(wide - 4),
            planes(wide),
            (5, cells_x, 8, 128),
            (size_y, 2 * 192 // fold + 8, 128),
        ],
        start,
        rim,
        pair,
        spread,
        labels,
        scratch=[rows_scratch, pltpu.VMEM(planes(wide - 2), F32), pltpu.VMEM(planes(wide - 2), F32)],
    )

    def local_part(mix, now):
        return call(
            functools.partial(acoustic_local_body, mix),
            [held],
            now,
            sound,
            deriv_rows,
            deriv_lanes,
            speed,
            near,
            scratch=sides,
            cost=1,
        )[0]

    partial = local_part(MIXES[0], sound)
    sound_one, to_a, to_b = call(
        functools.partial(acoustic_far_body, MIXES[0], "first"),
        [held, faces, (faces[0] + 32, size)],
        partial,
        got_a,
        got_b,
        far,
        received,
        send,
        scratch=sides + [rows_scratch],
        last=1,
    )
    source_two, source_three = call(place_body, [(3, 64, 128)] * 2, route(send))
    got_a, got_b = traces(to_a, to_b)
    flow_state = call(flow_last_body, [(5, cells_x, 8, 128)], second, derived, ends, start)[0]
    partial = local_part(MIXES[1], sound_one)
    sound_two, to_a, to_b = call(
        functools.partial(acoustic_far_body, MIXES[1], "second"),
        [held, faces, (faces[0] + 32, size)],
        partial,
        got_a,
        got_b,
        far,
        source_two,
        scratch=sides,
    )
    got_a, got_b = traces(to_a, to_b)
    partial = local_part(MIXES[2], sound_two)
    sound_state = call(
        functools.partial(acoustic_far_body, MIXES[2], "last"),
        [(elements, 4, 512)],
        partial,
        got_a,
        got_b,
        far,
        source_three,
        scratch=sides + [pltpu.VMEM(held, F32)] + turning,
    )[0]
    return (flow_state, sound_state)


def solution(mesh):
    placed = (
        P("fx", "fy", "fz"),
        P(None, "fx", "fy", "fz"),
        P("fx", "fy", "fz"),
        P(("fx", "fy", "fz"), None, None),
        P(("fx", "fy", "fz")),
        P(),
        P(),
        P(("fx", "fy", "fz"), None),
        P("fx", "fy", "fz", None, None),
        P("fx", "fy", "fz", None),
    )
    return jax.shard_map(
        per_device,
        mesh=mesh,
        in_specs=placed,
        out_specs=(P(None, "fx", "fy", "fz"), P(("fx", "fy", "fz"), None, None)),
        check_vma=False,
    )
```

```python
import functools

import jax
import jax.numpy as jnp
import numpy as np
from jax import lax
from jax.experimental import pallas as pl
from jax.experimental.pallas import tpu as pltpu
from jax.sharding import PartitionSpec as P

HEAT_RATIO = 1.4
TIME_STEP = 0.1
VISCOSITY = 0.05
PENALTY = 0.5
HALO = 3
F32 = jnp.float32
BF16 = jnp.bfloat16
PARAMS = pltpu.CompilerParams(vmem_limit_bytes=24 * 1024 * 1024)
MIXES = ((0.0, 1.0), (0.75, 0.25), (1.0 / 3.0, 2.0 / 3.0))


def parts(values):
    high = values.astype(BF16)
    return high, (values - high.astype(F32)).astype(BF16)


def dot(left, right):
    return lax.dot_general(left, right, (((1,), (0,)), ((), ())), preferred_element_type=F32)


def dot_three(left, right):
    left_high, left_low = parts(left)
    right_high, right_low = parts(right)
    return dot(left_high, right_high) + dot(left_high, right_low) + dot(left_low, right_high)


def dot_full(left, right, dims=((1,), (0,))):
    return lax.dot_general(
        left, right, (dims, ((), ())), precision=lax.Precision.HIGHEST, preferred_element_type=F32
    )


def dot_exact_right(left, right):
    left_high, left_low = parts(left)
    return dot(left_high, right) + dot(left_low, right)


def call(body, outs, *operands, scratch=(), last=0, cost=None):
    whole = pl.BlockSpec(memory_space=pltpu.VMEM)
    outs = [out if isinstance(out, jax.ShapeDtypeStruct) else jax.ShapeDtypeStruct(out, F32) for out in outs]
    anywhere = pl.BlockSpec(memory_space=pl.ANY)
    return pl.pallas_call(
        body,
        out_shape=outs,
        in_specs=[whole] * (len(operands) - last) + [anywhere] * last,
        out_specs=[whole] * len(outs),
        scratch_shapes=list(scratch),
        compiler_params=PARAMS,
        cost_estimate=None if cost is None else pl.CostEstimate(flops=cost, bytes_accessed=cost, transcendentals=0),
    )(*operands)


def capacity_of(peers, blocks):
    return max(2, 2 * blocks // peers)


def fold_of(peers, blocks):
    return 128 // (8 * capacity_of(peers, blocks))


def is_odd(axis):
    return lax.axis_index(axis) % 2 == 1


def paired(odd, to_next, to_last):
    return jnp.where(odd, to_last, to_next), jnp.where(odd, to_next, to_last)


def pack_start_body(state, message_a, message_b, along_x):
    odd = is_odd("fz")
    rows = state[...].reshape(-1, 128)
    count = rows.shape[0]
    for tile in range(message_a.shape[0] // 8):
        piece = rows[tile * 128 : min(count, tile * 128 + 128)]
        if piece.shape[0] < 128:
            piece = jnp.concatenate([piece, jnp.zeros((128 - piece.shape[0], 128), F32)], 0)
        turned = piece.T
        first, second = paired(odd, turned[120:128], turned[0:8])
        message_a[tile * 8 : tile * 8 + 8] = first
        message_b[tile * 8 : tile * 8 + 8] = second
    cells_x = state.shape[1]
    for f in range(5):
        for s, x in enumerate(x_planes(cells_x)):
            at = (f * 2 * HALO + s) * 8
            along_x[at : at + 8] = state[f, x]


def pack_next_body(state, sent_a, sent_b, got_a, got_b, _, edge):
    cells_x = state.shape[1]
    odd_z = is_odd("fz")
    high, low = paired(odd_z, sent_a[...], sent_b[...])
    above, below = paired(odd_z, got_a[...], got_b[...])
    row = lax.broadcasted_iota(jnp.int32, (8, 128), 0)
    x_of_lane = lax.broadcasted_iota(jnp.int32, (16, 128), 1) // 8 % cells_x
    for tile in range(high.shape[0] // 8):
        rows = slice(tile * 8, tile * 8 + 8)
        upper = jnp.where(row < 3, pltpu.roll(high[rows], 3, 0), pltpu.roll(above[rows], 3, 0))
        lower = jnp.where(row < 3, pltpu.roll(below[rows], 3, 0), pltpu.roll(low[rows], 3, 0))
        slots = jnp.concatenate([upper, lower], 0)
        spread = jnp.concatenate([jnp.where(x_of_lane == x, slots, 0.0) for x in range(8)], 0).T
        for half in range(16 // cells_x):
            f = tile * (16 // cells_x) + half
            if f < 5:
                at = half * cells_x * 8
                total = spread[at : at + 8]
                for x in range(1, cells_x):
                    total = total + spread[at + x * 8 : at + x * 8 + 8]
                edge[f * 8 : f * 8 + 8] = total


def x_planes(cells_x):
    return [cells_x - HALO + i for i in range(HALO)] + list(range(HALO))


def sides_of(beside_x):
    return beside_x[0], beside_x[-1]


def beyond(edges_x, f):
    after, before = sides_of(edges_x)
    at = f * 8
    if after is before:
        return after[at : at + 8]
    lane = lax.broadcasted_iota(jnp.int32, (8, 128), 1)
    return jnp.where(lane < 64, after[at : at + 8], before[at : at + 8])


def pack_last_body(state, edge, *refs):
    (y_a, y_b), refs = refs[-2:], refs[:-2]
    beside_x, edges_x = refs[: len(refs) // 2], refs[len(refs) // 2 :]
    cells_x = state.shape[1]
    odd = is_odd("fy")
    after, before = sides_of(beside_x)

    def put(at, values, height):
        first, second = paired(odd, values[8 - height : 8], values[0:height])
        y_a[at : at + height] = first
        y_b[at : at + height] = second

    lines = 5 * cells_x * HALO
    for f in range(5):
        for x in range(cells_x):
            put((f * cells_x + x) * HALO, state[f, x], HALO)
        at = lines + f * 6
        for slot, height in ((1, 1), (2, 2), (3, 2), (4, 1)):
            source = (f * 2 * HALO + slot) * 8
            put(at, (before if slot < HALO else after)[source : source + 8], height)
            at += height
        put(lines + 30 + f * 2, edge[f * 8 : f * 8 + 8], 2)
        put(lines + 40 + f, beyond(edges_x, f), 1)


def assemble(wide, rim, state, edge, beside_x, edges_x, above, below):
    cells_x = state.shape[1]
    after, before = sides_of(beside_x)
    lines = 5 * cells_x * HALO
    for f in range(5):
        for x in range(cells_x):
            wide[f, HALO + x, 0:8] = state[f, x]
            at = (f * cells_x + x) * HALO
            wide[f, HALO + x, 8 : 8 + HALO] = above[at : at + HALO]
            wide[f, HALO + x, 16 - HALO : 16] = below[at : at + HALO]
        for slot in range(2 * HALO):
            plane = slot if slot < HALO else cells_x + slot
            at = (f * 2 * HALO + slot) * 8
            wide[f, plane, 0:8] = (before if slot < HALO else after)[at : at + 8]
        at = lines + f * 6
        for slot, height in ((1, 1), (2, 2), (3, 2), (4, 1)):
            plane = slot if slot < HALO else cells_x + slot
            wide[f, plane, 8 : 8 + height] = above[at : at + height]
            wide[f, plane, 16 - height : 16] = below[at : at + height]
            at += height
        rim[f, 0:8, 0:128] = edge[f * 8 : f * 8 + 8]
        rim[f, 0:8, 128:256] = beyond(edges_x, f)
        at = lines + 30 + f * 2
        rim[f, 8:10, 0:128] = above[at : at + 2]
        rim[f, 14:16, 0:128] = below[at : at + 2]
        at = lines + 40 + f
        rim[f, 8:9, 128:256] = above[at : at + 1]
        rim[f, 15:16, 128:256] = below[at : at + 1]


def primitive(rho, mx, my, mz, energy):
    inverse = 1.0 / rho
    u, v, w = mx * inverse, my * inverse, mz * inverse
    p = (HEAT_RATIO - 1.0) * (energy - 0.5 * (mx * u + my * v + mz * w))
    return u, v, w, p, jnp.sqrt(HEAT_RATIO * jnp.abs(p) * inverse)


def chunks(first, last, size):
    return [(i, min(i + size, last)) for i in range(first, last, size)]


def derive_planes(wide, derived, first, last):
    for i, j in chunks(first, last, 4):
        for k, value in enumerate(primitive(*[wide[f, i:j] for f in range(5)])):
            derived[k, i:j] = value


def derive_speeds(wide, derived, first, last):
    for i, j in chunks(first, last, 5):
        inverse = 1.0 / wide[0, i:j]
        for k in range(3):
            derived[k, i:j] = wide[1 + k, i:j] * inverse


def with_flux(fields, other, along):
    speed, p = other[along], other[3]
    out = [fields[1 + along]]
    for k in range(3):
        value = fields[1 + k] * speed
        out.append(value + p if k == along else value)
    out.append((fields[4] + p) * speed)
    return fields, out, jnp.abs(speed) + other[4]


def face(left, right):
    (fields_l, flux_l, speed_l), (fields_r, flux_r, speed_r) = left, right
    speed = jnp.maximum(speed_l, speed_r)
    viscous = speed + 2.0 * VISCOSITY
    return [
        (flux_l[f] + flux_r[f]) - (viscous if 1 <= f <= 3 else speed) * (fields_r[f] - fields_l[f])
        for f in range(5)
    ]


def rolled(here, shift, axis):
    fields, flux, speed = here
    return (
        [pltpu.roll(a, shift, axis) for a in fields],
        [pltpu.roll(a, shift, axis) for a in flux],
        pltpu.roll(speed, shift, axis),
    )


def rim_section(fields, start, mix):
    other = primitive(*fields)
    here = with_flux(fields, other, 2)
    along_z = face(here, rolled(here, 255, 1))
    if mix is None:
        return other, along_z, None
    total = [g - pltpu.roll(g, 1, 1) for g in along_z]
    for along, step, axis, size in ((0, 16, 1, 256), (1, 1, 0, 16)):
        here = with_flux(fields, other, along)
        faces = face(here, rolled(here, size - step, axis))
        total = [total[f] + (faces[f] - pltpu.roll(faces[f], step, axis)) for f in range(5)]
    out = []
    for f in range(5):
        value = fields[f] - (0.5 * TIME_STEP) * total[f]
        out.append(mix[0] * start[f] + mix[1] * value if mix[0] != 0.0 else value)
    return other, along_z, out


def to_ends(values, after, rows, first, last, ends):
    slot = lax.broadcasted_iota(jnp.int32, (rows, 256), 1) % 16
    for f, value in enumerate(values):
        value = value[0:rows]
        value = jnp.where(slot == 9, pltpu.roll(value, 9 - after, 1), value)
        for x in range(first, last):
            at = x % 16 // 8 * 128
            move = (118 - x % 8 * 16) % 128
            tile = value[:, at : at + 128]
            ends[f, x - first, 0:rows] = pltpu.roll(tile, move, 1) if move else tile


def flow_rate_section(wide, derived, ends, start, offset, mix, write, inner=False):
    depth = wide.shape[1]
    rows = slice(0, 8) if inner else slice(None)
    size = 4 if inner else 2

    def planes(i, j, kept, along):
        fields = [wide[f, i:j, kept] for f in range(5)]
        return with_flux(fields, [derived[f, i:j, kept] for f in range(5)], along)

    def cut(here, i, j):
        return [a[i:j] for a in here[0]], [a[i:j] for a in here[1]], here[2][i:j]

    for i, j in chunks(1, depth - 1, size):
        count = j - i
        lane = lax.broadcasted_iota(jnp.int32, (count, 8 if inner else 16, 128), 2)
        here = planes(i - 1, j + 1, rows, 0)
        faces = face(cut(here, 0, count + 1), cut(here, 1, count + 2))
        total = [g[1:] - g[:-1] for g in faces]
        here = planes(i, j, slice(None), 1)
        faces = face(here, rolled(here, 15, 1))
        for f in range(5):
            change = faces[f] - pltpu.roll(faces[f], 1, 1)
            total[f] = total[f] + (change[:, 0:8] if inner else change)
        here = planes(i, j, rows, 2)
        faces = face(here, rolled(here, 127, 2))
        for f in range(5):
            end = ends[f, i - 1 : j - 1, rows]
            value = jnp.where(lane == 127, end, faces[f])
            total[f] = total[f] + (value - jnp.where(lane == 0, end, pltpu.roll(value, 1, 2)))
        for f in range(5):
            value = wide[f, i:j, rows] - (0.5 * TIME_STEP) * total[f]
            if mix[0] != 0.0:
                value = mix[0] * start[f, i + offset : j + offset, rows] + mix[1] * value
            write(slice(i - 1, j - 1), f, value)


def lamb(derived, ends, first, cells_x, lamb_rows):
    for i, j in chunks(first, first + cells_x, 4):
        count = j - i
        lane = lax.broadcasted_iota(jnp.int32, (count, 8, 128), 2)
        vel = [derived[c, i:j, 0:8] for c in range(3)]
        along_x = [derived[c, i + 1 : j + 1, 0:8] - derived[c, i - 1 : j - 1, 0:8] for c in range(3)]
        along_y = []
        for c in range(3):
            column = derived[c, i:j]
            along_y.append((pltpu.roll(column, 15, 1) - pltpu.roll(column, 1, 1))[:, 0:8])
        along_z = []
        for c in range(2):
            end = ends[c, i - first : j - first, 0:8]
            after = jnp.where(lane == 127, end, pltpu.roll(vel[c], 127, 2))
            along_z.append(after - jnp.where(lane == 0, end, pltpu.roll(vel[c], 1, 2)))
        curl = [
            0.5 * (along_y[2] - along_z[1]),
            0.5 * (along_z[0] - along_x[2]),
            0.5 * (along_x[1] - along_y[0]),
        ]
        at = slice((i - first) * 8, (j - first) * 8)
        lamb_rows[0, at] = (curl[1] * vel[2] - curl[2] * vel[1]).reshape(count * 8, 128)
        lamb_rows[1, at] = (curl[2] * vel[0] - curl[0] * vel[2]).reshape(count * 8, 128)
        lamb_rows[2, at] = (curl[0] * vel[1] - curl[1] * vel[0]).reshape(count * 8, 128)


def project(lamb_rows, pair, spread, send, base):
    peers = send.shape[0]
    fold = fold_of(peers, spread.shape[0] // 8)
    height = 64 // fold
    group = lax.broadcasted_iota(jnp.int32, (height, 128), 1) // (128 // fold)
    modes = dot_three(pair[...], jnp.concatenate([lamb_rows[c] for c in range(3)], 1))
    modes = jnp.concatenate([modes[:, c * 128 : c * 128 + 128] for c in range(3)], 0)
    sent = dot_three(modes, spread[...])
    for c in range(3):
        for peer in range(peers):
            mine = sent[c * 64 : c * 64 + 64, peer * 128 : peer * 128 + 128]
            folded = mine[0:height]
            for g in range(1, fold):
                folded = jnp.where(group == g, mine[g * height : g * height + height], folded)
            send[peer, base + c * height : base + c * height + height] = folded


def flow_sources_body(count, state, edge, *refs):
    beside_x, edges_x, refs = refs[:count], refs[count : 2 * count], refs[2 * count :]
    got_a, got_b, pair, spread, labels, _ = refs[:6]
    wide, rim, send, derived, lamb_rows, ends, above, below = refs[6:]
    cells_x = state.shape[1]
    above[...], below[...] = paired(is_odd("fy"), got_a[...], got_b[...])
    assemble(wide, rim, state, edge, beside_x, edges_x, above, below)
    derive_speeds(wide, derived, HALO - 1, HALO + cells_x + 1)
    inverse = 1.0 / rim[0, 0:8]
    to_ends([rim[1, 0:8] * inverse, rim[2, 0:8] * inverse], 3, 8, 0, cells_x, ends)
    lamb(derived, ends, HALO, cells_x, lamb_rows)
    project(lamb_rows, pair, spread, send, 0)
    send[:, send.shape[1] - 8 :] = labels[...]


def writer(target):
    def write(i, f, value):
        target[f, i] = value

    return write


def flow_stages_body(wide, rim, pair, spread, labels, second, derived, ends_out, send, lamb_rows, ends, first):
    planes = wide.shape[1]
    cells_x = planes - 2 * HALO
    size = (send.shape[1] - 8) // 2
    rim_start = [rim[f] for f in range(5)]
    derive_planes(wide, derived, 0, planes)
    _, along_z, rim_first = rim_section(rim_start, None, MIXES[0])
    to_ends(along_z, 2, 16, -2, cells_x + 2, ends)
    flow_rate_section(wide, derived, ends, wide, 0, MIXES[0], writer(first))
    derive_planes(first, derived, 0, planes - 2)
    other, along_z, rim_second = rim_section(rim_first, [rim[f] for f in range(5)], MIXES[1])
    to_ends(other[0:2], 3, 8, 0, cells_x, ends)
    lamb(derived, ends, 2, cells_x, lamb_rows)
    project(lamb_rows, pair, spread, send, 0)
    to_ends(along_z, 2, 16, -1, cells_x + 1, ends)
    flow_rate_section(first, derived, ends, wide, 1, MIXES[1], writer(second))
    derive_planes(second, derived, 0, planes - 4)
    other, along_z, _ = rim_section(rim_second, None, None)
    to_ends(other[0:2], 3, 8, 0, cells_x, ends)
    lamb(derived, ends, 1, cells_x, lamb_rows)
    project(lamb_rows, pair, spread, send, size)
    send[:, 2 * size :] = labels[...]
    to_ends(along_z, 2, 8, 0, cells_x, ends_out)


def flow_last_body(second, derived, ends, wide, out):
    flow_rate_section(second, derived, ends, wide, 2, MIXES[2], writer(out), inner=True)


def faces_out(state, rear, front):
    lane = lax.broadcasted_iota(jnp.int32, (32, 128), 1) // 16
    for c in range(4):
        front[c * 8 : c * 8 + 8] = state[c, 56:64]
        rear[c * 8 : c * 8 + 8] = state[c, 0:8]
        front[32 + c * 8 : 40 + c * 8] = state[c, pl.ds(7, 8, stride=8), :]
        rear[32 + c * 8 : 40 + c * 8] = state[c, pl.ds(0, 8, stride=8), :]
    rows = state[...].reshape(256, 128)
    last = jnp.zeros((32, 128), F32)
    first = jnp.zeros((32, 128), F32)
    for j in range(8):
        piece = rows[j * 32 : j * 32 + 32]
        last = jnp.where(lane == j, pltpu.roll(piece, (j * 16 + 16) % 128, 1), last)
        first = jnp.where(lane == j, pltpu.roll(piece, j * 16, 1) if j else piece, first)
    front[64:96] = last
    rear[64:96] = first


def faces_sent(odd, state, message_a, message_b):
    size = message_a.shape[0]
    faces_out(state, message_b, message_a)
    message_a[...], message_b[0:size] = paired(odd, message_a[...], message_b[0:size])
    message_b[size:] = jnp.zeros((message_b.shape[0] - size, 128), F32)


def lift(total, before, after, sides, factor):
    def place(face, rows, target):
        value = factor * dot_exact_right(rows, sides[face])
        for c in range(4):
            total[c, target, :] += value[c * 8 : c * 8 + 8]

    place(0, before[0:32], pl.ds(0, 8))
    place(1, after[0:32], pl.ds(56, 8))
    place(2, before[32:64], pl.ds(0, 8, stride=8))
    place(3, after[32:64], pl.ds(7, 8, stride=8))


def rate_local(state, deriv_rows, deriv_lanes, speed, sides):
    fields = [state[c] for c in range(4)]
    by_rows = dot_three(deriv_rows[...], jnp.concatenate(fields[0:3], 1))
    by_lanes = dot_three(jnp.concatenate([fields[0], fields[3]], 0), deriv_lanes[...])
    divergence = by_rows[0:64, 128:256] + by_rows[64:128, 256:384] + by_lanes[64:128]
    rates = [
        -(speed[...] * speed[...]) * divergence,
        -by_rows[0:64, 0:128],
        -by_rows[64:128, 0:128],
        -by_lanes[0:64],
    ]
    row = lax.broadcasted_iota(jnp.int32, (64, 128), 0)
    lane = lax.broadcasted_iota(jnp.int32, (64, 128), 1)
    count = jnp.zeros((64, 128), F32)
    for value in (row // 8, row % 8, lane // 16):
        count = count + jnp.where((value == 0) | (value == 7), PENALTY, 0.0)
    side = PENALTY * dot_exact_right(state[...].reshape(256, 128), sides[4])
    return [rates[c] - count * fields[c] + side[c * 64 : c * 64 + 64] for c in range(4)]


def acoustic_local_body(mix, state, start, deriv_rows, deriv_lanes, speed, sides, out, front, rear):
    rates = rate_local(state, deriv_rows, deriv_lanes, speed, sides)
    for c in range(4):
        value = state[c] + TIME_STEP * rates[c]
        if mix[0] != 0.0:
            value = mix[0] * start[c] + mix[1] * value
        out[c] = value
    faces_out(state, rear, front)
    lift(out, front, rear, sides, TIME_STEP * mix[1] * PENALTY)


def acoustic_start_body(given, _, state, message_a, message_b, turned, stored):
    count = given.shape[0]
    for e in range(count):
        for t in range(4):
            stored[t, 4 * e : 4 * e + 4] = given[e, :, t * 128 : t * 128 + 128]
    for t in range(4):
        rows = [stored[t, pl.ds(c, count, stride=4), :] for c in range(4)]
        rows = jnp.concatenate(rows + [jnp.zeros((128 - 4 * count, 128), F32)], 0)
        turned[t * 128 : t * 128 + 128] = rows.T
    lane = lax.broadcasted_iota(jnp.int32, (64, 128), 1) // count
    fields = [jnp.zeros((64, 128), F32)] * 4
    for z in range(8):
        piece = turned[pl.ds(z, 64, stride=8), :]
        for c in range(4):
            move = (z - c) * count % 128
            fields[c] = jnp.where(lane == z, pltpu.roll(piece, move, 1) if move else piece, fields[c])
    for c in range(4):
        state[c] = fields[c]
    faces_sent(is_odd("fz"), state, message_a, message_b)


def natural_order(state, out, turned, stored):
    count = out.shape[0]
    lane = lax.broadcasted_iota(jnp.int32, (64, 128), 1) // count
    for z in range(8):
        value = jnp.zeros((64, 128), F32)
        for c in range(4):
            move = (c - z) * count % 128
            value = jnp.where(lane == c, pltpu.roll(state[c], move, 1) if move else state[c], value)
        turned[pl.ds(z, 64, stride=8), :] = value
    for t in range(4):
        rows = turned[t * 128 : t * 128 + 128].T
        for c in range(4):
            stored[t, pl.ds(c, count, stride=4), :] = rows[c * count : c * count + count]
    for e in range(count):
        for t in range(4):
            out[e, :, t * 128 : t * 128 + 128] = stored[t, 4 * e : 4 * e + 4]


def remote_part(out, before, after, sides_far, factor):
    lift(out, before, after, sides_far, factor)
    lane = lax.broadcasted_iota(jnp.int32, (32, 128), 1) // 16
    last, first = before[64:96], after[64:96]
    pieces = []
    for j in range(8):
        left = pltpu.roll(last, 128 - j * 16, 1) if j else last
        right = pltpu.roll(first, (144 - j * 16) % 128, 1) if j != 1 else first
        pieces.append(jnp.where(lane == 0, left, jnp.where(lane == 1, right, 0.0)))
    value = factor * dot_exact_right(jnp.concatenate(pieces, 0), sides_far[4])
    for c in range(4):
        out[c] += value[c * 64 : c * 64 + 64]


def acoustic_far_body(mix, kind, partial, got_a, got_b, sides_far, received, *refs):
    if kind == "last":
        given_out, before, after, out, turned, stored = refs
    elif kind == "first":
        _, out, message_a, message_b, before, after, source = refs
        place_body(received, source)
        received = source
    else:
        out, message_a, message_b, before, after = refs
    odd = is_odd("fz")
    after[...], before[...] = paired(odd, got_a[0:96], got_b[0:96])
    out[0] = partial[0]
    for c in range(3):
        out[1 + c] = partial[1 + c] + (TIME_STEP * mix[1]) * received[c]
    remote_part(out, before, after, sides_far, TIME_STEP * mix[1] * PENALTY)
    if kind == "last":
        natural_order(out, given_out, turned, stored)
    else:
        faces_sent(odd, out, message_a, message_b)


def place_body(received, *outs):
    peers, size = received.shape[0], received.shape[1]
    fold = 192 * len(outs) // (size - 8)
    height = 64 // fold
    target = lax.broadcasted_iota(jnp.int32, (128, 128), 0)
    lane = lax.broadcasted_iota(jnp.int32, (128, 128), 1)
    total = None
    for peer in range(peers):
        label = received[peer, size - 8 : size - 7, :]
        label = jnp.broadcast_to(label, (128, 128)).astype(jnp.int32)
        hit = (label == target % 16) & (lane % 8 == target // 16)
        chosen = [jnp.where(hit & (lane // (128 // fold) == g), 1.0, 0.0) for g in range(fold)]
        chosen = jnp.concatenate(chosen, 0).astype(BF16)
        high, low = parts(received[peer, 0 : size - 8])
        dims = (((1,), (1,)), ((), ()))
        value = lax.dot_general(high, chosen, dims, preferred_element_type=F32)
        value = value + lax.dot_general(low, chosen, dims, preferred_element_type=F32)
        total = value if total is None else total + value
    for k, out in enumerate(outs):
        for c in range(3):
            for g in range(fold):
                at = (k * 3 + c) * height
                out[c, g * height : g * height + height] = total[at : at + height, g * 128 : g * 128 + 128]


def kron_part(matrix, shape, rows_by, columns_by):
    row = lax.broadcasted_iota(jnp.int32, (shape[0], 8), 0)
    level = lax.broadcasted_iota(jnp.int32, (shape[0], 8), 1)
    left = (row // rows_by % 8 == level).astype(F32)
    level = lax.broadcasted_iota(jnp.int32, (8, shape[1]), 0)
    column = lax.broadcasted_iota(jnp.int32, (8, shape[1]), 1)
    right = (column // columns_by % 8 == level).astype(F32)
    return dot_full(dot_full(left, matrix), right)


def tables_body(
    packed,
    near,
    far,
    deriv_rows,
    deriv_lanes,
    pair,
    spread,
    labels,
    speed,
):
    size = near.shape[1]
    count = size // 8
    blocks = spread.shape[0] // 8

    def place_of(shape):
        return (lax.broadcasted_iota(jnp.int32, shape, 0), lax.broadcasted_iota(jnp.int32, shape, 1))

    row, column = place_of((count, size))
    repeat = (column % count == row).astype(F32)
    speed[...] = dot_full(packed[24:25, 0:count], repeat)
    wanted = dot_full(packed[16:24, 0:count], repeat).astype(jnp.int32)
    row, column = place_of((size, size))
    level, element = row // count, row % count
    level_out = column // count
    for facet in range(4):
        shift = -count if facet % 2 == 0 else count
        choice = jnp.broadcast_to(wanted[facet : facet + 1], (size, size))
        near[facet] = jnp.where((level == level_out) & (element == choice), 1.0, 0.0).astype(BF16)
        far[facet] = jnp.where((level == level_out) & (element + shift == choice), 1.0, 0.0).astype(BF16)
    lower = jnp.broadcast_to(wanted[4:5], (size, size))
    upper = jnp.broadcast_to(wanted[5:6], (size, size))
    hit = (level == 7) & (level_out == 0) & (element == lower)
    hit = hit | ((level == 0) & (level_out == 7) & (element == upper))
    near[4] = jnp.where(hit, 1.0, 0.0).astype(BF16)
    hit = (level == 0) & (level_out == 0) & (element - count == lower)
    hit = hit | ((level == 1) & (level_out == 7) & (element + count == upper))
    far[4] = jnp.where(hit, 1.0, 0.0).astype(BF16)

    row, column = place_of((64, 64))
    slopes, modes = packed[0:8, 0:8], packed[8:16, 0:8]
    outer = kron_part(slopes, (64, 64), 8, 8)
    inner = kron_part(slopes, (64, 64), 1, 1)
    deriv_rows[0:64] = jnp.where(row % 8 == column % 8, outer, 0.0)
    deriv_rows[64:128] = jnp.where(row // 8 == column // 8, inner, 0.0)
    row, column = place_of((size, size))
    lanes = kron_part(slopes.T, (size, size), count, count)
    deriv_lanes[...] = jnp.where(row % count == column % count, lanes, 0.0)
    pair[...] = kron_part(modes, (64, 64), 8, 8) * kron_part(modes, (64, 64), 1, 1)

    peers = labels.shape[0]
    capacity = capacity_of(peers, blocks)
    row, column = place_of((blocks, blocks))

    def upright(values):
        return jnp.sum(jnp.where(row == column, values, 0.0), 1, keepdims=True)

    owner_row = packed[25:26, 0:blocks]
    owner_column = upright(owner_row)
    earlier = (owner_column == owner_row) & (column < row)
    position = jnp.sum(jnp.where(earlier, 1.0, 0.0), 1, keepdims=True)
    slot = owner_column * capacity + position
    element_column = upright(packed[26:27, 0:blocks])
    row, column = place_of((8 * blocks, blocks))
    repeat = (row // 8 == column).astype(F32)
    slot = dot_full(repeat, jnp.broadcast_to(slot, (blocks, 128)))
    element = dot_full(repeat, jnp.broadcast_to(element_column, (blocks, 128)))
    row, column = place_of((8 * blocks, 128))
    values = kron_part(modes.T, (8 * blocks, 128), 1, 1)
    inside = column % (8 * capacity) // 8
    for peer in range(peers):
        chosen = slot == (inside + peer * capacity).astype(F32)
        spread[:, peer * 128 : peer * 128 + 128] = jnp.where(chosen, values, 0.0)
        named = jnp.where(chosen & (row % 8 == 0), element + 1.0, 0.0)
        labels[peer] = jnp.broadcast_to(jnp.sum(named, 0, keepdims=True) - 1.0, (8, 128))


def shifted(sizes, shifts):
    pairs = []
    for index in np.ndindex(*sizes):
        source = [(i + s) % n for i, s, n in zip(index, shifts, sizes)]
        pairs.append((int(np.ravel_multi_index(source, sizes)), int(np.ravel_multi_index(index, sizes))))
    return pairs


def partners(sizes, axis, second):
    pairs = []
    for index in np.ndindex(*sizes):
        source = list(index)
        step = 1 if (index[axis] % 2 == 0) != second else -1
        source[axis] = (index[axis] + step) % sizes[axis]
        pairs.append((int(np.ravel_multi_index(source, sizes)), int(np.ravel_multi_index(index, sizes))))
    return pairs


def per_device(
    density,
    velocity,
    pressure,
    acoustic,
    sound_speed,
    derivative,
    mode_basis,
    neighbours,
    block_owner,
    block_element,
):
    size_x, size_y, size_z = lax.axis_size("fx"), lax.axis_size("fy"), lax.axis_size("fz")
    devices = size_x * size_y * size_z
    cells_x = density.shape[0]
    elements = acoustic.shape[0]
    device = lax.axis_index(("fx", "fy", "fz"))

    names = ("fx", "fy", "fz")

    rows = 5 * cells_x * 8
    tiles = -(-rows // 128)
    square = velocity[0] * velocity[0] + velocity[1] * velocity[1] + velocity[2] * velocity[2]
    energy = pressure / (HEAT_RATIO - 1.0) + 0.5 * density * square
    rest = ((0, 0), (0, 0), (0, 0))
    state = jnp.pad(density[None], ((0, 4),) + rest) + jnp.pad(density * velocity, ((1, 1),) + rest)
    state = state + jnp.pad(energy[None], ((4, 0),) + rest)
    x_rows = 5 * 2 * HALO * 8
    flow_a, flow_b, along_x = call(
        pack_start_body, [(tiles * 8, 128), (tiles * 8, 128), (x_rows, 128)], state
    )
    edge_a = lax.ppermute(flow_a, "fz", partners((size_z,), 0, False))
    edge_b = lax.ppermute(flow_b, "fz", partners((size_z,), 0, True))
    x_steps = (1,) if size_x == 2 else (1, -1)
    beside_x = [lax.ppermute(along_x, "fx", shifted((size_x,), (step,))) for step in x_steps]

    near_pairs = [(i ^ 1, i) for i in range(devices)]
    far_pairs = [pair for i in range(1, devices - 1, 2) for pair in ((i, i + 1), (i + 1, i))]

    def traces(to_a, to_b):
        far_got = lax.ppermute(to_b, names, far_pairs)
        return lax.ppermute(to_a, names, near_pairs), far_got

    size = 8 * elements
    held = (4, 64, size)
    faces = (96, size)
    sides = [pltpu.VMEM(faces, F32)] * 2
    turning = [pltpu.VMEM((512, 128), F32), pltpu.VMEM((4, 4 * elements, 128), F32)]
    sound, to_a, to_b = call(
        acoustic_start_body,
        [held, faces, (2 * faces[0], size)],
        acoustic,
        edge_a,
        scratch=turning,
        last=1,
    )
    got_a, got_b = traces(to_a, to_b)

    edge = call(
        pack_next_body,
        [(40, 128)],
        state,
        flow_a,
        flow_b,
        edge_a,
        edge_b,
        got_a,
        last=1,
    )[0]
    edges_x = [lax.ppermute(edge, "fx", shifted((size_x,), (step,))) for step in x_steps]
    y_shape = (5 * cells_x * HALO + 48, 128)
    y_a, y_b = call(pack_last_body, [y_shape, y_shape], state, edge, *beside_x, *edges_x, cost=1)
    y_second = lax.ppermute(y_b, "fy", partners((size_y,), 0, True))
    y_first = lax.ppermute(y_a, "fy", partners((size_y,), 0, False))

    local = (neighbours - device * elements).T
    blocks = block_owner.size
    width = max(elements, blocks)

    def piece(values, first):
        values = values.astype(F32)
        return jnp.pad(values, ((first, 32 - first - values.shape[0]), (0, width - values.shape[1])))

    packed = (
        piece(derivative, 0)
        + piece(mode_basis, 8)
        + piece(local, 16)
        + piece(sound_speed.reshape(1, elements), 24)
        + piece(block_owner.reshape(1, blocks), 25)
        + piece(block_element.reshape(1, blocks), 26)
    )
    table = jax.ShapeDtypeStruct((5, size, size), BF16)
    near, far, deriv_rows, deriv_lanes, pair, spread, labels, speed = call(
        tables_body,
        [
            table,
            table,
            (128, 64),
            (size, size),
            (64, 64),
            (8 * blocks, size_y * 128),
            (size_y, 8, 128),
            (1, size),
        ],
        packed,
        cost=1,
    )

    fold = fold_of(size_y, blocks)
    wide = cells_x + 2 * HALO
    rows_scratch = pltpu.VMEM((3, 64, 128), F32)

    def planes(count):
        return (5, count, 16, 128)

    def route(send):
        return lax.all_to_all(send, "fy", split_axis=0, concat_axis=0, tiled=True)

    start, rim, send = call(
        functools.partial(flow_sources_body, len(beside_x)),
        [planes(wide), (5, 16, 256), (size_y, 192 // fold + 8, 128)],
        state,
        edge,
        *beside_x,
        *edges_x,
        y_first,
        y_second,
        pair,
        spread,
        labels,
        got_b,
        last=1,
        scratch=[
            pltpu.VMEM((3, wide, 16, 128), F32),
            rows_scratch,
            pltpu.VMEM((2, cells_x, 8, 128), F32),
            pltpu.VMEM(y_shape, F32),
            pltpu.VMEM(y_shape, F32),
        ],
    )
    received = route(send)
    second, derived, ends, send = call(
        flow_stages_body,
        [
            planes(wide - 4),
            planes(wide),
            (5, cells_x, 8, 128),
            (size_y, 2 * 192 // fold + 8, 128),
        ],
        start,
        rim,
        pair,
        spread,
        labels,
        scratch=[rows_scratch, pltpu.VMEM(planes(wide - 2), F32), pltpu.VMEM(planes(wide - 2), F32)],
    )

    def local_part(mix, now):
        return call(
            functools.partial(acoustic_local_body, mix),
            [held],
            now,
            sound,
            deriv_rows,
            deriv_lanes,
            speed,
            near,
            scratch=sides,
            cost=1,
        )[0]

    partial = local_part(MIXES[0], sound)
    sound_one, to_a, to_b = call(
        functools.partial(acoustic_far_body, MIXES[0], "first"),
        [held, faces, (faces[0] + 32, size)],
        partial,
        got_a,
        got_b,
        far,
        received,
        send,
        scratch=sides + [rows_scratch],
        last=1,
    )
    source_two, source_three = call(place_body, [(3, 64, 128)] * 2, route(send))
    got_a, got_b = traces(to_a, to_b)
    flow_state = call(flow_last_body, [(5, cells_x, 8, 128)], second, derived, ends, start)[0]
    partial = local_part(MIXES[1], sound_one)
    sound_two, to_a, to_b = call(
        functools.partial(acoustic_far_body, MIXES[1], "second"),
        [held, faces, (faces[0] + 32, size)],
        partial,
        got_a,
        got_b,
        far,
        source_two,
        scratch=sides,
    )
    got_a, got_b = traces(to_a, to_b)
    partial = local_part(MIXES[2], sound_two)
    sound_state = call(
        functools.partial(acoustic_far_body, MIXES[2], "last"),
        [(elements, 4, 512)],
        partial,
        got_a,
        got_b,
        far,
        source_three,
        scratch=sides + [pltpu.VMEM(held, F32)] + turning,
    )[0]
    return (flow_state, sound_state)


def solution(mesh):
    placed = (
        P("fx", "fy", "fz"),
        P(None, "fx", "fy", "fz"),
        P("fx", "fy", "fz"),
        P(("fx", "fy", "fz"), None, None),
        P(("fx", "fy", "fz")),
        P(),
        P(),
        P(("fx", "fy", "fz"), None),
        P("fx", "fy", "fz", None, None),
        P("fx", "fy", "fz", None),
    )
    return jax.shard_map(
        per_device,
        mesh=mesh,
        in_specs=placed,
        out_specs=(P(None, "fx", "fy", "fz"), P(("fx", "fy", "fz"), None, None)),
        check_vma=False,
    )
```

```python
import functools

import jax
import jax.numpy as jnp
import numpy as np
from jax import lax
from jax.experimental import pallas as pl
from jax.experimental.pallas import tpu as pltpu
from jax.sharding import PartitionSpec as P

HEAT_RATIO = 1.4
TIME_STEP = 0.1
VISCOSITY = 0.05
PENALTY = 0.5
HALO = 3
F32 = jnp.float32
BF16 = jnp.bfloat16
PARAMS = pltpu.CompilerParams(vmem_limit_bytes=24 * 1024 * 1024)
MIXES = ((0.0, 1.0), (0.75, 0.25), (1.0 / 3.0, 2.0 / 3.0))


def parts(values):
    high = values.astype(BF16)
    return high, (values - high.astype(F32)).astype(BF16)


def dot(left, right):
    return lax.dot_general(left, right, (((1,), (0,)), ((), ())), preferred_element_type=F32)


def dot_three(left, right):
    left_high, left_low = parts(left)
    right_high, right_low = parts(right)
    return dot(left_high, right_high) + dot(left_high, right_low) + dot(left_low, right_high)


def dot_full(left, right, dims=((1,), (0,))):
    return lax.dot_general(
        left, right, (dims, ((), ())), precision=lax.Precision.HIGHEST, preferred_element_type=F32
    )


def dot_exact_right(left, right):
    left_high, left_low = parts(left)
    return dot(left_high, right) + dot(left_low, right)


def call(body, outs, *operands, scratch=(), last=0, cost=None):
    whole = pl.BlockSpec(memory_space=pltpu.VMEM)
    outs = [out if isinstance(out, jax.ShapeDtypeStruct) else jax.ShapeDtypeStruct(out, F32) for out in outs]
    anywhere = pl.BlockSpec(memory_space=pl.ANY)
    return pl.pallas_call(
        body,
        out_shape=outs,
        in_specs=[whole] * (len(operands) - last) + [anywhere] * last,
        out_specs=[whole] * len(outs),
        scratch_shapes=list(scratch),
        compiler_params=PARAMS,
        cost_estimate=None if cost is None else pl.CostEstimate(flops=cost, bytes_accessed=cost, transcendentals=0),
    )(*operands)


def capacity_of(peers, blocks):
    return max(2, 2 * blocks // peers)


def fold_of(peers, blocks):
    return 128 // (8 * capacity_of(peers, blocks))


def is_odd(axis):
    return lax.axis_index(axis) % 2 == 1


def paired(odd, to_next, to_last):
    return jnp.where(odd, to_last, to_next), jnp.where(odd, to_next, to_last)


def pack_start_body(state, message_a, message_b, along_x, y_a, y_b):
    odd = is_odd("fz")
    rows = state[...].reshape(-1, 128)
    count = rows.shape[0]
    for tile in range(message_a.shape[0] // 8):
        piece = rows[tile * 128 : min(count, tile * 128 + 128)]
        if piece.shape[0] < 128:
            piece = jnp.concatenate([piece, jnp.zeros((128 - piece.shape[0], 128), F32)], 0)
        turned = piece.T
        first, second = paired(odd, turned[120:128], turned[0:8])
        message_a[tile * 8 : tile * 8 + 8] = first
        message_b[tile * 8 : tile * 8 + 8] = second
    cells_x = state.shape[1]
    for f in range(5):
        for s, x in enumerate(x_planes(cells_x)):
            at = (f * 2 * HALO + s) * 8
            along_x[at : at + 8] = state[f, x]
        for x in range(cells_x):
            put_rows(y_a, y_b, (f * cells_x + x) * HALO, state[f, x], HALO)


def put_rows(message_a, message_b, at, values, height):
    first, second = paired(is_odd("fy"), values[8 - height : 8], values[0:height])
    message_a[at : at + height] = first
    message_b[at : at + height] = second


def pack_next_body(state, sent_a, sent_b, got_a, got_b, faces, _, edge, far_faces):
    far_faces[...] = faces[...]
    cells_x = state.shape[1]
    odd_z = is_odd("fz")
    high, low = paired(odd_z, sent_a[...], sent_b[...])
    above, below = paired(odd_z, got_a[...], got_b[...])
    row = lax.broadcasted_iota(jnp.int32, (8, 128), 0)
    x_of_lane = lax.broadcasted_iota(jnp.int32, (16, 128), 1) // 8 % cells_x
    for tile in range(high.shape[0] // 8):
        rows = slice(tile * 8, tile * 8 + 8)
        upper = jnp.where(row < 3, pltpu.roll(high[rows], 3, 0), pltpu.roll(above[rows], 3, 0))
        lower = jnp.where(row < 3, pltpu.roll(below[rows], 3, 0), pltpu.roll(low[rows], 3, 0))
        slots = jnp.concatenate([upper, lower], 0)
        spread = jnp.concatenate([jnp.where(x_of_lane == x, slots, 0.0) for x in range(8)], 0).T
        for half in range(16 // cells_x):
            f = tile * (16 // cells_x) + half
            if f < 5:
                at = half * cells_x * 8
                total = spread[at : at + 8]
                for x in range(1, cells_x):
                    total = total + spread[at + x * 8 : at + x * 8 + 8]
                edge[f * 8 : f * 8 + 8] = total


def x_planes(cells_x):
    return [cells_x - HALO + i for i in range(HALO)] + list(range(HALO))


def sides_of(beside_x):
    return beside_x[0], beside_x[-1]


def beyond(edges_x, f):
    after, before = sides_of(edges_x)
    at = f * 8
    if after is before:
        return after[at : at + 8]
    lane = lax.broadcasted_iota(jnp.int32, (8, 128), 1)
    return jnp.where(lane < 64, after[at : at + 8], before[at : at + 8])


def pack_last_body(edge, *refs):
    (y_a, y_b), refs = refs[-2:], refs[:-2]
    beside_x, edges_x = refs[: len(refs) // 2], refs[len(refs) // 2 :]
    after, before = sides_of(beside_x)
    for f in range(5):
        at = f * 6
        for slot, height in ((1, 1), (2, 2), (3, 2), (4, 1)):
            source = (f * 2 * HALO + slot) * 8
            values = (before if slot < HALO else after)[source : source + 8]
            put_rows(y_a, y_b, at, values, height)
            at += height
        put_rows(y_a, y_b, 30 + f * 2, edge[f * 8 : f * 8 + 8], 2)
        put_rows(y_a, y_b, 40 + f, beyond(edges_x, f), 1)


def assemble(wide, state, beside_x, above, below):
    cells_x = state.shape[1]
    after, before = sides_of(beside_x)
    for f in range(5):
        for x in range(cells_x):
            wide[f, HALO + x, 0:8] = state[f, x]
            at = (f * cells_x + x) * HALO
            wide[f, HALO + x, 8 : 8 + HALO] = above[at : at + HALO]
            wide[f, HALO + x, 16 - HALO : 16] = below[at : at + HALO]
        for slot in range(2 * HALO):
            plane = slot if slot < HALO else cells_x + slot
            at = (f * 2 * HALO + slot) * 8
            wide[f, plane, 0:8] = (before if slot < HALO else after)[at : at + 8]


def assemble_rest(wide, rim, edge, edges_x, above, below):
    cells_x = wide.shape[1] - 2 * HALO
    for f in range(5):
        at = f * 6
        for slot, height in ((1, 1), (2, 2), (3, 2), (4, 1)):
            plane = slot if slot < HALO else cells_x + slot
            wide[f, plane, 8 : 8 + height] = above[at : at + height]
            wide[f, plane, 16 - height : 16] = below[at : at + height]
            at += height
        rim[f, 0:8, 0:128] = edge[f * 8 : f * 8 + 8]
        rim[f, 0:8, 128:256] = beyond(edges_x, f)
        at = 30 + f * 2
        rim[f, 8:10, 0:128] = above[at : at + 2]
        rim[f, 14:16, 0:128] = below[at : at + 2]
        at = 40 + f
        rim[f, 8:9, 128:256] = above[at : at + 1]
        rim[f, 15:16, 128:256] = below[at : at + 1]


def primitive(rho, mx, my, mz, energy):
    inverse = 1.0 / rho
    u, v, w = mx * inverse, my * inverse, mz * inverse
    p = (HEAT_RATIO - 1.0) * (energy - 0.5 * (mx * u + my * v + mz * w))
    return u, v, w, p, jnp.sqrt(HEAT_RATIO * jnp.abs(p) * inverse)


def chunks(first, last, size):
    return [(i, min(i + size, last)) for i in range(first, last, size)]


def derive_planes(wide, derived, first, last):
    for i, j in chunks(first, last, 4):
        for k, value in enumerate(primitive(*[wide[f, i:j] for f in range(5)])):
            derived[k, i:j] = value


def derive_speeds(wide, derived, first, last):
    for i, j in chunks(first, last, 5):
        inverse = 1.0 / wide[0, i:j]
        for k in range(3):
            derived[k, i:j] = wide[1 + k, i:j] * inverse


def with_flux(fields, other, along):
    speed, p = other[along], other[3]
    out = [fields[1 + along]]
    for k in range(3):
        value = fields[1 + k] * speed
        out.append(value + p if k == along else value)
    out.append((fields[4] + p) * speed)
    return fields, out, jnp.abs(speed) + other[4]


def face(left, right):
    (fields_l, flux_l, speed_l), (fields_r, flux_r, speed_r) = left, right
    speed = jnp.maximum(speed_l, speed_r)
    viscous = speed + 2.0 * VISCOSITY
    return [
        (flux_l[f] + flux_r[f]) - (viscous if 1 <= f <= 3 else speed) * (fields_r[f] - fields_l[f])
        for f in range(5)
    ]


def rolled(here, shift, axis):
    fields, flux, speed = here
    return (
        [pltpu.roll(a, shift, axis) for a in fields],
        [pltpu.roll(a, shift, axis) for a in flux],
        pltpu.roll(speed, shift, axis),
    )


def rim_section(fields, start, mix):
    other = primitive(*fields)
    here = with_flux(fields, other, 2)
    along_z = face(here, rolled(here, 255, 1))
    if mix is None:
        return other, along_z, None
    total = [g - pltpu.roll(g, 1, 1) for g in along_z]
    for along, step, axis, size in ((0, 16, 1, 256), (1, 1, 0, 16)):
        here = with_flux(fields, other, along)
        faces = face(here, rolled(here, size - step, axis))
        total = [total[f] + (faces[f] - pltpu.roll(faces[f], step, axis)) for f in range(5)]
    out = []
    for f in range(5):
        value = fields[f] - (0.5 * TIME_STEP) * total[f]
        out.append(mix[0] * start[f] + mix[1] * value if mix[0] != 0.0 else value)
    return other, along_z, out


def to_ends(values, after, rows, first, last, ends):
    slot = lax.broadcasted_iota(jnp.int32, (rows, 256), 1) % 16
    for f, value in enumerate(values):
        value = value[0:rows]
        value = jnp.where(slot == 9, pltpu.roll(value, 9 - after, 1), value)
        for x in range(first, last):
            at = x % 16 // 8 * 128
            move = (118 - x % 8 * 16) % 128
            tile = value[:, at : at + 128]
            ends[f, x - first, 0:rows] = pltpu.roll(tile, move, 1) if move else tile


def flow_rate_section(wide, derived, ends, start, offset, mix, write, inner=False):
    depth = wide.shape[1]
    rows = slice(0, 8) if inner else slice(None)
    size = 4 if inner else 2

    def planes(i, j, kept, along):
        fields = [wide[f, i:j, kept] for f in range(5)]
        return with_flux(fields, [derived[f, i:j, kept] for f in range(5)], along)

    def cut(here, i, j):
        return [a[i:j] for a in here[0]], [a[i:j] for a in here[1]], here[2][i:j]

    for i, j in chunks(1, depth - 1, size):
        count = j - i
        lane = lax.broadcasted_iota(jnp.int32, (count, 8 if inner else 16, 128), 2)
        here = planes(i - 1, j + 1, rows, 0)
        faces = face(cut(here, 0, count + 1), cut(here, 1, count + 2))
        total = [g[1:] - g[:-1] for g in faces]
        here = planes(i, j, slice(None), 1)
        faces = face(here, rolled(here, 15, 1))
        for f in range(5):
            change = faces[f] - pltpu.roll(faces[f], 1, 1)
            total[f] = total[f] + (change[:, 0:8] if inner else change)
        here = planes(i, j, rows, 2)
        faces = face(here, rolled(here, 127, 2))
        for f in range(5):
            end = ends[f, i - 1 : j - 1, rows]
            value = jnp.where(lane == 127, end, faces[f])
            total[f] = total[f] + (value - jnp.where(lane == 0, end, pltpu.roll(value, 1, 2)))
        for f in range(5):
            value = wide[f, i:j, rows] - (0.5 * TIME_STEP) * total[f]
            if mix[0] != 0.0:
                value = mix[0] * start[f, i + offset : j + offset, rows] + mix[1] * value
            write(slice(i - 1, j - 1), f, value)


def lamb(derived, ends, first, cells_x, lamb_rows):
    for i, j in chunks(first, first + cells_x, 4):
        count = j - i
        lane = lax.broadcasted_iota(jnp.int32, (count, 8, 128), 2)
        vel = [derived[c, i:j, 0:8] for c in range(3)]
        along_x = [derived[c, i + 1 : j + 1, 0:8] - derived[c, i - 1 : j - 1, 0:8] for c in range(3)]
        along_y = []
        for c in range(3):
            column = derived[c, i:j]
            along_y.append((pltpu.roll(column, 15, 1) - pltpu.roll(column, 1, 1))[:, 0:8])
        along_z = []
        for c in range(2):
            end = ends[c, i - first : j - first, 0:8]
            after = jnp.where(lane == 127, end, pltpu.roll(vel[c], 127, 2))
            along_z.append(after - jnp.where(lane == 0, end, pltpu.roll(vel[c], 1, 2)))
        curl = [
            0.5 * (along_y[2] - along_z[1]),
            0.5 * (along_z[0] - along_x[2]),
            0.5 * (along_x[1] - along_y[0]),
        ]
        at = slice((i - first) * 8, (j - first) * 8)
        lamb_rows[0, at] = (curl[1] * vel[2] - curl[2] * vel[1]).reshape(count * 8, 128)
        lamb_rows[1, at] = (curl[2] * vel[0] - curl[0] * vel[2]).reshape(count * 8, 128)
        lamb_rows[2, at] = (curl[0] * vel[1] - curl[1] * vel[0]).reshape(count * 8, 128)


def project(lamb_rows, pair, spread, send, base):
    peers = send.shape[0]
    fold = fold_of(peers, spread.shape[0] // 8)
    height = 64 // fold
    group = lax.broadcasted_iota(jnp.int32, (height, 128), 1) // (128 // fold)
    modes = dot_three(pair[...], jnp.concatenate([lamb_rows[c] for c in range(3)], 1))
    modes = jnp.concatenate([modes[:, c * 128 : c * 128 + 128] for c in range(3)], 0)
    sent = dot_three(modes, spread[...])
    for c in range(3):
        for peer in range(peers):
            mine = sent[c * 64 : c * 64 + 64, peer * 128 : peer * 128 + 128]
            folded = mine[0:height]
            for g in range(1, fold):
                folded = jnp.where(group == g, mine[g * height : g * height + height], folded)
            send[peer, base + c * height : base + c * height + height] = folded


def flow_sources_body(count, state, edge, *refs):
    beside_x, refs = refs[:count], refs[count:]
    got_a, got_b, pair, spread, labels, _ = refs[:6]
    wide, send, derived, lamb_rows, ends, above, below = refs[6:]
    cells_x = state.shape[1]
    above[...], below[...] = paired(is_odd("fy"), got_a[...], got_b[...])
    assemble(wide, state, beside_x, above, below)
    derive_speeds(wide, derived, HALO - 1, HALO + cells_x + 1)
    inverse = 1.0 / edge[0:8]
    speeds = [jnp.concatenate([edge[k * 8 : k * 8 + 8] * inverse] * 2, 1) for k in (1, 2)]
    to_ends(speeds, 3, 8, 0, cells_x, ends)
    lamb(derived, ends, HALO, cells_x, lamb_rows)
    project(lamb_rows, pair, spread, send, 0)
    send[:, send.shape[1] - 8 :] = labels[...]


def writer(target):
    def write(i, f, value):
        target[f, i] = value

    return write


def flow_stages_body(count, start, edge, *refs):
    edges_x, refs = refs[:count], refs[count:]
    got_a, got_b, pair, spread, labels, second, derived, ends_out, send, *refs = refs
    lamb_rows, ends, first, wide, rim, above, below = refs
    above[...], below[...] = paired(is_odd("fy"), got_a[...], got_b[...])
    wide[...] = start[...]
    assemble_rest(wide, rim, edge, edges_x, above, below)
    planes = wide.shape[1]
    cells_x = planes - 2 * HALO
    size = (send.shape[1] - 8) // 2
    rim_start = [rim[f] for f in range(5)]
    derive_planes(wide, derived, 0, planes)
    _, along_z, rim_first = rim_section(rim_start, None, MIXES[0])
    to_ends(along_z, 2, 16, -2, cells_x + 2, ends)
    flow_rate_section(wide, derived, ends, wide, 0, MIXES[0], writer(first))
    derive_planes(first, derived, 0, planes - 2)
    other, along_z, rim_second = rim_section(rim_first, [rim[f] for f in range(5)], MIXES[1])
    to_ends(other[0:2], 3, 8, 0, cells_x, ends)
    lamb(derived, ends, 2, cells_x, lamb_rows)
    project(lamb_rows, pair, spread, send, 0)
    to_ends(along_z, 2, 16, -1, cells_x + 1, ends)
    flow_rate_section(first, derived, ends, wide, 1, MIXES[1], writer(second))
    derive_planes(second, derived, 0, planes - 4)
    other, along_z, _ = rim_section(rim_second, None, None)
    to_ends(other[0:2], 3, 8, 0, cells_x, ends)
    lamb(derived, ends, 1, cells_x, lamb_rows)
    project(lamb_rows, pair, spread, send, size)
    send[:, 2 * size :] = labels[...]
    to_ends(along_z, 2, 8, 0, cells_x, ends_out)


def flow_last_body(second, derived, ends, wide, out):
    flow_rate_section(second, derived, ends, wide, 2, MIXES[2], writer(out), inner=True)


def faces_out(state, rear, front):
    lane = lax.broadcasted_iota(jnp.int32, (32, 128), 1) // 16
    for c in range(4):
        front[c * 8 : c * 8 + 8] = state[c, 56:64]
        rear[c * 8 : c * 8 + 8] = state[c, 0:8]
        front[32 + c * 8 : 40 + c * 8] = state[c, pl.ds(7, 8, stride=8), :]
        rear[32 + c * 8 : 40 + c * 8] = state[c, pl.ds(0, 8, stride=8), :]
    rows = state[...].reshape(256, 128)
    last = jnp.zeros((32, 128), F32)
    first = jnp.zeros((32, 128), F32)
    for j in range(8):
        piece = rows[j * 32 : j * 32 + 32]
        last = jnp.where(lane == j, pltpu.roll(piece, (j * 16 + 16) % 128, 1), last)
        first = jnp.where(lane == j, pltpu.roll(piece, j * 16, 1) if j else piece, first)
    front[64:96] = last
    rear[64:96] = first


def faces_sent(odd, state, message_a, message_b):
    size = message_a.shape[0]
    faces_out(state, message_b, message_a)
    message_a[...], message_b[0:size] = paired(odd, message_a[...], message_b[0:size])
    if message_b.shape[0] > size:
        message_b[size:] = jnp.zeros((message_b.shape[0] - size, 128), F32)


def lift(total, before, after, sides, factor):
    def place(face, rows, target):
        value = factor * dot_exact_right(rows, sides[face])
        for c in range(4):
            total[c, target, :] += value[c * 8 : c * 8 + 8]

    place(0, before[0:32], pl.ds(0, 8))
    place(1, after[0:32], pl.ds(56, 8))
    place(2, before[32:64], pl.ds(0, 8, stride=8))
    place(3, after[32:64], pl.ds(7, 8, stride=8))


def rate_local(state, deriv_rows, deriv_lanes, speed, sides):
    fields = [state[c] for c in range(4)]
    by_rows = dot_three(deriv_rows[...], jnp.concatenate(fields[0:3], 1))
    by_lanes = dot_three(jnp.concatenate([fields[0], fields[3]], 0), deriv_lanes[...])
    divergence = by_rows[0:64, 128:256] + by_rows[64:128, 256:384] + by_lanes[64:128]
    rates = [
        -(speed[...] * speed[...]) * divergence,
        -by_rows[0:64, 0:128],
        -by_rows[64:128, 0:128],
        -by_lanes[0:64],
    ]
    row = lax.broadcasted_iota(jnp.int32, (64, 128), 0)
    lane = lax.broadcasted_iota(jnp.int32, (64, 128), 1)
    count = jnp.zeros((64, 128), F32)
    for value in (row // 8, row % 8, lane // 16):
        count = count + jnp.where((value == 0) | (value == 7), PENALTY, 0.0)
    side = PENALTY * dot_exact_right(state[...].reshape(256, 128), sides[4])
    return [rates[c] - count * fields[c] + side[c * 64 : c * 64 + 64] for c in range(4)]


def acoustic_local_body(mix, state, start, deriv_rows, deriv_lanes, speed, sides, out, front, rear):
    rates = rate_local(state, deriv_rows, deriv_lanes, speed, sides)
    for c in range(4):
        value = state[c] + TIME_STEP * rates[c]
        if mix[0] != 0.0:
            value = mix[0] * start[c] + mix[1] * value
        out[c] = value
    faces_out(state, rear, front)
    lift(out, front, rear, sides, TIME_STEP * mix[1] * PENALTY)


def acoustic_start_body(given, _, state, message_a, message_b, turned, stored):
    count = given.shape[0]
    for e in range(count):
        for t in range(4):
            stored[t, 4 * e : 4 * e + 4] = given[e, :, t * 128 : t * 128 + 128]
    for t in range(4):
        rows = [stored[t, pl.ds(c, count, stride=4), :] for c in range(4)]
        rows = jnp.concatenate(rows + [jnp.zeros((128 - 4 * count, 128), F32)], 0)
        turned[t * 128 : t * 128 + 128] = rows.T
    lane = lax.broadcasted_iota(jnp.int32, (64, 128), 1) // count
    fields = [jnp.zeros((64, 128), F32)] * 4
    for z in range(8):
        piece = turned[pl.ds(z, 64, stride=8), :]
        for c in range(4):
            move = (z - c) * count % 128
            fields[c] = jnp.where(lane == z, pltpu.roll(piece, move, 1) if move else piece, fields[c])
    for c in range(4):
        state[c] = fields[c]
    faces_sent(is_odd("fz"), state, message_a, message_b)


def natural_order(state, out, turned, stored):
    count = out.shape[0]
    lane = lax.broadcasted_iota(jnp.int32, (64, 128), 1) // count
    for z in range(8):
        value = jnp.zeros((64, 128), F32)
        for c in range(4):
            move = (c - z) * count % 128
            value = jnp.where(lane == c, pltpu.roll(state[c], move, 1) if move else state[c], value)
        turned[pl.ds(z, 64, stride=8), :] = value
    for t in range(4):
        rows = turned[t * 128 : t * 128 + 128].T
        for c in range(4):
            stored[t, pl.ds(c, count, stride=4), :] = rows[c * count : c * count + count]
    for e in range(count):
        for t in range(4):
            out[e, :, t * 128 : t * 128 + 128] = stored[t, 4 * e : 4 * e + 4]


def remote_part(out, before, after, sides_far, factor):
    lift(out, before, after, sides_far, factor)
    lane = lax.broadcasted_iota(jnp.int32, (32, 128), 1) // 16
    last, first = before[64:96], after[64:96]
    pieces = []
    for j in range(8):
        left = pltpu.roll(last, 128 - j * 16, 1) if j else last
        right = pltpu.roll(first, (144 - j * 16) % 128, 1) if j != 1 else first
        pieces.append(jnp.where(lane == 0, left, jnp.where(lane == 1, right, 0.0)))
    value = factor * dot_exact_right(jnp.concatenate(pieces, 0), sides_far[4])
    for c in range(4):
        out[c] += value[c * 64 : c * 64 + 64]


def acoustic_far_body(mix, kind, partial, got_a, got_b, sides_far, received, *refs):
    if kind == "last":
        given_out, before, after, out, turned, stored = refs
    elif kind == "first":
        _, out, message_a, message_b, before, after, source = refs
        place_body(received, source)
        received = source
    else:
        out, message_a, message_b, before, after = refs
    odd = is_odd("fz")
    after[...], before[...] = paired(odd, got_a[0:96], got_b[0:96])
    out[0] = partial[0]
    for c in range(3):
        out[1 + c] = partial[1 + c] + (TIME_STEP * mix[1]) * received[c]
    remote_part(out, before, after, sides_far, TIME_STEP * mix[1] * PENALTY)
    if kind == "last":
        natural_order(out, given_out, turned, stored)
    else:
        faces_sent(odd, out, message_a, message_b)


def place_body(received, *outs):
    peers, size = received.shape[0], received.shape[1]
    fold = 192 * len(outs) // (size - 8)
    height = 64 // fold
    target = lax.broadcasted_iota(jnp.int32, (128, 128), 0)
    lane = lax.broadcasted_iota(jnp.int32, (128, 128), 1)
    total = None
    for peer in range(peers):
        label = received[peer, size - 8 : size - 7, :]
        label = jnp.broadcast_to(label, (128, 128)).astype(jnp.int32)
        hit = (label == target % 16) & (lane % 8 == target // 16)
        chosen = [jnp.where(hit & (lane // (128 // fold) == g), 1.0, 0.0) for g in range(fold)]
        chosen = jnp.concatenate(chosen, 0).astype(BF16)
        high, low = parts(received[peer, 0 : size - 8])
        dims = (((1,), (1,)), ((), ()))
        value = lax.dot_general(high, chosen, dims, preferred_element_type=F32)
        value = value + lax.dot_general(low, chosen, dims, preferred_element_type=F32)
        total = value if total is None else total + value
    for k, out in enumerate(outs):
        for c in range(3):
            for g in range(fold):
                at = (k * 3 + c) * height
                out[c, g * height : g * height + height] = total[at : at + height, g * 128 : g * 128 + 128]


def kron_part(matrix, shape, rows_by, columns_by):
    row = lax.broadcasted_iota(jnp.int32, (shape[0], 8), 0)
    level = lax.broadcasted_iota(jnp.int32, (shape[0], 8), 1)
    left = (row // rows_by % 8 == level).astype(F32)
    level = lax.broadcasted_iota(jnp.int32, (8, shape[1]), 0)
    column = lax.broadcasted_iota(jnp.int32, (8, shape[1]), 1)
    right = (column // columns_by % 8 == level).astype(F32)
    return dot_full(dot_full(left, matrix), right)


def tables_body(
    packed,
    near,
    far,
    deriv_rows,
    deriv_lanes,
    pair,
    spread,
    labels,
    speed,
):
    size = near.shape[1]
    count = size // 8
    blocks = spread.shape[0] // 8

    def place_of(shape):
        return (lax.broadcasted_iota(jnp.int32, shape, 0), lax.broadcasted_iota(jnp.int32, shape, 1))

    row, column = place_of((count, size))
    repeat = (column % count == row).astype(F32)
    speed[...] = dot_full(packed[24:25, 0:count], repeat)
    wanted = dot_full(packed[16:24, 0:count], repeat).astype(jnp.int32)
    row, column = place_of((size, size))
    level, element = row // count, row % count
    level_out = column // count
    for facet in range(4):
        shift = -count if facet % 2 == 0 else count
        choice = jnp.broadcast_to(wanted[facet : facet + 1], (size, size))
        near[facet] = jnp.where((level == level_out) & (element == choice), 1.0, 0.0).astype(BF16)
        far[facet] = jnp.where((level == level_out) & (element + shift == choice), 1.0, 0.0).astype(BF16)
    lower = jnp.broadcast_to(wanted[4:5], (size, size))
    upper = jnp.broadcast_to(wanted[5:6], (size, size))
    hit = (level == 7) & (level_out == 0) & (element == lower)
    hit = hit | ((level == 0) & (level_out == 7) & (element == upper))
    near[4] = jnp.where(hit, 1.0, 0.0).astype(BF16)
    hit = (level == 0) & (level_out == 0) & (element - count == lower)
    hit = hit | ((level == 1) & (level_out == 7) & (element + count == upper))
    far[4] = jnp.where(hit, 1.0, 0.0).astype(BF16)

    row, column = place_of((64, 64))
    slopes, modes = packed[0:8, 0:8], packed[8:16, 0:8]
    outer = kron_part(slopes, (64, 64), 8, 8)
    inner = kron_part(slopes, (64, 64), 1, 1)
    deriv_rows[0:64] = jnp.where(row % 8 == column % 8, outer, 0.0)
    deriv_rows[64:128] = jnp.where(row // 8 == column // 8, inner, 0.0)
    row, column = place_of((size, size))
    lanes = kron_part(slopes.T, (size, size), count, count)
    deriv_lanes[...] = jnp.where(row % count == column % count, lanes, 0.0)
    pair[...] = kron_part(modes, (64, 64), 8, 8) * kron_part(modes, (64, 64), 1, 1)

    peers = labels.shape[0]
    capacity = capacity_of(peers, blocks)
    row, column = place_of((blocks, blocks))

    def upright(values):
        return jnp.sum(jnp.where(row == column, values, 0.0), 1, keepdims=True)

    owner_row = packed[25:26, 0:blocks]
    owner_column = upright(owner_row)
    earlier = (owner_column == owner_row) & (column < row)
    position = jnp.sum(jnp.where(earlier, 1.0, 0.0), 1, keepdims=True)
    slot = owner_column * capacity + position
    element_column = upright(packed[26:27, 0:blocks])
    row, column = place_of((8 * blocks, blocks))
    repeat = (row // 8 == column).astype(F32)
    slot = dot_full(repeat, jnp.broadcast_to(slot, (blocks, 128)))
    element = dot_full(repeat, jnp.broadcast_to(element_column, (blocks, 128)))
    row, column = place_of((8 * blocks, 128))
    values = kron_part(modes.T, (8 * blocks, 128), 1, 1)
    inside = column % (8 * capacity) // 8
    for peer in range(peers):
        chosen = slot == (inside + peer * capacity).astype(F32)
        spread[:, peer * 128 : peer * 128 + 128] = jnp.where(chosen, values, 0.0)
        named = jnp.where(chosen & (row % 8 == 0), element + 1.0, 0.0)
        labels[peer] = jnp.broadcast_to(jnp.sum(named, 0, keepdims=True) - 1.0, (8, 128))


def shifted(sizes, shifts):
    pairs = []
    for index in np.ndindex(*sizes):
        source = [(i + s) % n for i, s, n in zip(index, shifts, sizes)]
        pairs.append((int(np.ravel_multi_index(source, sizes)), int(np.ravel_multi_index(index, sizes))))
    return pairs


def partners(sizes, axis, second):
    pairs = []
    for index in np.ndindex(*sizes):
        source = list(index)
        step = 1 if (index[axis] % 2 == 0) != second else -1
        source[axis] = (index[axis] + step) % sizes[axis]
        pairs.append((int(np.ravel_multi_index(source, sizes)), int(np.ravel_multi_index(index, sizes))))
    return pairs


def per_device(
    density,
    velocity,
    pressure,
    acoustic,
    sound_speed,
    derivative,
    mode_basis,
    neighbours,
    block_owner,
    block_element,
):
    size_x, size_y, size_z = lax.axis_size("fx"), lax.axis_size("fy"), lax.axis_size("fz")
    devices = size_x * size_y * size_z
    cells_x = density.shape[0]
    elements = acoustic.shape[0]
    device = lax.axis_index(("fx", "fy", "fz"))

    names = ("fx", "fy", "fz")

    rows = 5 * cells_x * 8
    tiles = -(-rows // 128)
    square = velocity[0] * velocity[0] + velocity[1] * velocity[1] + velocity[2] * velocity[2]
    energy = pressure / (HEAT_RATIO - 1.0) + 0.5 * density * square
    rest = ((0, 0), (0, 0), (0, 0))
    state = jnp.pad(density[None], ((0, 4),) + rest) + jnp.pad(density * velocity, ((1, 1),) + rest)
    state = state + jnp.pad(energy[None], ((4, 0),) + rest)
    x_rows = 5 * 2 * HALO * 8
    y_shape, y_last_shape = (5 * cells_x * HALO, 128), (48, 128)
    flow_a, flow_b, along_x, y_a, y_b = call(
        pack_start_body, [(tiles * 8, 128), (tiles * 8, 128), (x_rows, 128), y_shape, y_shape], state
    )
    edge_a = lax.ppermute(flow_a, "fz", partners((size_z,), 0, False))
    edge_b = lax.ppermute(flow_b, "fz", partners((size_z,), 0, True))
    x_steps = (1,) if size_x == 2 else (1, -1)
    beside_x = [lax.ppermute(along_x, "fx", shifted((size_x,), (step,))) for step in x_steps]

    def along_y(to_a, to_b):
        second = lax.ppermute(to_b, "fy", partners((size_y,), 0, True))
        return lax.ppermute(to_a, "fy", partners((size_y,), 0, False)), second

    y_first, y_second = along_y(y_a, y_b)

    near_pairs = [(i ^ 1, i) for i in range(devices)]
    far_pairs = [pair for i in range(1, devices - 1, 2) for pair in ((i, i + 1), (i + 1, i))]

    def traces(to_a, to_b):
        far_got = lax.ppermute(to_b, names, far_pairs)
        return lax.ppermute(to_a, names, near_pairs), far_got

    size = 8 * elements
    held = (4, 64, size)
    faces = (96, size)
    sides = [pltpu.VMEM(faces, F32)] * 2
    turning = [pltpu.VMEM((512, 128), F32), pltpu.VMEM((4, 4 * elements, 128), F32)]
    sound, to_a, to_b = call(
        acoustic_start_body,
        [held, faces, faces],
        acoustic,
        edge_a,
        scratch=turning,
        last=1,
    )
    got_a = lax.ppermute(to_a, names, near_pairs)

    edge, to_b = call(
        pack_next_body,
        [(40, 128), to_b.shape],
        state,
        flow_a,
        flow_b,
        edge_a,
        edge_b,
        to_b,
        got_a,
        last=1,
    )
    got_b = lax.ppermute(to_b, names, far_pairs)
    edges_x = [lax.ppermute(edge, "fx", shifted((size_x,), (step,))) for step in x_steps]
    y_a, y_b = call(pack_last_body, [y_last_shape] * 2, edge, *beside_x, *edges_x, cost=1)
    y_first_last, y_second_last = along_y(y_a, y_b)

    local = (neighbours - device * elements).T
    blocks = block_owner.size
    width = max(elements, blocks)

    def piece(values, first):
        values = values.astype(F32)
        return jnp.pad(values, ((first, 32 - first - values.shape[0]), (0, width - values.shape[1])))

    packed = (
        piece(derivative, 0)
        + piece(mode_basis, 8)
        + piece(local, 16)
        + piece(sound_speed.reshape(1, elements), 24)
        + piece(block_owner.reshape(1, blocks), 25)
        + piece(block_element.reshape(1, blocks), 26)
    )
    table = jax.ShapeDtypeStruct((5, size, size), BF16)
    near, far, deriv_rows, deriv_lanes, pair, spread, labels, speed = call(
        tables_body,
        [
            table,
            table,
            (128, 64),
            (size, size),
            (64, 64),
            (8 * blocks, size_y * 128),
            (size_y, 8, 128),
            (1, size),
        ],
        packed,
        cost=1,
    )

    fold = fold_of(size_y, blocks)
    wide = cells_x + 2 * HALO
    rows_scratch = pltpu.VMEM((3, 64, 128), F32)

    def planes(count):
        return (5, count, 16, 128)

    def route(send):
        return lax.all_to_all(send, "fy", split_axis=0, concat_axis=0, tiled=True)

    start, send = call(
        functools.partial(flow_sources_body, len(beside_x)),
        [planes(wide), (size_y, 192 // fold + 8, 128)],
        state,
        edge,
        *beside_x,
        y_first,
        y_second,
        pair,
        spread,
        labels,
        got_b,
        last=1,
        scratch=[
            pltpu.VMEM((3, wide, 16, 128), F32),
            rows_scratch,
            pltpu.VMEM((2, cells_x, 8, 128), F32),
            pltpu.VMEM(y_shape, F32),
            pltpu.VMEM(y_shape, F32),
        ],
    )
    received = route(send)
    second, derived, ends, send = call(
        functools.partial(flow_stages_body, len(edges_x)),
        [
            planes(wide - 4),
            planes(wide),
            (5, cells_x, 8, 128),
            (size_y, 2 * 192 // fold + 8, 128),
        ],
        start,
        edge,
        *edges_x,
        y_first_last,
        y_second_last,
        pair,
        spread,
        labels,
        scratch=[
            rows_scratch,
            pltpu.VMEM(planes(wide - 2), F32),
            pltpu.VMEM(planes(wide - 2), F32),
            pltpu.VMEM(planes(wide), F32),
            pltpu.VMEM((5, 16, 256), F32),
            pltpu.VMEM(y_last_shape, F32),
            pltpu.VMEM(y_last_shape, F32),
        ],
    )

    def local_part(mix, now):
        return call(
            functools.partial(acoustic_local_body, mix),
            [held],
            now,
            sound,
            deriv_rows,
            deriv_lanes,
            speed,
            near,
            scratch=sides,
            cost=1,
        )[0]

    partial = local_part(MIXES[0], sound)
    sound_one, to_a, to_b = call(
        functools.partial(acoustic_far_body, MIXES[0], "first"),
        [held, faces, (faces[0] + 32, size)],
        partial,
        got_a,
        got_b,
        far,
        received,
        send,
        scratch=sides + [rows_scratch],
        last=1,
    )
    source_two, source_three = call(place_body, [(3, 64, 128)] * 2, route(send))
    got_a, got_b = traces(to_a, to_b)
    flow_state = call(flow_last_body, [(5, cells_x, 8, 128)], second, derived, ends, start)[0]
    partial = local_part(MIXES[1], sound_one)
    sound_two, to_a, to_b = call(
        functools.partial(acoustic_far_body, MIXES[1], "second"),
        [held, faces, (faces[0] + 32, size)],
        partial,
        got_a,
        got_b,
        far,
        source_two,
        scratch=sides,
    )
    got_a, got_b = traces(to_a, to_b)
    partial = local_part(MIXES[2], sound_two)
    sound_state = call(
        functools.partial(acoustic_far_body, MIXES[2], "last"),
        [(elements, 4, 512)],
        partial,
        got_a,
        got_b,
        far,
        source_three,
        scratch=sides + [pltpu.VMEM(held, F32)] + turning,
    )[0]
    return (flow_state, sound_state)


def solution(mesh):
    placed = (
        P("fx", "fy", "fz"),
        P(None, "fx", "fy", "fz"),
        P("fx", "fy", "fz"),
        P(("fx", "fy", "fz"), None, None),
        P(("fx", "fy", "fz")),
        P(),
        P(),
        P(("fx", "fy", "fz"), None),
        P("fx", "fy", "fz", None, None),
        P("fx", "fy", "fz", None),
    )
    return jax.shard_map(
        per_device,
        mesh=mesh,
        in_specs=placed,
        out_specs=(P(None, "fx", "fy", "fz"), P(("fx", "fy", "fz"), None, None)),
        check_vma=False,
    )
```

```python
import functools

import jax
import jax.numpy as jnp
import numpy as np
from jax import lax
from jax.experimental import pallas as pl
from jax.experimental.pallas import tpu as pltpu
from jax.sharding import PartitionSpec as P

HEAT_RATIO = 1.4
TIME_STEP = 0.1
VISCOSITY = 0.05
PENALTY = 0.5
HALO = 3
F32 = jnp.float32
BF16 = jnp.bfloat16
PARAMS = pltpu.CompilerParams(vmem_limit_bytes=24 * 1024 * 1024)
MIXES = ((0.0, 1.0), (0.75, 0.25), (1.0 / 3.0, 2.0 / 3.0))


def parts(values):
    high = values.astype(BF16)
    return high, (values - high.astype(F32)).astype(BF16)


def dot(left, right):
    return lax.dot_general(left, right, (((1,), (0,)), ((), ())), preferred_element_type=F32)


def dot_three(left, right):
    left_high, left_low = parts(left)
    right_high, right_low = parts(right)
    return dot(left_high, right_high) + dot(left_high, right_low) + dot(left_low, right_high)


def dot_full(left, right, dims=((1,), (0,))):
    return lax.dot_general(
        left, right, (dims, ((), ())), precision=lax.Precision.HIGHEST, preferred_element_type=F32
    )


def dot_exact_right(left, right):
    left_high, left_low = parts(left)
    return dot(left_high, right) + dot(left_low, right)


def call(body, outs, *operands, scratch=(), last=0, cost=None):
    whole = pl.BlockSpec(memory_space=pltpu.VMEM)
    outs = [out if isinstance(out, jax.ShapeDtypeStruct) else jax.ShapeDtypeStruct(out, F32) for out in outs]
    anywhere = pl.BlockSpec(memory_space=pl.ANY)
    return pl.pallas_call(
        body,
        out_shape=outs,
        in_specs=[whole] * (len(operands) - last) + [anywhere] * last,
        out_specs=[whole] * len(outs),
        scratch_shapes=list(scratch),
        compiler_params=PARAMS,
        cost_estimate=None if cost is None else pl.CostEstimate(flops=cost, bytes_accessed=cost, transcendentals=0),
    )(*operands)


def capacity_of(peers, blocks):
    return max(2, 2 * blocks // peers)


def fold_of(peers, blocks):
    return 128 // (8 * capacity_of(peers, blocks))


def is_odd(axis):
    return lax.axis_index(axis) % 2 == 1


def paired(odd, to_next, to_last):
    return jnp.where(odd, to_last, to_next), jnp.where(odd, to_next, to_last)


def pack_start_body(state, message_a, message_b, along_x):
    odd = is_odd("fz")
    rows = state[...].reshape(-1, 128)
    count = rows.shape[0]
    for tile in range(message_a.shape[0] // 8):
        piece = rows[tile * 128 : min(count, tile * 128 + 128)]
        if piece.shape[0] < 128:
            piece = jnp.concatenate([piece, jnp.zeros((128 - piece.shape[0], 128), F32)], 0)
        turned = piece.T
        first, second = paired(odd, turned[120:128], turned[0:8])
        message_a[tile * 8 : tile * 8 + 8] = first
        message_b[tile * 8 : tile * 8 + 8] = second
    cells_x = state.shape[1]
    for f in range(5):
        for s, x in enumerate(x_planes(cells_x)):
            at = (f * 2 * HALO + s) * 8
            along_x[at : at + 8] = state[f, x]


def pack_next_body(state, sent_a, sent_b, got_a, got_b, _, edge):
    cells_x = state.shape[1]
    odd_z = is_odd("fz")
    high, low = paired(odd_z, sent_a[...], sent_b[...])
    above, below = paired(odd_z, got_a[...], got_b[...])
    row = lax.broadcasted_iota(jnp.int32, (8, 128), 0)
    x_of_lane = lax.broadcasted_iota(jnp.int32, (16, 128), 1) // 8 % cells_x
    for tile in range(high.shape[0] // 8):
        rows = slice(tile * 8, tile * 8 + 8)
        upper = jnp.where(row < 3, pltpu.roll(high[rows], 3, 0), pltpu.roll(above[rows], 3, 0))
        lower = jnp.where(row < 3, pltpu.roll(below[rows], 3, 0), pltpu.roll(low[rows], 3, 0))
        slots = jnp.concatenate([upper, lower], 0)
        spread = jnp.concatenate([jnp.where(x_of_lane == x, slots, 0.0) for x in range(8)], 0).T
        for half in range(16 // cells_x):
            f = tile * (16 // cells_x) + half
            if f < 5:
                at = half * cells_x * 8
                total = spread[at : at + 8]
                for x in range(1, cells_x):
                    total = total + spread[at + x * 8 : at + x * 8 + 8]
                edge[f * 8 : f * 8 + 8] = total


def x_planes(cells_x):
    return [cells_x - HALO + i for i in range(HALO)] + list(range(HALO))


def sides_of(beside_x):
    return beside_x[0], beside_x[-1]


def beyond(edges_x, f):
    after, before = sides_of(edges_x)
    at = f * 8
    if after is before:
        return after[at : at + 8]
    lane = lax.broadcasted_iota(jnp.int32, (8, 128), 1)
    return jnp.where(lane < 64, after[at : at + 8], before[at : at + 8])


def pack_last_body(state, edge, *refs):
    (y_a, y_b), refs = refs[-2:], refs[:-2]
    beside_x, edges_x = refs[: len(refs) // 2], refs[len(refs) // 2 :]
    cells_x = state.shape[1]
    odd = is_odd("fy")
    after, before = sides_of(beside_x)

    def put(at, values, height):
        first, second = paired(odd, values[8 - height : 8], values[0:height])
        y_a[at : at + height] = first
        y_b[at : at + height] = second

    lines = 5 * cells_x * HALO
    for f in range(5):
        for x in range(cells_x):
            put((f * cells_x + x) * HALO, state[f, x], HALO)
        at = lines + f * 6
        for slot, height in ((1, 1), (2, 2), (3, 2), (4, 1)):
            source = (f * 2 * HALO + slot) * 8
            put(at, (before if slot < HALO else after)[source : source + 8], height)
            at += height
        put(lines + 30 + f * 2, edge[f * 8 : f * 8 + 8], 2)
        put(lines + 40 + f, beyond(edges_x, f), 1)


def assemble_speeds(wide, state, beside_x, above, below):
    cells_x = state.shape[1]
    after, before = sides_of(beside_x)
    for f in range(4):
        for x in range(cells_x):
            wide[f, 1 + x, 0:8] = state[f, x]
            at = (f * cells_x + x) * HALO
            wide[f, 1 + x, 8:9] = above[at : at + 1]
            wide[f, 1 + x, 15:16] = below[at + HALO - 1 : at + HALO]
        for slot, plane, source in ((HALO - 1, 0, before), (HALO, cells_x + 1, after)):
            at = (f * 2 * HALO + slot) * 8
            wide[f, plane, 0:8] = source[at : at + 8]


def assemble(wide, rim, state, edge, beside_x, edges_x, above, below):
    cells_x = state.shape[1]
    after, before = sides_of(beside_x)
    lines = 5 * cells_x * HALO
    for f in range(5):
        for x in range(cells_x):
            wide[f, HALO + x, 0:8] = state[f, x]
            at = (f * cells_x + x) * HALO
            wide[f, HALO + x, 8 : 8 + HALO] = above[at : at + HALO]
            wide[f, HALO + x, 16 - HALO : 16] = below[at : at + HALO]
        for slot in range(2 * HALO):
            plane = slot if slot < HALO else cells_x + slot
            at = (f * 2 * HALO + slot) * 8
            wide[f, plane, 0:8] = (before if slot < HALO else after)[at : at + 8]
        at = lines + f * 6
        for slot, height in ((1, 1), (2, 2), (3, 2), (4, 1)):
            plane = slot if slot < HALO else cells_x + slot
            wide[f, plane, 8 : 8 + height] = above[at : at + height]
            wide[f, plane, 16 - height : 16] = below[at : at + height]
            at += height
        rim[f, 0:8, 0:128] = edge[f * 8 : f * 8 + 8]
        rim[f, 0:8, 128:256] = beyond(edges_x, f)
        at = lines + 30 + f * 2
        rim[f, 8:10, 0:128] = above[at : at + 2]
        rim[f, 14:16, 0:128] = below[at : at + 2]
        at = lines + 40 + f
        rim[f, 8:9, 128:256] = above[at : at + 1]
        rim[f, 15:16, 128:256] = below[at : at + 1]


def primitive(rho, mx, my, mz, energy):
    inverse = 1.0 / rho
    u, v, w = mx * inverse, my * inverse, mz * inverse
    p = (HEAT_RATIO - 1.0) * (energy - 0.5 * (mx * u + my * v + mz * w))
    return u, v, w, p, jnp.sqrt(HEAT_RATIO * jnp.abs(p) * inverse)


def chunks(first, last, size):
    return [(i, min(i + size, last)) for i in range(first, last, size)]


def derive_planes(wide, derived, first, last):
    for i, j in chunks(first, last, 4):
        for k, value in enumerate(primitive(*[wide[f, i:j] for f in range(5)])):
            derived[k, i:j] = value


def derive_speeds(wide, derived, first, last):
    for i, j in chunks(first, last, 5):
        inverse = 1.0 / wide[0, i:j]
        for k in range(3):
            derived[k, i:j] = wide[1 + k, i:j] * inverse


def with_flux(fields, other, along):
    speed, p = other[along], other[3]
    out = [fields[1 + along]]
    for k in range(3):
        value = fields[1 + k] * speed
        out.append(value + p if k == along else value)
    out.append((fields[4] + p) * speed)
    return fields, out, jnp.abs(speed) + other[4]


def face(left, right):
    (fields_l, flux_l, speed_l), (fields_r, flux_r, speed_r) = left, right
    speed = jnp.maximum(speed_l, speed_r)
    viscous = speed + 2.0 * VISCOSITY
    return [
        (flux_l[f] + flux_r[f]) - (viscous if 1 <= f <= 3 else speed) * (fields_r[f] - fields_l[f])
        for f in range(5)
    ]


def rolled(here, shift, axis):
    fields, flux, speed = here
    return (
        [pltpu.roll(a, shift, axis) for a in fields],
        [pltpu.roll(a, shift, axis) for a in flux],
        pltpu.roll(speed, shift, axis),
    )


def rim_section(fields, start, mix):
    other = primitive(*fields)
    here = with_flux(fields, other, 2)
    along_z = face(here, rolled(here, 255, 1))
    if mix is None:
        return other, along_z, None
    total = [g - pltpu.roll(g, 1, 1) for g in along_z]
    for along, step, axis, size in ((0, 16, 1, 256), (1, 1, 0, 16)):
        here = with_flux(fields, other, along)
        faces = face(here, rolled(here, size - step, axis))
        total = [total[f] + (faces[f] - pltpu.roll(faces[f], step, axis)) for f in range(5)]
    out = []
    for f in range(5):
        value = fields[f] - (0.5 * TIME_STEP) * total[f]
        out.append(mix[0] * start[f] + mix[1] * value if mix[0] != 0.0 else value)
    return other, along_z, out


def to_ends(values, after, rows, first, last, ends):
    slot = lax.broadcasted_iota(jnp.int32, (rows, 256), 1) % 16
    for f, value in enumerate(values):
        value = value[0:rows]
        value = jnp.where(slot == 9, pltpu.roll(value, 9 - after, 1), value)
        for x in range(first, last):
            at = x % 16 // 8 * 128
            move = (118 - x % 8 * 16) % 128
            tile = value[:, at : at + 128]
            ends[f, x - first, 0:rows] = pltpu.roll(tile, move, 1) if move else tile


def flow_rate_section(wide, derived, ends, start, offset, mix, write, inner=False):
    depth = wide.shape[1]
    rows = slice(0, 8) if inner else slice(None)
    size = 4 if inner else 2

    def planes(i, j, kept, along):
        fields = [wide[f, i:j, kept] for f in range(5)]
        return with_flux(fields, [derived[f, i:j, kept] for f in range(5)], along)

    def cut(here, i, j):
        return [a[i:j] for a in here[0]], [a[i:j] for a in here[1]], here[2][i:j]

    for i, j in chunks(1, depth - 1, size):
        count = j - i
        lane = lax.broadcasted_iota(jnp.int32, (count, 8 if inner else 16, 128), 2)
        here = planes(i - 1, j + 1, rows, 0)
        faces = face(cut(here, 0, count + 1), cut(here, 1, count + 2))
        total = [g[1:] - g[:-1] for g in faces]
        here = planes(i, j, slice(None), 1)
        faces = face(here, rolled(here, 15, 1))
        for f in range(5):
            change = faces[f] - pltpu.roll(faces[f], 1, 1)
            total[f] = total[f] + (change[:, 0:8] if inner else change)
        here = planes(i, j, rows, 2)
        faces = face(here, rolled(here, 127, 2))
        for f in range(5):
            end = ends[f, i - 1 : j - 1, rows]
            value = jnp.where(lane == 127, end, faces[f])
            total[f] = total[f] + (value - jnp.where(lane == 0, end, pltpu.roll(value, 1, 2)))
        for f in range(5):
            value = wide[f, i:j, rows] - (0.5 * TIME_STEP) * total[f]
            if mix[0] != 0.0:
                value = mix[0] * start[f, i + offset : j + offset, rows] + mix[1] * value
            write(slice(i - 1, j - 1), f, value)


def lamb(derived, ends, first, cells_x, lamb_rows):
    for i, j in chunks(first, first + cells_x, 4):
        count = j - i
        lane = lax.broadcasted_iota(jnp.int32, (count, 8, 128), 2)
        vel = [derived[c, i:j, 0:8] for c in range(3)]
        along_x = [derived[c, i + 1 : j + 1, 0:8] - derived[c, i - 1 : j - 1, 0:8] for c in range(3)]
        along_y = []
        for c in range(3):
            column = derived[c, i:j]
            along_y.append((pltpu.roll(column, 15, 1) - pltpu.roll(column, 1, 1))[:, 0:8])
        along_z = []
        for c in range(2):
            end = ends[c, i - first : j - first, 0:8]
            after = jnp.where(lane == 127, end, pltpu.roll(vel[c], 127, 2))
            along_z.append(after - jnp.where(lane == 0, end, pltpu.roll(vel[c], 1, 2)))
        curl = [
            0.5 * (along_y[2] - along_z[1]),
            0.5 * (along_z[0] - along_x[2]),
            0.5 * (along_x[1] - along_y[0]),
        ]
        at = slice((i - first) * 8, (j - first) * 8)
        lamb_rows[0, at] = (curl[1] * vel[2] - curl[2] * vel[1]).reshape(count * 8, 128)
        lamb_rows[1, at] = (curl[2] * vel[0] - curl[0] * vel[2]).reshape(count * 8, 128)
        lamb_rows[2, at] = (curl[0] * vel[1] - curl[1] * vel[0]).reshape(count * 8, 128)


def project(lamb_rows, pair, spread, send, base):
    peers = send.shape[0]
    fold = fold_of(peers, spread.shape[0] // 8)
    height = 64 // fold
    group = lax.broadcasted_iota(jnp.int32, (height, 128), 1) // (128 // fold)
    modes = dot_three(pair[...], jnp.concatenate([lamb_rows[c] for c in range(3)], 1))
    modes = jnp.concatenate([modes[:, c * 128 : c * 128 + 128] for c in range(3)], 0)
    sent = dot_three(modes, spread[...])
    for c in range(3):
        for peer in range(peers):
            mine = sent[c * 64 : c * 64 + 64, peer * 128 : peer * 128 + 128]
            folded = mine[0:height]
            for g in range(1, fold):
                folded = jnp.where(group == g, mine[g * height : g * height + height], folded)
            send[peer, base + c * height : base + c * height + height] = folded


def flow_sources_body(count, state, edge, *refs):
    beside_x, refs = refs[:count], refs[count:]
    got_a, got_b, pair, spread, labels, _, send, wide, derived, lamb_rows, ends, above, below = refs
    cells_x = state.shape[1]
    above[...], below[...] = paired(is_odd("fy"), got_a[...], got_b[...])
    assemble_speeds(wide, state, beside_x, above, below)
    derive_speeds(wide, derived, 0, cells_x + 2)
    inverse = 1.0 / edge[0:8]
    speeds = [jnp.concatenate([edge[k * 8 : k * 8 + 8] * inverse] * 2, 1) for k in (1, 2)]
    to_ends(speeds, 3, 8, 0, cells_x, ends)
    lamb(derived, ends, 1, cells_x, lamb_rows)
    project(lamb_rows, pair, spread, send, 0)
    send[:, send.shape[1] - 8 :] = labels[...]


def writer(target):
    def write(i, f, value):
        target[f, i] = value

    return write


def flow_stages_body(count, state, edge, *refs):
    beside_x, edges_x, refs = refs[:count], refs[count : 2 * count], refs[2 * count :]
    got_a, got_b, pair, spread, _, second, derived, ends_out, send, *refs = refs
    lamb_rows, ends, first, wide, rim, above, below = refs
    above[...], below[...] = paired(is_odd("fy"), got_a[...], got_b[...])
    assemble(wide, rim, state, edge, beside_x, edges_x, above, below)
    planes = wide.shape[1]
    cells_x = planes - 2 * HALO
    size = send.shape[1] // 2
    rim_start = [rim[f] for f in range(5)]
    derive_planes(wide, derived, 0, planes)
    _, along_z, rim_first = rim_section(rim_start, None, MIXES[0])
    to_ends(along_z, 2, 16, -2, cells_x + 2, ends)
    flow_rate_section(wide, derived, ends, wide, 0, MIXES[0], writer(first))
    derive_planes(first, derived, 0, planes - 2)
    other, along_z, rim_second = rim_section(rim_first, [rim[f] for f in range(5)], MIXES[1])
    to_ends(other[0:2], 3, 8, 0, cells_x, ends)
    lamb(derived, ends, 2, cells_x, lamb_rows)
    project(lamb_rows, pair, spread, send, 0)
    to_ends(along_z, 2, 16, -1, cells_x + 1, ends)
    flow_rate_section(first, derived, ends, wide, 1, MIXES[1], writer(second))
    derive_planes(second, derived, 0, planes - 4)
    other, along_z, _ = rim_section(rim_second, None, None)
    to_ends(other[0:2], 3, 8, 0, cells_x, ends)
    lamb(derived, ends, 1, cells_x, lamb_rows)
    project(lamb_rows, pair, spread, send, size)
    to_ends(along_z, 2, 8, 0, cells_x, ends_out)


def flow_last_body(second, derived, ends, state, out):
    flow_rate_section(second, derived, ends, state, -1, MIXES[2], writer(out), inner=True)


def faces_out(state, rear, front):
    lane = lax.broadcasted_iota(jnp.int32, (32, 128), 1) // 16
    for c in range(4):
        front[c * 8 : c * 8 + 8] = state[c, 56:64]
        rear[c * 8 : c * 8 + 8] = state[c, 0:8]
        front[32 + c * 8 : 40 + c * 8] = state[c, pl.ds(7, 8, stride=8), :]
        rear[32 + c * 8 : 40 + c * 8] = state[c, pl.ds(0, 8, stride=8), :]
    rows = state[...].reshape(256, 128)
    last = jnp.zeros((32, 128), F32)
    first = jnp.zeros((32, 128), F32)
    for j in range(8):
        piece = rows[j * 32 : j * 32 + 32]
        last = jnp.where(lane == j, pltpu.roll(piece, (j * 16 + 16) % 128, 1), last)
        first = jnp.where(lane == j, pltpu.roll(piece, j * 16, 1) if j else piece, first)
    front[64:96] = last
    rear[64:96] = first


def faces_sent(odd, state, message_a, message_b):
    size = message_a.shape[0]
    faces_out(state, message_b, message_a)
    message_a[...], message_b[0:size] = paired(odd, message_a[...], message_b[0:size])
    message_b[size:] = jnp.zeros((message_b.shape[0] - size, 128), F32)


def lift(total, before, after, sides, factor):
    def place(face, rows, target):
        value = factor * dot_exact_right(rows, sides[face])
        for c in range(4):
            total[c, target, :] += value[c * 8 : c * 8 + 8]

    place(0, before[0:32], pl.ds(0, 8))
    place(1, after[0:32], pl.ds(56, 8))
    place(2, before[32:64], pl.ds(0, 8, stride=8))
    place(3, after[32:64], pl.ds(7, 8, stride=8))


def rate_local(state, deriv_rows, deriv_lanes, speed, sides):
    fields = [state[c] for c in range(4)]
    by_rows = dot_three(deriv_rows[...], jnp.concatenate(fields[0:3], 1))
    by_lanes = dot_three(jnp.concatenate([fields[0], fields[3]], 0), deriv_lanes[...])
    divergence = by_rows[0:64, 128:256] + by_rows[64:128, 256:384] + by_lanes[64:128]
    rates = [
        -(speed[...] * speed[...]) * divergence,
        -by_rows[0:64, 0:128],
        -by_rows[64:128, 0:128],
        -by_lanes[0:64],
    ]
    row = lax.broadcasted_iota(jnp.int32, (64, 128), 0)
    lane = lax.broadcasted_iota(jnp.int32, (64, 128), 1)
    count = jnp.zeros((64, 128), F32)
    for value in (row // 8, row % 8, lane // 16):
        count = count + jnp.where((value == 0) | (value == 7), PENALTY, 0.0)
    side = PENALTY * dot_exact_right(state[...].reshape(256, 128), sides[4])
    return [rates[c] - count * fields[c] + side[c * 64 : c * 64 + 64] for c in range(4)]


def acoustic_local_body(mix, state, start, deriv_rows, deriv_lanes, speed, sides, out, front, rear):
    rates = rate_local(state, deriv_rows, deriv_lanes, speed, sides)
    for c in range(4):
        value = state[c] + TIME_STEP * rates[c]
        if mix[0] != 0.0:
            value = mix[0] * start[c] + mix[1] * value
        out[c] = value
    faces_out(state, rear, front)
    lift(out, front, rear, sides, TIME_STEP * mix[1] * PENALTY)


def acoustic_start_body(given, _, state, message_a, message_b, turned, stored):
    count = given.shape[0]
    for e in range(count):
        for t in range(4):
            stored[t, 4 * e : 4 * e + 4] = given[e, :, t * 128 : t * 128 + 128]
    for t in range(4):
        rows = [stored[t, pl.ds(c, count, stride=4), :] for c in range(4)]
        rows = jnp.concatenate(rows + [jnp.zeros((128 - 4 * count, 128), F32)], 0)
        turned[t * 128 : t * 128 + 128] = rows.T
    lane = lax.broadcasted_iota(jnp.int32, (64, 128), 1) // count
    fields = [jnp.zeros((64, 128), F32)] * 4
    for z in range(8):
        piece = turned[pl.ds(z, 64, stride=8), :]
        for c in range(4):
            move = (z - c) * count % 128
            fields[c] = jnp.where(lane == z, pltpu.roll(piece, move, 1) if move else piece, fields[c])
    for c in range(4):
        state[c] = fields[c]
    faces_sent(is_odd("fz"), state, message_a, message_b)


def natural_order(state, out, turned, stored):
    count = out.shape[0]
    lane = lax.broadcasted_iota(jnp.int32, (64, 128), 1) // count
    for z in range(8):
        value = jnp.zeros((64, 128), F32)
        for c in range(4):
            move = (c - z) * count % 128
            value = jnp.where(lane == c, pltpu.roll(state[c], move, 1) if move else state[c], value)
        turned[pl.ds(z, 64, stride=8), :] = value
    for t in range(4):
        rows = turned[t * 128 : t * 128 + 128].T
        for c in range(4):
            stored[t, pl.ds(c, count, stride=4), :] = rows[c * count : c * count + count]
    for e in range(count):
        for t in range(4):
            out[e, :, t * 128 : t * 128 + 128] = stored[t, 4 * e : 4 * e + 4]


def remote_part(out, before, after, sides_far, factor):
    lift(out, before, after, sides_far, factor)
    lane = lax.broadcasted_iota(jnp.int32, (32, 128), 1) // 16
    last, first = before[64:96], after[64:96]
    pieces = []
    for j in range(8):
        left = pltpu.roll(last, 128 - j * 16, 1) if j else last
        right = pltpu.roll(first, (144 - j * 16) % 128, 1) if j != 1 else first
        pieces.append(jnp.where(lane == 0, left, jnp.where(lane == 1, right, 0.0)))
    value = factor * dot_exact_right(jnp.concatenate(pieces, 0), sides_far[4])
    for c in range(4):
        out[c] += value[c * 64 : c * 64 + 64]


def acoustic_far_body(mix, kind, partial, got_a, got_b, sides_far, received, *refs):
    if kind == "last":
        given_out, before, after, out, turned, stored = refs
    elif kind == "first":
        _, out, message_a, message_b, before, after, source = refs
        place(received, received, source, 0)
        received = source
    else:
        labelled, out, message_a, message_b, before, after, source = refs
        place(received, labelled, source, 0)
        received = source
    odd = is_odd("fz")
    after[...], before[...] = paired(odd, got_a[0:96], got_b[0:96])
    out[0] = partial[0]
    for c in range(3):
        out[1 + c] = partial[1 + c] + (TIME_STEP * mix[1]) * received[c]
    remote_part(out, before, after, sides_far, TIME_STEP * mix[1] * PENALTY)
    if kind == "last":
        natural_order(out, given_out, turned, stored)
    else:
        faces_sent(odd, out, message_a, message_b)


def place(received, labelled, out, base):
    peers, size = labelled.shape[0], labelled.shape[1]
    fold = 192 // (size - 8)
    height = 64 // fold
    target = lax.broadcasted_iota(jnp.int32, (128, 128), 0)
    lane = lax.broadcasted_iota(jnp.int32, (128, 128), 1)
    total = None
    for peer in range(peers):
        label = labelled[peer, size - 8 : size - 7, :]
        label = jnp.broadcast_to(label, (128, 128)).astype(jnp.int32)
        hit = (label == target % 16) & (lane % 8 == target // 16)
        chosen = [jnp.where(hit & (lane // (128 // fold) == g), 1.0, 0.0) for g in range(fold)]
        chosen = jnp.concatenate(chosen, 0).astype(BF16)
        high, low = parts(received[peer, base : base + 3 * height])
        dims = (((1,), (1,)), ((), ()))
        value = lax.dot_general(high, chosen, dims, preferred_element_type=F32)
        value = value + lax.dot_general(low, chosen, dims, preferred_element_type=F32)
        total = value if total is None else total + value
    for c in range(3):
        for g in range(fold):
            at = c * height
            out[c, g * height : g * height + height] = total[at : at + height, g * 128 : g * 128 + 128]


def place_last_body(received, labelled, out):
    place(received, labelled, out, received.shape[1] // 2)


def kron_part(matrix, shape, rows_by, columns_by):
    row = lax.broadcasted_iota(jnp.int32, (shape[0], 8), 0)
    level = lax.broadcasted_iota(jnp.int32, (shape[0], 8), 1)
    left = (row // rows_by % 8 == level).astype(F32)
    level = lax.broadcasted_iota(jnp.int32, (8, shape[1]), 0)
    column = lax.broadcasted_iota(jnp.int32, (8, shape[1]), 1)
    right = (column // columns_by % 8 == level).astype(F32)
    return dot_full(dot_full(left, matrix), right)


def tables_body(
    packed,
    near,
    far,
    deriv_rows,
    deriv_lanes,
    pair,
    spread,
    labels,
    speed,
):
    size = near.shape[1]
    count = size // 8
    blocks = spread.shape[0] // 8

    def place_of(shape):
        return (lax.broadcasted_iota(jnp.int32, shape, 0), lax.broadcasted_iota(jnp.int32, shape, 1))

    row, column = place_of((count, size))
    repeat = (column % count == row).astype(F32)
    speed[...] = dot_full(packed[24:25, 0:count], repeat)
    wanted = dot_full(packed[16:24, 0:count], repeat).astype(jnp.int32)
    row, column = place_of((size, size))
    level, element = row // count, row % count
    level_out = column // count
    for facet in range(4):
        shift = -count if facet % 2 == 0 else count
        choice = jnp.broadcast_to(wanted[facet : facet + 1], (size, size))
        near[facet] = jnp.where((level == level_out) & (element == choice), 1.0, 0.0).astype(BF16)
        far[facet] = jnp.where((level == level_out) & (element + shift == choice), 1.0, 0.0).astype(BF16)
    lower = jnp.broadcast_to(wanted[4:5], (size, size))
    upper = jnp.broadcast_to(wanted[5:6], (size, size))
    hit = (level == 7) & (level_out == 0) & (element == lower)
    hit = hit | ((level == 0) & (level_out == 7) & (element == upper))
    near[4] = jnp.where(hit, 1.0, 0.0).astype(BF16)
    hit = (level == 0) & (level_out == 0) & (element - count == lower)
    hit = hit | ((level == 1) & (level_out == 7) & (element + count == upper))
    far[4] = jnp.where(hit, 1.0, 0.0).astype(BF16)

    row, column = place_of((64, 64))
    slopes, modes = packed[0:8, 0:8], packed[8:16, 0:8]
    outer = kron_part(slopes, (64, 64), 8, 8)
    inner = kron_part(slopes, (64, 64), 1, 1)
    deriv_rows[0:64] = jnp.where(row % 8 == column % 8, outer, 0.0)
    deriv_rows[64:128] = jnp.where(row // 8 == column // 8, inner, 0.0)
    row, column = place_of((size, size))
    lanes = kron_part(slopes.T, (size, size), count, count)
    deriv_lanes[...] = jnp.where(row % count == column % count, lanes, 0.0)
    pair[...] = kron_part(modes, (64, 64), 8, 8) * kron_part(modes, (64, 64), 1, 1)

    peers = labels.shape[0]
    capacity = capacity_of(peers, blocks)
    row, column = place_of((blocks, blocks))

    def upright(values):
        return jnp.sum(jnp.where(row == column, values, 0.0), 1, keepdims=True)

    owner_row = packed[25:26, 0:blocks]
    owner_column = upright(owner_row)
    earlier = (owner_column == owner_row) & (column < row)
    position = jnp.sum(jnp.where(earlier, 1.0, 0.0), 1, keepdims=True)
    slot = owner_column * capacity + position
    element_column = upright(packed[26:27, 0:blocks])
    row, column = place_of((8 * blocks, blocks))
    repeat = (row // 8 == column).astype(F32)
    slot = dot_full(repeat, jnp.broadcast_to(slot, (blocks, 128)))
    element = dot_full(repeat, jnp.broadcast_to(element_column, (blocks, 128)))
    row, column = place_of((8 * blocks, 128))
    values = kron_part(modes.T, (8 * blocks, 128), 1, 1)
    inside = column % (8 * capacity) // 8
    for peer in range(peers):
        chosen = slot == (inside + peer * capacity).astype(F32)
        spread[:, peer * 128 : peer * 128 + 128] = jnp.where(chosen, values, 0.0)
        named = jnp.where(chosen & (row % 8 == 0), element + 1.0, 0.0)
        labels[peer] = jnp.broadcast_to(jnp.sum(named, 0, keepdims=True) - 1.0, (8, 128))


def shifted(sizes, shifts):
    pairs = []
    for index in np.ndindex(*sizes):
        source = [(i + s) % n for i, s, n in zip(index, shifts, sizes)]
        pairs.append((int(np.ravel_multi_index(source, sizes)), int(np.ravel_multi_index(index, sizes))))
    return pairs


def partners(sizes, axis, second):
    pairs = []
    for index in np.ndindex(*sizes):
        source = list(index)
        step = 1 if (index[axis] % 2 == 0) != second else -1
        source[axis] = (index[axis] + step) % sizes[axis]
        pairs.append((int(np.ravel_multi_index(source, sizes)), int(np.ravel_multi_index(index, sizes))))
    return pairs


def per_device(
    density,
    velocity,
    pressure,
    acoustic,
    sound_speed,
    derivative,
    mode_basis,
    neighbours,
    block_owner,
    block_element,
):
    size_x, size_y, size_z = lax.axis_size("fx"), lax.axis_size("fy"), lax.axis_size("fz")
    devices = size_x * size_y * size_z
    cells_x = density.shape[0]
    elements = acoustic.shape[0]
    device = lax.axis_index(("fx", "fy", "fz"))

    names = ("fx", "fy", "fz")

    rows = 5 * cells_x * 8
    tiles = -(-rows // 128)
    square = velocity[0] * velocity[0] + velocity[1] * velocity[1] + velocity[2] * velocity[2]
    energy = pressure / (HEAT_RATIO - 1.0) + 0.5 * density * square
    rest = ((0, 0), (0, 0), (0, 0))
    state = jnp.pad(density[None], ((0, 4),) + rest) + jnp.pad(density * velocity, ((1, 1),) + rest)
    state = state + jnp.pad(energy[None], ((4, 0),) + rest)
    x_rows = 5 * 2 * HALO * 8
    flow_a, flow_b, along_x = call(
        pack_start_body, [(tiles * 8, 128), (tiles * 8, 128), (x_rows, 128)], state
    )
    edge_a = lax.ppermute(flow_a, "fz", partners((size_z,), 0, False))
    edge_b = lax.ppermute(flow_b, "fz", partners((size_z,), 0, True))
    x_steps = (1,) if size_x == 2 else (1, -1)
    beside_x = [lax.ppermute(along_x, "fx", shifted((size_x,), (step,))) for step in x_steps]

    near_pairs = [(i ^ 1, i) for i in range(devices)]
    far_pairs = [pair for i in range(1, devices - 1, 2) for pair in ((i, i + 1), (i + 1, i))]

    def traces(to_a, to_b):
        far_got = lax.ppermute(to_b, names, far_pairs)
        return lax.ppermute(to_a, names, near_pairs), far_got

    size = 8 * elements
    held = (4, 64, size)
    faces = (96, size)
    sides = [pltpu.VMEM(faces, F32)] * 2
    turning = [pltpu.VMEM((512, 128), F32), pltpu.VMEM((4, 4 * elements, 128), F32)]
    sound, to_a, to_b = call(
        acoustic_start_body,
        [held, faces, (2 * faces[0], size)],
        acoustic,
        edge_a,
        scratch=turning,
        last=1,
    )
    got_a, got_b = traces(to_a, to_b)

    edge = call(
        pack_next_body,
        [(40, 128)],
        state,
        flow_a,
        flow_b,
        edge_a,
        edge_b,
        got_a,
        last=1,
    )[0]
    edges_x = [lax.ppermute(edge, "fx", shifted((size_x,), (step,))) for step in x_steps]
    y_shape = (5 * cells_x * HALO + 48, 128)
    y_a, y_b = call(pack_last_body, [y_shape, y_shape], state, edge, *beside_x, *edges_x, cost=1)
    y_second = lax.ppermute(y_b, "fy", partners((size_y,), 0, True))
    y_first = lax.ppermute(y_a, "fy", partners((size_y,), 0, False))

    local = (neighbours - device * elements).T
    blocks = block_owner.size
    width = max(elements, blocks)

    def piece(values, first):
        values = values.astype(F32)
        return jnp.pad(values, ((first, 32 - first - values.shape[0]), (0, width - values.shape[1])))

    packed = (
        piece(derivative, 0)
        + piece(mode_basis, 8)
        + piece(local, 16)
        + piece(sound_speed.reshape(1, elements), 24)
        + piece(block_owner.reshape(1, blocks), 25)
        + piece(block_element.reshape(1, blocks), 26)
    )
    table = jax.ShapeDtypeStruct((5, size, size), BF16)
    near, far, deriv_rows, deriv_lanes, pair, spread, labels, speed = call(
        tables_body,
        [
            table,
            table,
            (128, 64),
            (size, size),
            (64, 64),
            (8 * blocks, size_y * 128),
            (size_y, 8, 128),
            (1, size),
        ],
        packed,
        cost=1,
    )

    fold = fold_of(size_y, blocks)
    wide = cells_x + 2 * HALO
    rows_scratch = pltpu.VMEM((3, 64, 128), F32)

    def planes(count):
        return (5, count, 16, 128)

    def route(send):
        return lax.all_to_all(send, "fy", split_axis=0, concat_axis=0, tiled=True)

    def local_part(mix, now):
        return call(
            functools.partial(acoustic_local_body, mix),
            [held],
            now,
            sound,
            deriv_rows,
            deriv_lanes,
            speed,
            near,
            scratch=sides,
            cost=1,
        )[0]

    partial = local_part(MIXES[0], sound)
    y_scratch = [pltpu.VMEM(y_shape, F32), pltpu.VMEM(y_shape, F32)]
    send = call(
        functools.partial(flow_sources_body, len(beside_x)),
        [(size_y, 192 // fold + 8, 128)],
        state,
        edge,
        *beside_x,
        y_first,
        y_second,
        pair,
        spread,
        labels,
        got_b,
        last=1,
        scratch=[
            pltpu.VMEM((4, cells_x + 2, 16, 128), F32),
            pltpu.VMEM((3, cells_x + 2, 16, 128), F32),
            rows_scratch,
            pltpu.VMEM((2, cells_x, 8, 128), F32),
        ]
        + y_scratch,
    )[0]
    received = route(send)
    second, derived, ends, send = call(
        functools.partial(flow_stages_body, len(edges_x)),
        [
            planes(wide - 4),
            planes(wide),
            (5, cells_x, 8, 128),
            (size_y, 2 * 192 // fold, 128),
        ],
        state,
        edge,
        *beside_x,
        *edges_x,
        y_first,
        y_second,
        pair,
        spread,
        partial,
        last=1,
        scratch=[
            rows_scratch,
            pltpu.VMEM(planes(wide - 2), F32),
            pltpu.VMEM(planes(wide - 2), F32),
            pltpu.VMEM(planes(wide), F32),
            pltpu.VMEM((5, 16, 256), F32),
        ]
        + y_scratch,
    )

    sound_one, to_a, to_b = call(
        functools.partial(acoustic_far_body, MIXES[0], "first"),
        [held, faces, (faces[0] + 32, size)],
        partial,
        got_a,
        got_b,
        far,
        received,
        send,
        scratch=sides + [rows_scratch],
        last=1,
    )
    labelled, received = received, route(send)
    got_a, got_b = traces(to_a, to_b)
    flow_state = call(flow_last_body, [(5, cells_x, 8, 128)], second, derived, ends, state)[0]
    partial = local_part(MIXES[1], sound_one)
    sound_two, to_a, to_b = call(
        functools.partial(acoustic_far_body, MIXES[1], "second"),
        [held, faces, (faces[0] + 32, size)],
        partial,
        got_a,
        got_b,
        far,
        received,
        labelled,
        scratch=sides + [rows_scratch],
    )
    source_three = call(place_last_body, [(3, 64, 128)], received, labelled)[0]
    got_a, got_b = traces(to_a, to_b)
    partial = local_part(MIXES[2], sound_two)
    sound_state = call(
        functools.partial(acoustic_far_body, MIXES[2], "last"),
        [(elements, 4, 512)],
        partial,
        got_a,
        got_b,
        far,
        source_three,
        scratch=sides + [pltpu.VMEM(held, F32)] + turning,
    )[0]
    return (flow_state, sound_state)


def solution(mesh):
    placed = (
        P("fx", "fy", "fz"),
        P(None, "fx", "fy", "fz"),
        P("fx", "fy", "fz"),
        P(("fx", "fy", "fz"), None, None),
        P(("fx", "fy", "fz")),
        P(),
        P(),
        P(("fx", "fy", "fz"), None),
        P("fx", "fy", "fz", None, None),
        P("fx", "fy", "fz", None),
    )
    return jax.shard_map(
        per_device,
        mesh=mesh,
        in_specs=placed,
        out_specs=(P(None, "fx", "fy", "fz"), P(("fx", "fy", "fz"), None, None)),
        check_vma=False,
    )
```

```python
import functools

import jax
import jax.numpy as jnp
import numpy as np
from jax import lax
from jax.experimental import pallas as pl
from jax.experimental.pallas import tpu as pltpu
from jax.sharding import PartitionSpec as P

HEAT_RATIO = 1.4
TIME_STEP = 0.1
VISCOSITY = 0.05
PENALTY = 0.5
HALO = 3
F32 = jnp.float32
BF16 = jnp.bfloat16
PARAMS = pltpu.CompilerParams(vmem_limit_bytes=24 * 1024 * 1024)
MIXES = ((0.0, 1.0), (0.75, 0.25), (1.0 / 3.0, 2.0 / 3.0))


def parts(values):
    high = values.astype(BF16)
    return high, (values - high.astype(F32)).astype(BF16)


def dot(left, right):
    return lax.dot_general(left, right, (((1,), (0,)), ((), ())), preferred_element_type=F32)


def dot_three(left, right):
    left_high, left_low = parts(left)
    right_high, right_low = parts(right)
    return dot(left_high, right_high) + dot(left_high, right_low) + dot(left_low, right_high)


def dot_full(left, right, dims=((1,), (0,))):
    return lax.dot_general(
        left, right, (dims, ((), ())), precision=lax.Precision.HIGHEST, preferred_element_type=F32
    )


def dot_exact_right(left, right):
    left_high, left_low = parts(left)
    return dot(left_high, right) + dot(left_low, right)


def call(body, outs, *operands, scratch=(), last=0, cost=None):
    whole = pl.BlockSpec(memory_space=pltpu.VMEM)
    outs = [out if isinstance(out, jax.ShapeDtypeStruct) else jax.ShapeDtypeStruct(out, F32) for out in outs]
    anywhere = pl.BlockSpec(memory_space=pl.ANY)
    return pl.pallas_call(
        body,
        out_shape=outs,
        in_specs=[whole] * (len(operands) - last) + [anywhere] * last,
        out_specs=[whole] * len(outs),
        scratch_shapes=list(scratch),
        compiler_params=PARAMS,
        cost_estimate=None if cost is None else pl.CostEstimate(flops=cost, bytes_accessed=cost, transcendentals=0),
    )(*operands)


def capacity_of(peers, blocks):
    return max(2, 2 * blocks // peers)


def fold_of(peers, blocks):
    return 128 // (8 * capacity_of(peers, blocks))


def is_odd(axis):
    return lax.axis_index(axis) % 2 == 1


def paired(odd, to_next, to_last):
    return jnp.where(odd, to_last, to_next), jnp.where(odd, to_next, to_last)


def pack_start_body(state, message_a, message_b, along_x):
    odd = is_odd("fz")
    rows = state[...].reshape(-1, 128)
    count = rows.shape[0]
    for tile in range(message_a.shape[0] // 8):
        piece = rows[tile * 128 : min(count, tile * 128 + 128)]
        if piece.shape[0] < 128:
            piece = jnp.concatenate([piece, jnp.zeros((128 - piece.shape[0], 128), F32)], 0)
        turned = piece.T
        first, second = paired(odd, turned[120:128], turned[0:8])
        message_a[tile * 8 : tile * 8 + 8] = first
        message_b[tile * 8 : tile * 8 + 8] = second
    cells_x = state.shape[1]
    for f in range(5):
        for s, x in enumerate(x_planes(cells_x)):
            at = (f * 2 * HALO + s) * 8
            along_x[at : at + 8] = state[f, x]


def pack_next_body(state, sent_a, sent_b, got_a, got_b, _, edge):
    cells_x = state.shape[1]
    odd_z = is_odd("fz")
    high, low = paired(odd_z, sent_a[...], sent_b[...])
    above, below = paired(odd_z, got_a[...], got_b[...])
    row = lax.broadcasted_iota(jnp.int32, (8, 128), 0)
    x_of_lane = lax.broadcasted_iota(jnp.int32, (16, 128), 1) // 8 % cells_x
    for tile in range(high.shape[0] // 8):
        rows = slice(tile * 8, tile * 8 + 8)
        upper = jnp.where(row < 3, pltpu.roll(high[rows], 3, 0), pltpu.roll(above[rows], 3, 0))
        lower = jnp.where(row < 3, pltpu.roll(below[rows], 3, 0), pltpu.roll(low[rows], 3, 0))
        slots = jnp.concatenate([upper, lower], 0)
        spread = jnp.concatenate([jnp.where(x_of_lane == x, slots, 0.0) for x in range(8)], 0).T
        for half in range(16 // cells_x):
            f = tile * (16 // cells_x) + half
            if f < 5:
                at = half * cells_x * 8
                total = spread[at : at + 8]
                for x in range(1, cells_x):
                    total = total + spread[at + x * 8 : at + x * 8 + 8]
                edge[f * 8 : f * 8 + 8] = total


def x_planes(cells_x):
    return [cells_x - HALO + i for i in range(HALO)] + list(range(HALO))


def sides_of(beside_x):
    return beside_x[0], beside_x[-1]


def beyond(edges_x, f):
    after, before = sides_of(edges_x)
    at = f * 8
    if after is before:
        return after[at : at + 8]
    lane = lax.broadcasted_iota(jnp.int32, (8, 128), 1)
    return jnp.where(lane < 64, after[at : at + 8], before[at : at + 8])


def pack_last_body(state, edge, *refs):
    (y_a, y_b), refs = refs[-2:], refs[:-2]
    beside_x, edges_x = refs[: len(refs) // 2], refs[len(refs) // 2 :]
    cells_x = state.shape[1]
    odd = is_odd("fy")
    after, before = sides_of(beside_x)

    def put(at, values, height):
        first, second = paired(odd, values[8 - height : 8], values[0:height])
        y_a[at : at + height] = first
        y_b[at : at + height] = second

    lines = 5 * cells_x * HALO
    for f in range(5):
        for x in range(cells_x):
            put((f * cells_x + x) * HALO, state[f, x], HALO)
        at = lines + f * 6
        for slot, height in ((1, 1), (2, 2), (3, 2), (4, 1)):
            source = (f * 2 * HALO + slot) * 8
            put(at, (before if slot < HALO else after)[source : source + 8], height)
            at += height
        put(lines + 30 + f * 2, edge[f * 8 : f * 8 + 8], 2)
        put(lines + 40 + f, beyond(edges_x, f), 1)


def assemble_speeds(wide, state, beside_x, above, below):
    cells_x = state.shape[1]
    after, before = sides_of(beside_x)
    for f in range(4):
        for x in range(cells_x):
            wide[f, 1 + x, 0:8] = state[f, x]
            at = (f * cells_x + x) * HALO
            wide[f, 1 + x, 8:9] = above[at : at + 1]
            wide[f, 1 + x, 15:16] = below[at + HALO - 1 : at + HALO]
        for slot, plane, source in ((HALO - 1, 0, before), (HALO, cells_x + 1, after)):
            at = (f * 2 * HALO + slot) * 8
            wide[f, plane, 0:8] = source[at : at + 8]


def assemble(wide, rim, state, edge, beside_x, edges_x, above, below):
    cells_x = state.shape[1]
    after, before = sides_of(beside_x)
    lines = 5 * cells_x * HALO
    for f in range(5):
        for x in range(cells_x):
            wide[f, HALO + x, 0:8] = state[f, x]
            at = (f * cells_x + x) * HALO
            wide[f, HALO + x, 8 : 8 + HALO] = above[at : at + HALO]
            wide[f, HALO + x, 16 - HALO : 16] = below[at : at + HALO]
        for slot in range(2 * HALO):
            plane = slot if slot < HALO else cells_x + slot
            at = (f * 2 * HALO + slot) * 8
            wide[f, plane, 0:8] = (before if slot < HALO else after)[at : at + 8]
        at = lines + f * 6
        for slot, height in ((1, 1), (2, 2), (3, 2), (4, 1)):
            plane = slot if slot < HALO else cells_x + slot
            wide[f, plane, 8 : 8 + height] = above[at : at + height]
            wide[f, plane, 16 - height : 16] = below[at : at + height]
            at += height
        rim[f, 0:8, 0:128] = edge[f * 8 : f * 8 + 8]
        rim[f, 0:8, 128:256] = beyond(edges_x, f)
        at = lines + 30 + f * 2
        rim[f, 8:10, 0:128] = above[at : at + 2]
        rim[f, 14:16, 0:128] = below[at : at + 2]
        at = lines + 40 + f
        rim[f, 8:9, 128:256] = above[at : at + 1]
        rim[f, 15:16, 128:256] = below[at : at + 1]


def primitive(rho, mx, my, mz, energy):
    inverse = 1.0 / rho
    u, v, w = mx * inverse, my * inverse, mz * inverse
    p = (HEAT_RATIO - 1.0) * (energy - 0.5 * (mx * u + my * v + mz * w))
    return u, v, w, p, jnp.sqrt(HEAT_RATIO * jnp.abs(p) * inverse)


def chunks(first, last, size):
    return [(i, min(i + size, last)) for i in range(first, last, size)]


def derive_planes(wide, derived, first, last):
    for i, j in chunks(first, last, 4):
        for k, value in enumerate(primitive(*[wide[f, i:j] for f in range(5)])):
            derived[k, i:j] = value


def derive_speeds(wide, derived, first, last):
    for i, j in chunks(first, last, 5):
        inverse = 1.0 / wide[0, i:j]
        for k in range(3):
            derived[k, i:j] = wide[1 + k, i:j] * inverse


def with_flux(fields, other, along):
    speed, p = other[along], other[3]
    out = [fields[1 + along]]
    for k in range(3):
        value = fields[1 + k] * speed
        out.append(value + p if k == along else value)
    out.append((fields[4] + p) * speed)
    return fields, out, jnp.abs(speed) + other[4]


def face(left, right):
    (fields_l, flux_l, speed_l), (fields_r, flux_r, speed_r) = left, right
    speed = jnp.maximum(speed_l, speed_r)
    viscous = speed + 2.0 * VISCOSITY
    return [
        (flux_l[f] + flux_r[f]) - (viscous if 1 <= f <= 3 else speed) * (fields_r[f] - fields_l[f])
        for f in range(5)
    ]


def rolled(here, shift, axis):
    fields, flux, speed = here
    return (
        [pltpu.roll(a, shift, axis) for a in fields],
        [pltpu.roll(a, shift, axis) for a in flux],
        pltpu.roll(speed, shift, axis),
    )


def rim_section(fields, start, mix):
    other = primitive(*fields)
    here = with_flux(fields, other, 2)
    along_z = face(here, rolled(here, 255, 1))
    if mix is None:
        return other, along_z, None
    total = [g - pltpu.roll(g, 1, 1) for g in along_z]
    for along, step, axis, size in ((0, 16, 1, 256), (1, 1, 0, 16)):
        here = with_flux(fields, other, along)
        faces = face(here, rolled(here, size - step, axis))
        total = [total[f] + (faces[f] - pltpu.roll(faces[f], step, axis)) for f in range(5)]
    out = []
    for f in range(5):
        value = fields[f] - (0.5 * TIME_STEP) * total[f]
        out.append(mix[0] * start[f] + mix[1] * value if mix[0] != 0.0 else value)
    return other, along_z, out


def to_ends(values, after, rows, first, last, ends):
    slot = lax.broadcasted_iota(jnp.int32, (rows, 256), 1) % 16
    for f, value in enumerate(values):
        value = value[0:rows]
        value = jnp.where(slot == 9, pltpu.roll(value, 9 - after, 1), value)
        for x in range(first, last):
            at = x % 16 // 8 * 128
            move = (118 - x % 8 * 16) % 128
            tile = value[:, at : at + 128]
            ends[f, x - first, 0:rows] = pltpu.roll(tile, move, 1) if move else tile


def flow_rate_section(wide, derived, ends, start, offset, mix, write, inner=False):
    depth = wide.shape[1]
    rows = slice(0, 8) if inner else slice(None)
    size = 4 if inner else 2

    def planes(i, j, kept, along):
        fields = [wide[f, i:j, kept] for f in range(5)]
        return with_flux(fields, [derived[f, i:j, kept] for f in range(5)], along)

    def cut(here, i, j):
        return [a[i:j] for a in here[0]], [a[i:j] for a in here[1]], here[2][i:j]

    for i, j in chunks(1, depth - 1, size):
        count = j - i
        lane = lax.broadcasted_iota(jnp.int32, (count, 8 if inner else 16, 128), 2)
        here = planes(i - 1, j + 1, rows, 0)
        faces = face(cut(here, 0, count + 1), cut(here, 1, count + 2))
        total = [g[1:] - g[:-1] for g in faces]
        here = planes(i, j, slice(None), 1)
        faces = face(here, rolled(here, 15, 1))
        for f in range(5):
            change = faces[f] - pltpu.roll(faces[f], 1, 1)
            total[f] = total[f] + (change[:, 0:8] if inner else change)
        here = planes(i, j, rows, 2)
        faces = face(here, rolled(here, 127, 2))
        for f in range(5):
            end = ends[f, i - 1 : j - 1, rows]
            value = jnp.where(lane == 127, end, faces[f])
            total[f] = total[f] + (value - jnp.where(lane == 0, end, pltpu.roll(value, 1, 2)))
        for f in range(5):
            value = wide[f, i:j, rows] - (0.5 * TIME_STEP) * total[f]
            if mix[0] != 0.0:
                value = mix[0] * start[f, i + offset : j + offset, rows] + mix[1] * value
            write(slice(i - 1, j - 1), f, value)


def lamb(derived, ends, first, cells_x, lamb_rows):
    for i, j in chunks(first, first + cells_x, 4):
        count = j - i
        lane = lax.broadcasted_iota(jnp.int32, (count, 8, 128), 2)
        vel = [derived[c, i:j, 0:8] for c in range(3)]
        along_x = [derived[c, i + 1 : j + 1, 0:8] - derived[c, i - 1 : j - 1, 0:8] for c in range(3)]
        along_y = []
        for c in range(3):
            column = derived[c, i:j]
            along_y.append((pltpu.roll(column, 15, 1) - pltpu.roll(column, 1, 1))[:, 0:8])
        along_z = []
        for c in range(2):
            end = ends[c, i - first : j - first, 0:8]
            after = jnp.where(lane == 127, end, pltpu.roll(vel[c], 127, 2))
            along_z.append(after - jnp.where(lane == 0, end, pltpu.roll(vel[c], 1, 2)))
        curl = [
            0.5 * (along_y[2] - along_z[1]),
            0.5 * (along_z[0] - along_x[2]),
            0.5 * (along_x[1] - along_y[0]),
        ]
        at = slice((i - first) * 8, (j - first) * 8)
        lamb_rows[0, at] = (curl[1] * vel[2] - curl[2] * vel[1]).reshape(count * 8, 128)
        lamb_rows[1, at] = (curl[2] * vel[0] - curl[0] * vel[2]).reshape(count * 8, 128)
        lamb_rows[2, at] = (curl[0] * vel[1] - curl[1] * vel[0]).reshape(count * 8, 128)


def project(lamb_rows, pair, spread, send, base):
    peers = send.shape[0]
    fold = fold_of(peers, spread.shape[0] // 8)
    height = 64 // fold
    group = lax.broadcasted_iota(jnp.int32, (height, 128), 1) // (128 // fold)
    modes = dot_three(pair[...], jnp.concatenate([lamb_rows[c] for c in range(3)], 1))
    modes = jnp.concatenate([modes[:, c * 128 : c * 128 + 128] for c in range(3)], 0)
    sent = dot_three(modes, spread[...])
    for c in range(3):
        for peer in range(peers):
            mine = sent[c * 64 : c * 64 + 64, peer * 128 : peer * 128 + 128]
            folded = mine[0:height]
            for g in range(1, fold):
                folded = jnp.where(group == g, mine[g * height : g * height + height], folded)
            send[peer, base + c * height : base + c * height + height] = folded


def flow_sources_body(count, state, edge, *refs):
    beside_x, refs = refs[:count], refs[count:]
    got_a, got_b, pair, spread, labels, send, wide, derived, lamb_rows, ends, above, below = refs
    cells_x = state.shape[1]
    above[...], below[...] = paired(is_odd("fy"), got_a[...], got_b[...])
    assemble_speeds(wide, state, beside_x, above, below)
    derive_speeds(wide, derived, 0, cells_x + 2)
    inverse = 1.0 / edge[0:8]
    speeds = [jnp.concatenate([edge[k * 8 : k * 8 + 8] * inverse] * 2, 1) for k in (1, 2)]
    to_ends(speeds, 3, 8, 0, cells_x, ends)
    lamb(derived, ends, 1, cells_x, lamb_rows)
    project(lamb_rows, pair, spread, send, 0)
    send[:, send.shape[1] - 8 :] = labels[...]


def writer(target):
    def write(i, f, value):
        target[f, i] = value

    return write


def flow_stages_body(count, state, edge, *refs):
    beside_x, edges_x, refs = refs[:count], refs[count : 2 * count], refs[2 * count :]
    got_a, got_b, pair, spread, _, _, second, derived, ends_out, send, *refs = refs
    lamb_rows, ends, first, wide, rim, above, below = refs
    above[...], below[...] = paired(is_odd("fy"), got_a[...], got_b[...])
    assemble(wide, rim, state, edge, beside_x, edges_x, above, below)
    planes = wide.shape[1]
    cells_x = planes - 2 * HALO
    size = send.shape[1] // 2
    rim_start = [rim[f] for f in range(5)]
    derive_planes(wide, derived, 0, planes)
    _, along_z, rim_first = rim_section(rim_start, None, MIXES[0])
    to_ends(along_z, 2, 16, -2, cells_x + 2, ends)
    flow_rate_section(wide, derived, ends, wide, 0, MIXES[0], writer(first))
    derive_planes(first, derived, 0, planes - 2)
    other, along_z, rim_second = rim_section(rim_first, [rim[f] for f in range(5)], MIXES[1])
    to_ends(other[0:2], 3, 8, 0, cells_x, ends)
    lamb(derived, ends, 2, cells_x, lamb_rows)
    project(lamb_rows, pair, spread, send, 0)
    to_ends(along_z, 2, 16, -1, cells_x + 1, ends)
    flow_rate_section(first, derived, ends, wide, 1, MIXES[1], writer(second))
    derive_planes(second, derived, 0, planes - 4)
    other, along_z, _ = rim_section(rim_second, None, None)
    to_ends(other[0:2], 3, 8, 0, cells_x, ends)
    lamb(derived, ends, 1, cells_x, lamb_rows)
    project(lamb_rows, pair, spread, send, size)
    to_ends(along_z, 2, 8, 0, cells_x, ends_out)


def flow_last_body(second, derived, ends, state, out):
    flow_rate_section(second, derived, ends, state, -1, MIXES[2], writer(out), inner=True)


def faces_out(state, rear, front):
    lane = lax.broadcasted_iota(jnp.int32, (32, 128), 1) // 16
    for c in range(4):
        front[c * 8 : c * 8 + 8] = state[c, 56:64]
        rear[c * 8 : c * 8 + 8] = state[c, 0:8]
        front[32 + c * 8 : 40 + c * 8] = state[c, pl.ds(7, 8, stride=8), :]
        rear[32 + c * 8 : 40 + c * 8] = state[c, pl.ds(0, 8, stride=8), :]
    rows = state[...].reshape(256, 128)
    last = jnp.zeros((32, 128), F32)
    first = jnp.zeros((32, 128), F32)
    for j in range(8):
        piece = rows[j * 32 : j * 32 + 32]
        last = jnp.where(lane == j, pltpu.roll(piece, (j * 16 + 16) % 128, 1), last)
        first = jnp.where(lane == j, pltpu.roll(piece, j * 16, 1) if j else piece, first)
    front[64:96] = last
    rear[64:96] = first


def faces_sent(odd, state, message_a, message_b):
    size = message_a.shape[0]
    faces_out(state, message_b, message_a)
    message_a[...], message_b[0:size] = paired(odd, message_a[...], message_b[0:size])
    if message_b.shape[0] > size:
        message_b[size:] = jnp.zeros((message_b.shape[0] - size, 128), F32)


def lift(total, before, after, sides, factor):
    def place(face, rows, target):
        value = factor * dot_exact_right(rows, sides[face])
        for c in range(4):
            total[c, target, :] += value[c * 8 : c * 8 + 8]

    place(0, before[0:32], pl.ds(0, 8))
    place(1, after[0:32], pl.ds(56, 8))
    place(2, before[32:64], pl.ds(0, 8, stride=8))
    place(3, after[32:64], pl.ds(7, 8, stride=8))


def rate_local(state, deriv_rows, deriv_lanes, speed, sides):
    fields = [state[c] for c in range(4)]
    by_rows = dot_three(deriv_rows[...], jnp.concatenate(fields[0:3], 1))
    by_lanes = dot_three(jnp.concatenate([fields[0], fields[3]], 0), deriv_lanes[...])
    divergence = by_rows[0:64, 128:256] + by_rows[64:128, 256:384] + by_lanes[64:128]
    rates = [
        -(speed[...] * speed[...]) * divergence,
        -by_rows[0:64, 0:128],
        -by_rows[64:128, 0:128],
        -by_lanes[0:64],
    ]
    row = lax.broadcasted_iota(jnp.int32, (64, 128), 0)
    lane = lax.broadcasted_iota(jnp.int32, (64, 128), 1)
    count = jnp.zeros((64, 128), F32)
    for value in (row // 8, row % 8, lane // 16):
        count = count + jnp.where((value == 0) | (value == 7), PENALTY, 0.0)
    side = PENALTY * dot_exact_right(state[...].reshape(256, 128), sides[4])
    return [rates[c] - count * fields[c] + side[c * 64 : c * 64 + 64] for c in range(4)]


def acoustic_local_body(mix, state, start, deriv_rows, deriv_lanes, speed, sides, out, front, rear):
    rates = rate_local(state, deriv_rows, deriv_lanes, speed, sides)
    for c in range(4):
        value = state[c] + TIME_STEP * rates[c]
        if mix[0] != 0.0:
            value = mix[0] * start[c] + mix[1] * value
        out[c] = value
    faces_out(state, rear, front)
    lift(out, front, rear, sides, TIME_STEP * mix[1] * PENALTY)


def acoustic_start_body(given, _, state, message_a, message_b, turned, stored):
    count = given.shape[0]
    for e in range(count):
        for t in range(4):
            stored[t, 4 * e : 4 * e + 4] = given[e, :, t * 128 : t * 128 + 128]
    for t in range(4):
        rows = [stored[t, pl.ds(c, count, stride=4), :] for c in range(4)]
        rows = jnp.concatenate(rows + [jnp.zeros((128 - 4 * count, 128), F32)], 0)
        turned[t * 128 : t * 128 + 128] = rows.T
    lane = lax.broadcasted_iota(jnp.int32, (64, 128), 1) // count
    fields = [jnp.zeros((64, 128), F32)] * 4
    for z in range(8):
        piece = turned[pl.ds(z, 64, stride=8), :]
        for c in range(4):
            move = (z - c) * count % 128
            fields[c] = jnp.where(lane == z, pltpu.roll(piece, move, 1) if move else piece, fields[c])
    for c in range(4):
        state[c] = fields[c]
    faces_sent(is_odd("fz"), state, message_a, message_b)


def natural_order(state, out, turned, stored):
    count = out.shape[0]
    lane = lax.broadcasted_iota(jnp.int32, (64, 128), 1) // count
    for z in range(8):
        value = jnp.zeros((64, 128), F32)
        for c in range(4):
            move = (c - z) * count % 128
            value = jnp.where(lane == c, pltpu.roll(state[c], move, 1) if move else state[c], value)
        turned[pl.ds(z, 64, stride=8), :] = value
    for t in range(4):
        rows = turned[t * 128 : t * 128 + 128].T
        for c in range(4):
            stored[t, pl.ds(c, count, stride=4), :] = rows[c * count : c * count + count]
    for e in range(count):
        for t in range(4):
            out[e, :, t * 128 : t * 128 + 128] = stored[t, 4 * e : 4 * e + 4]


def remote_part(out, before, after, sides_far, factor):
    lift(out, before, after, sides_far, factor)
    lane = lax.broadcasted_iota(jnp.int32, (32, 128), 1) // 16
    last, first = before[64:96], after[64:96]
    pieces = []
    for j in range(8):
        left = pltpu.roll(last, 128 - j * 16, 1) if j else last
        right = pltpu.roll(first, (144 - j * 16) % 128, 1) if j != 1 else first
        pieces.append(jnp.where(lane == 0, left, jnp.where(lane == 1, right, 0.0)))
    value = factor * dot_exact_right(jnp.concatenate(pieces, 0), sides_far[4])
    for c in range(4):
        out[c] += value[c * 64 : c * 64 + 64]


def acoustic_far_body(mix, kind, partial, got_a, got_b, sides_far, received, *refs):
    if kind == "last":
        given_out, before, after, out, turned, stored = refs
    elif kind == "first":
        _, out, message_a, message_b, before, after, source = refs
        place(received, received, source, 0)
        received = source
    else:
        labelled, out, message_a, message_b, before, after, source = refs
        place(received, labelled, source, 0)
        received = source
    odd = is_odd("fz")
    after[...], before[...] = paired(odd, got_a[0:96], got_b[0:96])
    out[0] = partial[0]
    for c in range(3):
        out[1 + c] = partial[1 + c] + (TIME_STEP * mix[1]) * received[c]
    remote_part(out, before, after, sides_far, TIME_STEP * mix[1] * PENALTY)
    if kind == "last":
        natural_order(out, given_out, turned, stored)
    else:
        faces_sent(odd, out, message_a, message_b)


def place(received, labelled, out, base):
    peers, size = labelled.shape[0], labelled.shape[1]
    fold = 192 // (size - 8)
    height = 64 // fold
    target = lax.broadcasted_iota(jnp.int32, (128, 128), 0)
    lane = lax.broadcasted_iota(jnp.int32, (128, 128), 1)
    total = None
    for peer in range(peers):
        label = labelled[peer, size - 8 : size - 7, :]
        label = jnp.broadcast_to(label, (128, 128)).astype(jnp.int32)
        hit = (label == target % 16) & (lane % 8 == target // 16)
        chosen = [jnp.where(hit & (lane // (128 // fold) == g), 1.0, 0.0) for g in range(fold)]
        chosen = jnp.concatenate(chosen, 0).astype(BF16)
        high, low = parts(received[peer, base : base + 3 * height])
        dims = (((1,), (1,)), ((), ()))
        value = lax.dot_general(high, chosen, dims, preferred_element_type=F32)
        value = value + lax.dot_general(low, chosen, dims, preferred_element_type=F32)
        total = value if total is None else total + value
    for c in range(3):
        for g in range(fold):
            at = c * height
            out[c, g * height : g * height + height] = total[at : at + height, g * 128 : g * 128 + 128]


def place_last_body(received, labelled, out):
    place(received, labelled, out, received.shape[1] // 2)


def kron_part(matrix, shape, rows_by, columns_by):
    row = lax.broadcasted_iota(jnp.int32, (shape[0], 8), 0)
    level = lax.broadcasted_iota(jnp.int32, (shape[0], 8), 1)
    left = (row // rows_by % 8 == level).astype(F32)
    level = lax.broadcasted_iota(jnp.int32, (8, shape[1]), 0)
    column = lax.broadcasted_iota(jnp.int32, (8, shape[1]), 1)
    right = (column // columns_by % 8 == level).astype(F32)
    return dot_full(dot_full(left, matrix), right)


def tables_body(
    packed,
    faces,
    far_faces,
    near,
    far,
    deriv_rows,
    deriv_lanes,
    pair,
    spread,
    labels,
    speed,
):
    far_faces[0 : faces.shape[0]] = faces[...]
    far_faces[faces.shape[0] :] = jnp.zeros((far_faces.shape[0] - faces.shape[0], 128), F32)
    size = near.shape[1]
    count = size // 8
    blocks = spread.shape[0] // 8

    def place_of(shape):
        return (lax.broadcasted_iota(jnp.int32, shape, 0), lax.broadcasted_iota(jnp.int32, shape, 1))

    row, column = place_of((count, size))
    repeat = (column % count == row).astype(F32)
    speed[...] = dot_full(packed[24:25, 0:count], repeat)
    wanted = dot_full(packed[16:24, 0:count], repeat).astype(jnp.int32)
    row, column = place_of((size, size))
    level, element = row // count, row % count
    level_out = column // count
    for facet in range(4):
        shift = -count if facet % 2 == 0 else count
        choice = jnp.broadcast_to(wanted[facet : facet + 1], (size, size))
        near[facet] = jnp.where((level == level_out) & (element == choice), 1.0, 0.0).astype(BF16)
        far[facet] = jnp.where((level == level_out) & (element + shift == choice), 1.0, 0.0).astype(BF16)
    lower = jnp.broadcast_to(wanted[4:5], (size, size))
    upper = jnp.broadcast_to(wanted[5:6], (size, size))
    hit = (level == 7) & (level_out == 0) & (element == lower)
    hit = hit | ((level == 0) & (level_out == 7) & (element == upper))
    near[4] = jnp.where(hit, 1.0, 0.0).astype(BF16)
    hit = (level == 0) & (level_out == 0) & (element - count == lower)
    hit = hit | ((level == 1) & (level_out == 7) & (element + count == upper))
    far[4] = jnp.where(hit, 1.0, 0.0).astype(BF16)

    row, column = place_of((64, 64))
    slopes, modes = packed[0:8, 0:8], packed[8:16, 0:8]
    outer = kron_part(slopes, (64, 64), 8, 8)
    inner = kron_part(slopes, (64, 64), 1, 1)
    deriv_rows[0:64] = jnp.where(row % 8 == column % 8, outer, 0.0)
    deriv_rows[64:128] = jnp.where(row // 8 == column // 8, inner, 0.0)
    row, column = place_of((size, size))
    lanes = kron_part(slopes.T, (size, size), count, count)
    deriv_lanes[...] = jnp.where(row % count == column % count, lanes, 0.0)
    pair[...] = kron_part(modes, (64, 64), 8, 8) * kron_part(modes, (64, 64), 1, 1)

    peers = labels.shape[0]
    capacity = capacity_of(peers, blocks)
    row, column = place_of((blocks, blocks))

    def upright(values):
        return jnp.sum(jnp.where(row == column, values, 0.0), 1, keepdims=True)

    owner_row = packed[25:26, 0:blocks]
    owner_column = upright(owner_row)
    earlier = (owner_column == owner_row) & (column < row)
    position = jnp.sum(jnp.where(earlier, 1.0, 0.0), 1, keepdims=True)
    slot = owner_column * capacity + position
    element_column = upright(packed[26:27, 0:blocks])
    row, column = place_of((8 * blocks, blocks))
    repeat = (row // 8 == column).astype(F32)
    slot = dot_full(repeat, jnp.broadcast_to(slot, (blocks, 128)))
    element = dot_full(repeat, jnp.broadcast_to(element_column, (blocks, 128)))
    row, column = place_of((8 * blocks, 128))
    values = kron_part(modes.T, (8 * blocks, 128), 1, 1)
    inside = column % (8 * capacity) // 8
    for peer in range(peers):
        chosen = slot == (inside + peer * capacity).astype(F32)
        spread[:, peer * 128 : peer * 128 + 128] = jnp.where(chosen, values, 0.0)
        named = jnp.where(chosen & (row % 8 == 0), element + 1.0, 0.0)
        labels[peer] = jnp.broadcast_to(jnp.sum(named, 0, keepdims=True) - 1.0, (8, 128))


def shifted(sizes, shifts):
    pairs = []
    for index in np.ndindex(*sizes):
        source = [(i + s) % n for i, s, n in zip(index, shifts, sizes)]
        pairs.append((int(np.ravel_multi_index(source, sizes)), int(np.ravel_multi_index(index, sizes))))
    return pairs


def partners(sizes, axis, second):
    pairs = []
    for index in np.ndindex(*sizes):
        source = list(index)
        step = 1 if (index[axis] % 2 == 0) != second else -1
        source[axis] = (index[axis] + step) % sizes[axis]
        pairs.append((int(np.ravel_multi_index(source, sizes)), int(np.ravel_multi_index(index, sizes))))
    return pairs


def per_device(
    density,
    velocity,
    pressure,
    acoustic,
    sound_speed,
    derivative,
    mode_basis,
    neighbours,
    block_owner,
    block_element,
):
    size_x, size_y, size_z = lax.axis_size("fx"), lax.axis_size("fy"), lax.axis_size("fz")
    devices = size_x * size_y * size_z
    cells_x = density.shape[0]
    elements = acoustic.shape[0]
    device = lax.axis_index(("fx", "fy", "fz"))

    names = ("fx", "fy", "fz")

    rows = 5 * cells_x * 8
    tiles = -(-rows // 128)
    square = velocity[0] * velocity[0] + velocity[1] * velocity[1] + velocity[2] * velocity[2]
    energy = pressure / (HEAT_RATIO - 1.0) + 0.5 * density * square
    rest = ((0, 0), (0, 0), (0, 0))
    state = jnp.pad(density[None], ((0, 4),) + rest) + jnp.pad(density * velocity, ((1, 1),) + rest)
    state = state + jnp.pad(energy[None], ((4, 0),) + rest)
    x_rows = 5 * 2 * HALO * 8
    flow_a, flow_b, along_x = call(
        pack_start_body, [(tiles * 8, 128), (tiles * 8, 128), (x_rows, 128)], state
    )
    edge_a = lax.ppermute(flow_a, "fz", partners((size_z,), 0, False))
    edge_b = lax.ppermute(flow_b, "fz", partners((size_z,), 0, True))
    x_steps = (1,) if size_x == 2 else (1, -1)
    beside_x = [lax.ppermute(along_x, "fx", shifted((size_x,), (step,))) for step in x_steps]

    near_pairs = [(i ^ 1, i) for i in range(devices)]
    far_pairs = [pair for i in range(1, devices - 1, 2) for pair in ((i, i + 1), (i + 1, i))]

    def traces(to_a, to_b):
        far_got = lax.ppermute(to_b, names, far_pairs)
        return lax.ppermute(to_a, names, near_pairs), far_got

    size = 8 * elements
    held = (4, 64, size)
    faces = (96, size)
    sides = [pltpu.VMEM(faces, F32)] * 2
    turning = [pltpu.VMEM((512, 128), F32), pltpu.VMEM((4, 4 * elements, 128), F32)]
    sound, to_a, to_b = call(
        acoustic_start_body,
        [held, faces, faces],
        acoustic,
        edge_a,
        scratch=turning,
        last=1,
    )
    got_a = lax.ppermute(to_a, names, near_pairs)

    edge = call(
        pack_next_body,
        [(40, 128)],
        state,
        flow_a,
        flow_b,
        edge_a,
        edge_b,
        got_a,
        last=1,
    )[0]
    edges_x = [lax.ppermute(edge, "fx", shifted((size_x,), (step,))) for step in x_steps]
    y_shape = (5 * cells_x * HALO + 48, 128)
    y_a, y_b = call(pack_last_body, [y_shape, y_shape], state, edge, *beside_x, *edges_x, cost=1)
    y_second = lax.ppermute(y_b, "fy", partners((size_y,), 0, True))
    y_first = lax.ppermute(y_a, "fy", partners((size_y,), 0, False))

    local = (neighbours - device * elements).T
    blocks = block_owner.size
    width = max(elements, blocks)

    def piece(values, first):
        values = values.astype(F32)
        return jnp.pad(values, ((first, 32 - first - values.shape[0]), (0, width - values.shape[1])))

    packed = (
        piece(derivative, 0)
        + piece(mode_basis, 8)
        + piece(local, 16)
        + piece(sound_speed.reshape(1, elements), 24)
        + piece(block_owner.reshape(1, blocks), 25)
        + piece(block_element.reshape(1, blocks), 26)
    )
    table = jax.ShapeDtypeStruct((5, size, size), BF16)
    to_b, near, far, deriv_rows, deriv_lanes, pair, spread, labels, speed = call(
        tables_body,
        [
            (256, size),
            table,
            table,
            (128, 64),
            (size, size),
            (64, 64),
            (8 * blocks, size_y * 128),
            (size_y, 8, 128),
            (1, size),
        ],
        packed,
        to_b,
        cost=1,
    )
    got_b = lax.ppermute(to_b, names, far_pairs)

    fold = fold_of(size_y, blocks)
    wide = cells_x + 2 * HALO
    rows_scratch = pltpu.VMEM((3, 64, 128), F32)

    def planes(count):
        return (5, count, 16, 128)

    def route(send):
        return lax.all_to_all(send, "fy", split_axis=0, concat_axis=0, tiled=True)

    def local_part(mix, now):
        return call(
            functools.partial(acoustic_local_body, mix),
            [held],
            now,
            sound,
            deriv_rows,
            deriv_lanes,
            speed,
            near,
            scratch=sides,
            cost=1,
        )[0]

    partial = local_part(MIXES[0], sound)
    y_scratch = [pltpu.VMEM(y_shape, F32), pltpu.VMEM(y_shape, F32)]
    send = call(
        functools.partial(flow_sources_body, len(beside_x)),
        [(size_y, 192 // fold + 8, 128)],
        state,
        edge,
        *beside_x,
        y_first,
        y_second,
        pair,
        spread,
        labels,
        scratch=[
            pltpu.VMEM((4, cells_x + 2, 16, 128), F32),
            pltpu.VMEM((3, cells_x + 2, 16, 128), F32),
            rows_scratch,
            pltpu.VMEM((2, cells_x, 8, 128), F32),
        ]
        + y_scratch,
    )[0]
    received = route(send)
    second, derived, ends, send = call(
        functools.partial(flow_stages_body, len(edges_x)),
        [
            planes(wide - 4),
            planes(wide),
            (5, cells_x, 8, 128),
            (size_y, 2 * 192 // fold, 128),
        ],
        state,
        edge,
        *beside_x,
        *edges_x,
        y_first,
        y_second,
        pair,
        spread,
        partial,
        got_b,
        last=2,
        scratch=[
            rows_scratch,
            pltpu.VMEM(planes(wide - 2), F32),
            pltpu.VMEM(planes(wide - 2), F32),
            pltpu.VMEM(planes(wide), F32),
            pltpu.VMEM((5, 16, 256), F32),
        ]
        + y_scratch,
    )

    sound_one, to_a, to_b = call(
        functools.partial(acoustic_far_body, MIXES[0], "first"),
        [held, faces, (faces[0] + 32, size)],
        partial,
        got_a,
        got_b,
        far,
        received,
        send,
        scratch=sides + [rows_scratch],
        last=1,
    )
    labelled, received = received, route(send)
    got_a, got_b = traces(to_a, to_b)
    flow_state = call(flow_last_body, [(5, cells_x, 8, 128)], second, derived, ends, state)[0]
    partial = local_part(MIXES[1], sound_one)
    sound_two, to_a, to_b = call(
        functools.partial(acoustic_far_body, MIXES[1], "second"),
        [held, faces, (faces[0] + 32, size)],
        partial,
        got_a,
        got_b,
        far,
        received,
        labelled,
        scratch=sides + [rows_scratch],
    )
    source_three = call(place_last_body, [(3, 64, 128)], received, labelled)[0]
    got_a, got_b = traces(to_a, to_b)
    partial = local_part(MIXES[2], sound_two)
    sound_state = call(
        functools.partial(acoustic_far_body, MIXES[2], "last"),
        [(elements, 4, 512)],
        partial,
        got_a,
        got_b,
        far,
        source_three,
        scratch=sides + [pltpu.VMEM(held, F32)] + turning,
    )[0]
    return (flow_state, sound_state)


def solution(mesh):
    placed = (
        P("fx", "fy", "fz"),
        P(None, "fx", "fy", "fz"),
        P("fx", "fy", "fz"),
        P(("fx", "fy", "fz"), None, None),
        P(("fx", "fy", "fz")),
        P(),
        P(),
        P(("fx", "fy", "fz"), None),
        P("fx", "fy", "fz", None, None),
        P("fx", "fy", "fz", None),
    )
    return jax.shard_map(
        per_device,
        mesh=mesh,
        in_specs=placed,
        out_specs=(P(None, "fx", "fy", "fz"), P(("fx", "fy", "fz"), None, None)),
        check_vma=False,
    )
```

```python
import functools

import jax
import jax.numpy as jnp
import numpy as np
from jax import lax
from jax.experimental import pallas as pl
from jax.experimental.pallas import tpu as pltpu
from jax.sharding import PartitionSpec as P

HEAT_RATIO = 1.4
TIME_STEP = 0.1
VISCOSITY = 0.05
PENALTY = 0.5
HALO = 3
F32 = jnp.float32
BF16 = jnp.bfloat16
PARAMS = pltpu.CompilerParams(vmem_limit_bytes=24 * 1024 * 1024)
MIXES = ((0.0, 1.0), (0.75, 0.25), (1.0 / 3.0, 2.0 / 3.0))


def parts(values):
    high = values.astype(BF16)
    return high, (values - high.astype(F32)).astype(BF16)


def dot(left, right):
    return lax.dot_general(left, right, (((1,), (0,)), ((), ())), preferred_element_type=F32)


def dot_three(left, right):
    left_high, left_low = parts(left)
    right_high, right_low = parts(right)
    return dot(left_high, right_high) + dot(left_high, right_low) + dot(left_low, right_high)


def dot_full(left, right, dims=((1,), (0,))):
    return lax.dot_general(
        left, right, (dims, ((), ())), precision=lax.Precision.HIGHEST, preferred_element_type=F32
    )


def dot_exact_right(left, right):
    left_high, left_low = parts(left)
    return dot(left_high, right) + dot(left_low, right)


def call(body, outs, *operands, scratch=(), last=0, cost=None):
    whole = pl.BlockSpec(memory_space=pltpu.VMEM)
    outs = [out if isinstance(out, jax.ShapeDtypeStruct) else jax.ShapeDtypeStruct(out, F32) for out in outs]
    anywhere = pl.BlockSpec(memory_space=pl.ANY)
    return pl.pallas_call(
        body,
        out_shape=outs,
        in_specs=[whole] * (len(operands) - last) + [anywhere] * last,
        out_specs=[whole] * len(outs),
        scratch_shapes=list(scratch),
        compiler_params=PARAMS,
        cost_estimate=None if cost is None else pl.CostEstimate(flops=cost, bytes_accessed=cost, transcendentals=0),
    )(*operands)


def capacity_of(peers, blocks):
    return max(2, 2 * blocks // peers)


def fold_of(peers, blocks):
    return 128 // (8 * capacity_of(peers, blocks))


def is_odd(axis):
    return lax.axis_index(axis) % 2 == 1


def paired(odd, to_next, to_last):
    return jnp.where(odd, to_last, to_next), jnp.where(odd, to_next, to_last)


def pack_start_body(state, message_a, message_b, along_x):
    odd = is_odd("fz")
    rows = state[...].reshape(-1, 128)
    count = rows.shape[0]
    for tile in range(message_a.shape[0] // 8):
        piece = rows[tile * 128 : min(count, tile * 128 + 128)]
        if piece.shape[0] < 128:
            piece = jnp.concatenate([piece, jnp.zeros((128 - piece.shape[0], 128), F32)], 0)
        turned = piece.T
        first, second = paired(odd, turned[120:128], turned[0:8])
        message_a[tile * 8 : tile * 8 + 8] = first
        message_b[tile * 8 : tile * 8 + 8] = second
    cells_x = state.shape[1]
    for f in range(5):
        for s, x in enumerate(x_planes(cells_x)):
            at = (f * 2 * HALO + s) * 8
            along_x[at : at + 8] = state[f, x]


def pack_next_body(state, sent_a, sent_b, got_a, got_b, _, edge):
    cells_x = state.shape[1]
    odd_z = is_odd("fz")
    high, low = paired(odd_z, sent_a[...], sent_b[...])
    above, below = paired(odd_z, got_a[...], got_b[...])
    row = lax.broadcasted_iota(jnp.int32, (8, 128), 0)
    x_of_lane = lax.broadcasted_iota(jnp.int32, (16, 128), 1) // 8 % cells_x
    for tile in range(high.shape[0] // 8):
        rows = slice(tile * 8, tile * 8 + 8)
        upper = jnp.where(row < 3, pltpu.roll(high[rows], 3, 0), pltpu.roll(above[rows], 3, 0))
        lower = jnp.where(row < 3, pltpu.roll(below[rows], 3, 0), pltpu.roll(low[rows], 3, 0))
        slots = jnp.concatenate([upper, lower], 0)
        spread = jnp.concatenate([jnp.where(x_of_lane == x, slots, 0.0) for x in range(8)], 0).T
        for half in range(16 // cells_x):
            f = tile * (16 // cells_x) + half
            if f < 5:
                at = half * cells_x * 8
                total = spread[at : at + 8]
                for x in range(1, cells_x):
                    total = total + spread[at + x * 8 : at + x * 8 + 8]
                edge[f * 8 : f * 8 + 8] = total


def x_planes(cells_x):
    return [cells_x - HALO + i for i in range(HALO)] + list(range(HALO))


def sides_of(beside_x):
    return beside_x[0], beside_x[-1]


def beyond(edges_x, f):
    after, before = sides_of(edges_x)
    at = f * 8
    if after is before:
        return after[at : at + 8]
    lane = lax.broadcasted_iota(jnp.int32, (8, 128), 1)
    return jnp.where(lane < 64, after[at : at + 8], before[at : at + 8])


def pack_last_body(state, edge, *refs):
    (y_a, y_b), refs = refs[-2:], refs[:-3]
    beside_x, edges_x = refs[: len(refs) // 2], refs[len(refs) // 2 :]
    cells_x = state.shape[1]
    odd = is_odd("fy")
    after, before = sides_of(beside_x)

    def put(at, values, height):
        first, second = paired(odd, values[8 - height : 8], values[0:height])
        y_a[at : at + height] = first
        y_b[at : at + height] = second

    lines = 5 * cells_x * HALO
    for f in range(5):
        for x in range(cells_x):
            put((f * cells_x + x) * HALO, state[f, x], HALO)
        at = lines + f * 6
        for slot, height in ((1, 1), (2, 2), (3, 2), (4, 1)):
            source = (f * 2 * HALO + slot) * 8
            put(at, (before if slot < HALO else after)[source : source + 8], height)
            at += height
        put(lines + 30 + f * 2, edge[f * 8 : f * 8 + 8], 2)
        put(lines + 40 + f, beyond(edges_x, f), 1)


def assemble_speeds(wide, state, beside_x, above, below):
    cells_x = state.shape[1]
    after, before = sides_of(beside_x)
    for f in range(4):
        for x in range(cells_x):
            wide[f, 1 + x, 0:8] = state[f, x]
            at = (f * cells_x + x) * HALO
            wide[f, 1 + x, 8:9] = above[at : at + 1]
            wide[f, 1 + x, 15:16] = below[at + HALO - 1 : at + HALO]
        for slot, plane, source in ((HALO - 1, 0, before), (HALO, cells_x + 1, after)):
            at = (f * 2 * HALO + slot) * 8
            wide[f, plane, 0:8] = source[at : at + 8]


def assemble(wide, rim, state, edge, beside_x, edges_x, above, below):
    cells_x = state.shape[1]
    after, before = sides_of(beside_x)
    lines = 5 * cells_x * HALO
    for f in range(5):
        for x in range(cells_x):
            wide[f, HALO + x, 0:8] = state[f, x]
            at = (f * cells_x + x) * HALO
            wide[f, HALO + x, 8 : 8 + HALO] = above[at : at + HALO]
            wide[f, HALO + x, 16 - HALO : 16] = below[at : at + HALO]
        for slot in range(2 * HALO):
            plane = slot if slot < HALO else cells_x + slot
            at = (f * 2 * HALO + slot) * 8
            wide[f, plane, 0:8] = (before if slot < HALO else after)[at : at + 8]
        at = lines + f * 6
        for slot, height in ((1, 1), (2, 2), (3, 2), (4, 1)):
            plane = slot if slot < HALO else cells_x + slot
            wide[f, plane, 8 : 8 + height] = above[at : at + height]
            wide[f, plane, 16 - height : 16] = below[at : at + height]
            at += height
        rim[f, 0:8, 0:128] = edge[f * 8 : f * 8 + 8]
        rim[f, 0:8, 128:256] = beyond(edges_x, f)
        at = lines + 30 + f * 2
        rim[f, 8:10, 0:128] = above[at : at + 2]
        rim[f, 14:16, 0:128] = below[at : at + 2]
        at = lines + 40 + f
        rim[f, 8:9, 128:256] = above[at : at + 1]
        rim[f, 15:16, 128:256] = below[at : at + 1]


def primitive(rho, mx, my, mz, energy):
    inverse = 1.0 / rho
    u, v, w = mx * inverse, my * inverse, mz * inverse
    p = (HEAT_RATIO - 1.0) * (energy - 0.5 * (mx * u + my * v + mz * w))
    return u, v, w, p, jnp.sqrt(HEAT_RATIO * jnp.abs(p) * inverse)


def chunks(first, last, size):
    return [(i, min(i + size, last)) for i in range(first, last, size)]


def derive_planes(wide, derived, first, last):
    for i, j in chunks(first, last, 4):
        for k, value in enumerate(primitive(*[wide[f, i:j] for f in range(5)])):
            derived[k, i:j] = value


def derive_speeds(wide, derived, first, last):
    for i, j in chunks(first, last, 5):
        inverse = 1.0 / wide[0, i:j]
        for k in range(3):
            derived[k, i:j] = wide[1 + k, i:j] * inverse


def with_flux(fields, other, along):
    speed, p = other[along], other[3]
    out = [fields[1 + along]]
    for k in range(3):
        value = fields[1 + k] * speed
        out.append(value + p if k == along else value)
    out.append((fields[4] + p) * speed)
    return fields, out, jnp.abs(speed) + other[4]


def face(left, right):
    (fields_l, flux_l, speed_l), (fields_r, flux_r, speed_r) = left, right
    speed = jnp.maximum(speed_l, speed_r)
    viscous = speed + 2.0 * VISCOSITY
    return [
        (flux_l[f] + flux_r[f]) - (viscous if 1 <= f <= 3 else speed) * (fields_r[f] - fields_l[f])
        for f in range(5)
    ]


def rolled(here, shift, axis):
    fields, flux, speed = here
    return (
        [pltpu.roll(a, shift, axis) for a in fields],
        [pltpu.roll(a, shift, axis) for a in flux],
        pltpu.roll(speed, shift, axis),
    )


def rim_section(fields, start, mix):
    other = primitive(*fields)
    here = with_flux(fields, other, 2)
    along_z = face(here, rolled(here, 255, 1))
    if mix is None:
        return other, along_z, None
    total = [g - pltpu.roll(g, 1, 1) for g in along_z]
    for along, step, axis, size in ((0, 16, 1, 256), (1, 1, 0, 16)):
        here = with_flux(fields, other, along)
        faces = face(here, rolled(here, size - step, axis))
        total = [total[f] + (faces[f] - pltpu.roll(faces[f], step, axis)) for f in range(5)]
    out = []
    for f in range(5):
        value = fields[f] - (0.5 * TIME_STEP) * total[f]
        out.append(mix[0] * start[f] + mix[1] * value if mix[0] != 0.0 else value)
    return other, along_z, out


def to_ends(values, after, rows, first, last, ends):
    slot = lax.broadcasted_iota(jnp.int32, (rows, 256), 1) % 16
    for f, value in enumerate(values):
        value = value[0:rows]
        value = jnp.where(slot == 9, pltpu.roll(value, 9 - after, 1), value)
        for x in range(first, last):
            at = x % 16 // 8 * 128
            move = (118 - x % 8 * 16) % 128
            tile = value[:, at : at + 128]
            ends[f, x - first, 0:rows] = pltpu.roll(tile, move, 1) if move else tile


def flow_rate_section(wide, derived, ends, start, offset, mix, write, inner=False):
    depth = wide.shape[1]
    rows = slice(0, 8) if inner else slice(None)
    size = 4 if inner else 2

    def planes(i, j, kept, along):
        fields = [wide[f, i:j, kept] for f in range(5)]
        return with_flux(fields, [derived[f, i:j, kept] for f in range(5)], along)

    def cut(here, i, j):
        return [a[i:j] for a in here[0]], [a[i:j] for a in here[1]], here[2][i:j]

    for i, j in chunks(1, depth - 1, size):
        count = j - i
        lane = lax.broadcasted_iota(jnp.int32, (count, 8 if inner else 16, 128), 2)
        here = planes(i - 1, j + 1, rows, 0)
        faces = face(cut(here, 0, count + 1), cut(here, 1, count + 2))
        total = [g[1:] - g[:-1] for g in faces]
        here = planes(i, j, slice(None), 1)
        faces = face(here, rolled(here, 15, 1))
        for f in range(5):
            change = faces[f] - pltpu.roll(faces[f], 1, 1)
            total[f] = total[f] + (change[:, 0:8] if inner else change)
        here = planes(i, j, rows, 2)
        faces = face(here, rolled(here, 127, 2))
        for f in range(5):
            end = ends[f, i - 1 : j - 1, rows]
            value = jnp.where(lane == 127, end, faces[f])
            total[f] = total[f] + (value - jnp.where(lane == 0, end, pltpu.roll(value, 1, 2)))
        for f in range(5):
            value = wide[f, i:j, rows] - (0.5 * TIME_STEP) * total[f]
            if mix[0] != 0.0:
                value = mix[0] * start[f, i + offset : j + offset, rows] + mix[1] * value
            write(slice(i - 1, j - 1), f, value)


def lamb(derived, ends, first, cells_x, lamb_rows):
    for i, j in chunks(first, first + cells_x, 4):
        count = j - i
        lane = lax.broadcasted_iota(jnp.int32, (count, 8, 128), 2)
        vel = [derived[c, i:j, 0:8] for c in range(3)]
        along_x = [derived[c, i + 1 : j + 1, 0:8] - derived[c, i - 1 : j - 1, 0:8] for c in range(3)]
        along_y = []
        for c in range(3):
            column = derived[c, i:j]
            along_y.append((pltpu.roll(column, 15, 1) - pltpu.roll(column, 1, 1))[:, 0:8])
        along_z = []
        for c in range(2):
            end = ends[c, i - first : j - first, 0:8]
            after = jnp.where(lane == 127, end, pltpu.roll(vel[c], 127, 2))
            along_z.append(after - jnp.where(lane == 0, end, pltpu.roll(vel[c], 1, 2)))
        curl = [
            0.5 * (along_y[2] - along_z[1]),
            0.5 * (along_z[0] - along_x[2]),
            0.5 * (along_x[1] - along_y[0]),
        ]
        at = slice((i - first) * 8, (j - first) * 8)
        lamb_rows[0, at] = (curl[1] * vel[2] - curl[2] * vel[1]).reshape(count * 8, 128)
        lamb_rows[1, at] = (curl[2] * vel[0] - curl[0] * vel[2]).reshape(count * 8, 128)
        lamb_rows[2, at] = (curl[0] * vel[1] - curl[1] * vel[0]).reshape(count * 8, 128)


def project(lamb_rows, pair, spread, send, base):
    peers = send.shape[0]
    fold = fold_of(peers, spread.shape[0] // 8)
    height = 64 // fold
    group = lax.broadcasted_iota(jnp.int32, (height, 128), 1) // (128 // fold)
    modes = dot_three(pair[...], jnp.concatenate([lamb_rows[c] for c in range(3)], 1))
    modes = jnp.concatenate([modes[:, c * 128 : c * 128 + 128] for c in range(3)], 0)
    sent = dot_three(modes, spread[...])
    for c in range(3):
        for peer in range(peers):
            mine = sent[c * 64 : c * 64 + 64, peer * 128 : peer * 128 + 128]
            folded = mine[0:height]
            for g in range(1, fold):
                folded = jnp.where(group == g, mine[g * height : g * height + height], folded)
            send[peer, base + c * height : base + c * height + height] = folded


def flow_sources_body(count, state, edge, *refs):
    beside_x, refs = refs[:count], refs[count:]
    got_b, got_a, pair, spread, labels, _, send, wide, derived, lamb_rows, ends, above, below = refs
    cells_x = state.shape[1]
    above[...], below[...] = paired(is_odd("fy"), got_a[...], got_b[0 : got_a.shape[0]])
    assemble_speeds(wide, state, beside_x, above, below)
    derive_speeds(wide, derived, 0, cells_x + 2)
    inverse = 1.0 / edge[0:8]
    speeds = [jnp.concatenate([edge[k * 8 : k * 8 + 8] * inverse] * 2, 1) for k in (1, 2)]
    to_ends(speeds, 3, 8, 0, cells_x, ends)
    lamb(derived, ends, 1, cells_x, lamb_rows)
    project(lamb_rows, pair, spread, send, 0)
    send[:, send.shape[1] - 8 :] = labels[...]


def writer(target):
    def write(i, f, value):
        target[f, i] = value

    return write


def flow_stages_body(count, state, edge, *refs):
    beside_x, edges_x, refs = refs[:count], refs[count : 2 * count], refs[2 * count :]
    got_b, got_a, pair, spread, _, second, derived, ends_out, send, *refs = refs
    lamb_rows, ends, first, wide, rim, above, below = refs
    above[...], below[...] = paired(is_odd("fy"), got_a[...], got_b[0 : got_a.shape[0]])
    assemble(wide, rim, state, edge, beside_x, edges_x, above, below)
    planes = wide.shape[1]
    cells_x = planes - 2 * HALO
    size = send.shape[1] // 2
    rim_start = [rim[f] for f in range(5)]
    derive_planes(wide, derived, 0, planes)
    _, along_z, rim_first = rim_section(rim_start, None, MIXES[0])
    to_ends(along_z, 2, 16, -2, cells_x + 2, ends)
    flow_rate_section(wide, derived, ends, wide, 0, MIXES[0], writer(first))
    derive_planes(first, derived, 0, planes - 2)
    other, along_z, rim_second = rim_section(rim_first, [rim[f] for f in range(5)], MIXES[1])
    to_ends(other[0:2], 3, 8, 0, cells_x, ends)
    lamb(derived, ends, 2, cells_x, lamb_rows)
    project(lamb_rows, pair, spread, send, 0)
    to_ends(along_z, 2, 16, -1, cells_x + 1, ends)
    flow_rate_section(first, derived, ends, wide, 1, MIXES[1], writer(second))
    derive_planes(second, derived, 0, planes - 4)
    other, along_z, _ = rim_section(rim_second, None, None)
    to_ends(other[0:2], 3, 8, 0, cells_x, ends)
    lamb(derived, ends, 1, cells_x, lamb_rows)
    project(lamb_rows, pair, spread, send, size)
    to_ends(along_z, 2, 8, 0, cells_x, ends_out)


def flow_last_body(second, derived, ends, state, out):
    flow_rate_section(second, derived, ends, state, -1, MIXES[2], writer(out), inner=True)


def faces_out(state, rear, front):
    lane = lax.broadcasted_iota(jnp.int32, (32, 128), 1) // 16
    for c in range(4):
        front[c * 8 : c * 8 + 8] = state[c, 56:64]
        rear[c * 8 : c * 8 + 8] = state[c, 0:8]
        front[32 + c * 8 : 40 + c * 8] = state[c, pl.ds(7, 8, stride=8), :]
        rear[32 + c * 8 : 40 + c * 8] = state[c, pl.ds(0, 8, stride=8), :]
    rows = state[...].reshape(256, 128)
    last = jnp.zeros((32, 128), F32)
    first = jnp.zeros((32, 128), F32)
    for j in range(8):
        piece = rows[j * 32 : j * 32 + 32]
        last = jnp.where(lane == j, pltpu.roll(piece, (j * 16 + 16) % 128, 1), last)
        first = jnp.where(lane == j, pltpu.roll(piece, j * 16, 1) if j else piece, first)
    front[64:96] = last
    rear[64:96] = first


def faces_sent(odd, state, message_a, message_b):
    size = message_a.shape[0]
    faces_out(state, message_b, message_a)
    message_a[...], message_b[0:size] = paired(odd, message_a[...], message_b[0:size])
    if message_b.shape[0] > size:
        message_b[size:] = jnp.zeros((message_b.shape[0] - size, 128), F32)


def lift(total, before, after, sides, factor):
    def place(face, rows, target):
        value = factor * dot_exact_right(rows, sides[face])
        for c in range(4):
            total[c, target, :] += value[c * 8 : c * 8 + 8]

    place(0, before[0:32], pl.ds(0, 8))
    place(1, after[0:32], pl.ds(56, 8))
    place(2, before[32:64], pl.ds(0, 8, stride=8))
    place(3, after[32:64], pl.ds(7, 8, stride=8))


def rate_local(state, deriv_rows, deriv_lanes, speed, sides):
    fields = [state[c] for c in range(4)]
    by_rows = dot_three(deriv_rows[...], jnp.concatenate(fields[0:3], 1))
    by_lanes = dot_three(jnp.concatenate([fields[0], fields[3]], 0), deriv_lanes[...])
    divergence = by_rows[0:64, 128:256] + by_rows[64:128, 256:384] + by_lanes[64:128]
    rates = [
        -(speed[...] * speed[...]) * divergence,
        -by_rows[0:64, 0:128],
        -by_rows[64:128, 0:128],
        -by_lanes[0:64],
    ]
    row = lax.broadcasted_iota(jnp.int32, (64, 128), 0)
    lane = lax.broadcasted_iota(jnp.int32, (64, 128), 1)
    count = jnp.zeros((64, 128), F32)
    for value in (row // 8, row % 8, lane // 16):
        count = count + jnp.where((value == 0) | (value == 7), PENALTY, 0.0)
    side = PENALTY * dot_exact_right(state[...].reshape(256, 128), sides[4])
    return [rates[c] - count * fields[c] + side[c * 64 : c * 64 + 64] for c in range(4)]


def acoustic_local_body(mix, state, start, deriv_rows, deriv_lanes, speed, sides, out, front, rear):
    rates = rate_local(state, deriv_rows, deriv_lanes, speed, sides)
    for c in range(4):
        value = state[c] + TIME_STEP * rates[c]
        if mix[0] != 0.0:
            value = mix[0] * start[c] + mix[1] * value
        out[c] = value
    faces_out(state, rear, front)
    lift(out, front, rear, sides, TIME_STEP * mix[1] * PENALTY)


def acoustic_start_body(given, _, state, message_a, message_b, turned, stored):
    count = given.shape[0]
    for e in range(count):
        for t in range(4):
            stored[t, 4 * e : 4 * e + 4] = given[e, :, t * 128 : t * 128 + 128]
    for t in range(4):
        rows = [stored[t, pl.ds(c, count, stride=4), :] for c in range(4)]
        rows = jnp.concatenate(rows + [jnp.zeros((128 - 4 * count, 128), F32)], 0)
        turned[t * 128 : t * 128 + 128] = rows.T
    lane = lax.broadcasted_iota(jnp.int32, (64, 128), 1) // count
    fields = [jnp.zeros((64, 128), F32)] * 4
    for z in range(8):
        piece = turned[pl.ds(z, 64, stride=8), :]
        for c in range(4):
            move = (z - c) * count % 128
            fields[c] = jnp.where(lane == z, pltpu.roll(piece, move, 1) if move else piece, fields[c])
    for c in range(4):
        state[c] = fields[c]
    faces_sent(is_odd("fz"), state, message_a, message_b)


def natural_order(state, out, turned, stored):
    count = out.shape[0]
    lane = lax.broadcasted_iota(jnp.int32, (64, 128), 1) // count
    for z in range(8):
        value = jnp.zeros((64, 128), F32)
        for c in range(4):
            move = (c - z) * count % 128
            value = jnp.where(lane == c, pltpu.roll(state[c], move, 1) if move else state[c], value)
        turned[pl.ds(z, 64, stride=8), :] = value
    for t in range(4):
        rows = turned[t * 128 : t * 128 + 128].T
        for c in range(4):
            stored[t, pl.ds(c, count, stride=4), :] = rows[c * count : c * count + count]
    for e in range(count):
        for t in range(4):
            out[e, :, t * 128 : t * 128 + 128] = stored[t, 4 * e : 4 * e + 4]


def remote_part(out, before, after, sides_far, factor):
    lift(out, before, after, sides_far, factor)
    lane = lax.broadcasted_iota(jnp.int32, (32, 128), 1) // 16
    last, first = before[64:96], after[64:96]
    pieces = []
    for j in range(8):
        left = pltpu.roll(last, 128 - j * 16, 1) if j else last
        right = pltpu.roll(first, (144 - j * 16) % 128, 1) if j != 1 else first
        pieces.append(jnp.where(lane == 0, left, jnp.where(lane == 1, right, 0.0)))
    value = factor * dot_exact_right(jnp.concatenate(pieces, 0), sides_far[4])
    for c in range(4):
        out[c] += value[c * 64 : c * 64 + 64]


def acoustic_far_body(mix, kind, partial, got_a, got_b, sides_far, received, *refs):
    if kind == "last":
        given_out, before, after, out, turned, stored = refs
    elif kind == "first":
        _, out, message_a, message_b, before, after, source = refs
        place(received, received, source, 0)
        received = source
    else:
        labelled, out, message_a, message_b, before, after, source = refs
        place(received, labelled, source, 0)
        received = source
    odd = is_odd("fz")
    after[...], before[...] = paired(odd, got_a[0:96], got_b[0:96])
    out[0] = partial[0]
    for c in range(3):
        out[1 + c] = partial[1 + c] + (TIME_STEP * mix[1]) * received[c]
    remote_part(out, before, after, sides_far, TIME_STEP * mix[1] * PENALTY)
    if kind == "last":
        natural_order(out, given_out, turned, stored)
    else:
        faces_sent(odd, out, message_a, message_b)


def place(received, labelled, out, base):
    peers, size = labelled.shape[0], labelled.shape[1]
    fold = 192 // (size - 8)
    height = 64 // fold
    target = lax.broadcasted_iota(jnp.int32, (128, 128), 0)
    lane = lax.broadcasted_iota(jnp.int32, (128, 128), 1)
    total = None
    for peer in range(peers):
        label = labelled[peer, size - 8 : size - 7, :]
        label = jnp.broadcast_to(label, (128, 128)).astype(jnp.int32)
        hit = (label == target % 16) & (lane % 8 == target // 16)
        chosen = [jnp.where(hit & (lane // (128 // fold) == g), 1.0, 0.0) for g in range(fold)]
        chosen = jnp.concatenate(chosen, 0).astype(BF16)
        high, low = parts(received[peer, base : base + 3 * height])
        dims = (((1,), (1,)), ((), ()))
        value = lax.dot_general(high, chosen, dims, preferred_element_type=F32)
        value = value + lax.dot_general(low, chosen, dims, preferred_element_type=F32)
        total = value if total is None else total + value
    for c in range(3):
        for g in range(fold):
            at = c * height
            out[c, g * height : g * height + height] = total[at : at + height, g * 128 : g * 128 + 128]


def place_last_body(received, labelled, out):
    place(received, labelled, out, received.shape[1] // 2)


def kron_part(matrix, shape, rows_by, columns_by):
    row = lax.broadcasted_iota(jnp.int32, (shape[0], 8), 0)
    level = lax.broadcasted_iota(jnp.int32, (shape[0], 8), 1)
    left = (row // rows_by % 8 == level).astype(F32)
    level = lax.broadcasted_iota(jnp.int32, (8, shape[1]), 0)
    column = lax.broadcasted_iota(jnp.int32, (8, shape[1]), 1)
    right = (column // columns_by % 8 == level).astype(F32)
    return dot_full(dot_full(left, matrix), right)


def tables_body(
    packed,
    near,
    far,
    deriv_rows,
    deriv_lanes,
    pair,
    spread,
    labels,
    speed,
):
    size = near.shape[1]
    count = size // 8
    blocks = spread.shape[0] // 8

    def place_of(shape):
        return (lax.broadcasted_iota(jnp.int32, shape, 0), lax.broadcasted_iota(jnp.int32, shape, 1))

    row, column = place_of((count, size))
    repeat = (column % count == row).astype(F32)
    speed[...] = dot_full(packed[24:25, 0:count], repeat)
    wanted = dot_full(packed[16:24, 0:count], repeat).astype(jnp.int32)
    row, column = place_of((size, size))
    level, element = row // count, row % count
    level_out = column // count
    for facet in range(4):
        shift = -count if facet % 2 == 0 else count
        choice = jnp.broadcast_to(wanted[facet : facet + 1], (size, size))
        near[facet] = jnp.where((level == level_out) & (element == choice), 1.0, 0.0).astype(BF16)
        far[facet] = jnp.where((level == level_out) & (element + shift == choice), 1.0, 0.0).astype(BF16)
    lower = jnp.broadcast_to(wanted[4:5], (size, size))
    upper = jnp.broadcast_to(wanted[5:6], (size, size))
    hit = (level == 7) & (level_out == 0) & (element == lower)
    hit = hit | ((level == 0) & (level_out == 7) & (element == upper))
    near[4] = jnp.where(hit, 1.0, 0.0).astype(BF16)
    hit = (level == 0) & (level_out == 0) & (element - count == lower)
    hit = hit | ((level == 1) & (level_out == 7) & (element + count == upper))
    far[4] = jnp.where(hit, 1.0, 0.0).astype(BF16)

    row, column = place_of((64, 64))
    slopes, modes = packed[0:8, 0:8], packed[8:16, 0:8]
    outer = kron_part(slopes, (64, 64), 8, 8)
    inner = kron_part(slopes, (64, 64), 1, 1)
    deriv_rows[0:64] = jnp.where(row % 8 == column % 8, outer, 0.0)
    deriv_rows[64:128] = jnp.where(row // 8 == column // 8, inner, 0.0)
    row, column = place_of((size, size))
    lanes = kron_part(slopes.T, (size, size), count, count)
    deriv_lanes[...] = jnp.where(row % count == column % count, lanes, 0.0)
    pair[...] = kron_part(modes, (64, 64), 8, 8) * kron_part(modes, (64, 64), 1, 1)

    peers = labels.shape[0]
    capacity = capacity_of(peers, blocks)
    row, column = place_of((blocks, blocks))

    def upright(values):
        return jnp.sum(jnp.where(row == column, values, 0.0), 1, keepdims=True)

    owner_row = packed[25:26, 0:blocks]
    owner_column = upright(owner_row)
    earlier = (owner_column == owner_row) & (column < row)
    position = jnp.sum(jnp.where(earlier, 1.0, 0.0), 1, keepdims=True)
    slot = owner_column * capacity + position
    element_column = upright(packed[26:27, 0:blocks])
    row, column = place_of((8 * blocks, blocks))
    repeat = (row // 8 == column).astype(F32)
    slot = dot_full(repeat, jnp.broadcast_to(slot, (blocks, 128)))
    element = dot_full(repeat, jnp.broadcast_to(element_column, (blocks, 128)))
    row, column = place_of((8 * blocks, 128))
    values = kron_part(modes.T, (8 * blocks, 128), 1, 1)
    inside = column % (8 * capacity) // 8
    for peer in range(peers):
        chosen = slot == (inside + peer * capacity).astype(F32)
        spread[:, peer * 128 : peer * 128 + 128] = jnp.where(chosen, values, 0.0)
        named = jnp.where(chosen & (row % 8 == 0), element + 1.0, 0.0)
        labels[peer] = jnp.broadcast_to(jnp.sum(named, 0, keepdims=True) - 1.0, (8, 128))


def shifted(sizes, shifts):
    pairs = []
    for index in np.ndindex(*sizes):
        source = [(i + s) % n for i, s, n in zip(index, shifts, sizes)]
        pairs.append((int(np.ravel_multi_index(source, sizes)), int(np.ravel_multi_index(index, sizes))))
    return pairs


def partners(sizes, axis, second):
    pairs = []
    for index in np.ndindex(*sizes):
        source = list(index)
        step = 1 if (index[axis] % 2 == 0) != second else -1
        source[axis] = (index[axis] + step) % sizes[axis]
        pairs.append((int(np.ravel_multi_index(source, sizes)), int(np.ravel_multi_index(index, sizes))))
    return pairs


def per_device(
    density,
    velocity,
    pressure,
    acoustic,
    sound_speed,
    derivative,
    mode_basis,
    neighbours,
    block_owner,
    block_element,
):
    size_x, size_y, size_z = lax.axis_size("fx"), lax.axis_size("fy"), lax.axis_size("fz")
    devices = size_x * size_y * size_z
    cells_x = density.shape[0]
    elements = acoustic.shape[0]
    device = lax.axis_index(("fx", "fy", "fz"))

    names = ("fx", "fy", "fz")

    rows = 5 * cells_x * 8
    tiles = -(-rows // 128)
    square = velocity[0] * velocity[0] + velocity[1] * velocity[1] + velocity[2] * velocity[2]
    energy = pressure / (HEAT_RATIO - 1.0) + 0.5 * density * square
    rest = ((0, 0), (0, 0), (0, 0))
    state = jnp.pad(density[None], ((0, 4),) + rest) + jnp.pad(density * velocity, ((1, 1),) + rest)
    state = state + jnp.pad(energy[None], ((4, 0),) + rest)
    x_rows = 5 * 2 * HALO * 8
    flow_a, flow_b, along_x = call(
        pack_start_body, [(tiles * 8, 128), (tiles * 8, 128), (x_rows, 128)], state
    )
    edge_a = lax.ppermute(flow_a, "fz", partners((size_z,), 0, False))
    edge_b = lax.ppermute(flow_b, "fz", partners((size_z,), 0, True))
    x_steps = (1,) if size_x == 2 else (1, -1)
    beside_x = [lax.ppermute(along_x, "fx", shifted((size_x,), (step,))) for step in x_steps]

    near_pairs = [(i ^ 1, i) for i in range(devices)]
    far_pairs = [pair for i in range(1, devices - 1, 2) for pair in ((i, i + 1), (i + 1, i))]

    def traces(to_a, to_b):
        far_got = lax.ppermute(to_b, names, far_pairs)
        return lax.ppermute(to_a, names, near_pairs), far_got

    size = 8 * elements
    held = (4, 64, size)
    faces = (96, size)
    sides = [pltpu.VMEM(faces, F32)] * 2
    turning = [pltpu.VMEM((512, 128), F32), pltpu.VMEM((4, 4 * elements, 128), F32)]
    sound, to_a, to_b = call(
        acoustic_start_body,
        [held, faces, faces],
        acoustic,
        edge_a,
        scratch=turning,
        last=1,
    )
    got_a, got_b = traces(to_a, to_b)

    edge = call(
        pack_next_body,
        [(40, 128)],
        state,
        flow_a,
        flow_b,
        edge_a,
        edge_b,
        to_a,
        last=1,
    )[0]
    edges_x = [lax.ppermute(edge, "fx", shifted((size_x,), (step,))) for step in x_steps]
    y_shape = (5 * cells_x * HALO + 48, 128)
    y_a, y_b = call(pack_last_body, [y_shape, (y_shape[0] + 8, 128)], state, edge, *beside_x, *edges_x, got_a, last=1, cost=1)
    y_second = lax.ppermute(y_b, "fy", partners((size_y,), 0, True))
    y_first = lax.ppermute(y_a, "fy", partners((size_y,), 0, False))

    local = (neighbours - device * elements).T
    blocks = block_owner.size
    width = max(elements, blocks)

    def piece(values, first):
        values = values.astype(F32)
        return jnp.pad(values, ((first, 32 - first - values.shape[0]), (0, width - values.shape[1])))

    packed = (
        piece(derivative, 0)
        + piece(mode_basis, 8)
        + piece(local, 16)
        + piece(sound_speed.reshape(1, elements), 24)
        + piece(block_owner.reshape(1, blocks), 25)
        + piece(block_element.reshape(1, blocks), 26)
    )
    table = jax.ShapeDtypeStruct((5, size, size), BF16)
    near, far, deriv_rows, deriv_lanes, pair, spread, labels, speed = call(
        tables_body,
        [
            table,
            table,
            (128, 64),
            (size, size),
            (64, 64),
            (8 * blocks, size_y * 128),
            (size_y, 8, 128),
            (1, size),
        ],
        packed,
        cost=1,
    )

    fold = fold_of(size_y, blocks)
    wide = cells_x + 2 * HALO
    rows_scratch = pltpu.VMEM((3, 64, 128), F32)

    def planes(count):
        return (5, count, 16, 128)

    def route(send):
        return lax.all_to_all(send, "fy", split_axis=0, concat_axis=0, tiled=True)

    def local_part(mix, now):
        return call(
            functools.partial(acoustic_local_body, mix),
            [held],
            now,
            sound,
            deriv_rows,
            deriv_lanes,
            speed,
            near,
            scratch=sides,
            cost=1,
        )[0]

    partial = local_part(MIXES[0], sound)
    y_scratch = [pltpu.VMEM(y_shape, F32), pltpu.VMEM(y_shape, F32)]
    send = call(
        functools.partial(flow_sources_body, len(beside_x)),
        [(size_y, 192 // fold + 8, 128)],
        state,
        edge,
        *beside_x,
        y_second,
        y_first,
        pair,
        spread,
        labels,
        got_b,
        last=1,
        scratch=[
            pltpu.VMEM((4, cells_x + 2, 16, 128), F32),
            pltpu.VMEM((3, cells_x + 2, 16, 128), F32),
            rows_scratch,
            pltpu.VMEM((2, cells_x, 8, 128), F32),
        ]
        + y_scratch,
    )[0]
    received = route(send)
    second, derived, ends, send = call(
        functools.partial(flow_stages_body, len(edges_x)),
        [
            planes(wide - 4),
            planes(wide),
            (5, cells_x, 8, 128),
            (size_y, 2 * 192 // fold, 128),
        ],
        state,
        edge,
        *beside_x,
        *edges_x,
        y_second,
        y_first,
        pair,
        spread,
        partial,
        last=1,
        scratch=[
            rows_scratch,
            pltpu.VMEM(planes(wide - 2), F32),
            pltpu.VMEM(planes(wide - 2), F32),
            pltpu.VMEM(planes(wide), F32),
            pltpu.VMEM((5, 16, 256), F32),
        ]
        + y_scratch,
    )

    sound_one, to_a, to_b = call(
        functools.partial(acoustic_far_body, MIXES[0], "first"),
        [held, faces, (faces[0] + 32, size)],
        partial,
        got_a,
        got_b,
        far,
        received,
        send,
        scratch=sides + [rows_scratch],
        last=1,
    )
    labelled, received = received, route(send)
    got_a, got_b = traces(to_a, to_b)
    flow_state = call(flow_last_body, [(5, cells_x, 8, 128)], second, derived, ends, state)[0]
    partial = local_part(MIXES[1], sound_one)
    sound_two, to_a, to_b = call(
        functools.partial(acoustic_far_body, MIXES[1], "second"),
        [held, faces, (faces[0] + 32, size)],
        partial,
        got_a,
        got_b,
        far,
        received,
        labelled,
        scratch=sides + [rows_scratch],
    )
    source_three = call(place_last_body, [(3, 64, 128)], received, labelled)[0]
    got_a, got_b = traces(to_a, to_b)
    partial = local_part(MIXES[2], sound_two)
    sound_state = call(
        functools.partial(acoustic_far_body, MIXES[2], "last"),
        [(elements, 4, 512)],
        partial,
        got_a,
        got_b,
        far,
        source_three,
        scratch=sides + [pltpu.VMEM(held, F32)] + turning,
    )[0]
    return (flow_state, sound_state)


def solution(mesh):
    placed = (
        P("fx", "fy", "fz"),
        P(None, "fx", "fy", "fz"),
        P("fx", "fy", "fz"),
        P(("fx", "fy", "fz"), None, None),
        P(("fx", "fy", "fz")),
        P(),
        P(),
        P(("fx", "fy", "fz"), None),
        P("fx", "fy", "fz", None, None),
        P("fx", "fy", "fz", None),
    )
    return jax.shard_map(
        per_device,
        mesh=mesh,
        in_specs=placed,
        out_specs=(P(None, "fx", "fy", "fz"), P(("fx", "fy", "fz"), None, None)),
        check_vma=False,
    )
```

```python
import functools

import jax
import jax.numpy as jnp
import numpy as np
from jax import lax
from jax.experimental import pallas as pl
from jax.experimental.pallas import tpu as pltpu
from jax.sharding import PartitionSpec as P

HEAT_RATIO = 1.4
TIME_STEP = 0.1
VISCOSITY = 0.05
PENALTY = 0.5
HALO = 3
F32 = jnp.float32
BF16 = jnp.bfloat16
PARAMS = pltpu.CompilerParams(vmem_limit_bytes=24 * 1024 * 1024)
MIXES = ((0.0, 1.0), (0.75, 0.25), (1.0 / 3.0, 2.0 / 3.0))


def parts(values):
    high = values.astype(BF16)
    return high, (values - high.astype(F32)).astype(BF16)


def dot(left, right):
    return lax.dot_general(left, right, (((1,), (0,)), ((), ())), preferred_element_type=F32)


def dot_three(left, right):
    left_high, left_low = parts(left)
    right_high, right_low = parts(right)
    return dot(left_high, right_high) + dot(left_high, right_low) + dot(left_low, right_high)


def dot_full(left, right, dims=((1,), (0,))):
    return lax.dot_general(
        left, right, (dims, ((), ())), precision=lax.Precision.HIGHEST, preferred_element_type=F32
    )


def dot_exact_right(left, right):
    left_high, left_low = parts(left)
    return dot(left_high, right) + dot(left_low, right)


def call(body, outs, *operands, scratch=(), last=0, cost=None):
    whole = pl.BlockSpec(memory_space=pltpu.VMEM)
    outs = [out if isinstance(out, jax.ShapeDtypeStruct) else jax.ShapeDtypeStruct(out, F32) for out in outs]
    anywhere = pl.BlockSpec(memory_space=pl.ANY)
    return pl.pallas_call(
        body,
        out_shape=outs,
        in_specs=[whole] * (len(operands) - last) + [anywhere] * last,
        out_specs=[whole] * len(outs),
        scratch_shapes=list(scratch),
        compiler_params=PARAMS,
        cost_estimate=None if cost is None else pl.CostEstimate(flops=cost, bytes_accessed=cost, transcendentals=0),
    )(*operands)


def capacity_of(peers, blocks):
    return max(2, 2 * blocks // peers)


def fold_of(peers, blocks):
    return 128 // (8 * capacity_of(peers, blocks))


def is_odd(axis):
    return lax.axis_index(axis) % 2 == 1


def paired(odd, to_next, to_last):
    return jnp.where(odd, to_last, to_next), jnp.where(odd, to_next, to_last)


def pack_start_body(state, message_a, message_b, along_x):
    odd = is_odd("fz")
    rows = state[...].reshape(-1, 128)
    count = rows.shape[0]
    for tile in range(message_a.shape[0] // 8):
        piece = rows[tile * 128 : min(count, tile * 128 + 128)]
        if piece.shape[0] < 128:
            piece = jnp.concatenate([piece, jnp.zeros((128 - piece.shape[0], 128), F32)], 0)
        turned = piece.T
        first, second = paired(odd, turned[120:128], turned[0:8])
        message_a[tile * 8 : tile * 8 + 8] = first
        message_b[tile * 8 : tile * 8 + 8] = second
    cells_x = state.shape[1]
    for f in range(5):
        for s, x in enumerate(x_planes(cells_x)):
            at = (f * 2 * HALO + s) * 8
            along_x[at : at + 8] = state[f, x]


def pack_next_body(state, sent_a, sent_b, got_a, got_b, _, edge):
    cells_x = state.shape[1]
    odd_z = is_odd("fz")
    high, low = paired(odd_z, sent_a[...], sent_b[...])
    above, below = paired(odd_z, got_a[...], got_b[...])
    row = lax.broadcasted_iota(jnp.int32, (8, 128), 0)
    x_of_lane = lax.broadcasted_iota(jnp.int32, (16, 128), 1) // 8 % cells_x
    for tile in range(high.shape[0] // 8):
        rows = slice(tile * 8, tile * 8 + 8)
        upper = jnp.where(row < 3, pltpu.roll(high[rows], 3, 0), pltpu.roll(above[rows], 3, 0))
        lower = jnp.where(row < 3, pltpu.roll(below[rows], 3, 0), pltpu.roll(low[rows], 3, 0))
        slots = jnp.concatenate([upper, lower], 0)
        spread = jnp.concatenate([jnp.where(x_of_lane == x, slots, 0.0) for x in range(8)], 0).T
        for half in range(16 // cells_x):
            f = tile * (16 // cells_x) + half
            if f < 5:
                at = half * cells_x * 8
                total = spread[at : at + 8]
                for x in range(1, cells_x):
                    total = total + spread[at + x * 8 : at + x * 8 + 8]
                edge[f * 8 : f * 8 + 8] = total


def x_planes(cells_x):
    return [cells_x - HALO + i for i in range(HALO)] + list(range(HALO))


def sides_of(beside_x):
    return beside_x[0], beside_x[-1]


def beyond(edges_x, f):
    after, before = sides_of(edges_x)
    at = f * 8
    if after is before:
        return after[at : at + 8]
    lane = lax.broadcasted_iota(jnp.int32, (8, 128), 1)
    return jnp.where(lane < 64, after[at : at + 8], before[at : at + 8])


def pack_last_body(state, edge, *refs):
    (y_a, y_b), refs = refs[-2:], refs[:-3]
    beside_x, edges_x = refs[: len(refs) // 2], refs[len(refs) // 2 :]
    cells_x = state.shape[1]
    odd = is_odd("fy")
    after, before = sides_of(beside_x)

    def put(at, values, height):
        first, second = paired(odd, values[8 - height : 8], values[0:height])
        y_a[at : at + height] = first
        y_b[at : at + height] = second

    lines = 5 * cells_x * HALO
    for f in range(5):
        for x in range(cells_x):
            put((f * cells_x + x) * HALO, state[f, x], HALO)
        at = lines + f * 6
        for slot, height in ((1, 1), (2, 2), (3, 2), (4, 1)):
            source = (f * 2 * HALO + slot) * 8
            put(at, (before if slot < HALO else after)[source : source + 8], height)
            at += height
        put(lines + 30 + f * 2, edge[f * 8 : f * 8 + 8], 2)
        put(lines + 40 + f, beyond(edges_x, f), 1)


def assemble_speeds(wide, state, beside_x, above, below):
    cells_x = state.shape[1]
    after, before = sides_of(beside_x)
    for f in range(4):
        for x in range(cells_x):
            wide[f, 1 + x, 0:8] = state[f, x]
            at = (f * cells_x + x) * HALO
            wide[f, 1 + x, 8:9] = above[at : at + 1]
            wide[f, 1 + x, 15:16] = below[at + HALO - 1 : at + HALO]
        for slot, plane, source in ((HALO - 1, 0, before), (HALO, cells_x + 1, after)):
            at = (f * 2 * HALO + slot) * 8
            wide[f, plane, 0:8] = source[at : at + 8]


def assemble(wide, rim, state, edge, beside_x, edges_x, above, below):
    cells_x = state.shape[1]
    after, before = sides_of(beside_x)
    lines = 5 * cells_x * HALO
    for f in range(5):
        for x in range(cells_x):
            wide[f, HALO + x, 0:8] = state[f, x]
            at = (f * cells_x + x) * HALO
            wide[f, HALO + x, 8 : 8 + HALO] = above[at : at + HALO]
            wide[f, HALO + x, 16 - HALO : 16] = below[at : at + HALO]
        for slot in range(2 * HALO):
            plane = slot if slot < HALO else cells_x + slot
            at = (f * 2 * HALO + slot) * 8
            wide[f, plane, 0:8] = (before if slot < HALO else after)[at : at + 8]
        at = lines + f * 6
        for slot, height in ((1, 1), (2, 2), (3, 2), (4, 1)):
            plane = slot if slot < HALO else cells_x + slot
            wide[f, plane, 8 : 8 + height] = above[at : at + height]
            wide[f, plane, 16 - height : 16] = below[at : at + height]
            at += height
        rim[f, 0:8, 0:128] = edge[f * 8 : f * 8 + 8]
        rim[f, 0:8, 128:256] = beyond(edges_x, f)
        at = lines + 30 + f * 2
        rim[f, 8:10, 0:128] = above[at : at + 2]
        rim[f, 14:16, 0:128] = below[at : at + 2]
        at = lines + 40 + f
        rim[f, 8:9, 128:256] = above[at : at + 1]
        rim[f, 15:16, 128:256] = below[at : at + 1]


def primitive(rho, mx, my, mz, energy):
    inverse = 1.0 / rho
    u, v, w = mx * inverse, my * inverse, mz * inverse
    p = (HEAT_RATIO - 1.0) * (energy - 0.5 * (mx * u + my * v + mz * w))
    return u, v, w, p, jnp.sqrt(HEAT_RATIO * jnp.abs(p) * inverse)


def chunks(first, last, size):
    return [(i, min(i + size, last)) for i in range(first, last, size)]


def derive_planes(wide, derived, first, last):
    for i, j in chunks(first, last, 4):
        for k, value in enumerate(primitive(*[wide[f, i:j] for f in range(5)])):
            derived[k, i:j] = value


def derive_speeds(wide, derived, first, last):
    for i, j in chunks(first, last, 5):
        inverse = 1.0 / wide[0, i:j]
        for k in range(3):
            derived[k, i:j] = wide[1 + k, i:j] * inverse


def with_flux(fields, other, along):
    speed, p = other[along], other[3]
    out = [fields[1 + along]]
    for k in range(3):
        value = fields[1 + k] * speed
        out.append(value + p if k == along else value)
    out.append((fields[4] + p) * speed)
    return fields, out, jnp.abs(speed) + other[4]


def face(left, right):
    (fields_l, flux_l, speed_l), (fields_r, flux_r, speed_r) = left, right
    speed = jnp.maximum(speed_l, speed_r)
    viscous = speed + 2.0 * VISCOSITY
    return [
        (flux_l[f] + flux_r[f]) - (viscous if 1 <= f <= 3 else speed) * (fields_r[f] - fields_l[f])
        for f in range(5)
    ]


def rolled(here, shift, axis):
    fields, flux, speed = here
    return (
        [pltpu.roll(a, shift, axis) for a in fields],
        [pltpu.roll(a, shift, axis) for a in flux],
        pltpu.roll(speed, shift, axis),
    )


def rim_section(fields, start, mix):
    other = primitive(*fields)
    here = with_flux(fields, other, 2)
    along_z = face(here, rolled(here, 255, 1))
    if mix is None:
        return other, along_z, None
    total = [g - pltpu.roll(g, 1, 1) for g in along_z]
    for along, step, axis, size in ((0, 16, 1, 256), (1, 1, 0, 16)):
        here = with_flux(fields, other, along)
        faces = face(here, rolled(here, size - step, axis))
        total = [total[f] + (faces[f] - pltpu.roll(faces[f], step, axis)) for f in range(5)]
    out = []
    for f in range(5):
        value = fields[f] - (0.5 * TIME_STEP) * total[f]
        out.append(mix[0] * start[f] + mix[1] * value if mix[0] != 0.0 else value)
    return other, along_z, out


def to_ends(values, after, rows, first, last, ends):
    slot = lax.broadcasted_iota(jnp.int32, (rows, 256), 1) % 16
    for f, value in enumerate(values):
        value = value[0:rows]
        value = jnp.where(slot == 9, pltpu.roll(value, 9 - after, 1), value)
        for x in range(first, last):
            at = x % 16 // 8 * 128
            move = (118 - x % 8 * 16) % 128
            tile = value[:, at : at + 128]
            ends[f, x - first, 0:rows] = pltpu.roll(tile, move, 1) if move else tile


def flow_rate_section(wide, derived, ends, start, offset, mix, write, inner=False):
    depth = wide.shape[1]
    rows = slice(0, 8) if inner else slice(None)
    size = 4 if inner else 2

    def planes(i, j, kept, along):
        fields = [wide[f, i:j, kept] for f in range(5)]
        return with_flux(fields, [derived[f, i:j, kept] for f in range(5)], along)

    def cut(here, i, j):
        return [a[i:j] for a in here[0]], [a[i:j] for a in here[1]], here[2][i:j]

    for i, j in chunks(1, depth - 1, size):
        count = j - i
        lane = lax.broadcasted_iota(jnp.int32, (count, 8 if inner else 16, 128), 2)
        here = planes(i - 1, j + 1, rows, 0)
        faces = face(cut(here, 0, count + 1), cut(here, 1, count + 2))
        total = [g[1:] - g[:-1] for g in faces]
        here = planes(i, j, slice(None), 1)
        faces = face(here, rolled(here, 15, 1))
        for f in range(5):
            change = faces[f] - pltpu.roll(faces[f], 1, 1)
            total[f] = total[f] + (change[:, 0:8] if inner else change)
        here = planes(i, j, rows, 2)
        faces = face(here, rolled(here, 127, 2))
        for f in range(5):
            end = ends[f, i - 1 : j - 1, rows]
            value = jnp.where(lane == 127, end, faces[f])
            total[f] = total[f] + (value - jnp.where(lane == 0, end, pltpu.roll(value, 1, 2)))
        for f in range(5):
            value = wide[f, i:j, rows] - (0.5 * TIME_STEP) * total[f]
            if mix[0] != 0.0:
                value = mix[0] * start[f, i + offset : j + offset, rows] + mix[1] * value
            write(slice(i - 1, j - 1), f, value)


def lamb(derived, ends, first, cells_x, lamb_rows):
    for i, j in chunks(first, first + cells_x, 4):
        count = j - i
        lane = lax.broadcasted_iota(jnp.int32, (count, 8, 128), 2)
        vel = [derived[c, i:j, 0:8] for c in range(3)]
        along_x = [derived[c, i + 1 : j + 1, 0:8] - derived[c, i - 1 : j - 1, 0:8] for c in range(3)]
        along_y = []
        for c in range(3):
            column = derived[c, i:j]
            along_y.append((pltpu.roll(column, 15, 1) - pltpu.roll(column, 1, 1))[:, 0:8])
        along_z = []
        for c in range(2):
            end = ends[c, i - first : j - first, 0:8]
            after = jnp.where(lane == 127, end, pltpu.roll(vel[c], 127, 2))
            along_z.append(after - jnp.where(lane == 0, end, pltpu.roll(vel[c], 1, 2)))
        curl = [
            0.5 * (along_y[2] - along_z[1]),
            0.5 * (along_z[0] - along_x[2]),
            0.5 * (along_x[1] - along_y[0]),
        ]
        at = slice((i - first) * 8, (j - first) * 8)
        lamb_rows[0, at] = (curl[1] * vel[2] - curl[2] * vel[1]).reshape(count * 8, 128)
        lamb_rows[1, at] = (curl[2] * vel[0] - curl[0] * vel[2]).reshape(count * 8, 128)
        lamb_rows[2, at] = (curl[0] * vel[1] - curl[1] * vel[0]).reshape(count * 8, 128)


def project(lamb_rows, pair, spread, send, base):
    peers = send.shape[0]
    fold = fold_of(peers, spread.shape[0] // 8)
    height = 64 // fold
    group = lax.broadcasted_iota(jnp.int32, (height, 128), 1) // (128 // fold)
    modes = dot_three(pair[...], jnp.concatenate([lamb_rows[c] for c in range(3)], 1))
    modes = jnp.concatenate([modes[:, c * 128 : c * 128 + 128] for c in range(3)], 0)
    sent = dot_three(modes, spread[...])
    for c in range(3):
        for peer in range(peers):
            mine = sent[c * 64 : c * 64 + 64, peer * 128 : peer * 128 + 128]
            folded = mine[0:height]
            for g in range(1, fold):
                folded = jnp.where(group == g, mine[g * height : g * height + height], folded)
            send[peer, base + c * height : base + c * height + height] = folded


def flow_sources_body(count, state, edge, *refs):
    beside_x, refs = refs[:count], refs[count:]
    got_b, got_a, pair, spread, labels, _, send, wide, derived, lamb_rows, ends, above, below = refs
    cells_x = state.shape[1]
    above[...], below[...] = paired(is_odd("fy"), got_a[...], got_b[0 : got_a.shape[0]])
    assemble_speeds(wide, state, beside_x, above, below)
    derive_speeds(wide, derived, 0, cells_x + 2)
    inverse = 1.0 / edge[0:8]
    speeds = [jnp.concatenate([edge[k * 8 : k * 8 + 8] * inverse] * 2, 1) for k in (1, 2)]
    to_ends(speeds, 3, 8, 0, cells_x, ends)
    lamb(derived, ends, 1, cells_x, lamb_rows)
    project(lamb_rows, pair, spread, send, 0)
    send[:, send.shape[1] - 8 :] = labels[...]


def writer(target):
    def write(i, f, value):
        target[f, i] = value

    return write


def flow_stages_body(count, state, edge, *refs):
    beside_x, edges_x, refs = refs[:count], refs[count : 2 * count], refs[2 * count :]
    got_b, got_a, pair, spread, _, second, derived, ends_out, send, *refs = refs
    lamb_rows, ends, first, wide, rim, above, below = refs
    above[...], below[...] = paired(is_odd("fy"), got_a[...], got_b[0 : got_a.shape[0]])
    assemble(wide, rim, state, edge, beside_x, edges_x, above, below)
    planes = wide.shape[1]
    cells_x = planes - 2 * HALO
    size = send.shape[1] // 2
    rim_start = [rim[f] for f in range(5)]
    derive_planes(wide, derived, 0, planes)
    _, along_z, rim_first = rim_section(rim_start, None, MIXES[0])
    to_ends(along_z, 2, 16, -2, cells_x + 2, ends)
    flow_rate_section(wide, derived, ends, wide, 0, MIXES[0], writer(first))
    derive_planes(first, derived, 0, planes - 2)
    other, along_z, rim_second = rim_section(rim_first, [rim[f] for f in range(5)], MIXES[1])
    to_ends(other[0:2], 3, 8, 0, cells_x, ends)
    lamb(derived, ends, 2, cells_x, lamb_rows)
    project(lamb_rows, pair, spread, send, 0)
    to_ends(along_z, 2, 16, -1, cells_x + 1, ends)
    flow_rate_section(first, derived, ends, wide, 1, MIXES[1], writer(second))
    derive_planes(second, derived, 0, planes - 4)
    other, along_z, _ = rim_section(rim_second, None, None)
    to_ends(other[0:2], 3, 8, 0, cells_x, ends)
    lamb(derived, ends, 1, cells_x, lamb_rows)
    project(lamb_rows, pair, spread, send, size)
    to_ends(along_z, 2, 8, 0, cells_x, ends_out)


def flow_last_body(second, derived, ends, state, out):
    flow_rate_section(second, derived, ends, state, -1, MIXES[2], writer(out), inner=True)


def faces_out(state, rear, front):
    lane = lax.broadcasted_iota(jnp.int32, (32, 128), 1) // 16
    for c in range(4):
        front[c * 8 : c * 8 + 8] = state[c, 56:64]
        rear[c * 8 : c * 8 + 8] = state[c, 0:8]
        front[32 + c * 8 : 40 + c * 8] = state[c, pl.ds(7, 8, stride=8), :]
        rear[32 + c * 8 : 40 + c * 8] = state[c, pl.ds(0, 8, stride=8), :]
    rows = state[...].reshape(256, 128)
    last = jnp.zeros((32, 128), F32)
    first = jnp.zeros((32, 128), F32)
    for j in range(8):
        piece = rows[j * 32 : j * 32 + 32]
        last = jnp.where(lane == j, pltpu.roll(piece, (j * 16 + 16) % 128, 1), last)
        first = jnp.where(lane == j, pltpu.roll(piece, j * 16, 1) if j else piece, first)
    front[64:96] = last
    rear[64:96] = first


def faces_sent(odd, state, message_a, message_b):
    size = message_a.shape[0]
    faces_out(state, message_b, message_a)
    message_a[...], message_b[0:size] = paired(odd, message_a[...], message_b[0:size])
    if message_b.shape[0] > size:
        message_b[size:] = jnp.zeros((message_b.shape[0] - size, 128), F32)


def lift(total, before, after, sides, factor):
    def place(face, rows, target):
        value = factor * dot_exact_right(rows, sides[face])
        for c in range(4):
            total[c, target, :] += value[c * 8 : c * 8 + 8]

    place(0, before[0:32], pl.ds(0, 8))
    place(1, after[0:32], pl.ds(56, 8))
    place(2, before[32:64], pl.ds(0, 8, stride=8))
    place(3, after[32:64], pl.ds(7, 8, stride=8))


def rate_local(state, deriv_rows, deriv_lanes, speed, sides):
    fields = [state[c] for c in range(4)]
    by_rows = dot_three(deriv_rows[...], jnp.concatenate(fields[0:3], 1))
    by_lanes = dot_three(jnp.concatenate([fields[0], fields[3]], 0), deriv_lanes[...])
    divergence = by_rows[0:64, 128:256] + by_rows[64:128, 256:384] + by_lanes[64:128]
    rates = [
        -(speed[...] * speed[...]) * divergence,
        -by_rows[0:64, 0:128],
        -by_rows[64:128, 0:128],
        -by_lanes[0:64],
    ]
    row = lax.broadcasted_iota(jnp.int32, (64, 128), 0)
    lane = lax.broadcasted_iota(jnp.int32, (64, 128), 1)
    count = jnp.zeros((64, 128), F32)
    for value in (row // 8, row % 8, lane // 16):
        count = count + jnp.where((value == 0) | (value == 7), PENALTY, 0.0)
    side = PENALTY * dot_exact_right(state[...].reshape(256, 128), sides[4])
    return [rates[c] - count * fields[c] + side[c * 64 : c * 64 + 64] for c in range(4)]


def acoustic_local_body(mix, state, start, deriv_rows, deriv_lanes, speed, sides, out, front, rear):
    rates = rate_local(state, deriv_rows, deriv_lanes, speed, sides)
    for c in range(4):
        value = state[c] + TIME_STEP * rates[c]
        if mix[0] != 0.0:
            value = mix[0] * start[c] + mix[1] * value
        out[c] = value
    faces_out(state, rear, front)
    lift(out, front, rear, sides, TIME_STEP * mix[1] * PENALTY)


def acoustic_start_body(given, local, _, state, message_a, message_b, turned, stored):
    count = given.shape[0]
    for e in range(count):
        for t in range(4):
            stored[t, 4 * e : 4 * e + 4] = given[e, :, t * 128 : t * 128 + 128]
    for t in range(4):
        rows = [stored[t, pl.ds(c, count, stride=4), :] for c in range(4)]
        rows = jnp.concatenate(rows + [jnp.zeros((128 - 4 * count, 128), F32)], 0)
        turned[t * 128 : t * 128 + 128] = rows.T
    lane = lax.broadcasted_iota(jnp.int32, (64, 128), 1) // count
    fields = [jnp.zeros((64, 128), F32)] * 4
    for z in range(8):
        piece = turned[pl.ds(z, 64, stride=8), :]
        for c in range(4):
            move = (z - c) * count % 128
            fields[c] = jnp.where(lane == z, pltpu.roll(piece, move, 1) if move else piece, fields[c])
    for c in range(4):
        state[c] = fields[c]
    faces_sent(is_odd("fz"), state, message_a, message_b)
    message_b[96:104] = local[...]


def natural_order(state, out, turned, stored):
    count = out.shape[0]
    lane = lax.broadcasted_iota(jnp.int32, (64, 128), 1) // count
    for z in range(8):
        value = jnp.zeros((64, 128), F32)
        for c in range(4):
            move = (c - z) * count % 128
            value = jnp.where(lane == c, pltpu.roll(state[c], move, 1) if move else state[c], value)
        turned[pl.ds(z, 64, stride=8), :] = value
    for t in range(4):
        rows = turned[t * 128 : t * 128 + 128].T
        for c in range(4):
            stored[t, pl.ds(c, count, stride=4), :] = rows[c * count : c * count + count]
    for e in range(count):
        for t in range(4):
            out[e, :, t * 128 : t * 128 + 128] = stored[t, 4 * e : 4 * e + 4]


def remote_part(out, before, after, sides_far, factor):
    lift(out, before, after, sides_far, factor)
    lane = lax.broadcasted_iota(jnp.int32, (32, 128), 1) // 16
    last, first = before[64:96], after[64:96]
    pieces = []
    for j in range(8):
        left = pltpu.roll(last, 128 - j * 16, 1) if j else last
        right = pltpu.roll(first, (144 - j * 16) % 128, 1) if j != 1 else first
        pieces.append(jnp.where(lane == 0, left, jnp.where(lane == 1, right, 0.0)))
    value = factor * dot_exact_right(jnp.concatenate(pieces, 0), sides_far[4])
    for c in range(4):
        out[c] += value[c * 64 : c * 64 + 64]


def arrived(odd, got_a, got_b, before, after):
    none = jnp.zeros((96, 128), F32)
    near = none if got_a is None else got_a[0:96]
    after[...], before[...] = paired(odd, near, none if got_b is None else got_b[0:96])


def acoustic_first_body(partial, got_a, got_b, sides_far, received, _, out, message_a, message_b, before, after, source):
    odd = is_odd("fz")
    place(received, received, source, 0)
    arrived(odd, got_a, got_b, before, after)
    out[0] = partial[0]
    for c in range(3):
        out[1 + c] = partial[1 + c] + (TIME_STEP * MIXES[0][1]) * source[c]
    remote_part(out, before, after, sides_far, TIME_STEP * MIXES[0][1] * PENALTY)
    faces_sent(odd, out, message_a, message_b)


def acoustic_near_body(
    partial, got_a, sides_far, received, labelled, out, message_b, before, after, source, spare
):
    odd = is_odd("fz")
    place(received, labelled, source, 0)
    arrived(odd, got_a, None, before, after)
    out[0] = partial[0]
    for c in range(3):
        out[1 + c] = partial[1 + c] + (TIME_STEP * MIXES[1][1]) * source[c]
    remote_part(out, before, after, sides_far, TIME_STEP * MIXES[1][1] * PENALTY)
    faces_sent(odd, out, spare, message_b)


def acoustic_rest_body(partial, got_b, sides_far, out, message_a, before, after, spare):
    odd = is_odd("fz")
    arrived(odd, None, got_b, before, after)
    out[...] = partial[...]
    remote_part(out, before, after, sides_far, TIME_STEP * MIXES[1][1] * PENALTY)
    faces_sent(odd, out, message_a, spare)


def mirror_body(sent_b, sides_partner, change, before, after, spare, state):
    odd = jnp.logical_not(is_odd("fz"))
    arrived(odd, None, sent_b, before, after)
    state[...] = jnp.zeros(state.shape, F32)
    remote_part(state, before, after, sides_partner, TIME_STEP * MIXES[1][1] * PENALTY)
    faces_sent(odd, state, spare, change)


def acoustic_last_body(
    partial, got_a, got_b, change, sides_far, source, given_out, before, after, out, turned, stored
):
    odd = is_odd("fz")
    after[...], before[...] = paired(odd, got_a[0:96], got_b[0:96] + change[...])
    out[0] = partial[0]
    for c in range(3):
        out[1 + c] = partial[1 + c] + (TIME_STEP * MIXES[2][1]) * source[c]
    remote_part(out, before, after, sides_far, TIME_STEP * MIXES[2][1] * PENALTY)
    natural_order(out, given_out, turned, stored)


def place(received, labelled, out, base):
    peers, size = labelled.shape[0], labelled.shape[1]
    fold = 192 // (size - 8)
    height = 64 // fold
    target = lax.broadcasted_iota(jnp.int32, (128, 128), 0)
    lane = lax.broadcasted_iota(jnp.int32, (128, 128), 1)
    total = None
    for peer in range(peers):
        label = labelled[peer, size - 8 : size - 7, :]
        label = jnp.broadcast_to(label, (128, 128)).astype(jnp.int32)
        hit = (label == target % 16) & (lane % 8 == target // 16)
        chosen = [jnp.where(hit & (lane // (128 // fold) == g), 1.0, 0.0) for g in range(fold)]
        chosen = jnp.concatenate(chosen, 0).astype(BF16)
        high, low = parts(received[peer, base : base + 3 * height])
        dims = (((1,), (1,)), ((), ()))
        value = lax.dot_general(high, chosen, dims, preferred_element_type=F32)
        value = value + lax.dot_general(low, chosen, dims, preferred_element_type=F32)
        total = value if total is None else total + value
    for c in range(3):
        for g in range(fold):
            at = c * height
            out[c, g * height : g * height + height] = total[at : at + height, g * 128 : g * 128 + 128]


def place_last_body(received, labelled, out):
    place(received, labelled, out, received.shape[1] // 2)


def kron_part(matrix, shape, rows_by, columns_by):
    row = lax.broadcasted_iota(jnp.int32, (shape[0], 8), 0)
    level = lax.broadcasted_iota(jnp.int32, (shape[0], 8), 1)
    left = (row // rows_by % 8 == level).astype(F32)
    level = lax.broadcasted_iota(jnp.int32, (8, shape[1]), 0)
    column = lax.broadcasted_iota(jnp.int32, (8, shape[1]), 1)
    right = (column // columns_by % 8 == level).astype(F32)
    return dot_full(dot_full(left, matrix), right)


def far_tables(wanted, count, far):
    size = 8 * count
    row = lax.broadcasted_iota(jnp.int32, (size, size), 0)
    level_out = lax.broadcasted_iota(jnp.int32, (size, size), 1) // count
    level, element = row // count, row % count
    for facet in range(4):
        shift = -count if facet % 2 == 0 else count
        choice = jnp.broadcast_to(wanted[facet : facet + 1], (size, size))
        far[facet] = jnp.where((level == level_out) & (element + shift == choice), 1.0, 0.0).astype(BF16)
    lower = jnp.broadcast_to(wanted[4:5], (size, size))
    upper = jnp.broadcast_to(wanted[5:6], (size, size))
    hit = (level == 0) & (level_out == 0) & (element - count == lower)
    hit = hit | ((level == 1) & (level_out == 7) & (element + count == upper))
    far[4] = jnp.where(hit, 1.0, 0.0).astype(BF16)


def partner_tables_body(count, got_b, far):
    row = lax.broadcasted_iota(jnp.int32, (count, 8 * count), 0)
    column = lax.broadcasted_iota(jnp.int32, (count, 8 * count), 1)
    repeat = (column % count == row).astype(F32)
    wanted = dot_full(got_b[96:104, 0:count], repeat).astype(jnp.int32)
    far_tables(wanted, count, far)


def tables_body(
    packed,
    near,
    far,
    deriv_rows,
    deriv_lanes,
    pair,
    spread,
    labels,
    speed,
):
    size = near.shape[1]
    count = size // 8
    blocks = spread.shape[0] // 8

    def place_of(shape):
        return (lax.broadcasted_iota(jnp.int32, shape, 0), lax.broadcasted_iota(jnp.int32, shape, 1))

    row, column = place_of((count, size))
    repeat = (column % count == row).astype(F32)
    speed[...] = dot_full(packed[24:25, 0:count], repeat)
    wanted = dot_full(packed[16:24, 0:count], repeat).astype(jnp.int32)
    row, column = place_of((size, size))
    level, element = row // count, row % count
    level_out = column // count
    for facet in range(4):
        choice = jnp.broadcast_to(wanted[facet : facet + 1], (size, size))
        near[facet] = jnp.where((level == level_out) & (element == choice), 1.0, 0.0).astype(BF16)
    lower = jnp.broadcast_to(wanted[4:5], (size, size))
    upper = jnp.broadcast_to(wanted[5:6], (size, size))
    hit = (level == 7) & (level_out == 0) & (element == lower)
    hit = hit | ((level == 0) & (level_out == 7) & (element == upper))
    near[4] = jnp.where(hit, 1.0, 0.0).astype(BF16)
    far_tables(wanted, count, far)

    row, column = place_of((64, 64))
    slopes, modes = packed[0:8, 0:8], packed[8:16, 0:8]
    outer = kron_part(slopes, (64, 64), 8, 8)
    inner = kron_part(slopes, (64, 64), 1, 1)
    deriv_rows[0:64] = jnp.where(row % 8 == column % 8, outer, 0.0)
    deriv_rows[64:128] = jnp.where(row // 8 == column // 8, inner, 0.0)
    row, column = place_of((size, size))
    lanes = kron_part(slopes.T, (size, size), count, count)
    deriv_lanes[...] = jnp.where(row % count == column % count, lanes, 0.0)
    pair[...] = kron_part(modes, (64, 64), 8, 8) * kron_part(modes, (64, 64), 1, 1)

    peers = labels.shape[0]
    capacity = capacity_of(peers, blocks)
    row, column = place_of((blocks, blocks))

    def upright(values):
        return jnp.sum(jnp.where(row == column, values, 0.0), 1, keepdims=True)

    owner_row = packed[25:26, 0:blocks]
    owner_column = upright(owner_row)
    earlier = (owner_column == owner_row) & (column < row)
    position = jnp.sum(jnp.where(earlier, 1.0, 0.0), 1, keepdims=True)
    slot = owner_column * capacity + position
    element_column = upright(packed[26:27, 0:blocks])
    row, column = place_of((8 * blocks, blocks))
    repeat = (row // 8 == column).astype(F32)
    slot = dot_full(repeat, jnp.broadcast_to(slot, (blocks, 128)))
    element = dot_full(repeat, jnp.broadcast_to(element_column, (blocks, 128)))
    row, column = place_of((8 * blocks, 128))
    values = kron_part(modes.T, (8 * blocks, 128), 1, 1)
    inside = column % (8 * capacity) // 8
    for peer in range(peers):
        chosen = slot == (inside + peer * capacity).astype(F32)
        spread[:, peer * 128 : peer * 128 + 128] = jnp.where(chosen, values, 0.0)
        named = jnp.where(chosen & (row % 8 == 0), element + 1.0, 0.0)
        labels[peer] = jnp.broadcast_to(jnp.sum(named, 0, keepdims=True) - 1.0, (8, 128))


def shifted(sizes, shifts):
    pairs = []
    for index in np.ndindex(*sizes):
        source = [(i + s) % n for i, s, n in zip(index, shifts, sizes)]
        pairs.append((int(np.ravel_multi_index(source, sizes)), int(np.ravel_multi_index(index, sizes))))
    return pairs


def partners(sizes, axis, second):
    pairs = []
    for index in np.ndindex(*sizes):
        source = list(index)
        step = 1 if (index[axis] % 2 == 0) != second else -1
        source[axis] = (index[axis] + step) % sizes[axis]
        pairs.append((int(np.ravel_multi_index(source, sizes)), int(np.ravel_multi_index(index, sizes))))
    return pairs


def per_device(
    density,
    velocity,
    pressure,
    acoustic,
    sound_speed,
    derivative,
    mode_basis,
    neighbours,
    block_owner,
    block_element,
):
    size_x, size_y, size_z = lax.axis_size("fx"), lax.axis_size("fy"), lax.axis_size("fz")
    devices = size_x * size_y * size_z
    cells_x = density.shape[0]
    elements = acoustic.shape[0]
    device = lax.axis_index(("fx", "fy", "fz"))

    names = ("fx", "fy", "fz")

    rows = 5 * cells_x * 8
    tiles = -(-rows // 128)
    square = velocity[0] * velocity[0] + velocity[1] * velocity[1] + velocity[2] * velocity[2]
    energy = pressure / (HEAT_RATIO - 1.0) + 0.5 * density * square
    rest = ((0, 0), (0, 0), (0, 0))
    state = jnp.pad(density[None], ((0, 4),) + rest) + jnp.pad(density * velocity, ((1, 1),) + rest)
    state = state + jnp.pad(energy[None], ((4, 0),) + rest)
    x_rows = 5 * 2 * HALO * 8
    flow_a, flow_b, along_x = call(
        pack_start_body, [(tiles * 8, 128), (tiles * 8, 128), (x_rows, 128)], state
    )
    edge_a = lax.ppermute(flow_a, "fz", partners((size_z,), 0, False))
    edge_b = lax.ppermute(flow_b, "fz", partners((size_z,), 0, True))
    x_steps = (1,) if size_x == 2 else (1, -1)
    beside_x = [lax.ppermute(along_x, "fx", shifted((size_x,), (step,))) for step in x_steps]

    local = (neighbours - device * elements).T

    near_pairs = [(i ^ 1, i) for i in range(devices)]
    far_pairs = [pair for i in range(1, devices - 1, 2) for pair in ((i, i + 1), (i + 1, i))]

    def traces(to_a, to_b):
        far_got = lax.ppermute(to_b, names, far_pairs)
        return lax.ppermute(to_a, names, near_pairs), far_got

    size = 8 * elements
    held = (4, 64, size)
    faces = (96, size)
    sides = [pltpu.VMEM(faces, F32)] * 2
    turning = [pltpu.VMEM((512, 128), F32), pltpu.VMEM((4, 4 * elements, 128), F32)]
    sound, to_a, to_b = call(
        acoustic_start_body,
        [held, faces, (faces[0] + 8, size)],
        acoustic,
        jnp.pad(local.astype(F32), ((0, 2), (0, size - elements))),
        edge_a,
        scratch=turning,
        last=1,
    )
    got_a, got_b = traces(to_a, to_b)

    edge = call(
        pack_next_body,
        [(40, 128)],
        state,
        flow_a,
        flow_b,
        edge_a,
        edge_b,
        to_a,
        last=1,
    )[0]
    edges_x = [lax.ppermute(edge, "fx", shifted((size_x,), (step,))) for step in x_steps]
    y_shape = (5 * cells_x * HALO + 48, 128)
    y_a, y_b = call(pack_last_body, [y_shape, (y_shape[0] + 8, 128)], state, edge, *beside_x, *edges_x, got_a, last=1, cost=1)
    y_second = lax.ppermute(y_b, "fy", partners((size_y,), 0, True))
    y_first = lax.ppermute(y_a, "fy", partners((size_y,), 0, False))

    blocks = block_owner.size
    width = max(elements, blocks)

    def piece(values, first):
        values = values.astype(F32)
        return jnp.pad(values, ((first, 32 - first - values.shape[0]), (0, width - values.shape[1])))

    packed = (
        piece(derivative, 0)
        + piece(mode_basis, 8)
        + piece(local, 16)
        + piece(sound_speed.reshape(1, elements), 24)
        + piece(block_owner.reshape(1, blocks), 25)
        + piece(block_element.reshape(1, blocks), 26)
    )
    table = jax.ShapeDtypeStruct((5, size, size), BF16)
    near, far, deriv_rows, deriv_lanes, pair, spread, labels, speed = call(
        tables_body,
        [
            table,
            table,
            (128, 64),
            (size, size),
            (64, 64),
            (8 * blocks, size_y * 128),
            (size_y, 8, 128),
            (1, size),
        ],
        packed,
        cost=1,
    )

    fold = fold_of(size_y, blocks)
    wide = cells_x + 2 * HALO
    rows_scratch = pltpu.VMEM((3, 64, 128), F32)

    def planes(count):
        return (5, count, 16, 128)

    def route(send):
        return lax.all_to_all(send, "fy", split_axis=0, concat_axis=0, tiled=True)

    def local_part(mix, now):
        return call(
            functools.partial(acoustic_local_body, mix),
            [held],
            now,
            sound,
            deriv_rows,
            deriv_lanes,
            speed,
            near,
            scratch=sides,
            cost=1,
        )[0]

    partial = local_part(MIXES[0], sound)
    y_scratch = [pltpu.VMEM(y_shape, F32), pltpu.VMEM(y_shape, F32)]
    send = call(
        functools.partial(flow_sources_body, len(beside_x)),
        [(size_y, 192 // fold + 8, 128)],
        state,
        edge,
        *beside_x,
        y_second,
        y_first,
        pair,
        spread,
        labels,
        got_b,
        last=1,
        scratch=[
            pltpu.VMEM((4, cells_x + 2, 16, 128), F32),
            pltpu.VMEM((3, cells_x + 2, 16, 128), F32),
            rows_scratch,
            pltpu.VMEM((2, cells_x, 8, 128), F32),
        ]
        + y_scratch,
    )[0]
    received = route(send)
    second, derived, ends, send = call(
        functools.partial(flow_stages_body, len(edges_x)),
        [
            planes(wide - 4),
            planes(wide),
            (5, cells_x, 8, 128),
            (size_y, 2 * 192 // fold, 128),
        ],
        state,
        edge,
        *beside_x,
        *edges_x,
        y_second,
        y_first,
        pair,
        spread,
        partial,
        last=1,
        scratch=[
            rows_scratch,
            pltpu.VMEM(planes(wide - 2), F32),
            pltpu.VMEM(planes(wide - 2), F32),
            pltpu.VMEM(planes(wide), F32),
            pltpu.VMEM((5, 16, 256), F32),
        ]
        + y_scratch,
    )

    far_partner = call(functools.partial(partner_tables_body, elements), [table], got_b)[0]
    longer = (faces[0] + 32, size)
    near_face = pltpu.VMEM(faces, F32)
    sound_one, to_a, to_b = call(
        acoustic_first_body,
        [held, faces, longer],
        partial,
        got_a,
        got_b,
        far,
        received,
        send,
        scratch=sides + [rows_scratch],
        last=1,
    )
    labelled, received = received, route(send)
    got_a, got_b = traces(to_a, to_b)
    flow_state = call(flow_last_body, [(5, cells_x, 8, 128)], second, derived, ends, state)[0]
    partial = local_part(MIXES[1], sound_one)
    change = call(
        mirror_body, [faces], to_b, far_partner, scratch=sides + [near_face, pltpu.VMEM(held, F32)], cost=1
    )[0]
    partial, to_b = call(
        acoustic_near_body,
        [held, longer],
        partial,
        got_a,
        far,
        received,
        labelled,
        scratch=sides + [rows_scratch, near_face],
    )
    got_b_last = lax.ppermute(to_b, names, far_pairs)
    sound_two, to_a = call(
        acoustic_rest_body, [held, faces], partial, got_b, far, scratch=sides + [near_face]
    )
    got_a = lax.ppermute(to_a, names, near_pairs)
    source_three = call(place_last_body, [(3, 64, 128)], received, labelled)[0]
    partial = local_part(MIXES[2], sound_two)
    sound_state = call(
        acoustic_last_body,
        [(elements, 4, 512)],
        partial,
        got_a,
        got_b_last,
        change,
        far,
        source_three,
        scratch=sides + [pltpu.VMEM(held, F32)] + turning,
    )[0]
    return (flow_state, sound_state)


def solution(mesh):
    placed = (
        P("fx", "fy", "fz"),
        P(None, "fx", "fy", "fz"),
        P("fx", "fy", "fz"),
        P(("fx", "fy", "fz"), None, None),
        P(("fx", "fy", "fz")),
        P(),
        P(),
        P(("fx", "fy", "fz"), None),
        P("fx", "fy", "fz", None, None),
        P("fx", "fy", "fz", None),
    )
    return jax.shard_map(
        per_device,
        mesh=mesh,
        in_specs=placed,
        out_specs=(P(None, "fx", "fy", "fz"), P(("fx", "fy", "fz"), None, None)),
        check_vma=False,
    )
```

```python
import functools

import jax
import jax.numpy as jnp
import numpy as np
from jax import lax
from jax.experimental import pallas as pl
from jax.experimental.pallas import tpu as pltpu
from jax.sharding import PartitionSpec as P

HEAT_RATIO = 1.4
TIME_STEP = 0.1
VISCOSITY = 0.05
PENALTY = 0.5
HALO = 3
F32 = jnp.float32
BF16 = jnp.bfloat16
PARAMS = pltpu.CompilerParams(vmem_limit_bytes=24 * 1024 * 1024)
MIXES = ((0.0, 1.0), (0.75, 0.25), (1.0 / 3.0, 2.0 / 3.0))


def parts(values):
    high = values.astype(BF16)
    return high, (values - high.astype(F32)).astype(BF16)


def dot(left, right):
    return lax.dot_general(left, right, (((1,), (0,)), ((), ())), preferred_element_type=F32)


def dot_three(left, right):
    left_high, left_low = parts(left)
    right_high, right_low = parts(right)
    return dot(left_high, right_high) + dot(left_high, right_low) + dot(left_low, right_high)


def dot_full(left, right, dims=((1,), (0,))):
    return lax.dot_general(
        left, right, (dims, ((), ())), precision=lax.Precision.HIGHEST, preferred_element_type=F32
    )


def dot_exact_right(left, right):
    left_high, left_low = parts(left)
    return dot(left_high, right) + dot(left_low, right)


def call(body, outs, *operands, scratch=(), last=0, cost=None):
    whole = pl.BlockSpec(memory_space=pltpu.VMEM)
    outs = [out if isinstance(out, jax.ShapeDtypeStruct) else jax.ShapeDtypeStruct(out, F32) for out in outs]
    anywhere = pl.BlockSpec(memory_space=pl.ANY)
    return pl.pallas_call(
        body,
        out_shape=outs,
        in_specs=[whole] * (len(operands) - last) + [anywhere] * last,
        out_specs=[whole] * len(outs),
        scratch_shapes=list(scratch),
        compiler_params=PARAMS,
        cost_estimate=None if cost is None else pl.CostEstimate(flops=cost, bytes_accessed=cost, transcendentals=0),
    )(*operands)


def capacity_of(peers, blocks):
    return max(2, 2 * blocks // peers)


def fold_of(peers, blocks):
    return 128 // (8 * capacity_of(peers, blocks))


def is_odd(axis):
    return lax.axis_index(axis) % 2 == 1


def paired(odd, to_next, to_last):
    return jnp.where(odd, to_last, to_next), jnp.where(odd, to_next, to_last)


def pack_start_body(state, message_a, message_b, along_x):
    odd = is_odd("fz")
    rows = state[...].reshape(-1, 128)
    count = rows.shape[0]
    for tile in range(message_a.shape[0] // 8):
        piece = rows[tile * 128 : min(count, tile * 128 + 128)]
        if piece.shape[0] < 128:
            piece = jnp.concatenate([piece, jnp.zeros((128 - piece.shape[0], 128), F32)], 0)
        turned = piece.T
        first, second = paired(odd, turned[120:128], turned[0:8])
        message_a[tile * 8 : tile * 8 + 8] = first
        message_b[tile * 8 : tile * 8 + 8] = second
    cells_x = state.shape[1]
    for f in range(5):
        for s, x in enumerate(x_planes(cells_x)):
            at = (f * 2 * HALO + s) * 8
            along_x[at : at + 8] = state[f, x]


def pack_next_body(state, sent_a, sent_b, got_a, got_b, _, edge):
    cells_x = state.shape[1]
    odd_z = is_odd("fz")
    high, low = paired(odd_z, sent_a[...], sent_b[...])
    above, below = paired(odd_z, got_a[...], got_b[...])
    row = lax.broadcasted_iota(jnp.int32, (8, 128), 0)
    x_of_lane = lax.broadcasted_iota(jnp.int32, (16, 128), 1) // 8 % cells_x
    for tile in range(high.shape[0] // 8):
        rows = slice(tile * 8, tile * 8 + 8)
        upper = jnp.where(row < 3, pltpu.roll(high[rows], 3, 0), pltpu.roll(above[rows], 3, 0))
        lower = jnp.where(row < 3, pltpu.roll(below[rows], 3, 0), pltpu.roll(low[rows], 3, 0))
        slots = jnp.concatenate([upper, lower], 0)
        spread = jnp.concatenate([jnp.where(x_of_lane == x, slots, 0.0) for x in range(8)], 0).T
        for half in range(16 // cells_x):
            f = tile * (16 // cells_x) + half
            if f < 5:
                at = half * cells_x * 8
                total = spread[at : at + 8]
                for x in range(1, cells_x):
                    total = total + spread[at + x * 8 : at + x * 8 + 8]
                edge[f * 8 : f * 8 + 8] = total


def x_planes(cells_x):
    return [cells_x - HALO + i for i in range(HALO)] + list(range(HALO))


def sides_of(beside_x):
    return beside_x[0], beside_x[-1]


def beyond(edges_x, f):
    after, before = sides_of(edges_x)
    at = f * 8
    if after is before:
        return after[at : at + 8]
    lane = lax.broadcasted_iota(jnp.int32, (8, 128), 1)
    return jnp.where(lane < 64, after[at : at + 8], before[at : at + 8])


def pack_last_body(state, edge, *refs):
    (y_a, y_b), refs = refs[-2:], refs[:-3]
    beside_x, edges_x = refs[: len(refs) // 2], refs[len(refs) // 2 :]
    cells_x = state.shape[1]
    odd = is_odd("fy")
    after, before = sides_of(beside_x)

    def put(at, values, height):
        first, second = paired(odd, values[8 - height : 8], values[0:height])
        y_a[at : at + height] = first
        y_b[at : at + height] = second

    lines = 5 * cells_x * HALO
    for f in range(5):
        for x in range(cells_x):
            put((f * cells_x + x) * HALO, state[f, x], HALO)
        at = lines + f * 6
        for slot, height in ((1, 1), (2, 2), (3, 2), (4, 1)):
            source = (f * 2 * HALO + slot) * 8
            put(at, (before if slot < HALO else after)[source : source + 8], height)
            at += height
        put(lines + 30 + f * 2, edge[f * 8 : f * 8 + 8], 2)
        put(lines + 40 + f, beyond(edges_x, f), 1)


def assemble_speeds(wide, state, beside_x, above, below):
    cells_x = state.shape[1]
    after, before = sides_of(beside_x)
    for f in range(4):
        for x in range(cells_x):
            wide[f, 1 + x, 0:8] = state[f, x]
            at = (f * cells_x + x) * HALO
            wide[f, 1 + x, 8:9] = above[at : at + 1]
            wide[f, 1 + x, 15:16] = below[at + HALO - 1 : at + HALO]
        for slot, plane, source in ((HALO - 1, 0, before), (HALO, cells_x + 1, after)):
            at = (f * 2 * HALO + slot) * 8
            wide[f, plane, 0:8] = source[at : at + 8]


def assemble(wide, rim, state, edge, beside_x, edges_x, above, below):
    cells_x = state.shape[1]
    after, before = sides_of(beside_x)
    lines = 5 * cells_x * HALO
    for f in range(5):
        for x in range(cells_x):
            wide[f, HALO + x, 0:8] = state[f, x]
            at = (f * cells_x + x) * HALO
            wide[f, HALO + x, 8 : 8 + HALO] = above[at : at + HALO]
            wide[f, HALO + x, 16 - HALO : 16] = below[at : at + HALO]
        for slot in range(2 * HALO):
            plane = slot if slot < HALO else cells_x + slot
            at = (f * 2 * HALO + slot) * 8
            wide[f, plane, 0:8] = (before if slot < HALO else after)[at : at + 8]
        at = lines + f * 6
        for slot, height in ((1, 1), (2, 2), (3, 2), (4, 1)):
            plane = slot if slot < HALO else cells_x + slot
            wide[f, plane, 8 : 8 + height] = above[at : at + height]
            wide[f, plane, 16 - height : 16] = below[at : at + height]
            at += height
        rim[f, 0:8, 0:128] = edge[f * 8 : f * 8 + 8]
        rim[f, 0:8, 128:256] = beyond(edges_x, f)
        at = lines + 30 + f * 2
        rim[f, 8:10, 0:128] = above[at : at + 2]
        rim[f, 14:16, 0:128] = below[at : at + 2]
        at = lines + 40 + f
        rim[f, 8:9, 128:256] = above[at : at + 1]
        rim[f, 15:16, 128:256] = below[at : at + 1]


def primitive(rho, mx, my, mz, energy):
    inverse = 1.0 / rho
    u, v, w = mx * inverse, my * inverse, mz * inverse
    p = (HEAT_RATIO - 1.0) * (energy - 0.5 * (mx * u + my * v + mz * w))
    return u, v, w, p, jnp.sqrt(HEAT_RATIO * jnp.abs(p) * inverse)


def chunks(first, last, size):
    return [(i, min(i + size, last)) for i in range(first, last, size)]


def derive_planes(wide, derived, first, last):
    for i, j in chunks(first, last, 4):
        for k, value in enumerate(primitive(*[wide[f, i:j] for f in range(5)])):
            derived[k, i:j] = value


def derive_speeds(wide, derived, first, last):
    for i, j in chunks(first, last, 5):
        inverse = 1.0 / wide[0, i:j]
        for k in range(3):
            derived[k, i:j] = wide[1 + k, i:j] * inverse


def with_flux(fields, other, along):
    speed, p = other[along], other[3]
    out = [fields[1 + along]]
    for k in range(3):
        value = fields[1 + k] * speed
        out.append(value + p if k == along else value)
    out.append((fields[4] + p) * speed)
    return fields, out, jnp.abs(speed) + other[4]


def face(left, right):
    (fields_l, flux_l, speed_l), (fields_r, flux_r, speed_r) = left, right
    speed = jnp.maximum(speed_l, speed_r)
    viscous = speed + 2.0 * VISCOSITY
    return [
        (flux_l[f] + flux_r[f]) - (viscous if 1 <= f <= 3 else speed) * (fields_r[f] - fields_l[f])
        for f in range(5)
    ]


def rolled(here, shift, axis):
    fields, flux, speed = here
    return (
        [pltpu.roll(a, shift, axis) for a in fields],
        [pltpu.roll(a, shift, axis) for a in flux],
        pltpu.roll(speed, shift, axis),
    )


def rim_section(fields, start, mix):
    other = primitive(*fields)
    here = with_flux(fields, other, 2)
    along_z = face(here, rolled(here, 255, 1))
    if mix is None:
        return other, along_z, None
    total = [g - pltpu.roll(g, 1, 1) for g in along_z]
    for along, step, axis, size in ((0, 16, 1, 256), (1, 1, 0, 16)):
        here = with_flux(fields, other, along)
        faces = face(here, rolled(here, size - step, axis))
        total = [total[f] + (faces[f] - pltpu.roll(faces[f], step, axis)) for f in range(5)]
    out = []
    for f in range(5):
        value = fields[f] - (0.5 * TIME_STEP) * total[f]
        out.append(mix[0] * start[f] + mix[1] * value if mix[0] != 0.0 else value)
    return other, along_z, out


def to_ends(values, after, rows, first, last, ends):
    slot = lax.broadcasted_iota(jnp.int32, (rows, 256), 1) % 16
    for f, value in enumerate(values):
        value = value[0:rows]
        value = jnp.where(slot == 9, pltpu.roll(value, 9 - after, 1), value)
        for x in range(first, last):
            at = x % 16 // 8 * 128
            move = (118 - x % 8 * 16) % 128
            tile = value[:, at : at + 128]
            ends[f, x - first, 0:rows] = pltpu.roll(tile, move, 1) if move else tile


def flow_rate_section(wide, derived, ends, start, offset, mix, write, inner=False):
    depth = wide.shape[1]
    rows = slice(0, 8) if inner else slice(None)
    size = 4 if inner else 2

    def planes(i, j, kept, along):
        fields = [wide[f, i:j, kept] for f in range(5)]
        return with_flux(fields, [derived[f, i:j, kept] for f in range(5)], along)

    def cut(here, i, j):
        return [a[i:j] for a in here[0]], [a[i:j] for a in here[1]], here[2][i:j]

    for i, j in chunks(1, depth - 1, size):
        count = j - i
        lane = lax.broadcasted_iota(jnp.int32, (count, 8 if inner else 16, 128), 2)
        here = planes(i - 1, j + 1, rows, 0)
        faces = face(cut(here, 0, count + 1), cut(here, 1, count + 2))
        total = [g[1:] - g[:-1] for g in faces]
        here = planes(i, j, slice(None), 1)
        faces = face(here, rolled(here, 15, 1))
        for f in range(5):
            change = faces[f] - pltpu.roll(faces[f], 1, 1)
            total[f] = total[f] + (change[:, 0:8] if inner else change)
        here = planes(i, j, rows, 2)
        faces = face(here, rolled(here, 127, 2))
        for f in range(5):
            end = ends[f, i - 1 : j - 1, rows]
            value = jnp.where(lane == 127, end, faces[f])
            total[f] = total[f] + (value - jnp.where(lane == 0, end, pltpu.roll(value, 1, 2)))
        for f in range(5):
            value = wide[f, i:j, rows] - (0.5 * TIME_STEP) * total[f]
            if mix[0] != 0.0:
                value = mix[0] * start[f, i + offset : j + offset, rows] + mix[1] * value
            write(slice(i - 1, j - 1), f, value)


def lamb(derived, ends, first, cells_x, lamb_rows):
    for i, j in chunks(first, first + cells_x, 4):
        count = j - i
        lane = lax.broadcasted_iota(jnp.int32, (count, 8, 128), 2)
        vel = [derived[c, i:j, 0:8] for c in range(3)]
        along_x = [derived[c, i + 1 : j + 1, 0:8] - derived[c, i - 1 : j - 1, 0:8] for c in range(3)]
        along_y = []
        for c in range(3):
            column = derived[c, i:j]
            along_y.append((pltpu.roll(column, 15, 1) - pltpu.roll(column, 1, 1))[:, 0:8])
        along_z = []
        for c in range(2):
            end = ends[c, i - first : j - first, 0:8]
            after = jnp.where(lane == 127, end, pltpu.roll(vel[c], 127, 2))
            along_z.append(after - jnp.where(lane == 0, end, pltpu.roll(vel[c], 1, 2)))
        curl = [
            0.5 * (along_y[2] - along_z[1]),
            0.5 * (along_z[0] - along_x[2]),
            0.5 * (along_x[1] - along_y[0]),
        ]
        at = slice((i - first) * 8, (j - first) * 8)
        lamb_rows[0, at] = (curl[1] * vel[2] - curl[2] * vel[1]).reshape(count * 8, 128)
        lamb_rows[1, at] = (curl[2] * vel[0] - curl[0] * vel[2]).reshape(count * 8, 128)
        lamb_rows[2, at] = (curl[0] * vel[1] - curl[1] * vel[0]).reshape(count * 8, 128)


def project(lamb_rows, pair, spread, send, base):
    peers = send.shape[0]
    fold = fold_of(peers, spread.shape[0] // 8)
    height = 64 // fold
    group = lax.broadcasted_iota(jnp.int32, (height, 128), 1) // (128 // fold)
    modes = dot_three(pair[...], jnp.concatenate([lamb_rows[c] for c in range(3)], 1))
    modes = jnp.concatenate([modes[:, c * 128 : c * 128 + 128] for c in range(3)], 0)
    sent = dot_three(modes, spread[...])
    for c in range(3):
        for peer in range(peers):
            mine = sent[c * 64 : c * 64 + 64, peer * 128 : peer * 128 + 128]
            folded = mine[0:height]
            for g in range(1, fold):
                folded = jnp.where(group == g, mine[g * height : g * height + height], folded)
            send[peer, base + c * height : base + c * height + height] = folded


def flow_sources_body(count, state, edge, *refs):
    beside_x, refs = refs[:count], refs[count:]
    got_b, got_a, pair, spread, labels, _, send, wide, derived, lamb_rows, ends, above, below = refs
    cells_x = state.shape[1]
    above[...], below[...] = paired(is_odd("fy"), got_a[...], got_b[0 : got_a.shape[0]])
    assemble_speeds(wide, state, beside_x, above, below)
    derive_speeds(wide, derived, 0, cells_x + 2)
    inverse = 1.0 / edge[0:8]
    speeds = [jnp.concatenate([edge[k * 8 : k * 8 + 8] * inverse] * 2, 1) for k in (1, 2)]
    to_ends(speeds, 3, 8, 0, cells_x, ends)
    lamb(derived, ends, 1, cells_x, lamb_rows)
    project(lamb_rows, pair, spread, send, 0)
    send[:, send.shape[1] - 8 :] = labels[...]


def writer(target):
    def write(i, f, value):
        target[f, i] = value

    return write


def flow_stages_body(count, state, edge, *refs):
    beside_x, edges_x, refs = refs[:count], refs[count : 2 * count], refs[2 * count :]
    got_b, got_a, pair, spread, _, second, derived, ends_out, send, *refs = refs
    lamb_rows, ends, first, wide, rim, above, below = refs
    above[...], below[...] = paired(is_odd("fy"), got_a[...], got_b[0 : got_a.shape[0]])
    assemble(wide, rim, state, edge, beside_x, edges_x, above, below)
    planes = wide.shape[1]
    cells_x = planes - 2 * HALO
    size = send.shape[1] // 2
    rim_start = [rim[f] for f in range(5)]
    derive_planes(wide, derived, 0, planes)
    _, along_z, rim_first = rim_section(rim_start, None, MIXES[0])
    to_ends(along_z, 2, 16, -2, cells_x + 2, ends)
    flow_rate_section(wide, derived, ends, wide, 0, MIXES[0], writer(first))
    derive_planes(first, derived, 0, planes - 2)
    other, along_z, rim_second = rim_section(rim_first, [rim[f] for f in range(5)], MIXES[1])
    to_ends(other[0:2], 3, 8, 0, cells_x, ends)
    lamb(derived, ends, 2, cells_x, lamb_rows)
    project(lamb_rows, pair, spread, send, 0)
    to_ends(along_z, 2, 16, -1, cells_x + 1, ends)
    flow_rate_section(first, derived, ends, wide, 1, MIXES[1], writer(second))
    derive_planes(second, derived, 0, planes - 4)
    other, along_z, _ = rim_section(rim_second, None, None)
    to_ends(other[0:2], 3, 8, 0, cells_x, ends)
    lamb(derived, ends, 1, cells_x, lamb_rows)
    project(lamb_rows, pair, spread, send, size)
    to_ends(along_z, 2, 8, 0, cells_x, ends_out)


def flow_last_body(second, derived, ends, state, out):
    flow_rate_section(second, derived, ends, state, -1, MIXES[2], writer(out), inner=True)


def faces_out(state, rear, front):
    lane = lax.broadcasted_iota(jnp.int32, (32, 128), 1) // 16
    for c in range(4):
        front[c * 8 : c * 8 + 8] = state[c, 56:64]
        rear[c * 8 : c * 8 + 8] = state[c, 0:8]
        front[32 + c * 8 : 40 + c * 8] = state[c, pl.ds(7, 8, stride=8), :]
        rear[32 + c * 8 : 40 + c * 8] = state[c, pl.ds(0, 8, stride=8), :]
    rows = state[...].reshape(256, 128)
    last = jnp.zeros((32, 128), F32)
    first = jnp.zeros((32, 128), F32)
    for j in range(8):
        piece = rows[j * 32 : j * 32 + 32]
        last = jnp.where(lane == j, pltpu.roll(piece, (j * 16 + 16) % 128, 1), last)
        first = jnp.where(lane == j, pltpu.roll(piece, j * 16, 1) if j else piece, first)
    front[64:96] = last
    rear[64:96] = first


def faces_sent(odd, state, message_a, message_b):
    size = message_a.shape[0]
    faces_out(state, message_b, message_a)
    message_a[...], message_b[0:size] = paired(odd, message_a[...], message_b[0:size])
    if message_b.shape[0] > size:
        message_b[size:] = jnp.zeros((message_b.shape[0] - size, 128), F32)


def lift(total, before, after, sides, factor):
    def place(face, rows, target):
        value = factor * dot_exact_right(rows, sides[face])
        for c in range(4):
            total[c, target, :] += value[c * 8 : c * 8 + 8]

    place(0, before[0:32], pl.ds(0, 8))
    place(1, after[0:32], pl.ds(56, 8))
    place(2, before[32:64], pl.ds(0, 8, stride=8))
    place(3, after[32:64], pl.ds(7, 8, stride=8))


def rate_local(state, deriv_rows, deriv_lanes, speed, sides):
    fields = [state[c] for c in range(4)]
    by_rows = dot_three(deriv_rows[...], jnp.concatenate(fields[0:3], 1))
    by_lanes = dot_three(jnp.concatenate([fields[0], fields[3]], 0), deriv_lanes[...])
    divergence = by_rows[0:64, 128:256] + by_rows[64:128, 256:384] + by_lanes[64:128]
    rates = [
        -(speed[...] * speed[...]) * divergence,
        -by_rows[0:64, 0:128],
        -by_rows[64:128, 0:128],
        -by_lanes[0:64],
    ]
    row = lax.broadcasted_iota(jnp.int32, (64, 128), 0)
    lane = lax.broadcasted_iota(jnp.int32, (64, 128), 1)
    count = jnp.zeros((64, 128), F32)
    for value in (row // 8, row % 8, lane // 16):
        count = count + jnp.where((value == 0) | (value == 7), PENALTY, 0.0)
    side = PENALTY * dot_exact_right(state[...].reshape(256, 128), sides[4])
    return [rates[c] - count * fields[c] + side[c * 64 : c * 64 + 64] for c in range(4)]


def acoustic_local_body(mix, state, start, deriv_rows, deriv_lanes, speed, sides, out, front, rear):
    rates = rate_local(state, deriv_rows, deriv_lanes, speed, sides)
    for c in range(4):
        value = state[c] + TIME_STEP * rates[c]
        if mix[0] != 0.0:
            value = mix[0] * start[c] + mix[1] * value
        out[c] = value
    faces_out(state, rear, front)
    lift(out, front, rear, sides, TIME_STEP * mix[1] * PENALTY)


def acoustic_start_body(given, local, _, state, message_a, message_b, turned, stored):
    count = given.shape[0]
    for e in range(count):
        for t in range(4):
            stored[t, 4 * e : 4 * e + 4] = given[e, :, t * 128 : t * 128 + 128]
    for t in range(4):
        rows = [stored[t, pl.ds(c, count, stride=4), :] for c in range(4)]
        rows = jnp.concatenate(rows + [jnp.zeros((128 - 4 * count, 128), F32)], 0)
        turned[t * 128 : t * 128 + 128] = rows.T
    lane = lax.broadcasted_iota(jnp.int32, (64, 128), 1) // count
    fields = [jnp.zeros((64, 128), F32)] * 4
    for z in range(8):
        piece = turned[pl.ds(z, 64, stride=8), :]
        for c in range(4):
            move = (z - c) * count % 128
            fields[c] = jnp.where(lane == z, pltpu.roll(piece, move, 1) if move else piece, fields[c])
    for c in range(4):
        state[c] = fields[c]
    faces_sent(is_odd("fz"), state, message_a, message_b)
    message_b[96:104] = local[...]


def natural_order(state, out, turned, stored):
    count = out.shape[0]
    lane = lax.broadcasted_iota(jnp.int32, (64, 128), 1) // count
    for z in range(8):
        value = jnp.zeros((64, 128), F32)
        for c in range(4):
            move = (c - z) * count % 128
            value = jnp.where(lane == c, pltpu.roll(state[c], move, 1) if move else state[c], value)
        turned[pl.ds(z, 64, stride=8), :] = value
    for t in range(4):
        rows = turned[t * 128 : t * 128 + 128].T
        for c in range(4):
            stored[t, pl.ds(c, count, stride=4), :] = rows[c * count : c * count + count]
    for e in range(count):
        for t in range(4):
            out[e, :, t * 128 : t * 128 + 128] = stored[t, 4 * e : 4 * e + 4]


def remote_part(out, before, after, sides_far, factor):
    lift(out, before, after, sides_far, factor)
    lane = lax.broadcasted_iota(jnp.int32, (32, 128), 1) // 16
    last, first = before[64:96], after[64:96]
    pieces = []
    for j in range(8):
        left = pltpu.roll(last, 128 - j * 16, 1) if j else last
        right = pltpu.roll(first, (144 - j * 16) % 128, 1) if j != 1 else first
        pieces.append(jnp.where(lane == 0, left, jnp.where(lane == 1, right, 0.0)))
    value = factor * dot_exact_right(jnp.concatenate(pieces, 0), sides_far[4])
    for c in range(4):
        out[c] += value[c * 64 : c * 64 + 64]


def arrived(odd, got_a, got_b, before, after):
    none = jnp.zeros((96, 128), F32)
    near = none if got_a is None else got_a[0:96]
    after[...], before[...] = paired(odd, near, none if got_b is None else got_b[0:96])


def acoustic_first_body(partial, got_a, got_b, sides_far, received, _, out, message_a, message_b, before, after, source):
    odd = is_odd("fz")
    place(received, received, source, 0)
    arrived(odd, got_a, got_b, before, after)
    out[0] = partial[0]
    for c in range(3):
        out[1 + c] = partial[1 + c] + (TIME_STEP * MIXES[0][1]) * source[c]
    remote_part(out, before, after, sides_far, TIME_STEP * MIXES[0][1] * PENALTY)
    faces_sent(odd, out, message_a, message_b)


def acoustic_near_body(
    partial, got_a, sides_far, received, labelled, _, __, out, message_b, before, after, source, spare
):
    odd = is_odd("fz")
    place(received, labelled, source, 0)
    arrived(odd, got_a, None, before, after)
    out[0] = partial[0]
    for c in range(3):
        out[1 + c] = partial[1 + c] + (TIME_STEP * MIXES[1][1]) * source[c]
    remote_part(out, before, after, sides_far, TIME_STEP * MIXES[1][1] * PENALTY)
    faces_sent(odd, out, spare, message_b)


def acoustic_rest_body(partial, got_b, sides_far, out, message_a, before, after, spare):
    odd = is_odd("fz")
    arrived(odd, None, got_b, before, after)
    out[...] = partial[...]
    remote_part(out, before, after, sides_far, TIME_STEP * MIXES[1][1] * PENALTY)
    faces_sent(odd, out, message_a, spare)


def mirror_body(sent_b, sides_partner, change, before, after, spare, state):
    odd = jnp.logical_not(is_odd("fz"))
    arrived(odd, None, sent_b, before, after)
    state[...] = jnp.zeros(state.shape, F32)
    remote_part(state, before, after, sides_partner, TIME_STEP * MIXES[1][1] * PENALTY)
    faces_sent(odd, state, spare, change)


def acoustic_last_body(
    partial, got_a, got_b, change, sides_far, source, given_out, before, after, out, turned, stored
):
    odd = is_odd("fz")
    after[...], before[...] = paired(odd, got_a[0:96], got_b[0:96] + change[...])
    out[0] = partial[0]
    for c in range(3):
        out[1 + c] = partial[1 + c] + (TIME_STEP * MIXES[2][1]) * source[c]
    remote_part(out, before, after, sides_far, TIME_STEP * MIXES[2][1] * PENALTY)
    natural_order(out, given_out, turned, stored)


def place(received, labelled, out, base):
    peers, size = labelled.shape[0], labelled.shape[1]
    fold = 192 // (size - 8)
    height = 64 // fold
    target = lax.broadcasted_iota(jnp.int32, (128, 128), 0)
    lane = lax.broadcasted_iota(jnp.int32, (128, 128), 1)
    total = None
    for peer in range(peers):
        label = labelled[peer, size - 8 : size - 7, :]
        label = jnp.broadcast_to(label, (128, 128)).astype(jnp.int32)
        hit = (label == target % 16) & (lane % 8 == target // 16)
        chosen = [jnp.where(hit & (lane // (128 // fold) == g), 1.0, 0.0) for g in range(fold)]
        chosen = jnp.concatenate(chosen, 0).astype(BF16)
        high, low = parts(received[peer, base : base + 3 * height])
        dims = (((1,), (1,)), ((), ()))
        value = lax.dot_general(high, chosen, dims, preferred_element_type=F32)
        value = value + lax.dot_general(low, chosen, dims, preferred_element_type=F32)
        total = value if total is None else total + value
    for c in range(3):
        for g in range(fold):
            at = c * height
            out[c, g * height : g * height + height] = total[at : at + height, g * 128 : g * 128 + 128]


def place_last_body(received, labelled, out):
    place(received, labelled, out, received.shape[1] // 2)


def kron_part(matrix, shape, rows_by, columns_by):
    row = lax.broadcasted_iota(jnp.int32, (shape[0], 8), 0)
    level = lax.broadcasted_iota(jnp.int32, (shape[0], 8), 1)
    left = (row // rows_by % 8 == level).astype(F32)
    level = lax.broadcasted_iota(jnp.int32, (8, shape[1]), 0)
    column = lax.broadcasted_iota(jnp.int32, (8, shape[1]), 1)
    right = (column // columns_by % 8 == level).astype(F32)
    return dot_full(dot_full(left, matrix), right)


def far_tables(wanted, count, far):
    size = 8 * count
    row = lax.broadcasted_iota(jnp.int32, (size, size), 0)
    level_out = lax.broadcasted_iota(jnp.int32, (size, size), 1) // count
    level, element = row // count, row % count
    for facet in range(4):
        shift = -count if facet % 2 == 0 else count
        choice = jnp.broadcast_to(wanted[facet : facet + 1], (size, size))
        far[facet] = jnp.where((level == level_out) & (element + shift == choice), 1.0, 0.0).astype(BF16)
    lower = jnp.broadcast_to(wanted[4:5], (size, size))
    upper = jnp.broadcast_to(wanted[5:6], (size, size))
    hit = (level == 0) & (level_out == 0) & (element - count == lower)
    hit = hit | ((level == 1) & (level_out == 7) & (element + count == upper))
    far[4] = jnp.where(hit, 1.0, 0.0).astype(BF16)


def partner_tables_body(count, got_b, far):
    row = lax.broadcasted_iota(jnp.int32, (count, 8 * count), 0)
    column = lax.broadcasted_iota(jnp.int32, (count, 8 * count), 1)
    repeat = (column % count == row).astype(F32)
    wanted = dot_full(got_b[96:104, 0:count], repeat).astype(jnp.int32)
    far_tables(wanted, count, far)


def tables_body(
    packed,
    near,
    far,
    deriv_rows,
    deriv_lanes,
    pair,
    spread,
    labels,
    speed,
):
    size = near.shape[1]
    count = size // 8
    blocks = spread.shape[0] // 8

    def place_of(shape):
        return (lax.broadcasted_iota(jnp.int32, shape, 0), lax.broadcasted_iota(jnp.int32, shape, 1))

    row, column = place_of((count, size))
    repeat = (column % count == row).astype(F32)
    speed[...] = dot_full(packed[24:25, 0:count], repeat)
    wanted = dot_full(packed[16:24, 0:count], repeat).astype(jnp.int32)
    row, column = place_of((size, size))
    level, element = row // count, row % count
    level_out = column // count
    for facet in range(4):
        choice = jnp.broadcast_to(wanted[facet : facet + 1], (size, size))
        near[facet] = jnp.where((level == level_out) & (element == choice), 1.0, 0.0).astype(BF16)
    lower = jnp.broadcast_to(wanted[4:5], (size, size))
    upper = jnp.broadcast_to(wanted[5:6], (size, size))
    hit = (level == 7) & (level_out == 0) & (element == lower)
    hit = hit | ((level == 0) & (level_out == 7) & (element == upper))
    near[4] = jnp.where(hit, 1.0, 0.0).astype(BF16)
    far_tables(wanted, count, far)

    row, column = place_of((64, 64))
    slopes, modes = packed[0:8, 0:8], packed[8:16, 0:8]
    outer = kron_part(slopes, (64, 64), 8, 8)
    inner = kron_part(slopes, (64, 64), 1, 1)
    deriv_rows[0:64] = jnp.where(row % 8 == column % 8, outer, 0.0)
    deriv_rows[64:128] = jnp.where(row // 8 == column // 8, inner, 0.0)
    row, column = place_of((size, size))
    lanes = kron_part(slopes.T, (size, size), count, count)
    deriv_lanes[...] = jnp.where(row % count == column % count, lanes, 0.0)
    pair[...] = kron_part(modes, (64, 64), 8, 8) * kron_part(modes, (64, 64), 1, 1)

    peers = labels.shape[0]
    capacity = capacity_of(peers, blocks)
    row, column = place_of((blocks, blocks))

    def upright(values):
        return jnp.sum(jnp.where(row == column, values, 0.0), 1, keepdims=True)

    owner_row = packed[25:26, 0:blocks]
    owner_column = upright(owner_row)
    earlier = (owner_column == owner_row) & (column < row)
    position = jnp.sum(jnp.where(earlier, 1.0, 0.0), 1, keepdims=True)
    slot = owner_column * capacity + position
    element_column = upright(packed[26:27, 0:blocks])
    row, column = place_of((8 * blocks, blocks))
    repeat = (row // 8 == column).astype(F32)
    slot = dot_full(repeat, jnp.broadcast_to(slot, (blocks, 128)))
    element = dot_full(repeat, jnp.broadcast_to(element_column, (blocks, 128)))
    row, column = place_of((8 * blocks, 128))
    values = kron_part(modes.T, (8 * blocks, 128), 1, 1)
    inside = column % (8 * capacity) // 8
    for peer in range(peers):
        chosen = slot == (inside + peer * capacity).astype(F32)
        spread[:, peer * 128 : peer * 128 + 128] = jnp.where(chosen, values, 0.0)
        named = jnp.where(chosen & (row % 8 == 0), element + 1.0, 0.0)
        labels[peer] = jnp.broadcast_to(jnp.sum(named, 0, keepdims=True) - 1.0, (8, 128))


def shifted(sizes, shifts):
    pairs = []
    for index in np.ndindex(*sizes):
        source = [(i + s) % n for i, s, n in zip(index, shifts, sizes)]
        pairs.append((int(np.ravel_multi_index(source, sizes)), int(np.ravel_multi_index(index, sizes))))
    return pairs


def partners(sizes, axis, second):
    pairs = []
    for index in np.ndindex(*sizes):
        source = list(index)
        step = 1 if (index[axis] % 2 == 0) != second else -1
        source[axis] = (index[axis] + step) % sizes[axis]
        pairs.append((int(np.ravel_multi_index(source, sizes)), int(np.ravel_multi_index(index, sizes))))
    return pairs


def per_device(
    density,
    velocity,
    pressure,
    acoustic,
    sound_speed,
    derivative,
    mode_basis,
    neighbours,
    block_owner,
    block_element,
):
    size_x, size_y, size_z = lax.axis_size("fx"), lax.axis_size("fy"), lax.axis_size("fz")
    devices = size_x * size_y * size_z
    cells_x = density.shape[0]
    elements = acoustic.shape[0]
    device = lax.axis_index(("fx", "fy", "fz"))

    names = ("fx", "fy", "fz")

    rows = 5 * cells_x * 8
    tiles = -(-rows // 128)
    square = velocity[0] * velocity[0] + velocity[1] * velocity[1] + velocity[2] * velocity[2]
    energy = pressure / (HEAT_RATIO - 1.0) + 0.5 * density * square
    rest = ((0, 0), (0, 0), (0, 0))
    state = jnp.pad(density[None], ((0, 4),) + rest) + jnp.pad(density * velocity, ((1, 1),) + rest)
    state = state + jnp.pad(energy[None], ((4, 0),) + rest)
    x_rows = 5 * 2 * HALO * 8
    flow_a, flow_b, along_x = call(
        pack_start_body, [(tiles * 8, 128), (tiles * 8, 128), (x_rows, 128)], state
    )
    edge_a = lax.ppermute(flow_a, "fz", partners((size_z,), 0, False))
    edge_b = lax.ppermute(flow_b, "fz", partners((size_z,), 0, True))
    x_steps = (1,) if size_x == 2 else (1, -1)
    beside_x = [lax.ppermute(along_x, "fx", shifted((size_x,), (step,))) for step in x_steps]

    local = (neighbours - device * elements).T

    near_pairs = [(i ^ 1, i) for i in range(devices)]
    far_pairs = [pair for i in range(1, devices - 1, 2) for pair in ((i, i + 1), (i + 1, i))]

    def traces(to_a, to_b):
        far_got = lax.ppermute(to_b, names, far_pairs)
        return lax.ppermute(to_a, names, near_pairs), far_got

    size = 8 * elements
    held = (4, 64, size)
    faces = (96, size)
    sides = [pltpu.VMEM(faces, F32)] * 2
    turning = [pltpu.VMEM((512, 128), F32), pltpu.VMEM((4, 4 * elements, 128), F32)]
    sound, to_a, to_b = call(
        acoustic_start_body,
        [held, faces, (faces[0] + 8, size)],
        acoustic,
        jnp.pad(local.astype(F32), ((0, 2), (0, size - elements))),
        edge_a,
        scratch=turning,
        last=1,
    )
    got_a, got_b = traces(to_a, to_b)

    edge = call(
        pack_next_body,
        [(40, 128)],
        state,
        flow_a,
        flow_b,
        edge_a,
        edge_b,
        to_a,
        last=1,
    )[0]
    edges_x = [lax.ppermute(edge, "fx", shifted((size_x,), (step,))) for step in x_steps]
    y_shape = (5 * cells_x * HALO + 48, 128)
    y_a, y_b = call(pack_last_body, [y_shape, (y_shape[0] + 8, 128)], state, edge, *beside_x, *edges_x, got_a, last=1, cost=1)
    y_second = lax.ppermute(y_b, "fy", partners((size_y,), 0, True))
    y_first = lax.ppermute(y_a, "fy", partners((size_y,), 0, False))

    blocks = block_owner.size
    width = max(elements, blocks)

    def piece(values, first):
        values = values.astype(F32)
        return jnp.pad(values, ((first, 32 - first - values.shape[0]), (0, width - values.shape[1])))

    packed = (
        piece(derivative, 0)
        + piece(mode_basis, 8)
        + piece(local, 16)
        + piece(sound_speed.reshape(1, elements), 24)
        + piece(block_owner.reshape(1, blocks), 25)
        + piece(block_element.reshape(1, blocks), 26)
    )
    table = jax.ShapeDtypeStruct((5, size, size), BF16)
    near, far, deriv_rows, deriv_lanes, pair, spread, labels, speed = call(
        tables_body,
        [
            table,
            table,
            (128, 64),
            (size, size),
            (64, 64),
            (8 * blocks, size_y * 128),
            (size_y, 8, 128),
            (1, size),
        ],
        packed,
        cost=1,
    )

    fold = fold_of(size_y, blocks)
    wide = cells_x + 2 * HALO
    rows_scratch = pltpu.VMEM((3, 64, 128), F32)

    def planes(count):
        return (5, count, 16, 128)

    def route(send):
        return lax.all_to_all(send, "fy", split_axis=0, concat_axis=0, tiled=True)

    def local_part(mix, now):
        return call(
            functools.partial(acoustic_local_body, mix),
            [held],
            now,
            sound,
            deriv_rows,
            deriv_lanes,
            speed,
            near,
            scratch=sides,
            cost=1,
        )[0]

    partial = local_part(MIXES[0], sound)
    y_scratch = [pltpu.VMEM(y_shape, F32), pltpu.VMEM(y_shape, F32)]
    send = call(
        functools.partial(flow_sources_body, len(beside_x)),
        [(size_y, 192 // fold + 8, 128)],
        state,
        edge,
        *beside_x,
        y_second,
        y_first,
        pair,
        spread,
        labels,
        got_b,
        last=1,
        scratch=[
            pltpu.VMEM((4, cells_x + 2, 16, 128), F32),
            pltpu.VMEM((3, cells_x + 2, 16, 128), F32),
            rows_scratch,
            pltpu.VMEM((2, cells_x, 8, 128), F32),
        ]
        + y_scratch,
    )[0]
    received = route(send)
    second, derived, ends, send = call(
        functools.partial(flow_stages_body, len(edges_x)),
        [
            planes(wide - 4),
            planes(wide),
            (5, cells_x, 8, 128),
            (size_y, 2 * 192 // fold, 128),
        ],
        state,
        edge,
        *beside_x,
        *edges_x,
        y_second,
        y_first,
        pair,
        spread,
        partial,
        last=1,
        scratch=[
            rows_scratch,
            pltpu.VMEM(planes(wide - 2), F32),
            pltpu.VMEM(planes(wide - 2), F32),
            pltpu.VMEM(planes(wide), F32),
            pltpu.VMEM((5, 16, 256), F32),
        ]
        + y_scratch,
    )

    far_partner = call(functools.partial(partner_tables_body, elements), [table], got_b)[0]
    longer = (faces[0] + 32, size)
    near_face = pltpu.VMEM(faces, F32)
    sound_one, to_a, to_b = call(
        acoustic_first_body,
        [held, faces, longer],
        partial,
        got_a,
        got_b,
        far,
        received,
        send,
        scratch=sides + [rows_scratch],
        last=1,
    )
    labelled, received = received, route(send)
    got_a, got_b = traces(to_a, to_b)
    flow_state = call(flow_last_body, [(5, cells_x, 8, 128)], second, derived, ends, state)[0]
    partial = local_part(MIXES[1], sound_one)
    change = call(
        mirror_body, [faces], to_b, far_partner, scratch=sides + [near_face, pltpu.VMEM(held, F32)], cost=1
    )[0]
    partial, to_b = call(
        acoustic_near_body,
        [held, longer],
        partial,
        got_a,
        far,
        received,
        labelled,
        change,
        flow_state,
        last=2,
        scratch=sides + [rows_scratch, near_face],
    )
    got_b_last = lax.ppermute(to_b, names, far_pairs)
    sound_two, to_a = call(
        acoustic_rest_body, [held, faces], partial, got_b, far, scratch=sides + [near_face]
    )
    got_a = lax.ppermute(to_a, names, near_pairs)
    source_three = call(place_last_body, [(3, 64, 128)], received, labelled)[0]
    partial = local_part(MIXES[2], sound_two)
    sound_state = call(
        acoustic_last_body,
        [(elements, 4, 512)],
        partial,
        got_a,
        got_b_last,
        change,
        far,
        source_three,
        scratch=sides + [pltpu.VMEM(held, F32)] + turning,
    )[0]
    return (flow_state, sound_state)


def solution(mesh):
    placed = (
        P("fx", "fy", "fz"),
        P(None, "fx", "fy", "fz"),
        P("fx", "fy", "fz"),
        P(("fx", "fy", "fz"), None, None),
        P(("fx", "fy", "fz")),
        P(),
        P(),
        P(("fx", "fy", "fz"), None),
        P("fx", "fy", "fz", None, None),
        P("fx", "fy", "fz", None),
    )
    return jax.shard_map(
        per_device,
        mesh=mesh,
        in_specs=placed,
        out_specs=(P(None, "fx", "fy", "fz"), P(("fx", "fy", "fz"), None, None)),
        check_vma=False,
    )
```

```python
import functools

import jax
import jax.numpy as jnp
import numpy as np
from jax import lax
from jax.experimental import pallas as pl
from jax.experimental.pallas import tpu as pltpu
from jax.sharding import PartitionSpec as P

HEAT_RATIO = 1.4
TIME_STEP = 0.1
VISCOSITY = 0.05
PENALTY = 0.5
HALO = 3
F32 = jnp.float32
BF16 = jnp.bfloat16
PARAMS = pltpu.CompilerParams(vmem_limit_bytes=24 * 1024 * 1024)
MIXES = ((0.0, 1.0), (0.75, 0.25), (1.0 / 3.0, 2.0 / 3.0))


def parts(values):
    high = values.astype(BF16)
    return high, (values - high.astype(F32)).astype(BF16)


def dot(left, right):
    return lax.dot_general(left, right, (((1,), (0,)), ((), ())), preferred_element_type=F32)


def dot_three(left, right):
    left_high, left_low = parts(left)
    right_high, right_low = parts(right)
    return dot(left_high, right_high) + dot(left_high, right_low) + dot(left_low, right_high)


def dot_full(left, right, dims=((1,), (0,))):
    return lax.dot_general(
        left, right, (dims, ((), ())), precision=lax.Precision.HIGHEST, preferred_element_type=F32
    )


def dot_exact_right(left, right):
    left_high, left_low = parts(left)
    return dot(left_high, right) + dot(left_low, right)


def call(body, outs, *operands, scratch=(), last=0, cost=None):
    whole = pl.BlockSpec(memory_space=pltpu.VMEM)
    outs = [out if isinstance(out, jax.ShapeDtypeStruct) else jax.ShapeDtypeStruct(out, F32) for out in outs]
    anywhere = pl.BlockSpec(memory_space=pl.ANY)
    return pl.pallas_call(
        body,
        out_shape=outs,
        in_specs=[whole] * (len(operands) - last) + [anywhere] * last,
        out_specs=[whole] * len(outs),
        scratch_shapes=list(scratch),
        compiler_params=PARAMS,
        cost_estimate=None if cost is None else pl.CostEstimate(flops=cost, bytes_accessed=cost, transcendentals=0),
    )(*operands)


def capacity_of(peers, blocks):
    return max(2, 2 * blocks // peers)


def fold_of(peers, blocks):
    return 128 // (8 * capacity_of(peers, blocks))


def is_odd(axis):
    return lax.axis_index(axis) % 2 == 1


def paired(odd, to_next, to_last):
    return jnp.where(odd, to_last, to_next), jnp.where(odd, to_next, to_last)


def pack_start_body(state, message_a, message_b, along_x):
    odd = is_odd("fz")
    rows = state[...].reshape(-1, 128)
    count = rows.shape[0]
    for tile in range(message_a.shape[0] // 8):
        piece = rows[tile * 128 : min(count, tile * 128 + 128)]
        if piece.shape[0] < 128:
            piece = jnp.concatenate([piece, jnp.zeros((128 - piece.shape[0], 128), F32)], 0)
        turned = piece.T
        first, second = paired(odd, turned[120:128], turned[0:8])
        message_a[tile * 8 : tile * 8 + 8] = first
        message_b[tile * 8 : tile * 8 + 8] = second
    cells_x = state.shape[1]
    for f in range(5):
        for s, x in enumerate(x_planes(cells_x)):
            at = (f * 2 * HALO + s) * 8
            along_x[at : at + 8] = state[f, x]


def pack_next_body(state, sent_a, sent_b, got_a, got_b, _, edge):
    cells_x = state.shape[1]
    odd_z = is_odd("fz")
    high, low = paired(odd_z, sent_a[...], sent_b[...])
    above, below = paired(odd_z, got_a[...], got_b[...])
    row = lax.broadcasted_iota(jnp.int32, (8, 128), 0)
    x_of_lane = lax.broadcasted_iota(jnp.int32, (16, 128), 1) // 8 % cells_x
    for tile in range(high.shape[0] // 8):
        rows = slice(tile * 8, tile * 8 + 8)
        upper = jnp.where(row < 3, pltpu.roll(high[rows], 3, 0), pltpu.roll(above[rows], 3, 0))
        lower = jnp.where(row < 3, pltpu.roll(below[rows], 3, 0), pltpu.roll(low[rows], 3, 0))
        slots = jnp.concatenate([upper, lower], 0)
        spread = jnp.concatenate([jnp.where(x_of_lane == x, slots, 0.0) for x in range(8)], 0).T
        for half in range(16 // cells_x):
            f = tile * (16 // cells_x) + half
            if f < 5:
                at = half * cells_x * 8
                total = spread[at : at + 8]
                for x in range(1, cells_x):
                    total = total + spread[at + x * 8 : at + x * 8 + 8]
                edge[f * 8 : f * 8 + 8] = total


def x_planes(cells_x):
    return [cells_x - HALO + i for i in range(HALO)] + list(range(HALO))


def sides_of(beside_x):
    return beside_x[0], beside_x[-1]


def beyond(edges_x, f):
    after, before = sides_of(edges_x)
    at = f * 8
    if after is before:
        return after[at : at + 8]
    lane = lax.broadcasted_iota(jnp.int32, (8, 128), 1)
    return jnp.where(lane < 64, after[at : at + 8], before[at : at + 8])


def pack_last_body(state, edge, *refs):
    (y_a, y_b), refs = refs[-2:], refs[:-3]
    beside_x, edges_x = refs[: len(refs) // 2], refs[len(refs) // 2 :]
    cells_x = state.shape[1]
    odd = is_odd("fy")
    after, before = sides_of(beside_x)

    def put(at, values, height):
        first, second = paired(odd, values[8 - height : 8], values[0:height])
        y_a[at : at + height] = first
        y_b[at : at + height] = second

    lines = 5 * cells_x * HALO
    for f in range(5):
        for x in range(cells_x):
            put((f * cells_x + x) * HALO, state[f, x], HALO)
        at = lines + f * 6
        for slot, height in ((1, 1), (2, 2), (3, 2), (4, 1)):
            source = (f * 2 * HALO + slot) * 8
            put(at, (before if slot < HALO else after)[source : source + 8], height)
            at += height
        put(lines + 30 + f * 2, edge[f * 8 : f * 8 + 8], 2)
        put(lines + 40 + f, beyond(edges_x, f), 1)


def assemble_speeds(wide, state, beside_x, above, below):
    cells_x = state.shape[1]
    after, before = sides_of(beside_x)
    for f in range(4):
        for x in range(cells_x):
            wide[f, 1 + x, 0:8] = state[f, x]
            at = (f * cells_x + x) * HALO
            wide[f, 1 + x, 8:9] = above[at : at + 1]
            wide[f, 1 + x, 15:16] = below[at + HALO - 1 : at + HALO]
        for slot, plane, source in ((HALO - 1, 0, before), (HALO, cells_x + 1, after)):
            at = (f * 2 * HALO + slot) * 8
            wide[f, plane, 0:8] = source[at : at + 8]


def assemble(wide, rim, state, edge, beside_x, edges_x, above, below):
    cells_x = state.shape[1]
    after, before = sides_of(beside_x)
    lines = 5 * cells_x * HALO
    for f in range(5):
        for x in range(cells_x):
            wide[f, HALO + x, 0:8] = state[f, x]
            at = (f * cells_x + x) * HALO
            wide[f, HALO + x, 8 : 8 + HALO] = above[at : at + HALO]
            wide[f, HALO + x, 16 - HALO : 16] = below[at : at + HALO]
        for slot in range(2 * HALO):
            plane = slot if slot < HALO else cells_x + slot
            at = (f * 2 * HALO + slot) * 8
            wide[f, plane, 0:8] = (before if slot < HALO else after)[at : at + 8]
        at = lines + f * 6
        for slot, height in ((1, 1), (2, 2), (3, 2), (4, 1)):
            plane = slot if slot < HALO else cells_x + slot
            wide[f, plane, 8 : 8 + height] = above[at : at + height]
            wide[f, plane, 16 - height : 16] = below[at : at + height]
            at += height
        rim[f, 0:8, 0:128] = edge[f * 8 : f * 8 + 8]
        rim[f, 0:8, 128:256] = beyond(edges_x, f)
        at = lines + 30 + f * 2
        rim[f, 8:10, 0:128] = above[at : at + 2]
        rim[f, 14:16, 0:128] = below[at : at + 2]
        at = lines + 40 + f
        rim[f, 8:9, 128:256] = above[at : at + 1]
        rim[f, 15:16, 128:256] = below[at : at + 1]


def primitive(rho, mx, my, mz, energy):
    inverse = 1.0 / rho
    u, v, w = mx * inverse, my * inverse, mz * inverse
    p = (HEAT_RATIO - 1.0) * (energy - 0.5 * (mx * u + my * v + mz * w))
    return u, v, w, p, jnp.sqrt(HEAT_RATIO * jnp.abs(p) * inverse)


def chunks(first, last, size):
    return [(i, min(i + size, last)) for i in range(first, last, size)]


def derive_planes(wide, derived, first, last):
    for i, j in chunks(first, last, 4):
        for k, value in enumerate(primitive(*[wide[f, i:j] for f in range(5)])):
            derived[k, i:j] = value


def derive_speeds(wide, derived, first, last):
    for i, j in chunks(first, last, 5):
        inverse = 1.0 / wide[0, i:j]
        for k in range(3):
            derived[k, i:j] = wide[1 + k, i:j] * inverse


def with_flux(fields, other, along):
    speed, p = other[along], other[3]
    out = [fields[1 + along]]
    for k in range(3):
        value = fields[1 + k] * speed
        out.append(value + p if k == along else value)
    out.append((fields[4] + p) * speed)
    return fields, out, jnp.abs(speed) + other[4]


def face(left, right):
    (fields_l, flux_l, speed_l), (fields_r, flux_r, speed_r) = left, right
    speed = jnp.maximum(speed_l, speed_r)
    viscous = speed + 2.0 * VISCOSITY
    return [
        (flux_l[f] + flux_r[f]) - (viscous if 1 <= f <= 3 else speed) * (fields_r[f] - fields_l[f])
        for f in range(5)
    ]


def rolled(here, shift, axis):
    fields, flux, speed = here
    return (
        [pltpu.roll(a, shift, axis) for a in fields],
        [pltpu.roll(a, shift, axis) for a in flux],
        pltpu.roll(speed, shift, axis),
    )


def rim_section(fields, start, mix):
    other = primitive(*fields)
    here = with_flux(fields, other, 2)
    along_z = face(here, rolled(here, 255, 1))
    if mix is None:
        return other, along_z, None
    total = [g - pltpu.roll(g, 1, 1) for g in along_z]
    for along, step, axis, size in ((0, 16, 1, 256), (1, 1, 0, 16)):
        here = with_flux(fields, other, along)
        faces = face(here, rolled(here, size - step, axis))
        total = [total[f] + (faces[f] - pltpu.roll(faces[f], step, axis)) for f in range(5)]
    out = []
    for f in range(5):
        value = fields[f] - (0.5 * TIME_STEP) * total[f]
        out.append(mix[0] * start[f] + mix[1] * value if mix[0] != 0.0 else value)
    return other, along_z, out


def to_ends(values, after, rows, first, last, ends):
    slot = lax.broadcasted_iota(jnp.int32, (rows, 256), 1) % 16
    for f, value in enumerate(values):
        value = value[0:rows]
        value = jnp.where(slot == 9, pltpu.roll(value, 9 - after, 1), value)
        for x in range(first, last):
            at = x % 16 // 8 * 128
            move = (118 - x % 8 * 16) % 128
            tile = value[:, at : at + 128]
            ends[f, x - first, 0:rows] = pltpu.roll(tile, move, 1) if move else tile


def flow_rate_section(wide, derived, ends, start, offset, mix, write, inner=False):
    depth = wide.shape[1]
    rows = slice(0, 8) if inner else slice(None)
    size = 4 if inner else 2

    def planes(i, j, kept, along):
        fields = [wide[f, i:j, kept] for f in range(5)]
        return with_flux(fields, [derived[f, i:j, kept] for f in range(5)], along)

    def cut(here, i, j):
        return [a[i:j] for a in here[0]], [a[i:j] for a in here[1]], here[2][i:j]

    for i, j in chunks(1, depth - 1, size):
        count = j - i
        lane = lax.broadcasted_iota(jnp.int32, (count, 8 if inner else 16, 128), 2)
        here = planes(i - 1, j + 1, rows, 0)
        faces = face(cut(here, 0, count + 1), cut(here, 1, count + 2))
        total = [g[1:] - g[:-1] for g in faces]
        here = planes(i, j, slice(None), 1)
        faces = face(here, rolled(here, 15, 1))
        for f in range(5):
            change = faces[f] - pltpu.roll(faces[f], 1, 1)
            total[f] = total[f] + (change[:, 0:8] if inner else change)
        here = planes(i, j, rows, 2)
        faces = face(here, rolled(here, 127, 2))
        for f in range(5):
            end = ends[f, i - 1 : j - 1, rows]
            value = jnp.where(lane == 127, end, faces[f])
            total[f] = total[f] + (value - jnp.where(lane == 0, end, pltpu.roll(value, 1, 2)))
        for f in range(5):
            value = wide[f, i:j, rows] - (0.5 * TIME_STEP) * total[f]
            if mix[0] != 0.0:
                value = mix[0] * start[f, i + offset : j + offset, rows] + mix[1] * value
            write(slice(i - 1, j - 1), f, value)


def lamb(derived, ends, first, cells_x, lamb_rows):
    for i, j in chunks(first, first + cells_x, 4):
        count = j - i
        lane = lax.broadcasted_iota(jnp.int32, (count, 8, 128), 2)
        vel = [derived[c, i:j, 0:8] for c in range(3)]
        along_x = [derived[c, i + 1 : j + 1, 0:8] - derived[c, i - 1 : j - 1, 0:8] for c in range(3)]
        along_y = []
        for c in range(3):
            column = derived[c, i:j]
            along_y.append((pltpu.roll(column, 15, 1) - pltpu.roll(column, 1, 1))[:, 0:8])
        along_z = []
        for c in range(2):
            end = ends[c, i - first : j - first, 0:8]
            after = jnp.where(lane == 127, end, pltpu.roll(vel[c], 127, 2))
            along_z.append(after - jnp.where(lane == 0, end, pltpu.roll(vel[c], 1, 2)))
        curl = [
            0.5 * (along_y[2] - along_z[1]),
            0.5 * (along_z[0] - along_x[2]),
            0.5 * (along_x[1] - along_y[0]),
        ]
        at = slice((i - first) * 8, (j - first) * 8)
        lamb_rows[0, at] = (curl[1] * vel[2] - curl[2] * vel[1]).reshape(count * 8, 128)
        lamb_rows[1, at] = (curl[2] * vel[0] - curl[0] * vel[2]).reshape(count * 8, 128)
        lamb_rows[2, at] = (curl[0] * vel[1] - curl[1] * vel[0]).reshape(count * 8, 128)


def project(lamb_rows, pair, spread, send, base):
    peers = send.shape[0]
    fold = fold_of(peers, spread.shape[0] // 8)
    height = 64 // fold
    group = lax.broadcasted_iota(jnp.int32, (height, 128), 1) // (128 // fold)
    modes = dot_three(pair[...], jnp.concatenate([lamb_rows[c] for c in range(3)], 1))
    modes = jnp.concatenate([modes[:, c * 128 : c * 128 + 128] for c in range(3)], 0)
    sent = dot_three(modes, spread[...])
    for c in range(3):
        for peer in range(peers):
            mine = sent[c * 64 : c * 64 + 64, peer * 128 : peer * 128 + 128]
            folded = mine[0:height]
            for g in range(1, fold):
                folded = jnp.where(group == g, mine[g * height : g * height + height], folded)
            send[peer, base + c * height : base + c * height + height] = folded


def flow_sources_body(count, state, edge, *refs):
    beside_x, refs = refs[:count], refs[count:]
    got_b, got_a, pair, spread, labels, _, send, wide, derived, lamb_rows, ends, above, below = refs
    cells_x = state.shape[1]
    above[...], below[...] = paired(is_odd("fy"), got_a[...], got_b[0 : got_a.shape[0]])
    assemble_speeds(wide, state, beside_x, above, below)
    derive_speeds(wide, derived, 0, cells_x + 2)
    inverse = 1.0 / edge[0:8]
    speeds = [jnp.concatenate([edge[k * 8 : k * 8 + 8] * inverse] * 2, 1) for k in (1, 2)]
    to_ends(speeds, 3, 8, 0, cells_x, ends)
    lamb(derived, ends, 1, cells_x, lamb_rows)
    project(lamb_rows, pair, spread, send, 0)
    send[:, send.shape[1] - 8 :] = labels[...]


def writer(target):
    def write(i, f, value):
        target[f, i] = value

    return write


def flow_stages_body(count, state, edge, *refs):
    beside_x, edges_x, refs = refs[:count], refs[count : 2 * count], refs[2 * count :]
    got_b, got_a, pair, spread, _, second, derived, ends_out, send, *refs = refs
    lamb_rows, ends, first, wide, rim, above, below = refs
    above[...], below[...] = paired(is_odd("fy"), got_a[...], got_b[0 : got_a.shape[0]])
    assemble(wide, rim, state, edge, beside_x, edges_x, above, below)
    planes = wide.shape[1]
    cells_x = planes - 2 * HALO
    size = send.shape[1] // 2
    rim_start = [rim[f] for f in range(5)]
    derive_planes(wide, derived, 0, planes)
    _, along_z, rim_first = rim_section(rim_start, None, MIXES[0])
    to_ends(along_z, 2, 16, -2, cells_x + 2, ends)
    flow_rate_section(wide, derived, ends, wide, 0, MIXES[0], writer(first))
    derive_planes(first, derived, 0, planes - 2)
    other, along_z, rim_second = rim_section(rim_first, [rim[f] for f in range(5)], MIXES[1])
    to_ends(other[0:2], 3, 8, 0, cells_x, ends)
    lamb(derived, ends, 2, cells_x, lamb_rows)
    project(lamb_rows, pair, spread, send, 0)
    to_ends(along_z, 2, 16, -1, cells_x + 1, ends)
    flow_rate_section(first, derived, ends, wide, 1, MIXES[1], writer(second))
    derive_planes(second, derived, 0, planes - 4)
    other, along_z, _ = rim_section(rim_second, None, None)
    to_ends(other[0:2], 3, 8, 0, cells_x, ends)
    lamb(derived, ends, 1, cells_x, lamb_rows)
    project(lamb_rows, pair, spread, send, size)
    to_ends(along_z, 2, 8, 0, cells_x, ends_out)


def flow_last_body(second, derived, ends, state, out, done):
    done[...] = jnp.zeros(done.shape, F32)
    flow_rate_section(second, derived, ends, state, -1, MIXES[2], writer(out), inner=True)


def faces_out(state, rear, front):
    lane = lax.broadcasted_iota(jnp.int32, (32, 128), 1) // 16
    for c in range(4):
        front[c * 8 : c * 8 + 8] = state[c, 56:64]
        rear[c * 8 : c * 8 + 8] = state[c, 0:8]
        front[32 + c * 8 : 40 + c * 8] = state[c, pl.ds(7, 8, stride=8), :]
        rear[32 + c * 8 : 40 + c * 8] = state[c, pl.ds(0, 8, stride=8), :]
    rows = state[...].reshape(256, 128)
    last = jnp.zeros((32, 128), F32)
    first = jnp.zeros((32, 128), F32)
    for j in range(8):
        piece = rows[j * 32 : j * 32 + 32]
        last = jnp.where(lane == j, pltpu.roll(piece, (j * 16 + 16) % 128, 1), last)
        first = jnp.where(lane == j, pltpu.roll(piece, j * 16, 1) if j else piece, first)
    front[64:96] = last
    rear[64:96] = first


def faces_sent(odd, state, message_a, message_b):
    size = message_a.shape[0]
    faces_out(state, message_b, message_a)
    message_a[...], message_b[0:size] = paired(odd, message_a[...], message_b[0:size])
    if message_b.shape[0] > size:
        message_b[size:] = jnp.zeros((message_b.shape[0] - size, 128), F32)


def lift(total, before, after, sides, factor):
    def place(face, rows, target):
        value = factor * dot_exact_right(rows, sides[face])
        for c in range(4):
            total[c, target, :] += value[c * 8 : c * 8 + 8]

    place(0, before[0:32], pl.ds(0, 8))
    place(1, after[0:32], pl.ds(56, 8))
    place(2, before[32:64], pl.ds(0, 8, stride=8))
    place(3, after[32:64], pl.ds(7, 8, stride=8))


def rate_local(state, deriv_rows, deriv_lanes, speed, sides):
    fields = [state[c] for c in range(4)]
    by_rows = dot_three(deriv_rows[...], jnp.concatenate(fields[0:3], 1))
    by_lanes = dot_three(jnp.concatenate([fields[0], fields[3]], 0), deriv_lanes[...])
    divergence = by_rows[0:64, 128:256] + by_rows[64:128, 256:384] + by_lanes[64:128]
    rates = [
        -(speed[...] * speed[...]) * divergence,
        -by_rows[0:64, 0:128],
        -by_rows[64:128, 0:128],
        -by_lanes[0:64],
    ]
    row = lax.broadcasted_iota(jnp.int32, (64, 128), 0)
    lane = lax.broadcasted_iota(jnp.int32, (64, 128), 1)
    count = jnp.zeros((64, 128), F32)
    for value in (row // 8, row % 8, lane // 16):
        count = count + jnp.where((value == 0) | (value == 7), PENALTY, 0.0)
    side = PENALTY * dot_exact_right(state[...].reshape(256, 128), sides[4])
    return [rates[c] - count * fields[c] + side[c * 64 : c * 64 + 64] for c in range(4)]


def acoustic_local_body(mix, state, start, deriv_rows, deriv_lanes, speed, sides, out, front, rear):
    rates = rate_local(state, deriv_rows, deriv_lanes, speed, sides)
    for c in range(4):
        value = state[c] + TIME_STEP * rates[c]
        if mix[0] != 0.0:
            value = mix[0] * start[c] + mix[1] * value
        out[c] = value
    faces_out(state, rear, front)
    lift(out, front, rear, sides, TIME_STEP * mix[1] * PENALTY)


def acoustic_start_body(given, local, _, state, message_a, message_b, turned, stored):
    count = given.shape[0]
    for e in range(count):
        for t in range(4):
            stored[t, 4 * e : 4 * e + 4] = given[e, :, t * 128 : t * 128 + 128]
    for t in range(4):
        rows = [stored[t, pl.ds(c, count, stride=4), :] for c in range(4)]
        rows = jnp.concatenate(rows + [jnp.zeros((128 - 4 * count, 128), F32)], 0)
        turned[t * 128 : t * 128 + 128] = rows.T
    lane = lax.broadcasted_iota(jnp.int32, (64, 128), 1) // count
    fields = [jnp.zeros((64, 128), F32)] * 4
    for z in range(8):
        piece = turned[pl.ds(z, 64, stride=8), :]
        for c in range(4):
            move = (z - c) * count % 128
            fields[c] = jnp.where(lane == z, pltpu.roll(piece, move, 1) if move else piece, fields[c])
    for c in range(4):
        state[c] = fields[c]
    faces_sent(is_odd("fz"), state, message_a, message_b)
    message_b[96:104] = local[...]


def natural_order(state, out, turned, stored):
    count = out.shape[0]
    lane = lax.broadcasted_iota(jnp.int32, (64, 128), 1) // count
    for z in range(8):
        value = jnp.zeros((64, 128), F32)
        for c in range(4):
            move = (c - z) * count % 128
            value = jnp.where(lane == c, pltpu.roll(state[c], move, 1) if move else state[c], value)
        turned[pl.ds(z, 64, stride=8), :] = value
    for t in range(4):
        rows = turned[t * 128 : t * 128 + 128].T
        for c in range(4):
            stored[t, pl.ds(c, count, stride=4), :] = rows[c * count : c * count + count]
    for e in range(count):
        for t in range(4):
            out[e, :, t * 128 : t * 128 + 128] = stored[t, 4 * e : 4 * e + 4]


def remote_part(out, before, after, sides_far, factor):
    lift(out, before, after, sides_far, factor)
    lane = lax.broadcasted_iota(jnp.int32, (32, 128), 1) // 16
    last, first = before[64:96], after[64:96]
    pieces = []
    for j in range(8):
        left = pltpu.roll(last, 128 - j * 16, 1) if j else last
        right = pltpu.roll(first, (144 - j * 16) % 128, 1) if j != 1 else first
        pieces.append(jnp.where(lane == 0, left, jnp.where(lane == 1, right, 0.0)))
    value = factor * dot_exact_right(jnp.concatenate(pieces, 0), sides_far[4])
    for c in range(4):
        out[c] += value[c * 64 : c * 64 + 64]


def arrived(odd, got_a, got_b, before, after):
    none = jnp.zeros((96, 128), F32)
    near = none if got_a is None else got_a[0:96]
    after[...], before[...] = paired(odd, near, none if got_b is None else got_b[0:96])


def acoustic_first_body(partial, got_a, got_b, sides_far, received, _, out, message_a, message_b, before, after, source):
    odd = is_odd("fz")
    place(received, received, source, 0)
    arrived(odd, got_a, got_b, before, after)
    out[0] = partial[0]
    for c in range(3):
        out[1 + c] = partial[1 + c] + (TIME_STEP * MIXES[0][1]) * source[c]
    remote_part(out, before, after, sides_far, TIME_STEP * MIXES[0][1] * PENALTY)
    faces_sent(odd, out, message_a, message_b)


def acoustic_near_body(
    partial, got_a, sides_far, received, labelled, _, __, out, message_b, before, after, source, spare
):
    odd = is_odd("fz")
    place(received, labelled, source, 0)
    arrived(odd, got_a, None, before, after)
    out[0] = partial[0]
    for c in range(3):
        out[1 + c] = partial[1 + c] + (TIME_STEP * MIXES[1][1]) * source[c]
    remote_part(out, before, after, sides_far, TIME_STEP * MIXES[1][1] * PENALTY)
    faces_sent(odd, out, spare, message_b)


def acoustic_rest_body(partial, got_b, sides_far, out, message_a, before, after, spare):
    odd = is_odd("fz")
    arrived(odd, None, got_b, before, after)
    out[...] = partial[...]
    remote_part(out, before, after, sides_far, TIME_STEP * MIXES[1][1] * PENALTY)
    faces_sent(odd, out, message_a, spare)


def mirror_body(sent_b, sides_partner, change, before, after, spare, state):
    odd = jnp.logical_not(is_odd("fz"))
    arrived(odd, None, sent_b, before, after)
    state[...] = jnp.zeros(state.shape, F32)
    remote_part(state, before, after, sides_partner, TIME_STEP * MIXES[1][1] * PENALTY)
    faces_sent(odd, state, spare, change)


def acoustic_last_body(
    partial, got_a, got_b, change, sides_far, source, given_out, before, after, out, turned, stored
):
    odd = is_odd("fz")
    after[...], before[...] = paired(odd, got_a[0:96], got_b[0:96] + change[...])
    out[0] = partial[0]
    for c in range(3):
        out[1 + c] = partial[1 + c] + (TIME_STEP * MIXES[2][1]) * source[c]
    remote_part(out, before, after, sides_far, TIME_STEP * MIXES[2][1] * PENALTY)
    natural_order(out, given_out, turned, stored)


def place(received, labelled, out, base):
    peers, size = labelled.shape[0], labelled.shape[1]
    fold = 192 // (size - 8)
    height = 64 // fold
    target = lax.broadcasted_iota(jnp.int32, (128, 128), 0)
    lane = lax.broadcasted_iota(jnp.int32, (128, 128), 1)
    total = None
    for peer in range(peers):
        label = labelled[peer, size - 8 : size - 7, :]
        label = jnp.broadcast_to(label, (128, 128)).astype(jnp.int32)
        hit = (label == target % 16) & (lane % 8 == target // 16)
        chosen = [jnp.where(hit & (lane // (128 // fold) == g), 1.0, 0.0) for g in range(fold)]
        chosen = jnp.concatenate(chosen, 0).astype(BF16)
        high, low = parts(received[peer, base : base + 3 * height])
        dims = (((1,), (1,)), ((), ()))
        value = lax.dot_general(high, chosen, dims, preferred_element_type=F32)
        value = value + lax.dot_general(low, chosen, dims, preferred_element_type=F32)
        total = value if total is None else total + value
    for c in range(3):
        for g in range(fold):
            at = c * height
            out[c, g * height : g * height + height] = total[at : at + height, g * 128 : g * 128 + 128]


def place_last_body(received, labelled, out):
    place(received, labelled, out, received.shape[1] // 2)


def kron_part(matrix, shape, rows_by, columns_by):
    row = lax.broadcasted_iota(jnp.int32, (shape[0], 8), 0)
    level = lax.broadcasted_iota(jnp.int32, (shape[0], 8), 1)
    left = (row // rows_by % 8 == level).astype(F32)
    level = lax.broadcasted_iota(jnp.int32, (8, shape[1]), 0)
    column = lax.broadcasted_iota(jnp.int32, (8, shape[1]), 1)
    right = (column // columns_by % 8 == level).astype(F32)
    return dot_full(dot_full(left, matrix), right)


def far_tables(wanted, count, far):
    size = 8 * count
    row = lax.broadcasted_iota(jnp.int32, (size, size), 0)
    level_out = lax.broadcasted_iota(jnp.int32, (size, size), 1) // count
    level, element = row // count, row % count
    for facet in range(4):
        shift = -count if facet % 2 == 0 else count
        choice = jnp.broadcast_to(wanted[facet : facet + 1], (size, size))
        far[facet] = jnp.where((level == level_out) & (element + shift == choice), 1.0, 0.0).astype(BF16)
    lower = jnp.broadcast_to(wanted[4:5], (size, size))
    upper = jnp.broadcast_to(wanted[5:6], (size, size))
    hit = (level == 0) & (level_out == 0) & (element - count == lower)
    hit = hit | ((level == 1) & (level_out == 7) & (element + count == upper))
    far[4] = jnp.where(hit, 1.0, 0.0).astype(BF16)


def partner_tables_body(count, got_b, far):
    row = lax.broadcasted_iota(jnp.int32, (count, 8 * count), 0)
    column = lax.broadcasted_iota(jnp.int32, (count, 8 * count), 1)
    repeat = (column % count == row).astype(F32)
    wanted = dot_full(got_b[96:104, 0:count], repeat).astype(jnp.int32)
    far_tables(wanted, count, far)


def tables_body(
    packed,
    near,
    far,
    deriv_rows,
    deriv_lanes,
    pair,
    spread,
    labels,
    speed,
):
    size = near.shape[1]
    count = size // 8
    blocks = spread.shape[0] // 8

    def place_of(shape):
        return (lax.broadcasted_iota(jnp.int32, shape, 0), lax.broadcasted_iota(jnp.int32, shape, 1))

    row, column = place_of((count, size))
    repeat = (column % count == row).astype(F32)
    speed[...] = dot_full(packed[24:25, 0:count], repeat)
    wanted = dot_full(packed[16:24, 0:count], repeat).astype(jnp.int32)
    row, column = place_of((size, size))
    level, element = row // count, row % count
    level_out = column // count
    for facet in range(4):
        choice = jnp.broadcast_to(wanted[facet : facet + 1], (size, size))
        near[facet] = jnp.where((level == level_out) & (element == choice), 1.0, 0.0).astype(BF16)
    lower = jnp.broadcast_to(wanted[4:5], (size, size))
    upper = jnp.broadcast_to(wanted[5:6], (size, size))
    hit = (level == 7) & (level_out == 0) & (element == lower)
    hit = hit | ((level == 0) & (level_out == 7) & (element == upper))
    near[4] = jnp.where(hit, 1.0, 0.0).astype(BF16)
    far_tables(wanted, count, far)

    row, column = place_of((64, 64))
    slopes, modes = packed[0:8, 0:8], packed[8:16, 0:8]
    outer = kron_part(slopes, (64, 64), 8, 8)
    inner = kron_part(slopes, (64, 64), 1, 1)
    deriv_rows[0:64] = jnp.where(row % 8 == column % 8, outer, 0.0)
    deriv_rows[64:128] = jnp.where(row // 8 == column // 8, inner, 0.0)
    row, column = place_of((size, size))
    lanes = kron_part(slopes.T, (size, size), count, count)
    deriv_lanes[...] = jnp.where(row % count == column % count, lanes, 0.0)
    pair[...] = kron_part(modes, (64, 64), 8, 8) * kron_part(modes, (64, 64), 1, 1)

    peers = labels.shape[0]
    capacity = capacity_of(peers, blocks)
    row, column = place_of((blocks, blocks))

    def upright(values):
        return jnp.sum(jnp.where(row == column, values, 0.0), 1, keepdims=True)

    owner_row = packed[25:26, 0:blocks]
    owner_column = upright(owner_row)
    earlier = (owner_column == owner_row) & (column < row)
    position = jnp.sum(jnp.where(earlier, 1.0, 0.0), 1, keepdims=True)
    slot = owner_column * capacity + position
    element_column = upright(packed[26:27, 0:blocks])
    row, column = place_of((8 * blocks, blocks))
    repeat = (row // 8 == column).astype(F32)
    slot = dot_full(repeat, jnp.broadcast_to(slot, (blocks, 128)))
    element = dot_full(repeat, jnp.broadcast_to(element_column, (blocks, 128)))
    row, column = place_of((8 * blocks, 128))
    values = kron_part(modes.T, (8 * blocks, 128), 1, 1)
    inside = column % (8 * capacity) // 8
    for peer in range(peers):
        chosen = slot == (inside + peer * capacity).astype(F32)
        spread[:, peer * 128 : peer * 128 + 128] = jnp.where(chosen, values, 0.0)
        named = jnp.where(chosen & (row % 8 == 0), element + 1.0, 0.0)
        labels[peer] = jnp.broadcast_to(jnp.sum(named, 0, keepdims=True) - 1.0, (8, 128))


def shifted(sizes, shifts):
    pairs = []
    for index in np.ndindex(*sizes):
        source = [(i + s) % n for i, s, n in zip(index, shifts, sizes)]
        pairs.append((int(np.ravel_multi_index(source, sizes)), int(np.ravel_multi_index(index, sizes))))
    return pairs


def partners(sizes, axis, second):
    pairs = []
    for index in np.ndindex(*sizes):
        source = list(index)
        step = 1 if (index[axis] % 2 == 0) != second else -1
        source[axis] = (index[axis] + step) % sizes[axis]
        pairs.append((int(np.ravel_multi_index(source, sizes)), int(np.ravel_multi_index(index, sizes))))
    return pairs


def per_device(
    density,
    velocity,
    pressure,
    acoustic,
    sound_speed,
    derivative,
    mode_basis,
    neighbours,
    block_owner,
    block_element,
):
    size_x, size_y, size_z = lax.axis_size("fx"), lax.axis_size("fy"), lax.axis_size("fz")
    devices = size_x * size_y * size_z
    cells_x = density.shape[0]
    elements = acoustic.shape[0]
    device = lax.axis_index(("fx", "fy", "fz"))

    names = ("fx", "fy", "fz")

    rows = 5 * cells_x * 8
    tiles = -(-rows // 128)
    square = velocity[0] * velocity[0] + velocity[1] * velocity[1] + velocity[2] * velocity[2]
    energy = pressure / (HEAT_RATIO - 1.0) + 0.5 * density * square
    rest = ((0, 0), (0, 0), (0, 0))
    state = jnp.pad(density[None], ((0, 4),) + rest) + jnp.pad(density * velocity, ((1, 1),) + rest)
    state = state + jnp.pad(energy[None], ((4, 0),) + rest)
    x_rows = 5 * 2 * HALO * 8
    flow_a, flow_b, along_x = call(
        pack_start_body, [(tiles * 8, 128), (tiles * 8, 128), (x_rows, 128)], state
    )
    edge_a = lax.ppermute(flow_a, "fz", partners((size_z,), 0, False))
    edge_b = lax.ppermute(flow_b, "fz", partners((size_z,), 0, True))
    x_steps = (1,) if size_x == 2 else (1, -1)
    beside_x = [lax.ppermute(along_x, "fx", shifted((size_x,), (step,))) for step in x_steps]

    local = (neighbours - device * elements).T

    near_pairs = [(i ^ 1, i) for i in range(devices)]
    far_pairs = [pair for i in range(1, devices - 1, 2) for pair in ((i, i + 1), (i + 1, i))]

    def traces(to_a, to_b):
        far_got = lax.ppermute(to_b, names, far_pairs)
        return lax.ppermute(to_a, names, near_pairs), far_got

    size = 8 * elements
    held = (4, 64, size)
    faces = (96, size)
    sides = [pltpu.VMEM(faces, F32)] * 2
    turning = [pltpu.VMEM((512, 128), F32), pltpu.VMEM((4, 4 * elements, 128), F32)]
    sound, to_a, to_b = call(
        acoustic_start_body,
        [held, faces, (faces[0] + 8, size)],
        acoustic,
        jnp.pad(local.astype(F32), ((0, 2), (0, size - elements))),
        edge_a,
        scratch=turning,
        last=1,
    )
    got_a, got_b = traces(to_a, to_b)

    edge = call(
        pack_next_body,
        [(40, 128)],
        state,
        flow_a,
        flow_b,
        edge_a,
        edge_b,
        to_a,
        last=1,
    )[0]
    edges_x = [lax.ppermute(edge, "fx", shifted((size_x,), (step,))) for step in x_steps]
    y_shape = (5 * cells_x * HALO + 48, 128)
    y_a, y_b = call(pack_last_body, [y_shape, (y_shape[0] + 8, 128)], state, edge, *beside_x, *edges_x, got_a, last=1, cost=1)
    y_second = lax.ppermute(y_b, "fy", partners((size_y,), 0, True))
    y_first = lax.ppermute(y_a, "fy", partners((size_y,), 0, False))

    blocks = block_owner.size
    width = max(elements, blocks)

    def piece(values, first):
        values = values.astype(F32)
        return jnp.pad(values, ((first, 32 - first - values.shape[0]), (0, width - values.shape[1])))

    packed = (
        piece(derivative, 0)
        + piece(mode_basis, 8)
        + piece(local, 16)
        + piece(sound_speed.reshape(1, elements), 24)
        + piece(block_owner.reshape(1, blocks), 25)
        + piece(block_element.reshape(1, blocks), 26)
    )
    table = jax.ShapeDtypeStruct((5, size, size), BF16)
    near, far, deriv_rows, deriv_lanes, pair, spread, labels, speed = call(
        tables_body,
        [
            table,
            table,
            (128, 64),
            (size, size),
            (64, 64),
            (8 * blocks, size_y * 128),
            (size_y, 8, 128),
            (1, size),
        ],
        packed,
        cost=1,
    )

    fold = fold_of(size_y, blocks)
    wide = cells_x + 2 * HALO
    rows_scratch = pltpu.VMEM((3, 64, 128), F32)

    def planes(count):
        return (5, count, 16, 128)

    def route(send):
        return lax.all_to_all(send, "fy", split_axis=0, concat_axis=0, tiled=True)

    def local_part(mix, now):
        return call(
            functools.partial(acoustic_local_body, mix),
            [held],
            now,
            sound,
            deriv_rows,
            deriv_lanes,
            speed,
            near,
            scratch=sides,
            cost=1,
        )[0]

    partial = local_part(MIXES[0], sound)
    y_scratch = [pltpu.VMEM(y_shape, F32), pltpu.VMEM(y_shape, F32)]
    send = call(
        functools.partial(flow_sources_body, len(beside_x)),
        [(size_y, 192 // fold + 8, 128)],
        state,
        edge,
        *beside_x,
        y_second,
        y_first,
        pair,
        spread,
        labels,
        got_b,
        last=1,
        scratch=[
            pltpu.VMEM((4, cells_x + 2, 16, 128), F32),
            pltpu.VMEM((3, cells_x + 2, 16, 128), F32),
            rows_scratch,
            pltpu.VMEM((2, cells_x, 8, 128), F32),
        ]
        + y_scratch,
    )[0]
    received = route(send)
    second, derived, ends, send = call(
        functools.partial(flow_stages_body, len(edges_x)),
        [
            planes(wide - 4),
            planes(wide),
            (5, cells_x, 8, 128),
            (size_y, 2 * 192 // fold, 128),
        ],
        state,
        edge,
        *beside_x,
        *edges_x,
        y_second,
        y_first,
        pair,
        spread,
        partial,
        last=1,
        scratch=[
            rows_scratch,
            pltpu.VMEM(planes(wide - 2), F32),
            pltpu.VMEM(planes(wide - 2), F32),
            pltpu.VMEM(planes(wide), F32),
            pltpu.VMEM((5, 16, 256), F32),
        ]
        + y_scratch,
    )

    far_partner = call(functools.partial(partner_tables_body, elements), [table], got_b)[0]
    longer = (faces[0] + 32, size)
    near_face = pltpu.VMEM(faces, F32)
    sound_one, to_a, to_b = call(
        acoustic_first_body,
        [held, faces, longer],
        partial,
        got_a,
        got_b,
        far,
        received,
        send,
        scratch=sides + [rows_scratch],
        last=1,
    )
    labelled, received = received, route(send)
    got_a, got_b = traces(to_a, to_b)
    flow_state, done = call(
        flow_last_body, [(5, cells_x, 8, 128), (8, 128)], second, derived, ends, state
    )
    partial = local_part(MIXES[1], sound_one)
    change = call(
        mirror_body, [faces], to_b, far_partner, scratch=sides + [near_face, pltpu.VMEM(held, F32)], cost=1
    )[0]
    partial, to_b = call(
        acoustic_near_body,
        [held, longer],
        partial,
        got_a,
        far,
        received,
        labelled,
        change,
        done,
        scratch=sides + [rows_scratch, near_face],
    )
    got_b_last = lax.ppermute(to_b, names, far_pairs)
    sound_two, to_a = call(
        acoustic_rest_body, [held, faces], partial, got_b, far, scratch=sides + [near_face]
    )
    got_a = lax.ppermute(to_a, names, near_pairs)
    source_three = call(place_last_body, [(3, 64, 128)], received, labelled)[0]
    partial = local_part(MIXES[2], sound_two)
    sound_state = call(
        acoustic_last_body,
        [(elements, 4, 512)],
        partial,
        got_a,
        got_b_last,
        change,
        far,
        source_three,
        scratch=sides + [pltpu.VMEM(held, F32)] + turning,
    )[0]
    return (flow_state, sound_state)


def solution(mesh):
    placed = (
        P("fx", "fy", "fz"),
        P(None, "fx", "fy", "fz"),
        P("fx", "fy", "fz"),
        P(("fx", "fy", "fz"), None, None),
        P(("fx", "fy", "fz")),
        P(),
        P(),
        P(("fx", "fy", "fz"), None),
        P("fx", "fy", "fz", None, None),
        P("fx", "fy", "fz", None),
    )
    return jax.shard_map(
        per_device,
        mesh=mesh,
        in_specs=placed,
        out_specs=(P(None, "fx", "fy", "fz"), P(("fx", "fy", "fz"), None, None)),
        check_vma=False,
    )
```

```python
import functools

import jax
import jax.numpy as jnp
import numpy as np
from jax import lax
from jax.experimental import pallas as pl
from jax.experimental.pallas import tpu as pltpu
from jax.sharding import PartitionSpec as P

HEAT_RATIO = 1.4
TIME_STEP = 0.1
VISCOSITY = 0.05
PENALTY = 0.5
HALO = 3
F32 = jnp.float32
BF16 = jnp.bfloat16
PARAMS = pltpu.CompilerParams(vmem_limit_bytes=24 * 1024 * 1024)
MIXES = ((0.0, 1.0), (0.75, 0.25), (1.0 / 3.0, 2.0 / 3.0))


def parts(values):
    high = values.astype(BF16)
    return high, (values - high.astype(F32)).astype(BF16)


def dot(left, right):
    return lax.dot_general(left, right, (((1,), (0,)), ((), ())), preferred_element_type=F32)


def dot_three(left, right):
    left_high, left_low = parts(left)
    right_high, right_low = parts(right)
    return dot(left_high, right_high) + dot(left_high, right_low) + dot(left_low, right_high)


def dot_full(left, right, dims=((1,), (0,))):
    return lax.dot_general(
        left, right, (dims, ((), ())), precision=lax.Precision.HIGHEST, preferred_element_type=F32
    )


def dot_exact_right(left, right):
    left_high, left_low = parts(left)
    return dot(left_high, right) + dot(left_low, right)


def call(body, outs, *operands, scratch=(), last=0, cost=None):
    whole = pl.BlockSpec(memory_space=pltpu.VMEM)
    outs = [out if isinstance(out, jax.ShapeDtypeStruct) else jax.ShapeDtypeStruct(out, F32) for out in outs]
    anywhere = pl.BlockSpec(memory_space=pl.ANY)
    return pl.pallas_call(
        body,
        out_shape=outs,
        in_specs=[whole] * (len(operands) - last) + [anywhere] * last,
        out_specs=[whole] * len(outs),
        scratch_shapes=list(scratch),
        compiler_params=PARAMS,
        cost_estimate=None if cost is None else pl.CostEstimate(flops=cost, bytes_accessed=cost, transcendentals=0),
    )(*operands)


def capacity_of(peers, blocks):
    return max(2, 2 * blocks // peers)


def fold_of(peers, blocks):
    return 128 // (8 * capacity_of(peers, blocks))


def is_odd(axis):
    return lax.axis_index(axis) % 2 == 1


def paired(odd, to_next, to_last):
    return jnp.where(odd, to_last, to_next), jnp.where(odd, to_next, to_last)


def pack_start_body(state, message_a, message_b, along_x):
    odd = is_odd("fz")
    rows = state[...].reshape(-1, 128)
    count = rows.shape[0]
    for tile in range(message_a.shape[0] // 8):
        piece = rows[tile * 128 : min(count, tile * 128 + 128)]
        if piece.shape[0] < 128:
            piece = jnp.concatenate([piece, jnp.zeros((128 - piece.shape[0], 128), F32)], 0)
        turned = piece.T
        first, second = paired(odd, turned[120:128], turned[0:8])
        message_a[tile * 8 : tile * 8 + 8] = first
        message_b[tile * 8 : tile * 8 + 8] = second
    cells_x = state.shape[1]
    for f in range(5):
        for s, x in enumerate(x_planes(cells_x)):
            at = (f * 2 * HALO + s) * 8
            along_x[at : at + 8] = state[f, x]


def pack_next_body(state, sent_a, sent_b, got_a, got_b, _, edge):
    cells_x = state.shape[1]
    odd_z = is_odd("fz")
    high, low = paired(odd_z, sent_a[...], sent_b[...])
    above, below = paired(odd_z, got_a[...], got_b[...])
    row = lax.broadcasted_iota(jnp.int32, (8, 128), 0)
    x_of_lane = lax.broadcasted_iota(jnp.int32, (16, 128), 1) // 8 % cells_x
    for tile in range(high.shape[0] // 8):
        rows = slice(tile * 8, tile * 8 + 8)
        upper = jnp.where(row < 3, pltpu.roll(high[rows], 3, 0), pltpu.roll(above[rows], 3, 0))
        lower = jnp.where(row < 3, pltpu.roll(below[rows], 3, 0), pltpu.roll(low[rows], 3, 0))
        slots = jnp.concatenate([upper, lower], 0)
        spread = jnp.concatenate([jnp.where(x_of_lane == x, slots, 0.0) for x in range(8)], 0).T
        for half in range(16 // cells_x):
            f = tile * (16 // cells_x) + half
            if f < 5:
                at = half * cells_x * 8
                total = spread[at : at + 8]
                for x in range(1, cells_x):
                    total = total + spread[at + x * 8 : at + x * 8 + 8]
                edge[f * 8 : f * 8 + 8] = total


def x_planes(cells_x):
    return [cells_x - HALO + i for i in range(HALO)] + list(range(HALO))


def sides_of(beside_x):
    return beside_x[0], beside_x[-1]


def beyond(edges_x, f):
    after, before = sides_of(edges_x)
    at = f * 8
    if after is before:
        return after[at : at + 8]
    lane = lax.broadcasted_iota(jnp.int32, (8, 128), 1)
    return jnp.where(lane < 64, after[at : at + 8], before[at : at + 8])


def pack_last_body(state, edge, *refs):
    (y_a, y_b), refs = refs[-2:], refs[:-3]
    beside_x, edges_x = refs[: len(refs) // 2], refs[len(refs) // 2 :]
    cells_x = state.shape[1]
    odd = is_odd("fy")
    after, before = sides_of(beside_x)

    def put(at, values, height):
        first, second = paired(odd, values[8 - height : 8], values[0:height])
        y_a[at : at + height] = first
        y_b[at : at + height] = second

    lines = 5 * cells_x * HALO
    for f in range(5):
        for x in range(cells_x):
            put((f * cells_x + x) * HALO, state[f, x], HALO)
        at = lines + f * 6
        for slot, height in ((1, 1), (2, 2), (3, 2), (4, 1)):
            source = (f * 2 * HALO + slot) * 8
            put(at, (before if slot < HALO else after)[source : source + 8], height)
            at += height
        put(lines + 30 + f * 2, edge[f * 8 : f * 8 + 8], 2)
        put(lines + 40 + f, beyond(edges_x, f), 1)


def assemble_speeds(wide, state, beside_x, above, below):
    cells_x = state.shape[1]
    after, before = sides_of(beside_x)
    for f in range(4):
        for x in range(cells_x):
            wide[f, 1 + x, 0:8] = state[f, x]
            at = (f * cells_x + x) * HALO
            wide[f, 1 + x, 8:9] = above[at : at + 1]
            wide[f, 1 + x, 15:16] = below[at + HALO - 1 : at + HALO]
        for slot, plane, source in ((HALO - 1, 0, before), (HALO, cells_x + 1, after)):
            at = (f * 2 * HALO + slot) * 8
            wide[f, plane, 0:8] = source[at : at + 8]


def assemble(wide, rim, state, edge, beside_x, edges_x, above, below):
    cells_x = state.shape[1]
    after, before = sides_of(beside_x)
    lines = 5 * cells_x * HALO
    for f in range(5):
        for x in range(cells_x):
            wide[f, HALO + x, 0:8] = state[f, x]
            at = (f * cells_x + x) * HALO
            wide[f, HALO + x, 8 : 8 + HALO] = above[at : at + HALO]
            wide[f, HALO + x, 16 - HALO : 16] = below[at : at + HALO]
        for slot in range(2 * HALO):
            plane = slot if slot < HALO else cells_x + slot
            at = (f * 2 * HALO + slot) * 8
            wide[f, plane, 0:8] = (before if slot < HALO else after)[at : at + 8]
        at = lines + f * 6
        for slot, height in ((1, 1), (2, 2), (3, 2), (4, 1)):
            plane = slot if slot < HALO else cells_x + slot
            wide[f, plane, 8 : 8 + height] = above[at : at + height]
            wide[f, plane, 16 - height : 16] = below[at : at + height]
            at += height
        rim[f, 0:8, 0:128] = edge[f * 8 : f * 8 + 8]
        rim[f, 0:8, 128:256] = beyond(edges_x, f)
        at = lines + 30 + f * 2
        rim[f, 8:10, 0:128] = above[at : at + 2]
        rim[f, 14:16, 0:128] = below[at : at + 2]
        at = lines + 40 + f
        rim[f, 8:9, 128:256] = above[at : at + 1]
        rim[f, 15:16, 128:256] = below[at : at + 1]


def primitive(rho, mx, my, mz, energy):
    inverse = 1.0 / rho
    u, v, w = mx * inverse, my * inverse, mz * inverse
    p = (HEAT_RATIO - 1.0) * (energy - 0.5 * (mx * u + my * v + mz * w))
    return u, v, w, p, jnp.sqrt(HEAT_RATIO * jnp.abs(p) * inverse)


def chunks(first, last, size):
    return [(i, min(i + size, last)) for i in range(first, last, size)]


def derive_planes(wide, derived, first, last):
    for i, j in chunks(first, last, 4):
        for k, value in enumerate(primitive(*[wide[f, i:j] for f in range(5)])):
            derived[k, i:j] = value


def derive_speeds(wide, derived, first, last):
    for i, j in chunks(first, last, 5):
        inverse = 1.0 / wide[0, i:j]
        for k in range(3):
            derived[k, i:j] = wide[1 + k, i:j] * inverse


def with_flux(fields, other, along):
    speed, p = other[along], other[3]
    out = [fields[1 + along]]
    for k in range(3):
        value = fields[1 + k] * speed
        out.append(value + p if k == along else value)
    out.append((fields[4] + p) * speed)
    return fields, out, jnp.abs(speed) + other[4]


def face(left, right):
    (fields_l, flux_l, speed_l), (fields_r, flux_r, speed_r) = left, right
    speed = jnp.maximum(speed_l, speed_r)
    viscous = speed + 2.0 * VISCOSITY
    return [
        (flux_l[f] + flux_r[f]) - (viscous if 1 <= f <= 3 else speed) * (fields_r[f] - fields_l[f])
        for f in range(5)
    ]


def rolled(here, shift, axis):
    fields, flux, speed = here
    return (
        [pltpu.roll(a, shift, axis) for a in fields],
        [pltpu.roll(a, shift, axis) for a in flux],
        pltpu.roll(speed, shift, axis),
    )


def rim_section(fields, start, mix):
    other = primitive(*fields)
    here = with_flux(fields, other, 2)
    along_z = face(here, rolled(here, 255, 1))
    if mix is None:
        return other, along_z, None
    total = [g - pltpu.roll(g, 1, 1) for g in along_z]
    for along, step, axis, size in ((0, 16, 1, 256), (1, 1, 0, 16)):
        here = with_flux(fields, other, along)
        faces = face(here, rolled(here, size - step, axis))
        total = [total[f] + (faces[f] - pltpu.roll(faces[f], step, axis)) for f in range(5)]
    out = []
    for f in range(5):
        value = fields[f] - (0.5 * TIME_STEP) * total[f]
        out.append(mix[0] * start[f] + mix[1] * value if mix[0] != 0.0 else value)
    return other, along_z, out


def to_ends(values, after, rows, first, last, ends):
    slot = lax.broadcasted_iota(jnp.int32, (rows, 256), 1) % 16
    for f, value in enumerate(values):
        value = value[0:rows]
        value = jnp.where(slot == 9, pltpu.roll(value, 9 - after, 1), value)
        for x in range(first, last):
            at = x % 16 // 8 * 128
            move = (118 - x % 8 * 16) % 128
            tile = value[:, at : at + 128]
            ends[f, x - first, 0:rows] = pltpu.roll(tile, move, 1) if move else tile


def flow_rate_section(wide, derived, ends, start, offset, mix, write, inner=False):
    depth = wide.shape[1]
    rows = slice(0, 8) if inner else slice(None)
    size = 4 if inner else 2

    def planes(i, j, kept, along):
        fields = [wide[f, i:j, kept] for f in range(5)]
        return with_flux(fields, [derived[f, i:j, kept] for f in range(5)], along)

    def cut(here, i, j):
        return [a[i:j] for a in here[0]], [a[i:j] for a in here[1]], here[2][i:j]

    for i, j in chunks(1, depth - 1, size):
        count = j - i
        lane = lax.broadcasted_iota(jnp.int32, (count, 8 if inner else 16, 128), 2)
        here = planes(i - 1, j + 1, rows, 0)
        faces = face(cut(here, 0, count + 1), cut(here, 1, count + 2))
        total = [g[1:] - g[:-1] for g in faces]
        here = planes(i, j, slice(None), 1)
        faces = face(here, rolled(here, 15, 1))
        for f in range(5):
            change = faces[f] - pltpu.roll(faces[f], 1, 1)
            total[f] = total[f] + (change[:, 0:8] if inner else change)
        here = planes(i, j, rows, 2)
        faces = face(here, rolled(here, 127, 2))
        for f in range(5):
            end = ends[f, i - 1 : j - 1, rows]
            value = jnp.where(lane == 127, end, faces[f])
            total[f] = total[f] + (value - jnp.where(lane == 0, end, pltpu.roll(value, 1, 2)))
        for f in range(5):
            value = wide[f, i:j, rows] - (0.5 * TIME_STEP) * total[f]
            if mix[0] != 0.0:
                value = mix[0] * start[f, i + offset : j + offset, rows] + mix[1] * value
            write(slice(i - 1, j - 1), f, value)


def lamb(derived, ends, first, cells_x, lamb_rows):
    for i, j in chunks(first, first + cells_x, 4):
        count = j - i
        lane = lax.broadcasted_iota(jnp.int32, (count, 8, 128), 2)
        vel = [derived[c, i:j, 0:8] for c in range(3)]
        along_x = [derived[c, i + 1 : j + 1, 0:8] - derived[c, i - 1 : j - 1, 0:8] for c in range(3)]
        along_y = []
        for c in range(3):
            column = derived[c, i:j]
            along_y.append((pltpu.roll(column, 15, 1) - pltpu.roll(column, 1, 1))[:, 0:8])
        along_z = []
        for c in range(2):
            end = ends[c, i - first : j - first, 0:8]
            after = jnp.where(lane == 127, end, pltpu.roll(vel[c], 127, 2))
            along_z.append(after - jnp.where(lane == 0, end, pltpu.roll(vel[c], 1, 2)))
        curl = [
            0.5 * (along_y[2] - along_z[1]),
            0.5 * (along_z[0] - along_x[2]),
            0.5 * (along_x[1] - along_y[0]),
        ]
        at = slice((i - first) * 8, (j - first) * 8)
        lamb_rows[0, at] = (curl[1] * vel[2] - curl[2] * vel[1]).reshape(count * 8, 128)
        lamb_rows[1, at] = (curl[2] * vel[0] - curl[0] * vel[2]).reshape(count * 8, 128)
        lamb_rows[2, at] = (curl[0] * vel[1] - curl[1] * vel[0]).reshape(count * 8, 128)


def project(lamb_rows, pair, spread, send, base):
    peers = send.shape[0]
    fold = fold_of(peers, spread.shape[0] // 8)
    height = 64 // fold
    group = lax.broadcasted_iota(jnp.int32, (height, 128), 1) // (128 // fold)
    modes = dot_three(pair[...], jnp.concatenate([lamb_rows[c] for c in range(3)], 1))
    modes = jnp.concatenate([modes[:, c * 128 : c * 128 + 128] for c in range(3)], 0)
    sent = dot_three(modes, spread[...])
    for c in range(3):
        for peer in range(peers):
            mine = sent[c * 64 : c * 64 + 64, peer * 128 : peer * 128 + 128]
            folded = mine[0:height]
            for g in range(1, fold):
                folded = jnp.where(group == g, mine[g * height : g * height + height], folded)
            send[peer, base + c * height : base + c * height + height] = folded


def flow_sources_body(count, state, edge, *refs):
    beside_x, refs = refs[:count], refs[count:]
    got_b, got_a, pair, spread, labels, _, send, wide, derived, lamb_rows, ends, above, below = refs
    cells_x = state.shape[1]
    above[...], below[...] = paired(is_odd("fy"), got_a[...], got_b[0 : got_a.shape[0]])
    assemble_speeds(wide, state, beside_x, above, below)
    derive_speeds(wide, derived, 0, cells_x + 2)
    inverse = 1.0 / edge[0:8]
    speeds = [jnp.concatenate([edge[k * 8 : k * 8 + 8] * inverse] * 2, 1) for k in (1, 2)]
    to_ends(speeds, 3, 8, 0, cells_x, ends)
    lamb(derived, ends, 1, cells_x, lamb_rows)
    project(lamb_rows, pair, spread, send, 0)
    send[:, send.shape[1] - 8 :] = labels[...]


def writer(target):
    def write(i, f, value):
        target[f, i] = value

    return write


def flow_stages_body(count, state, edge, *refs):
    beside_x, edges_x, refs = refs[:count], refs[count : 2 * count], refs[2 * count :]
    got_b, got_a, pair, spread, _, second, derived, ends_out, send, *refs = refs
    lamb_rows, ends, first, wide, rim, above, below = refs
    above[...], below[...] = paired(is_odd("fy"), got_a[...], got_b[0 : got_a.shape[0]])
    assemble(wide, rim, state, edge, beside_x, edges_x, above, below)
    planes = wide.shape[1]
    cells_x = planes - 2 * HALO
    size = send.shape[1] // 2
    rim_start = [rim[f] for f in range(5)]
    derive_planes(wide, derived, 0, planes)
    _, along_z, rim_first = rim_section(rim_start, None, MIXES[0])
    to_ends(along_z, 2, 16, -2, cells_x + 2, ends)
    flow_rate_section(wide, derived, ends, wide, 0, MIXES[0], writer(first))
    derive_planes(first, derived, 0, planes - 2)
    other, along_z, rim_second = rim_section(rim_first, [rim[f] for f in range(5)], MIXES[1])
    to_ends(other[0:2], 3, 8, 0, cells_x, ends)
    lamb(derived, ends, 2, cells_x, lamb_rows)
    project(lamb_rows, pair, spread, send, 0)
    to_ends(along_z, 2, 16, -1, cells_x + 1, ends)
    flow_rate_section(first, derived, ends, wide, 1, MIXES[1], writer(second))
    derive_planes(second, derived, 0, planes - 4)
    other, along_z, _ = rim_section(rim_second, None, None)
    to_ends(other[0:2], 3, 8, 0, cells_x, ends)
    lamb(derived, ends, 1, cells_x, lamb_rows)
    project(lamb_rows, pair, spread, send, size)
    to_ends(along_z, 2, 8, 0, cells_x, ends_out)


def flow_last_body(second, derived, ends, state, out, done):
    done[...] = jnp.zeros(done.shape, F32)
    flow_rate_section(second, derived, ends, state, -1, MIXES[2], writer(out), inner=True)


def faces_out(state, rear, front):
    lane = lax.broadcasted_iota(jnp.int32, (32, 128), 1) // 16
    for c in range(4):
        front[c * 8 : c * 8 + 8] = state[c, 56:64]
        rear[c * 8 : c * 8 + 8] = state[c, 0:8]
        front[32 + c * 8 : 40 + c * 8] = state[c, pl.ds(7, 8, stride=8), :]
        rear[32 + c * 8 : 40 + c * 8] = state[c, pl.ds(0, 8, stride=8), :]
    rows = state[...].reshape(256, 128)
    last = jnp.zeros((32, 128), F32)
    first = jnp.zeros((32, 128), F32)
    for j in range(8):
        piece = rows[j * 32 : j * 32 + 32]
        last = jnp.where(lane == j, pltpu.roll(piece, (j * 16 + 16) % 128, 1), last)
        first = jnp.where(lane == j, pltpu.roll(piece, j * 16, 1) if j else piece, first)
    front[64:96] = last
    rear[64:96] = first


def faces_sent(odd, state, message_a, message_b):
    size = message_a.shape[0]
    faces_out(state, message_b, message_a)
    message_a[...], message_b[0:size] = paired(odd, message_a[...], message_b[0:size])
    if message_b.shape[0] > size:
        message_b[size:] = jnp.zeros((message_b.shape[0] - size, 128), F32)


def lift(total, before, after, sides, factor):
    def place(face, rows, target):
        value = factor * dot_exact_right(rows, sides[face])
        for c in range(4):
            total[c, target, :] += value[c * 8 : c * 8 + 8]

    place(0, before[0:32], pl.ds(0, 8))
    place(1, after[0:32], pl.ds(56, 8))
    place(2, before[32:64], pl.ds(0, 8, stride=8))
    place(3, after[32:64], pl.ds(7, 8, stride=8))


def rate_local(state, deriv_rows, deriv_lanes, speed, sides):
    fields = [state[c] for c in range(4)]
    by_rows = dot_three(deriv_rows[...], jnp.concatenate(fields[0:3], 1))
    by_lanes = dot_three(jnp.concatenate([fields[0], fields[3]], 0), deriv_lanes[...])
    divergence = by_rows[0:64, 128:256] + by_rows[64:128, 256:384] + by_lanes[64:128]
    rates = [
        -(speed[...] * speed[...]) * divergence,
        -by_rows[0:64, 0:128],
        -by_rows[64:128, 0:128],
        -by_lanes[0:64],
    ]
    row = lax.broadcasted_iota(jnp.int32, (64, 128), 0)
    lane = lax.broadcasted_iota(jnp.int32, (64, 128), 1)
    count = jnp.zeros((64, 128), F32)
    for value in (row // 8, row % 8, lane // 16):
        count = count + jnp.where((value == 0) | (value == 7), PENALTY, 0.0)
    side = PENALTY * dot_exact_right(state[...].reshape(256, 128), sides[4])
    return [rates[c] - count * fields[c] + side[c * 64 : c * 64 + 64] for c in range(4)]


def acoustic_local_body(mix, state, start, deriv_rows, deriv_lanes, speed, sides, out, front, rear):
    rates = rate_local(state, deriv_rows, deriv_lanes, speed, sides)
    for c in range(4):
        value = state[c] + TIME_STEP * rates[c]
        if mix[0] != 0.0:
            value = mix[0] * start[c] + mix[1] * value
        out[c] = value
    faces_out(state, rear, front)
    lift(out, front, rear, sides, TIME_STEP * mix[1] * PENALTY)


def acoustic_start_body(given, local, _, state, message_a, message_b, turned, stored):
    count = given.shape[0]
    for e in range(count):
        for t in range(4):
            stored[t, 4 * e : 4 * e + 4] = given[e, :, t * 128 : t * 128 + 128]
    for t in range(4):
        rows = [stored[t, pl.ds(c, count, stride=4), :] for c in range(4)]
        rows = jnp.concatenate(rows + [jnp.zeros((128 - 4 * count, 128), F32)], 0)
        turned[t * 128 : t * 128 + 128] = rows.T
    lane = lax.broadcasted_iota(jnp.int32, (64, 128), 1) // count
    fields = [jnp.zeros((64, 128), F32)] * 4
    for z in range(8):
        piece = turned[pl.ds(z, 64, stride=8), :]
        for c in range(4):
            move = (z - c) * count % 128
            fields[c] = jnp.where(lane == z, pltpu.roll(piece, move, 1) if move else piece, fields[c])
    for c in range(4):
        state[c] = fields[c]
    faces_sent(is_odd("fz"), state, message_a, message_b)
    message_b[96:104] = local[...]


def natural_order(state, out, turned, stored):
    count = out.shape[0]
    lane = lax.broadcasted_iota(jnp.int32, (64, 128), 1) // count
    for z in range(8):
        value = jnp.zeros((64, 128), F32)
        for c in range(4):
            move = (c - z) * count % 128
            value = jnp.where(lane == c, pltpu.roll(state[c], move, 1) if move else state[c], value)
        turned[pl.ds(z, 64, stride=8), :] = value
    for t in range(4):
        rows = turned[t * 128 : t * 128 + 128].T
        for c in range(4):
            stored[t, pl.ds(c, count, stride=4), :] = rows[c * count : c * count + count]
    for e in range(count):
        for t in range(4):
            out[e, :, t * 128 : t * 128 + 128] = stored[t, 4 * e : 4 * e + 4]


def remote_part(out, before, after, sides_far, factor):
    lift(out, before, after, sides_far, factor)
    lane = lax.broadcasted_iota(jnp.int32, (32, 128), 1) // 16
    last, first = before[64:96], after[64:96]
    pieces = []
    for j in range(8):
        left = pltpu.roll(last, 128 - j * 16, 1) if j else last
        right = pltpu.roll(first, (144 - j * 16) % 128, 1) if j != 1 else first
        pieces.append(jnp.where(lane == 0, left, jnp.where(lane == 1, right, 0.0)))
    value = factor * dot_exact_right(jnp.concatenate(pieces, 0), sides_far[4])
    for c in range(4):
        out[c] += value[c * 64 : c * 64 + 64]


def arrived(odd, got_a, got_b, before, after):
    none = jnp.zeros((96, 128), F32)
    near = none if got_a is None else got_a[0:96]
    after[...], before[...] = paired(odd, near, none if got_b is None else got_b[0:96])


def acoustic_first_body(partial, got_a, got_b, sides_far, received, _, out, message_a, message_b, before, after, source):
    odd = is_odd("fz")
    place(received, received, source, 0)
    arrived(odd, got_a, got_b, before, after)
    out[0] = partial[0]
    for c in range(3):
        out[1 + c] = partial[1 + c] + (TIME_STEP * MIXES[0][1]) * source[c]
    remote_part(out, before, after, sides_far, TIME_STEP * MIXES[0][1] * PENALTY)
    faces_sent(odd, out, message_a, message_b)


def acoustic_near_body(
    partial, got_a, sides_far, received, labelled, _, __, out, message_b, before, after, source, spare
):
    odd = is_odd("fz")
    place(received, labelled, source, 0)
    arrived(odd, got_a, None, before, after)
    out[0] = partial[0]
    for c in range(3):
        out[1 + c] = partial[1 + c] + (TIME_STEP * MIXES[1][1]) * source[c]
    remote_part(out, before, after, sides_far, TIME_STEP * MIXES[1][1] * PENALTY)
    faces_sent(odd, out, spare, message_b)


def acoustic_rest_body(partial, got_b, sides_far, out, message_a, before, after, spare):
    odd = is_odd("fz")
    arrived(odd, None, got_b, before, after)
    out[...] = partial[...]
    remote_part(out, before, after, sides_far, TIME_STEP * MIXES[1][1] * PENALTY)
    faces_sent(odd, out, message_a, spare)


def mirror_body(sent_b, sides_partner, sent_a, change, later_a, before, after, spare, state):
    later_a[...] = sent_a[...]
    odd = jnp.logical_not(is_odd("fz"))
    arrived(odd, None, sent_b, before, after)
    state[...] = jnp.zeros(state.shape, F32)
    remote_part(state, before, after, sides_partner, TIME_STEP * MIXES[1][1] * PENALTY)
    faces_sent(odd, state, spare, change)


def acoustic_last_body(
    partial, got_a, got_b, change, sides_far, source, given_out, before, after, out, turned, stored
):
    odd = is_odd("fz")
    after[...], before[...] = paired(odd, got_a[0:96], got_b[0:96] + change[...])
    out[0] = partial[0]
    for c in range(3):
        out[1 + c] = partial[1 + c] + (TIME_STEP * MIXES[2][1]) * source[c]
    remote_part(out, before, after, sides_far, TIME_STEP * MIXES[2][1] * PENALTY)
    natural_order(out, given_out, turned, stored)


def place(received, labelled, out, base):
    peers, size = labelled.shape[0], labelled.shape[1]
    fold = 192 // (size - 8)
    height = 64 // fold
    target = lax.broadcasted_iota(jnp.int32, (128, 128), 0)
    lane = lax.broadcasted_iota(jnp.int32, (128, 128), 1)
    total = None
    for peer in range(peers):
        label = labelled[peer, size - 8 : size - 7, :]
        label = jnp.broadcast_to(label, (128, 128)).astype(jnp.int32)
        hit = (label == target % 16) & (lane % 8 == target // 16)
        chosen = [jnp.where(hit & (lane // (128 // fold) == g), 1.0, 0.0) for g in range(fold)]
        chosen = jnp.concatenate(chosen, 0).astype(BF16)
        high, low = parts(received[peer, base : base + 3 * height])
        dims = (((1,), (1,)), ((), ()))
        value = lax.dot_general(high, chosen, dims, preferred_element_type=F32)
        value = value + lax.dot_general(low, chosen, dims, preferred_element_type=F32)
        total = value if total is None else total + value
    for c in range(3):
        for g in range(fold):
            at = c * height
            out[c, g * height : g * height + height] = total[at : at + height, g * 128 : g * 128 + 128]


def place_last_body(received, labelled, out):
    place(received, labelled, out, received.shape[1] // 2)


def kron_part(matrix, shape, rows_by, columns_by):
    row = lax.broadcasted_iota(jnp.int32, (shape[0], 8), 0)
    level = lax.broadcasted_iota(jnp.int32, (shape[0], 8), 1)
    left = (row // rows_by % 8 == level).astype(F32)
    level = lax.broadcasted_iota(jnp.int32, (8, shape[1]), 0)
    column = lax.broadcasted_iota(jnp.int32, (8, shape[1]), 1)
    right = (column // columns_by % 8 == level).astype(F32)
    return dot_full(dot_full(left, matrix), right)


def far_tables(wanted, count, far):
    size = 8 * count
    row = lax.broadcasted_iota(jnp.int32, (size, size), 0)
    level_out = lax.broadcasted_iota(jnp.int32, (size, size), 1) // count
    level, element = row // count, row % count
    for facet in range(4):
        shift = -count if facet % 2 == 0 else count
        choice = jnp.broadcast_to(wanted[facet : facet + 1], (size, size))
        far[facet] = jnp.where((level == level_out) & (element + shift == choice), 1.0, 0.0).astype(BF16)
    lower = jnp.broadcast_to(wanted[4:5], (size, size))
    upper = jnp.broadcast_to(wanted[5:6], (size, size))
    hit = (level == 0) & (level_out == 0) & (element - count == lower)
    hit = hit | ((level == 1) & (level_out == 7) & (element + count == upper))
    far[4] = jnp.where(hit, 1.0, 0.0).astype(BF16)


def partner_tables_body(count, got_b, far):
    row = lax.broadcasted_iota(jnp.int32, (count, 8 * count), 0)
    column = lax.broadcasted_iota(jnp.int32, (count, 8 * count), 1)
    repeat = (column % count == row).astype(F32)
    wanted = dot_full(got_b[96:104, 0:count], repeat).astype(jnp.int32)
    far_tables(wanted, count, far)


def tables_body(
    packed,
    near,
    far,
    deriv_rows,
    deriv_lanes,
    pair,
    spread,
    labels,
    speed,
):
    size = near.shape[1]
    count = size // 8
    blocks = spread.shape[0] // 8

    def place_of(shape):
        return (lax.broadcasted_iota(jnp.int32, shape, 0), lax.broadcasted_iota(jnp.int32, shape, 1))

    row, column = place_of((count, size))
    repeat = (column % count == row).astype(F32)
    speed[...] = dot_full(packed[24:25, 0:count], repeat)
    wanted = dot_full(packed[16:24, 0:count], repeat).astype(jnp.int32)
    row, column = place_of((size, size))
    level, element = row // count, row % count
    level_out = column // count
    for facet in range(4):
        choice = jnp.broadcast_to(wanted[facet : facet + 1], (size, size))
        near[facet] = jnp.where((level == level_out) & (element == choice), 1.0, 0.0).astype(BF16)
    lower = jnp.broadcast_to(wanted[4:5], (size, size))
    upper = jnp.broadcast_to(wanted[5:6], (size, size))
    hit = (level == 7) & (level_out == 0) & (element == lower)
    hit = hit | ((level == 0) & (level_out == 7) & (element == upper))
    near[4] = jnp.where(hit, 1.0, 0.0).astype(BF16)
    far_tables(wanted, count, far)

    row, column = place_of((64, 64))
    slopes, modes = packed[0:8, 0:8], packed[8:16, 0:8]
    outer = kron_part(slopes, (64, 64), 8, 8)
    inner = kron_part(slopes, (64, 64), 1, 1)
    deriv_rows[0:64] = jnp.where(row % 8 == column % 8, outer, 0.0)
    deriv_rows[64:128] = jnp.where(row // 8 == column // 8, inner, 0.0)
    row, column = place_of((size, size))
    lanes = kron_part(slopes.T, (size, size), count, count)
    deriv_lanes[...] = jnp.where(row % count == column % count, lanes, 0.0)
    pair[...] = kron_part(modes, (64, 64), 8, 8) * kron_part(modes, (64, 64), 1, 1)

    peers = labels.shape[0]
    capacity = capacity_of(peers, blocks)
    row, column = place_of((blocks, blocks))

    def upright(values):
        return jnp.sum(jnp.where(row == column, values, 0.0), 1, keepdims=True)

    owner_row = packed[25:26, 0:blocks]
    owner_column = upright(owner_row)
    earlier = (owner_column == owner_row) & (column < row)
    position = jnp.sum(jnp.where(earlier, 1.0, 0.0), 1, keepdims=True)
    slot = owner_column * capacity + position
    element_column = upright(packed[26:27, 0:blocks])
    row, column = place_of((8 * blocks, blocks))
    repeat = (row // 8 == column).astype(F32)
    slot = dot_full(repeat, jnp.broadcast_to(slot, (blocks, 128)))
    element = dot_full(repeat, jnp.broadcast_to(element_column, (blocks, 128)))
    row, column = place_of((8 * blocks, 128))
    values = kron_part(modes.T, (8 * blocks, 128), 1, 1)
    inside = column % (8 * capacity) // 8
    for peer in range(peers):
        chosen = slot == (inside + peer * capacity).astype(F32)
        spread[:, peer * 128 : peer * 128 + 128] = jnp.where(chosen, values, 0.0)
        named = jnp.where(chosen & (row % 8 == 0), element + 1.0, 0.0)
        labels[peer] = jnp.broadcast_to(jnp.sum(named, 0, keepdims=True) - 1.0, (8, 128))


def shifted(sizes, shifts):
    pairs = []
    for index in np.ndindex(*sizes):
        source = [(i + s) % n for i, s, n in zip(index, shifts, sizes)]
        pairs.append((int(np.ravel_multi_index(source, sizes)), int(np.ravel_multi_index(index, sizes))))
    return pairs


def partners(sizes, axis, second):
    pairs = []
    for index in np.ndindex(*sizes):
        source = list(index)
        step = 1 if (index[axis] % 2 == 0) != second else -1
        source[axis] = (index[axis] + step) % sizes[axis]
        pairs.append((int(np.ravel_multi_index(source, sizes)), int(np.ravel_multi_index(index, sizes))))
    return pairs


def per_device(
    density,
    velocity,
    pressure,
    acoustic,
    sound_speed,
    derivative,
    mode_basis,
    neighbours,
    block_owner,
    block_element,
):
    size_x, size_y, size_z = lax.axis_size("fx"), lax.axis_size("fy"), lax.axis_size("fz")
    devices = size_x * size_y * size_z
    cells_x = density.shape[0]
    elements = acoustic.shape[0]
    device = lax.axis_index(("fx", "fy", "fz"))

    names = ("fx", "fy", "fz")

    rows = 5 * cells_x * 8
    tiles = -(-rows // 128)
    square = velocity[0] * velocity[0] + velocity[1] * velocity[1] + velocity[2] * velocity[2]
    energy = pressure / (HEAT_RATIO - 1.0) + 0.5 * density * square
    rest = ((0, 0), (0, 0), (0, 0))
    state = jnp.pad(density[None], ((0, 4),) + rest) + jnp.pad(density * velocity, ((1, 1),) + rest)
    state = state + jnp.pad(energy[None], ((4, 0),) + rest)
    x_rows = 5 * 2 * HALO * 8
    flow_a, flow_b, along_x = call(
        pack_start_body, [(tiles * 8, 128), (tiles * 8, 128), (x_rows, 128)], state
    )
    edge_a = lax.ppermute(flow_a, "fz", partners((size_z,), 0, False))
    edge_b = lax.ppermute(flow_b, "fz", partners((size_z,), 0, True))
    x_steps = (1,) if size_x == 2 else (1, -1)
    beside_x = [lax.ppermute(along_x, "fx", shifted((size_x,), (step,))) for step in x_steps]

    local = (neighbours - device * elements).T

    near_pairs = [(i ^ 1, i) for i in range(devices)]
    far_pairs = [pair for i in range(1, devices - 1, 2) for pair in ((i, i + 1), (i + 1, i))]

    def traces(to_a, to_b):
        far_got = lax.ppermute(to_b, names, far_pairs)
        return lax.ppermute(to_a, names, near_pairs), far_got

    size = 8 * elements
    held = (4, 64, size)
    faces = (96, size)
    sides = [pltpu.VMEM(faces, F32)] * 2
    turning = [pltpu.VMEM((512, 128), F32), pltpu.VMEM((4, 4 * elements, 128), F32)]
    sound, to_a, to_b = call(
        acoustic_start_body,
        [held, faces, (faces[0] + 8, size)],
        acoustic,
        jnp.pad(local.astype(F32), ((0, 2), (0, size - elements))),
        edge_a,
        scratch=turning,
        last=1,
    )
    got_a, got_b = traces(to_a, to_b)

    edge = call(
        pack_next_body,
        [(40, 128)],
        state,
        flow_a,
        flow_b,
        edge_a,
        edge_b,
        to_a,
        last=1,
    )[0]
    edges_x = [lax.ppermute(edge, "fx", shifted((size_x,), (step,))) for step in x_steps]
    y_shape = (5 * cells_x * HALO + 48, 128)
    y_a, y_b = call(pack_last_body, [y_shape, (y_shape[0] + 8, 128)], state, edge, *beside_x, *edges_x, got_a, last=1, cost=1)
    y_second = lax.ppermute(y_b, "fy", partners((size_y,), 0, True))
    y_first = lax.ppermute(y_a, "fy", partners((size_y,), 0, False))

    blocks = block_owner.size
    width = max(elements, blocks)

    def piece(values, first):
        values = values.astype(F32)
        return jnp.pad(values, ((first, 32 - first - values.shape[0]), (0, width - values.shape[1])))

    packed = (
        piece(derivative, 0)
        + piece(mode_basis, 8)
        + piece(local, 16)
        + piece(sound_speed.reshape(1, elements), 24)
        + piece(block_owner.reshape(1, blocks), 25)
        + piece(block_element.reshape(1, blocks), 26)
    )
    table = jax.ShapeDtypeStruct((5, size, size), BF16)
    near, far, deriv_rows, deriv_lanes, pair, spread, labels, speed = call(
        tables_body,
        [
            table,
            table,
            (128, 64),
            (size, size),
            (64, 64),
            (8 * blocks, size_y * 128),
            (size_y, 8, 128),
            (1, size),
        ],
        packed,
        cost=1,
    )

    fold = fold_of(size_y, blocks)
    wide = cells_x + 2 * HALO
    rows_scratch = pltpu.VMEM((3, 64, 128), F32)

    def planes(count):
        return (5, count, 16, 128)

    def route(send):
        return lax.all_to_all(send, "fy", split_axis=0, concat_axis=0, tiled=True)

    def local_part(mix, now):
        return call(
            functools.partial(acoustic_local_body, mix),
            [held],
            now,
            sound,
            deriv_rows,
            deriv_lanes,
            speed,
            near,
            scratch=sides,
            cost=1,
        )[0]

    partial = local_part(MIXES[0], sound)
    y_scratch = [pltpu.VMEM(y_shape, F32), pltpu.VMEM(y_shape, F32)]
    send = call(
        functools.partial(flow_sources_body, len(beside_x)),
        [(size_y, 192 // fold + 8, 128)],
        state,
        edge,
        *beside_x,
        y_second,
        y_first,
        pair,
        spread,
        labels,
        got_b,
        last=1,
        scratch=[
            pltpu.VMEM((4, cells_x + 2, 16, 128), F32),
            pltpu.VMEM((3, cells_x + 2, 16, 128), F32),
            rows_scratch,
            pltpu.VMEM((2, cells_x, 8, 128), F32),
        ]
        + y_scratch,
    )[0]
    received = route(send)
    second, derived, ends, send = call(
        functools.partial(flow_stages_body, len(edges_x)),
        [
            planes(wide - 4),
            planes(wide),
            (5, cells_x, 8, 128),
            (size_y, 2 * 192 // fold, 128),
        ],
        state,
        edge,
        *beside_x,
        *edges_x,
        y_second,
        y_first,
        pair,
        spread,
        partial,
        last=1,
        scratch=[
            rows_scratch,
            pltpu.VMEM(planes(wide - 2), F32),
            pltpu.VMEM(planes(wide - 2), F32),
            pltpu.VMEM(planes(wide), F32),
            pltpu.VMEM((5, 16, 256), F32),
        ]
        + y_scratch,
    )

    far_partner = call(functools.partial(partner_tables_body, elements), [table], got_b)[0]
    longer = (faces[0] + 32, size)
    near_face = pltpu.VMEM(faces, F32)
    sound_one, to_a, to_b = call(
        acoustic_first_body,
        [held, faces, longer],
        partial,
        got_a,
        got_b,
        far,
        received,
        send,
        scratch=sides + [rows_scratch],
        last=1,
    )
    labelled, received = received, route(send)
    got_b = lax.ppermute(to_b, names, far_pairs)
    change, to_a = call(
        mirror_body,
        [faces, faces],
        to_b,
        far_partner,
        to_a,
        scratch=sides + [near_face, pltpu.VMEM(held, F32)],
        cost=1,
    )
    got_a = lax.ppermute(to_a, names, near_pairs)
    flow_state, done = call(
        flow_last_body, [(5, cells_x, 8, 128), (8, 128)], second, derived, ends, state
    )
    partial = local_part(MIXES[1], sound_one)
    partial, to_b = call(
        acoustic_near_body,
        [held, longer],
        partial,
        got_a,
        far,
        received,
        labelled,
        change,
        done,
        scratch=sides + [rows_scratch, near_face],
    )
    got_b_last = lax.ppermute(to_b, names, far_pairs)
    sound_two, to_a = call(
        acoustic_rest_body, [held, faces], partial, got_b, far, scratch=sides + [near_face]
    )
    got_a = lax.ppermute(to_a, names, near_pairs)
    source_three = call(place_last_body, [(3, 64, 128)], received, labelled)[0]
    partial = local_part(MIXES[2], sound_two)
    sound_state = call(
        acoustic_last_body,
        [(elements, 4, 512)],
        partial,
        got_a,
        got_b_last,
        change,
        far,
        source_three,
        scratch=sides + [pltpu.VMEM(held, F32)] + turning,
    )[0]
    return (flow_state, sound_state)


def solution(mesh):
    placed = (
        P("fx", "fy", "fz"),
        P(None, "fx", "fy", "fz"),
        P("fx", "fy", "fz"),
        P(("fx", "fy", "fz"), None, None),
        P(("fx", "fy", "fz")),
        P(),
        P(),
        P(("fx", "fy", "fz"), None),
        P("fx", "fy", "fz", None, None),
        P("fx", "fy", "fz", None),
    )
    return jax.shard_map(
        per_device,
        mesh=mesh,
        in_specs=placed,
        out_specs=(P(None, "fx", "fy", "fz"), P(("fx", "fy", "fz"), None, None)),
        check_vma=False,
    )
```
